128 devices in a mesh: blk: 32 (over x, z, core), head: 4 (over y).
Axes of the slice: x: 4, y: 4, z: 4, core: 2. Of those that a mesh axis runs over, the one named last changes fastest.
Arguments:
- tokens_in: bfloat16 [2, 16384, 1024], P(None, ('blk', 'head')), may hold values from -6 to 6
- grad_out: bfloat16 [2, 16384, 1024], P(None, ('blk', 'head')), may hold values from -6 to 6
- flags: int32 [2, 32], P(None, 'blk'), may hold values from 0 to 1, as said below
- attn_gain: float32 [1024], replicated, may hold values from 0.1 to 1.9
- mlp_gain: float32 [1024], replicated, may hold values from 0.1 to 1.9
- w_qkv: bfloat16 [1024, 3, 1024], P(None, None, 'head'), may hold values from -0.1875 to 0.1875
- w_out: bfloat16 [1024, 1024], P('head'), may hold values from -0.75 to 0.75
- rel_bias: float32 [32, 8], P(None, 'head'), may hold values from -4 to 4
- state_query: bfloat16 [512, 1024], P(None, 'head'), may hold values from -5 to 5
- state_proj: bfloat16 [8, 128, 256], P('head'), may hold values from -0.5 to 0.5
- forget_bias: float32 [1024], P('head'), may hold values from -2 to 5
- forget_scale: float32 [1024], P('head'), may hold values from -6 to 6
- w_up: bfloat16 [1024, 4096], P(None, 'head'), may hold values from -0.1875 to 0.1875
- w_down: bfloat16 [4096, 1024], P('head'), may hold values from -0.09375 to 0.09375
Outputs:
- out_tokens: float32 [2, 16384, 1024], P(None, ('blk', 'head'))
- grad_tokens: float32 [2, 16384, 1024], P(None, ('blk', 'head'))
- block_states: float32 [2, 32, 512, 1024], P(None, 'blk', None, 'head')
- grad_attn_gain: float32 [1024], replicated
- grad_mlp_gain: float32 [1024], replicated
- grad_qkv: float32 [1024, 3, 1024], P(None, None, 'head')
- grad_out_proj: float32 [1024, 1024], P('head')
- grad_rel_bias: float32 [32, 8], P(None, 'head')
- grad_state_query: float32 [512, 1024], P(None, 'head')
- grad_state_proj: float32 [8, 128, 256], P('head')
- grad_forget_bias: float32 [1024], P('head')
- grad_forget_scale: float32 [1024], P('head')
- grad_up: float32 [1024, 4096], P(None, 'head')
- grad_down: float32 [4096, 1024], P('head')
The draws below stay inside these ranges and needn't reach their ends.
Inputs may be any that keep to these rules, and one draw needn't show every extreme that they name: flags[m, 0] is 1 for every micro-batch; in one micro-batch drawn from the seed every other entry is 0.
All inputs are finite; a program needn't handle non-finite values.
Results may differ from the reference program's by a relative error of at most 0.025.
Values may be sent and summed in bfloat16 or wider, within the bound.
A program may use at most 256 MiB of HBM per device.

```python
import math
import jax
import jax.numpy as jnp
from jax import lax

D = 1024
H = 8
FF = 4096
HD = 128
BLOCK = 512
S = 512
BUCKETS = 32
MAXDIST = 128
MB = 2
TOKENS = 16384
N_BLK = 32


def draw_flags(key, part):
    key = jax.random.fold_in(key, 7)
    first_key, second_key = jax.random.split(key)
    starts = (jax.random.randint(first_key, (MB, N_BLK), 0, 8) == 0).astype(jnp.int32)
    chosen = jax.random.randint(second_key, (), 0, MB)
    batch_pos = lax.broadcasted_iota(jnp.int32, (MB, N_BLK), 0)
    block_pos = lax.broadcasted_iota(jnp.int32, (MB, N_BLK), 1)
    starts = jnp.where(batch_pos == chosen, 0, starts)
    starts = jnp.where(block_pos == 0, 1, starts)
    return starts.astype(jnp.int32)


def level_of(rng, extent, cuts, smallest, largest):
    def one(axis_at, shards_of):
        heights = jax.random.uniform(jax.random.fold_in(jax.random.fold_in(rng, 6), axis_at), (shards_of,), jnp.float32, smallest / len(cuts), largest / len(cuts))
        return jnp.repeat(jnp.exp(heights), extent[axis_at] // shards_of).reshape((-1,) + (1,) * (len(extent) - axis_at - 1))

    loudness = one(*cuts[0])
    for cut in cuts[1:]:
        loudness = loudness * one(*cut)
    return loudness


def noise(stream_key, dims, width, reach, shards=(), kind=jnp.bfloat16):
    level = level_of(stream_key, dims, shards, -0.22, 0.18) if shards else 1.0
    array = jax.random.normal(stream_key, dims, jnp.float32) * width * level
    return jnp.minimum(jnp.maximum(array, -reach), reach).astype(kind)


def setup_inputs(seed: int = 0) -> dict:
    key_list = jax.random.split(jax.random.key(seed), 15)
    tokens_in = noise(key_list[0], (MB, TOKENS, D), 1.0, 6.0, ((1, 128),))
    grad_out = noise(key_list[1], (MB, TOKENS, D), 1.0, 6.0, ((1, 128),))
    flags = draw_flags(jax.random.fold_in(key_list[14], 71), 0)
    attn_gain = jnp.clip(1.0 + 0.18 * jax.random.normal(key_list[3], (D,), jnp.float32), 0.1, 1.9)
    mlp_gain = jnp.clip(1.0 + 0.18 * jax.random.normal(key_list[4], (D,), jnp.float32), 0.1, 1.9)
    w_qkv = noise(key_list[5], (D, 3, D), D ** -0.5, 0.1875, ((2, 4),))
    w_out = noise(key_list[6], (D, D), (D // 16) ** -0.5, 0.75, ((0, 4),))
    rel_bias = noise(key_list[7], (BUCKETS, H), 1.0, 4.0, ((1, 4),), jnp.float32)
    state_query = noise(key_list[8], (S, D), 1.0, 5.0, ((1, 4),))
    state_proj = noise(key_list[9], (H, HD, 2 * HD), HD ** -0.5, 0.5, ((0, 4),))
    forget_bias = jnp.clip(-2.0 + 7.0 * jax.random.uniform(key_list[10], (D,), jnp.float32) ** level_of(key_list[10], (D,), ((0, 4),), -0.2, 0.2), -2.0, 5.0)
    forget_scale = noise(key_list[11], (D,), 1.5, 6.0, ((0, 4),), jnp.float32)
    w_up = noise(key_list[12], (D, FF), D ** -0.5, 0.1875, ((1, 4),))
    w_down = noise(key_list[13], (FF, D), FF ** -0.5, 0.09375, ((0, 4),))
    return {"tokens_in": tokens_in, "grad_out": grad_out, "flags": flags, "attn_gain": attn_gain, "mlp_gain": mlp_gain, "w_qkv": w_qkv, "w_out": w_out, "rel_bias": rel_bias, "state_query": state_query, "state_proj": state_proj, "forget_bias": forget_bias, "forget_scale": forget_scale, "w_up": w_up, "w_down": w_down}


@jax.custom_vjp
def low(v):
    return lax.optimization_barrier(v.astype(jnp.bfloat16)).astype(jnp.float32)

@jax.custom_vjp
def low_back(v):
    return v

def low_keep(v):
    return (low(v), None)

def low_pass(kept, grad):
    return (grad,)

def back_keep(v):
    return (v, None)

def back_low(kept, grad):
    return (low(grad),)
low.defvjp(low_keep, low_pass)
low_back.defvjp(back_keep, back_low)
EPSILON = 1e-06
MASKED = -1e+30
HIGHEST = lax.Precision.HIGHEST

def bucket_index(distance):
    exact_part = BUCKETS // 2
    result = jnp.minimum(distance, exact_part)
    for level in range(1, BUCKETS - exact_part):
        boundary = int(math.ceil(exact_part * (MAXDIST / exact_part) ** (level / (BUCKETS - exact_part))))
        result = result + (distance >= boundary).astype(jnp.int32)
    return result

def window_layout(length):
    query_pos = lax.broadcasted_iota(jnp.int32, (length, 2 * length), 0)
    key_pos = lax.broadcasted_iota(jnp.int32, (length, 2 * length), 1)
    distance = query_pos + length - key_pos
    inside = (distance >= 0) & (distance < length)
    earlier = key_pos < length
    return (bucket_index(jnp.maximum(distance, 0)), inside, earlier)

def rms_norm(values, gain):
    return values * lax.rsqrt(lax.optimization_barrier(jnp.mean(values * values, axis=-1, keepdims=True)) + EPSILON) * gain

def softmax_rows(scores):
    highest = lax.optimization_barrier(jnp.max(scores, axis=-1, keepdims=True))
    expd = jnp.exp(scores - highest)
    return expd / lax.optimization_barrier(jnp.sum(expd, axis=-1, keepdims=True))

def block_step(params, bias_table, carry, inputs):
    attn_gain, mlp_gain, w_qkv, w_out, rel_unused, state_query, state_proj, forget_bias, forget_scale, w_up, w_down = params
    state_before, keys_before, values_before = carry
    rows, flag = inputs
    keep = (1 - flag).astype(jnp.float32)
    scale = HD ** (-0.5)
    bucket, inside, earlier = window_layout(BLOCK)
    normed = low(rms_norm(rows, attn_gain))
    mixed = jnp.dot(normed, w_qkv.reshape(D, 3 * D), precision=HIGHEST).reshape(BLOCK, 3, H, HD)
    queries = low_back(low(mixed[:, 0]))
    keys = low_back(low(mixed[:, 1]))
    values = low_back(low(mixed[:, 2]))
    query_heads = state_query.reshape(S, H, HD)
    update_scores = low_back(jnp.einsum('shd,jhd->hsj', query_heads, keys, precision=HIGHEST) * scale)
    update_weights = low(softmax_rows(update_scores))
    update = low_back(jnp.einsum('hsj,jhd->shd', update_weights, values, precision=HIGHEST))
    unit = (update * lax.rsqrt(lax.optimization_barrier(jnp.mean(update * update, axis=-1, keepdims=True)) + EPSILON)).reshape(S, D)
    forget = jax.nn.sigmoid(forget_bias + forget_scale * unit)
    prior = keep * state_before
    state_after = forget * prior + (1.0 - forget) * unit
    state_heads = low(prior).reshape(S, H, HD)
    state_kv = jnp.einsum('shd,hde->she', state_heads, state_proj, precision=HIGHEST)
    state_keys = low_back(low(state_kv[..., :HD]))
    state_values = low_back(low(state_kv[..., HD:]))
    all_keys = jnp.concatenate([keys_before, keys], 0)
    all_values = jnp.concatenate([values_before, values], 0)
    token_scores = low_back(jnp.einsum('ihd,jhd->hij', queries, all_keys, precision=HIGHEST) * scale) + bias_table
    usable = inside & (jnp.logical_not(earlier) | (flag == 0))
    token_scores = jnp.where(usable[None], token_scores, MASKED)
    state_scores = low_back(jnp.einsum('ihd,shd->his', queries, state_keys, precision=HIGHEST) * scale)
    weights = low(softmax_rows(jnp.concatenate([token_scores, state_scores], -1)))
    attended = jnp.einsum('hij,jhd->ihd', weights[..., :2 * BLOCK], all_values, precision=HIGHEST)
    attended = attended + jnp.einsum('his,shd->ihd', weights[..., 2 * BLOCK:], state_values, precision=HIGHEST)
    attended = low_back(low(attended.reshape(BLOCK, D)))
    branch = low_back(jnp.dot(attended, w_out, precision=HIGHEST))
    middle = rows + branch
    normed_mlp = low(rms_norm(middle, mlp_gain))
    hidden = low_back(jnp.dot(normed_mlp, w_up, precision=HIGHEST))
    active = low(jax.nn.gelu(hidden))
    branch_mlp = low_back(jnp.dot(active, w_down, precision=HIGHEST))
    output = middle + branch_mlp
    return ((state_after, keys, values), (output, state_after))

def forward(params, rows, flags_row):
    bucket, inside, earlier = window_layout(BLOCK)
    bias_table = jnp.moveaxis(params[4][bucket], -1, 0)
    checked = jax.checkpoint(block_step)

    def step(carry, inputs):
        return checked(params, bias_table, carry, inputs)
    start = (jnp.zeros((S, D), jnp.float32), jnp.zeros((BLOCK, H, HD), jnp.float32), jnp.zeros((BLOCK, H, HD), jnp.float32))
    ignored, (outputs, states) = lax.scan(step, start, (rows.reshape(N_BLK, BLOCK, D), flags_row))
    return (outputs.reshape(TOKENS, D), states)

def reference(tokens_in, grad_out, flags, attn_gain, mlp_gain, w_qkv, w_out, rel_bias, state_query, state_proj, forget_bias, forget_scale, w_up, w_down):
    params = tuple((p.astype(jnp.float32) for p in (attn_gain, mlp_gain, w_qkv, w_out, rel_bias, state_query, state_proj, forget_bias, forget_scale, w_up, w_down)))
    zero_grads = tuple((jnp.zeros_like(p) for p in params))

    def micro(total, inputs):
        rows, cotangent, flags_row = inputs
        (outputs, states), pullback = jax.vjp(lambda p, r: forward(p, r, flags_row), params, rows.astype(jnp.float32))
        grads, grad_rows = pullback((cotangent.astype(jnp.float32), jnp.zeros_like(states)))
        total = tuple((a + b for a, b in zip(total, grads)))
        return (total, (outputs, grad_rows, states))
    total, (outputs, grad_rows, states) = lax.scan(micro, zero_grads, (tokens_in, grad_out, flags))
    return (outputs, grad_rows, states, total[0], total[1], total[2], total[3], total[4], total[5], total[6], total[7], total[8], total[9], total[10])
```

```python
import functools
import math

import jax
import jax.numpy as jnp
from jax import lax
from jax.experimental import pallas as pl
from jax.experimental.pallas import tpu as pltpu
from jax.sharding import PartitionSpec as P

BUCKETS = 32
MAXDIST = 128
EPSILON = 1e-06
MASKED = -1e30
TILE = 128
MESH = pl.DeviceIdType.MESH
BF = jnp.bfloat16
F32 = jnp.float32


def bucket_index(distance):
    exact_part = BUCKETS // 2
    result = jnp.minimum(distance, exact_part)
    for level in range(1, BUCKETS - exact_part):
        boundary = int(
            math.ceil(exact_part * (MAXDIST / exact_part) ** (level / (BUCKETS - exact_part)))
        )
        result = result + (distance >= boundary).astype(jnp.int32)
    return result


def rms_norm(values, gain):
    return values * lax.rsqrt(jnp.mean(values * values, axis=-1, keepdims=True) + EPSILON) * gain


def rms_back(values, gain, grad):
    inverse = lax.rsqrt(jnp.mean(values * values, axis=-1, keepdims=True) + EPSILON)
    unit = values * inverse
    scaled = grad * gain
    inner = jnp.mean(scaled * unit, axis=-1, keepdims=True)
    return inverse * (scaled - unit * inner), jnp.sum(grad * unit, axis=0)


def ring(step):
    return [(i, (i + step) % 4) for i in range(4)]


def to_right(values):
    return lax.ppermute(values, "head", ring(1))


def to_left(values):
    return lax.ppermute(values, "head", ring(3))


def gather_ring(values):
    half = values.shape[0] // 2
    left = to_right(values)
    right = to_left(values)
    first = to_right(left[:half])
    second = to_left(right[half:])
    return jnp.concatenate([values, right, first, second, left], 0)


def reduce_ring(partial):
    rows = partial.shape[0] // 4
    half = rows // 2
    low = partial.astype(BF)
    own, right, opposite, left = (low[k * rows : (k + 1) * rows] for k in range(4))
    a = to_right(opposite[:half])
    b = to_left(opposite[half:])
    a = jnp.concatenate([(a.astype(F32) + right[:half].astype(F32)).astype(BF), right[half:]], 0)
    b = jnp.concatenate([left[:half], (b.astype(F32) + left[half:].astype(F32)).astype(BF)], 0)
    a = to_right(a)
    b = to_left(b)
    return partial[:rows] + a.astype(F32) + b.astype(F32)


def rolled(values, start):
    return lax.dynamic_slice_in_dim(
        jnp.concatenate([values, values], 0), start, values.shape[0], 0
    )


def shifted(block, distance):
    devices = range(lax.axis_size("blk"))
    route = [(i - distance, i) for i in devices if i - distance in devices]
    return lax.ppermute(block, "blk", route)


def enter_all(count, place):
    barrier = pltpu.get_barrier_semaphore()

    def greet(j, c):
        pl.semaphore_signal(
            barrier, inc=1, device_id={"blk": lax.rem(place + j, count)}, device_id_type=MESH
        )
        return c

    lax.fori_loop(1, count, greet, 0)
    pl.semaphore_wait(barrier, count - 1)


def exchange(count, place, source, target, send_sem, recv_sem, local_sem):
    def part(j):
        peer = lax.rem(place + j, count)
        return pltpu.make_async_remote_copy(
            src_ref=source.at[:, peer],
            dst_ref=target.at[:, place],
            send_sem=send_sem.at[j],
            recv_sem=recv_sem.at[j],
            device_id={"blk": peer},
            device_id_type=MESH,
        )

    def start(j, c):
        part(j).start()
        return c

    def finish(j, c):
        part(j).wait()
        return c

    lax.fori_loop(1, count, start, 0)
    own = pltpu.make_async_copy(source.at[:, place], target.at[:, place], local_sem)
    own.start()
    own.wait()
    lax.fori_loop(1, count, finish, 0)


def scan_kernel(
    count, own_keep, unit, bias, slope, prior, across, keep, held, s0, r0, s1, r1, s2, r2, local
):
    place = lax.axis_index("blk")
    enter_all(count, place)

    def tell(j):
        return pltpu.make_async_remote_copy(
            src_ref=own_keep,
            dst_ref=keep.at[place],
            send_sem=s0.at[j],
            recv_sem=r0.at[j],
            device_id={"blk": lax.rem(place + j, count)},
            device_id_type=MESH,
        )

    def tell_start(j, c):
        tell(j).start()
        return c

    def tell_wait(j, c):
        tell(j).wait()
        return c

    lax.fori_loop(1, count, tell_start, 0)
    own = pltpu.make_async_copy(own_keep, keep.at[place], local.at[2])
    own.start()
    own.wait()
    exchange(count, place, unit, across, s1, r1, local.at[0])
    lax.fori_loop(1, count, tell_wait, 0)
    for m in range(unit.shape[0]):
        def step(b, state, m=m):
            u = across[m, b].astype(F32)
            forget = jax.nn.sigmoid(bias[...] + slope[...] * u)
            before = keep[b, m : m + 1] * state
            held[m, b] = before.astype(BF)
            return forget * before + (1.0 - forget) * u

        lax.fori_loop(0, count, step, jnp.zeros(unit.shape[2:], F32))
    exchange(count, place, held, prior, s2, r2, local.at[1])


def scan_back_kernel(count, keep, grads, across, bias, slope, out, moved, held, s1, r1, s2, r2, local):
    place = lax.axis_index("blk")
    enter_all(count, place)
    exchange(count, place, grads, moved, s1, r1, local.at[0])
    for m in range(grads.shape[0]):
        def step(t, grad, m=m):
            b = count - 1 - t
            held[m, b] = grad.astype(BF)
            u = across[m, b].astype(F32)
            forget = jax.nn.sigmoid(bias[...] + slope[...] * u)
            return keep[b, m : m + 1] * (moved[m, b].astype(F32) + forget * grad)

        lax.fori_loop(0, count, step, jnp.zeros(grads.shape[2:], F32))
    exchange(count, place, held, out, s2, r2, local.at[1])


def semaphores(count):
    return [pltpu.SemaphoreType.DMA((count,))] * 4 + [pltpu.SemaphoreType.DMA((3,))]


VMEM = pl.BlockSpec(memory_space=pltpu.VMEM)
SMEM = pl.BlockSpec(memory_space=pltpu.SMEM)


def state_scan(keep, unit, bias, slope):
    count = lax.axis_size("blk")
    shape = jax.ShapeDtypeStruct(unit.shape, BF)
    return pl.pallas_call(
        functools.partial(scan_kernel, count),
        out_shape=(shape, shape, jax.ShapeDtypeStruct((count,) + keep.shape, F32)),
        in_specs=[VMEM, VMEM, VMEM, VMEM],
        out_specs=(VMEM, VMEM, VMEM),
        scratch_shapes=[pltpu.VMEM(unit.shape, BF)]
        + [pltpu.SemaphoreType.DMA((count,))] * 2
        + semaphores(count),
        compiler_params=pltpu.CompilerParams(collective_id=1, has_side_effects=True),
        name="state_scan",
    )(keep, unit, bias, slope)


def state_scan_back(keep, grads, across, bias, slope):
    count = lax.axis_size("blk")
    shape = jax.ShapeDtypeStruct(grads.shape, BF)
    return pl.pallas_call(
        functools.partial(scan_back_kernel, count),
        out_shape=shape,
        in_specs=[VMEM, VMEM, VMEM, VMEM, VMEM],
        out_specs=VMEM,
        scratch_shapes=[pltpu.VMEM(grads.shape, BF)] * 2 + semaphores(count),
        compiler_params=pltpu.CompilerParams(collective_id=2, has_side_effects=True),
        name="state_scan_back",
    )(keep, grads, across, bias, slope)


def dot(a, b, dims):
    return lax.dot_general(a, b, (dims, ((), ())), preferred_element_type=F32)


def body(
    tokens_in,
    grad_out,
    flags,
    attn_gain,
    mlp_gain,
    w_qkv,
    w_out,
    rel_bias,
    state_query,
    state_proj,
    forget_bias,
    forget_scale,
    w_up,
    w_down,
):
    micros, rows, width = tokens_in.shape
    place = lax.axis_index("head")
    block = rows * 4
    local_width = w_qkv.shape[2]
    heads = rel_bias.shape[1]
    head_size = local_width // heads
    states = state_query.shape[0]
    buckets = rel_bias.shape[0]
    scale = head_size ** (-0.5)
    tiles = block // TILE
    qkv_flat = w_qkv.reshape(width, 3 * local_width)
    query_heads = state_query.reshape(states, heads, head_size)
    to_absolute = lax.rem(4 - place, 4) * rows
    to_relative = place * rows

    keep_own = (1 - flags[:, 0]).astype(F32)
    keep_rows = jnp.zeros((8, local_width), F32).at[:micros].set(keep_own[:, None])

    near = (
        lax.broadcasted_iota(jnp.int32, (TILE, 2 * TILE), 0)
        + TILE
        - lax.broadcasted_iota(jnp.int32, (TILE, 2 * TILE), 1)
    )
    near_bucket = bucket_index(jnp.maximum(near, 0))
    near_bias = jnp.zeros((heads, TILE, 2 * TILE), F32)
    for level in range(buckets):
        near_bias = near_bias + jnp.where(
            (near_bucket == level)[None], rel_bias[level][:, None, None], 0.0
        )
    far = jnp.broadcast_to(rel_bias[buckets - 1][:, None, None], (heads, TILE, TILE))
    off = jnp.full((heads, TILE, TILE), MASKED, F32)
    iota0 = lax.broadcasted_iota(jnp.int32, (TILE, TILE), 0)
    iota1 = lax.broadcasted_iota(jnp.int32, (TILE, TILE), 1)
    diagonal = jnp.where((iota0 >= iota1)[None], near_bias[..., TILE:], MASKED)
    last = jnp.where((iota0 < iota1)[None], far, MASKED)
    by_offset = {0: last, tiles: diagonal, tiles - 1: near_bias[..., :TILE]}
    bias_table = jnp.concatenate(
        [
            jnp.concatenate(
                [
                    off if k < q or k > q + tiles else by_offset.get(k - q, far)
                    for k in range(2 * tiles)
                ],
                -1,
            )
            for q in range(tiles)
        ],
        1,
    )

    x = [tokens_in[m].astype(F32) for m in range(micros)]
    both = range(micros)
    whole = [gather_ring(rms_norm(x[m], attn_gain).astype(BF)) for m in both]

    queries, keys, values, earlier_kv = [], [], [], []
    update, unit, update_lse = [], [], []
    for m in both:
        mixed = rolled(dot(whole[m], qkv_flat, ((1,), (0,))).astype(BF), to_absolute).reshape(
            block, 3, heads, head_size
        )
        queries.append(mixed[:, 0])
        keys.append(mixed[:, 1])
        values.append(mixed[:, 2])
        earlier_kv.append(shifted(mixed[:, 1:], 1))
        scores = (
            jnp.einsum("shd,jhd->hsj", query_heads, keys[m], preferred_element_type=F32) * scale
        )
        top = jnp.max(scores, axis=-1, keepdims=True)
        raised = jnp.exp(scores - top)
        total = jnp.sum(raised, axis=-1, keepdims=True)
        update_lse.append(top + jnp.log(total))
        weights = (raised / total).astype(BF)
        update.append(
            jnp.einsum("hsj,jhd->shd", weights, values[m], preferred_element_type=F32)
        )
        unit.append(
            (
                update[m]
                * lax.rsqrt(jnp.mean(update[m] * update[m], axis=-1, keepdims=True) + EPSILON)
            ).reshape(states, local_width)
        )

    count = lax.axis_size("blk")
    split = (micros, count, states // count, local_width)
    bias_row, scale_row = forget_bias[None], forget_scale[None]
    prior_low, across, keeps = state_scan(
        keep_rows, jnp.stack(unit).astype(BF).reshape(split), bias_row, scale_row
    )
    prior_low = prior_low.reshape(micros, states, local_width)
    whole_grad = [gather_ring(grad_out[m]) for m in both]

    forget, state_after, state_kv = [], [], []
    all_keys, all_values, lse, attended, middle, whole_mlp = [], [], [], [], [], []
    for m in both:
        forget.append(jax.nn.sigmoid(forget_bias + forget_scale * unit[m]))
        state_after.append(
            forget[m] * prior_low[m].astype(F32) + (1.0 - forget[m]) * unit[m]
        )
        state_kv.append(
            jnp.einsum(
                "shd,hde->she",
                prior_low[m].reshape(states, heads, head_size),
                state_proj,
                preferred_element_type=F32,
            ).astype(BF)
        )
        all_keys.append(jnp.concatenate([earlier_kv[m][:, 0], keys[m]], 0))
        all_values.append(jnp.concatenate([earlier_kv[m][:, 1], values[m]], 0))

    def scores_of(m):
        closed = jnp.where(flags[m, 0] == 0, 0.0, MASKED)
        closed = jnp.concatenate(
            [jnp.broadcast_to(closed, (block,)), jnp.zeros((block,), F32)]
        )
        token_scores = (
            jnp.einsum("ihd,jhd->hij", queries[m], all_keys[m], preferred_element_type=F32)
            * scale
            + bias_table
            + closed[None, None]
        )
        state_scores = (
            jnp.einsum(
                "ihd,shd->his",
                queries[m],
                state_kv[m][..., :head_size],
                preferred_element_type=F32,
            )
            * scale
        )
        return token_scores, state_scores

    for m in both:
        token_scores, state_scores = scores_of(m)
        highest = jnp.maximum(
            jnp.max(token_scores, axis=-1, keepdims=True),
            jnp.max(state_scores, axis=-1, keepdims=True),
        )
        token_exp = jnp.exp(token_scores - highest)
        state_exp = jnp.exp(state_scores - highest)
        total = jnp.sum(token_exp, axis=-1, keepdims=True) + jnp.sum(
            state_exp, axis=-1, keepdims=True
        )
        lse.append(highest + jnp.log(total))
        att = jnp.einsum(
            "hij,jhd->ihd",
            (token_exp / total).astype(BF),
            all_values[m],
            preferred_element_type=F32,
        ) + jnp.einsum(
            "his,shd->ihd",
            (state_exp / total).astype(BF),
            state_kv[m][..., head_size:],
            preferred_element_type=F32,
        )
        attended.append(rolled(att.astype(BF).reshape(block, local_width), to_relative))
        branch = reduce_ring(dot(attended[m], w_out, ((1,), (0,))))
        middle.append(x[m] + branch)
        whole_mlp.append(gather_ring(rms_norm(middle[m], mlp_gain).astype(BF)))

    out, grad_middle, whole_gm = [], [], []
    active, grad_hidden = [], []
    g_mlp_gain = jnp.zeros(mlp_gain.shape, F32)
    root = math.sqrt(2.0 / math.pi)
    for m in both:
        hidden = dot(whole_mlp[m], w_up, ((1,), (0,)))
        square = hidden * hidden
        bent = jnp.tanh(root * hidden * (1.0 + 0.044715 * square))
        active.append((0.5 * hidden * (1.0 + bent)).astype(BF))
        slope = 0.5 * (1.0 + bent) + 0.5 * hidden * (1.0 - bent * bent) * root * (
            1.0 + 3.0 * 0.044715 * square
        )
        grad_active = dot(whole_grad[m], w_down, ((1,), (1,)))
        grad_hidden.append((grad_active * slope).astype(BF))
        grad_normed = reduce_ring(dot(grad_hidden[m], w_up, ((1,), (1,))))
        part, gain = rms_back(middle[m], mlp_gain, grad_normed)
        g_mlp_gain = g_mlp_gain + gain
        grad_middle.append(grad_out[m].astype(F32) + part)
        whole_gm.append(gather_ring(grad_middle[m].astype(BF)))
        out.append(middle[m] + reduce_ring(dot(active[m], w_down, ((1,), (0,)))))

    def joined(parts):
        return jnp.concatenate(parts, 0)

    g_up = dot(joined(whole_mlp), joined(grad_hidden), ((0,), (0,)))
    g_down = dot(joined(active), joined(whole_grad), ((0,), (0,)))

    def summed(values):
        return lax.psum(values.astype(BF), "blk").astype(F32)

    g_up, g_down = summed((g_up)), summed((g_down))

    near_acc = jnp.zeros((heads, TILE, 2 * TILE), F32)
    all_acc = jnp.zeros((heads,), F32)
    g_proj = jnp.zeros(state_proj.shape, F32)
    grad_queries, grad_keys, grad_values, earlier_grads, grad_prior = [], [], [], [], []
    for m in both:
        grad_att = rolled(dot(whole_gm[m], w_out, ((1,), (1,))).astype(BF), to_absolute).reshape(
            block, heads, head_size
        )
        state_keys = state_kv[m][..., :head_size]
        state_values = state_kv[m][..., head_size:]
        token_scores, state_scores = scores_of(m)
        token_probs = jnp.exp(token_scores - lse[m])
        state_probs = jnp.exp(state_scores - lse[m])
        grad_token_probs = jnp.einsum(
            "ihd,jhd->hij", grad_att, all_values[m], preferred_element_type=F32
        )
        grad_state_probs = jnp.einsum(
            "ihd,shd->his", grad_att, state_values, preferred_element_type=F32
        )
        delta = jnp.sum(token_probs * grad_token_probs, axis=-1, keepdims=True) + jnp.sum(
            state_probs * grad_state_probs, axis=-1, keepdims=True
        )
        grad_token_scores = token_probs * (grad_token_probs - delta)
        grad_state_scores = state_probs * (grad_state_probs - delta)
        for q in range(tiles):
            near_acc = near_acc + grad_token_scores[
                :, q * TILE : (q + 1) * TILE, (q + tiles - 1) * TILE : (q + tiles + 1) * TILE
            ]
        all_acc = all_acc + jnp.sum(grad_token_scores, axis=(1, 2))
        token_low = grad_token_scores.astype(BF)
        state_low = grad_state_scores.astype(BF)
        grad_values_all = jnp.einsum(
            "hij,ihd->jhd", token_probs.astype(BF), grad_att, preferred_element_type=F32
        )
        grad_state_values = jnp.einsum(
            "his,ihd->shd", state_probs.astype(BF), grad_att, preferred_element_type=F32
        )
        grad_queries.append(
            scale
            * (
                jnp.einsum("hij,jhd->ihd", token_low, all_keys[m], preferred_element_type=F32)
                + jnp.einsum("his,shd->ihd", state_low, state_keys, preferred_element_type=F32)
            )
        )
        grad_keys_all = scale * jnp.einsum(
            "hij,ihd->jhd", token_low, queries[m], preferred_element_type=F32
        )
        grad_state_keys = scale * jnp.einsum(
            "his,ihd->shd", state_low, queries[m], preferred_element_type=F32
        )
        earlier_grads.append(
            shifted(
                jnp.stack([grad_keys_all[:block], grad_values_all[:block]], 1).astype(BF), -1
            )
        )
        grad_keys.append(grad_keys_all[block:])
        grad_values.append(grad_values_all[block:])
        grad_state_kv = jnp.concatenate([grad_state_keys, grad_state_values], -1).astype(BF)
        g_proj = g_proj + jnp.einsum(
            "shd,she->hde",
            prior_low[m].reshape(states, heads, head_size),
            grad_state_kv,
            preferred_element_type=F32,
        )
        grad_prior.append(
            jnp.einsum(
                "she,hde->shd", grad_state_kv, state_proj, preferred_element_type=F32
            ).reshape(states, local_width)
        )
    g_out = summed(dot(joined(attended), joined(whole_gm), ((0,), (0,))))

    grad_after_all = state_scan_back(
        keeps, jnp.stack(grad_prior).astype(BF).reshape(split), across, bias_row, scale_row
    ).reshape(micros, states, local_width)

    g_query = jnp.zeros((states, local_width), F32)
    g_bias = jnp.zeros(forget_bias.shape, F32)
    g_scale = jnp.zeros(forget_scale.shape, F32)
    grad_mixed = []
    for m in both:
        grad_after = grad_after_all[m].astype(F32)
        prior = prior_low[m].astype(F32)
        grad_gate = grad_after * (prior - unit[m]) * forget[m] * (1.0 - forget[m])
        g_bias = g_bias + jnp.sum(grad_gate, 0)
        g_scale = g_scale + jnp.sum(grad_gate * unit[m], 0)
        grad_unit = (
            (grad_after * (1.0 - forget[m]) + grad_gate * forget_scale)
        ).reshape(states, heads, head_size)
        inverse = lax.rsqrt(jnp.mean(update[m] * update[m], axis=-1, keepdims=True) + EPSILON)
        unit_heads = unit[m].reshape(states, heads, head_size)
        grad_update_low = (
            inverse
            * (grad_unit - unit_heads * jnp.mean(grad_unit * unit_heads, axis=-1, keepdims=True))
        ).astype(BF)
        scores = (
            jnp.einsum("shd,jhd->hsj", query_heads, keys[m], preferred_element_type=F32) * scale
        )
        probs = jnp.exp(scores - update_lse[m])
        grad_probs = jnp.einsum(
            "shd,jhd->hsj", grad_update_low, values[m], preferred_element_type=F32
        )
        delta = jnp.sum(probs * grad_probs, axis=-1, keepdims=True)
        grad_scores = (probs * (grad_probs - delta)).astype(BF)
        grad_values_update = jnp.einsum(
            "hsj,shd->jhd", probs.astype(BF), grad_update_low, preferred_element_type=F32
        )
        g_query = g_query + scale * jnp.einsum(
            "hsj,jhd->shd", grad_scores, keys[m], preferred_element_type=F32
        ).reshape(states, local_width)
        grad_keys_update = scale * jnp.einsum(
            "hsj,shd->jhd", grad_scores, query_heads, preferred_element_type=F32
        )
        later = earlier_grads[m].astype(F32)
        gk = grad_keys[m] + later[:, 0] + grad_keys_update
        gv = grad_values[m] + later[:, 1] + grad_values_update
        grad_mixed.append(
            rolled(
                jnp.stack([grad_queries[m], gk, gv], 1)
                .astype(BF)
                .reshape(block, 3 * local_width),
                to_relative,
            )
        )

    g_qkv = dot(joined(whole), joined(grad_mixed), ((0,), (0,))).reshape(width, 3, local_width)
    g_rel = jnp.stack(
        [
            jnp.sum(
                jnp.where(((near_bucket == level) & (near >= 0))[None], near_acc, 0.0),
                axis=(1, 2),
            )
            for level in range(buckets - 1)
        ],
        0,
    )
    g_rel = jnp.concatenate([g_rel, (all_acc - jnp.sum(g_rel, 0))[None]], 0)
    grad_x = []
    g_attn_gain = jnp.zeros(attn_gain.shape, F32)
    for m in both:
        grad_normed = reduce_ring(dot(grad_mixed[m], qkv_flat, ((1,), (1,))))
        part, gain = rms_back(x[m], attn_gain, grad_normed)
        g_attn_gain = g_attn_gain + gain
        grad_x.append(grad_middle[m] + part)
    def over_head(values):
        for step in (1, 2):
            values = values + lax.ppermute(values, "head", [(i, i ^ step) for i in range(4)])
        return values

    gains = over_head(jnp.stack([g_attn_gain, g_mlp_gain]).reshape(8, local_width))
    small = jnp.concatenate(
        [g_rel.reshape(1, buckets * heads), jnp.zeros((1, local_width - buckets * heads), F32)], 1
    )
    packed = jnp.concatenate(
        [g_query, gains, g_bias[None], g_scale[None], small, jnp.zeros((5, local_width), F32)], 0
    )
    g_qkv, packed, g_proj = (summed(part) for part in (g_qkv, packed, g_proj))
    g_query = packed[:states]
    gains = packed[states : states + 8].reshape(2, width)
    g_attn_gain, g_mlp_gain = gains[0], gains[1]
    g_bias, g_scale = packed[states + 8], packed[states + 9]
    g_rel = packed[states + 10, : buckets * heads].reshape(buckets, heads)
    return (
        jnp.stack(out),
        jnp.stack(grad_x),
        jnp.stack(state_after)[:, None],
        g_attn_gain,
        g_mlp_gain,
        g_qkv,
        g_out,
        g_rel,
        g_query,
        g_proj,
        g_bias,
        g_scale,
        g_up,
        g_down,
    )


def solution(mesh):
    return jax.shard_map(
        body,
        mesh=mesh,
        in_specs=(
            P(None, ("blk", "head"), None),
            P(None, ("blk", "head"), None),
            P(None, "blk"),
            P(),
            P(),
            P(None, None, "head"),
            P("head", None),
            P(None, "head"),
            P(None, "head"),
            P("head", None, None),
            P("head"),
            P("head"),
            P(None, "head"),
            P("head", None),
        ),
        out_specs=(
            P(None, ("blk", "head"), None),
            P(None, ("blk", "head"), None),
            P(None, "blk", None, "head"),
            P(),
            P(),
            P(None, None, "head"),
            P("head", None),
            P(None, "head"),
            P(None, "head"),
            P("head", None, None),
            P("head"),
            P("head"),
            P(None, "head"),
            P("head", None),
        ),
        check_vma=False,
    )
```

```python
import functools
import math

import jax
import jax.numpy as jnp
from jax import lax
from jax.experimental import pallas as pl
from jax.experimental.pallas import tpu as pltpu
from jax.sharding import PartitionSpec as P

BUCKETS = 32
MAXDIST = 128
EPSILON = 1e-06
MASKED = -1e30
TILE = 128
MESH = pl.DeviceIdType.MESH
BF = jnp.bfloat16
F32 = jnp.float32
VMEM = pl.BlockSpec(memory_space=pltpu.VMEM)
SMEM = pl.BlockSpec(memory_space=pltpu.SMEM)
LIMIT = 56 * 2**20
ROOT = math.sqrt(2.0 / math.pi)
CUBIC = 0.044715


def bucket_starts():
    exact = BUCKETS // 2
    levels = [
        int(math.ceil(exact * (MAXDIST / exact) ** (t / (BUCKETS - exact))))
        for t in range(1, BUCKETS - exact)
    ]
    return list(range(exact + 1)) + levels


STARTS = bucket_starts()


def nn(a, b):
    return lax.dot_general(a, b, (((1,), (0,)), ((), ())), preferred_element_type=F32)


def nt(a, b):
    return lax.dot_general(a, b, (((1,), (1,)), ((), ())), preferred_element_type=F32)


def tn(a, b):
    return lax.dot_general(a, b, (((0,), (0,)), ((), ())), preferred_element_type=F32)


def inverse_rms(values):
    return lax.rsqrt(jnp.mean(values * values, axis=-1, keepdims=True) + EPSILON)


def tile_of(index, size=TILE):
    return pl.ds(pl.multiple_of(index * size, size), size)


def loop(count, step):
    def run(i, c):
        step(i)
        return c

    lax.fori_loop(0, count, run, 0)


def remote(src, dst, send_sem, recv_sem, device):
    return pltpu.make_async_remote_copy(
        src_ref=src,
        dst_ref=dst,
        send_sem=send_sem,
        recv_sem=recv_sem,
        device_id=device,
        device_id_type=MESH,
    )


class Ring:
    def __init__(self, send, recv):
        self.me = lax.axis_index("head")
        self.right = lax.rem(self.me + 1, 4)
        self.left = lax.rem(self.me + 3, 4)
        self.send, self.recv, self.used = send, recv, 0

    def greet(self):
        barrier = pltpu.get_barrier_semaphore()
        for peer in (self.right, self.left):
            pl.semaphore_signal(barrier, inc=1, device_id={"head": peer}, device_id_type=MESH)
        return 2

    def go(self, src, dst, peer):
        copy = remote(
            src, dst, self.send.at[self.used], self.recv.at[self.used], {"head": peer}
        )
        self.used += 1
        copy.start()
        return copy

    def row_chunk(self, k):
        return tile_of(lax.rem(self.me + k, 4))


class Gather:
    def __init__(self, ring, buf):
        self.ring, self.buf = ring, buf
        self.half = buf.shape[1] // 2

    def start(self):
        r, b, h = self.ring, self.buf, self.half
        self.a0 = r.go(b.at[0, :h], b.at[3, :h], r.right)
        self.b0 = r.go(b.at[0, h:], b.at[1, h:], r.left)
        self.a1 = r.go(b.at[0, h:], b.at[3, h:], r.right)
        self.b1 = r.go(b.at[0, :h], b.at[1, :h], r.left)

    def relay(self):
        r, b, h = self.ring, self.buf, self.half
        self.a0.wait_recv()
        self.a2 = r.go(b.at[3, :h], b.at[2, :h], r.right)
        self.b0.wait_recv()
        self.b2 = r.go(b.at[1, h:], b.at[2, h:], r.left)

    def finish(self):
        for copy in (self.a1, self.b1, self.a2, self.b2):
            copy.wait_recv()

    def close(self):
        for copy in (self.a0, self.b0, self.a1, self.b1, self.a2, self.b2):
            copy.wait_send()


class Reduce:
    def __init__(self, ring, terms, mid, into):
        self.ring, self.terms, self.mid, self.into = ring, terms, mid, into
        self.half = terms.shape[1] // 2

    def start(self):
        r, t, h = self.ring, self.terms, self.half
        self.a0 = r.go(t.at[2, :h], self.mid.at[0], r.right)
        self.b0 = r.go(t.at[2, h:], self.mid.at[1], r.left)
        self.a1 = r.go(t.at[1, h:], self.into.at[0, h:], r.right)
        self.b1 = r.go(t.at[3, :h], self.into.at[1, :h], r.left)

    def relay(self):
        r, t, h, mid = self.ring, self.terms, self.half, self.mid
        self.a0.wait_recv()
        mid[2] = (mid[0].astype(F32) + t[1, :h].astype(F32)).astype(BF)
        self.a2 = r.go(mid.at[2], self.into.at[0, :h], r.right)
        self.b0.wait_recv()
        mid[3] = (mid[1].astype(F32) + t[3, h:].astype(F32)).astype(BF)
        self.b2 = r.go(mid.at[3], self.into.at[1, h:], r.left)

    def finish(self):
        for copy in (self.a1, self.b1, self.a2, self.b2):
            copy.wait_recv()
        return (
            self.terms[0].astype(F32) + self.into[0].astype(F32) + self.into[1].astype(F32)
        )

    def close(self):
        for copy in (self.a0, self.b0, self.a1, self.b1, self.a2, self.b2):
            copy.wait_send()


class Exchange:
    def __init__(self, source, target, send, recv, local):
        self.count = lax.axis_size("blk")
        self.place = lax.axis_index("blk")
        self.size = source.shape[0] // self.count
        self.source, self.target = source, target
        self.send, self.recv, self.local = send, recv, local

    def part(self, j):
        peer = lax.rem(self.place + j, self.count)
        return remote(
            self.source.at[tile_of(peer, self.size)],
            self.target.at[tile_of(self.place, self.size)],
            self.send.at[j],
            self.recv.at[j],
            {"blk": peer},
        )

    def own(self):
        rows = tile_of(self.place, self.size)
        return pltpu.make_async_copy(self.source.at[rows], self.target.at[rows], self.local)

    def start(self):
        loop(self.count - 1, lambda j: self.part(j + 1).start())
        self.own().start()

    def finish(self):
        self.own().wait()
        loop(self.count - 1, lambda j: self.part(j + 1).wait_recv())

    def close(self):
        loop(self.count - 1, lambda j: self.part(j + 1).wait_send())


def greet_blocks():
    barrier = pltpu.get_barrier_semaphore()
    count, place = lax.axis_size("blk"), lax.axis_index("blk")

    def greet(j):
        pl.semaphore_signal(
            barrier, inc=1, device_id={"blk": lax.rem(place + j + 1, count)}, device_id_type=MESH
        )

    loop(count - 1, greet)
    return count - 1


def front_kernel(x, gain, w, whole, qkv, send, recv):
    ring = Ring(send, recv)
    pl.semaphore_wait(pltpu.get_barrier_semaphore(), ring.greet())
    gathers = []
    for m in range(2):
        rows = x[m].astype(F32)
        whole[m, 0] = (rows * inverse_rms(rows) * gain[...]).astype(BF)
        gathers.append(Gather(ring, whole.at[m]))
        gathers[m].start()
    for m in range(2):
        gathers[m].relay()
    for m in range(2):
        gathers[m].finish()

        def columns(n, m=m):
            cols = tile_of(n, 256)
            part = nn(whole[m].reshape(512, 1024), w[:, cols]).astype(BF)
            for k in range(4):
                qkv[m, ring.row_chunk(k), cols] = part[k * TILE : (k + 1) * TILE]

        loop(3, columns)
    for m in range(2):
        gathers[m].close()


def closed_row(closed, qi):
    column = lax.broadcasted_iota(jnp.int32, closed.shape, 1) + qi * TILE
    return jnp.where(column < 512, closed, 0.0)


def head(h, size=TILE, base=0):
    return slice(base + h * size, base + (h + 1) * size)


def memory_kernel(
    qkv, state_query, state_proj, bias, slope, own_keep, closed, rel, g,
    prior, across, keeps, update, update_lse, state_after, kv_all, state_kv, attended, lse, table, whole_grad,
    unit_low, held, send, recv, s0, r0, s1, r1, s2, r2, s3, r3, local,
):
    scale = TILE**-0.5
    ring = Ring(send, recv)
    place, count = lax.axis_index("blk"), lax.axis_size("blk")
    pl.semaphore_wait(pltpu.get_barrier_semaphore(), ring.greet() + greet_blocks())
    gathers = []
    for m in range(2):
        whole_grad[m, 0] = g[m]
        gathers.append(Gather(ring, whole_grad.at[m]))
        gathers[m].start()
    after = {"blk": lax.rem(place + 1, count)}
    shifts = [
        remote(qkv.at[m, :, 256:768], kv_all.at[m, 0:512], s0.at[m], r0.at[m], after)
        for m in range(2)
    ]
    for copy in shifts:
        copy.start()

    def tell(j):
        return remote(
            own_keep, keeps.at[place], s3.at[j], r3.at[j], {"blk": lax.rem(place + j, count)}
        )

    loop(count - 1, lambda j: tell(j + 1).start())
    keeps[place] = own_keep[...]

    def update_tile(m):
        def step(t):
            rows = tile_of(t)
            for h in range(2):
                scores = nt(state_query[rows, head(h)], qkv[m, :, head(h, base=256)]) * scale
                top = jnp.max(scores, axis=-1, keepdims=True)
                raised = jnp.exp(scores - top)
                total = jnp.sum(raised, axis=-1, keepdims=True)
                update_lse[m, h, rows] = top + jnp.log(total)
                u = nn((raised / total).astype(BF), qkv[m, :, head(h, base=512)])
                update[m, rows, head(h)] = u
                unit_low[m, rows, head(h)] = (u * inverse_rms(u)).astype(BF)

        return step

    there = [
        Exchange(unit_low.at[m], across.at[m], s1.at[m], r1.at[m], local.at[m]) for m in range(2)
    ]
    back = [
        Exchange(held.at[m], prior.at[m], s2.at[m], r2.at[m], local.at[2 + m]) for m in range(2)
    ]
    for m in range(2):
        loop(4, update_tile(m))
        there[m].start()
    for m in range(2):
        gathers[m].relay()

    row = lax.broadcasted_iota(jnp.int32, (TILE, TILE), 0)
    col = lax.broadcasted_iota(jnp.int32, (TILE, TILE), 1)
    for h in range(2):
        far = jnp.full((TILE, TILE), rel[BUCKETS - 1, h], F32)
        table[h, :, 0:128] = jnp.where(row < col, far, MASKED)
        table[h, :, 128:256] = far
        table[h, :, 256:384] = far
        for shift, at in ((TILE, 384), (0, 512)):
            distance = row - col + shift
            total = jnp.full((TILE, TILE), rel[0, h], F32)
            for t in range(1, BUCKETS):
                total = jnp.where(distance >= STARTS[t], rel[t, h], total)
            table[h, :, at : at + TILE] = jnp.where(distance >= 0, total, MASKED)

    for m in range(2):
        kv_all[m, 512:1024] = qkv[m, :, 256:768]
    loop(count - 1, lambda j: tell(j + 1).wait_recv())
    for m in range(2):
        there[m].finish()

        def scan(b, state, m=m):
            rows = tile_of(b, 16)
            u = across[m, rows].astype(F32)
            forget = jax.nn.sigmoid(bias[...] + slope[...] * u)
            before = keeps[b, m : m + 1] * state
            held[m, rows] = before.astype(BF)
            return forget * before + (1.0 - forget) * u

        lax.fori_loop(0, count, scan, jnp.zeros((16, 256), F32))
        back[m].start()
    for m in range(2):
        back[m].finish()

        def state(t, m=m):
            rows = tile_of(t)
            before = prior[m, rows]
            for h in range(2):
                state_kv[m, rows, head(h, 256)] = nn(before[:, head(h)], state_proj[h]).astype(BF)
                u = update[m, rows, head(h)]
                u = u * inverse_rms(u)
                forget = jax.nn.sigmoid(bias[:, head(h)] + slope[:, head(h)] * u)
                state_after[m, rows, head(h)] = (
                    forget * before[:, head(h)].astype(F32) + (1.0 - forget) * u
                )

        loop(4, state)
        shifts[m].wait_recv()

        def attend(qi, m=m):
            rows = tile_of(qi)
            window = pl.ds(pl.multiple_of(qi * TILE, TILE), 5 * TILE)
            shut = closed_row(closed[m, 0:1], qi)
            for h in range(2):
                q = qkv[m, rows, head(h)]
                token = nt(q, kv_all[m, window, head(h)]) * scale + (table[h] + shut)
                from_state = nt(q, state_kv[m, :, h * 256 : h * 256 + TILE]) * scale
                top = jnp.maximum(
                    jnp.max(token, axis=-1, keepdims=True),
                    jnp.max(from_state, axis=-1, keepdims=True),
                )
                token = jnp.exp(token - top)
                from_state = jnp.exp(from_state - top)
                total = jnp.sum(token, axis=-1, keepdims=True) + jnp.sum(
                    from_state, axis=-1, keepdims=True
                )
                lse[m, h, rows] = top + jnp.log(total)
                out = nn(token.astype(BF), kv_all[m, window, head(h, base=256)]) + nn(
                    from_state.astype(BF), state_kv[m, :, h * 256 + TILE : (h + 1) * 256]
                )
                attended[m, rows, head(h)] = (out / total).astype(BF)

        loop(4, attend)
    for m in range(2):
        gathers[m].finish()
        gathers[m].close()
        shifts[m].wait_send()
        there[m].close()
        back[m].close()
    loop(count - 1, lambda j: tell(j + 1).wait_send())


def mlp_kernel(
    attended, x, g, whole_grad, w_out, w_up, w_down, gain,
    att_rel, middle, grad_middle, whole_gm, branch, g_up, g_down, g_gain,
    terms, whole_mlp, active, grad_hidden, grad_terms, mid, into, send, recv,
):
    ring = Ring(send, recv)
    pl.semaphore_wait(pltpu.get_barrier_semaphore(), ring.greet())
    first = [Reduce(ring, terms.at[m], mid.at[m], into.at[m]) for m in range(2)]
    for m in range(2):
        for k in range(4):
            att_rel[m, k] = attended[m, ring.row_chunk(k)]

        def columns(n, m=m):
            cols = tile_of(n, 256)
            part = nn(att_rel[m].reshape(512, 256), w_out[:, cols]).astype(BF)
            for k in range(4):
                terms[m, k, :, cols] = part[k * TILE : (k + 1) * TILE]

        loop(4, columns)
        first[m].start()
    for m in range(2):
        first[m].relay()
    second = [Gather(ring, whole_mlp.at[m]) for m in range(2)]
    for m in range(2):
        rows = x[m].astype(F32) + first[m].finish()
        middle[m] = rows
        whole_mlp[m, 0] = (rows * inverse_rms(rows) * gain[...]).astype(BF)
        second[m].start()
    for m in range(2):
        second[m].relay()
    third = [Reduce(ring, grad_terms.at[m], mid.at[2 + m], into.at[2 + m]) for m in range(2)]
    for m in range(2):
        second[m].finish()

        def hidden_columns(n, m=m):
            cols = tile_of(n, 256)
            hidden = nn(whole_mlp[m].reshape(512, 1024), w_up[:, cols])
            grad_active = nt(whole_grad[m].reshape(512, 1024), w_down[cols])
            square = hidden * hidden
            bent = jnp.tanh(ROOT * hidden * (1.0 + CUBIC * square))
            active[m, :, cols] = (0.5 * hidden * (1.0 + bent)).astype(BF)
            rise = 0.5 * (1.0 + bent) + 0.5 * hidden * (1.0 - bent * bent) * ROOT * (
                1.0 + 3.0 * CUBIC * square
            )
            grad_hidden[m, :, cols] = (grad_active * rise).astype(BF)

        loop(4, hidden_columns)

        def grad_columns(n, m=m):
            cols = tile_of(n, 256)
            part = nt(grad_hidden[m], w_up[cols]).astype(BF)
            for k in range(4):
                grad_terms[m, k, :, cols] = part[k * TILE : (k + 1) * TILE]

        loop(4, grad_columns)
        third[m].start()
    for m in range(2):
        third[m].relay()

        def branch_columns(n, m=m):
            cols = tile_of(n, 256)
            part = nn(active[m], w_down[:, cols]).astype(BF)
            for k in range(4):
                branch[m, k, :, cols] = part[k * TILE : (k + 1) * TILE]

        loop(4, branch_columns)

    fourth = [Gather(ring, whole_gm.at[m]) for m in range(2)]
    for m in range(2):
        grad_normed = third[m].finish()
        rows = middle[m]
        inverse = inverse_rms(rows)
        unit = rows * inverse
        part = jnp.sum(grad_normed * unit, axis=0, keepdims=True)
        g_gain[...] = part if m == 0 else g_gain[...] + part
        scaled = grad_normed * gain[...]
        inner = jnp.mean(scaled * unit, axis=-1, keepdims=True)
        total = g[m].astype(F32) + inverse * (scaled - unit * inner)
        grad_middle[m] = total
        whole_gm[m, 0] = total.astype(BF)
        fourth[m].start()

    def up_rows(n):
        rows = tile_of(n, 256)
        total = tn(whole_mlp[0, :, :, rows].reshape(512, 256), grad_hidden[0])
        total = total + tn(whole_mlp[1, :, :, rows].reshape(512, 256), grad_hidden[1])
        g_up[rows] = total.astype(BF)

    loop(2, up_rows)
    fourth[0].relay()
    fourth[1].relay()
    loop(2, lambda n: up_rows(n + 2))

    def down_rows(n):
        rows = tile_of(n, 256)
        total = tn(active[0, :, rows], whole_grad[0].reshape(512, 1024))
        total = total + tn(active[1, :, rows], whole_grad[1].reshape(512, 1024))
        g_down[rows] = total.astype(BF)

    loop(4, down_rows)
    for m in range(2):
        fourth[m].finish()
    for m in range(2):
        for step in (first, second, third, fourth):
            step[m].close()


def back_kernel(
    whole_gm, w_out, qkv, kv_all, state_kv, lse, table, closed, prior, update, update_lse, state_query, state_proj,
    bias, slope, across, keeps, branch, middle,
    dqkv, g_query, g_proj, g_rel, g_bias, g_scale, out,
    grad_att, grad_kv, grad_state, early, later, grad_prior, moved, held, grad_after, near, sums,
    mid, into, send, recv, s0, r0, s1, r1, s2, r2, local,
):
    scale = TILE**-0.5
    ring = Ring(send, recv)
    place, count = lax.axis_index("blk"), lax.axis_size("blk")
    pl.semaphore_wait(pltpu.get_barrier_semaphore(), ring.greet() + greet_blocks())
    outs = [Reduce(ring, branch.at[m], mid.at[m], into.at[m]) for m in range(2)]
    for m in range(2):
        outs[m].start()
    before = {"blk": lax.rem(place + count - 1, count)}
    shifts = [remote(early.at[m], later.at[m], s0.at[m], r0.at[m], before) for m in range(2)]
    there = [
        Exchange(grad_prior.at[m], moved.at[m], s1.at[m], r1.at[m], local.at[m]) for m in range(2)
    ]
    back = [
        Exchange(held.at[m], grad_after.at[m], s2.at[m], r2.at[m], local.at[2 + m])
        for m in range(2)
    ]
    near[...] = jnp.zeros(near.shape, F32)
    g_query[...] = jnp.zeros(g_query.shape, F32)
    g_bias[...] = jnp.zeros(g_bias.shape, F32)
    g_scale[...] = jnp.zeros(g_scale.shape, F32)
    grad_kv[...] = jnp.zeros(grad_kv.shape, F32)
    grad_state[...] = jnp.zeros(grad_state.shape, F32)

    def own_chunk(qi):
        return lax.rem(qi + 4 - ring.me, 4)

    for m in range(2):
        part = nt(whole_gm[m].reshape(512, 1024), w_out[...]).astype(BF)
        for k in range(4):
            grad_att[m, ring.row_chunk(k)] = part[k * TILE : (k + 1) * TILE]

        def attend(qi, m=m):
            rows = tile_of(qi)
            window = pl.ds(pl.multiple_of(qi * TILE, TILE), 5 * TILE)
            shut = closed_row(closed[m, 0:1], qi)
            for h in range(2):
                k_cols, v_cols = head(h), head(h, base=256)
                sk_cols = slice(h * 256, h * 256 + TILE)
                sv_cols = slice(h * 256 + TILE, (h + 1) * 256)
                q = qkv[m, rows, head(h)]
                d = grad_att[m, rows, head(h)]
                level = lse[m, h, rows]
                token = jnp.exp(
                    nt(q, kv_all[m, window, k_cols]) * scale + (table[h] + shut) - level
                )
                from_state = jnp.exp(nt(q, state_kv[m, :, sk_cols]) * scale - level)
                grad_token = nt(d, kv_all[m, window, v_cols])
                grad_from = nt(d, state_kv[m, :, sv_cols])
                delta = jnp.sum(token * grad_token, axis=-1, keepdims=True) + jnp.sum(
                    from_state * grad_from, axis=-1, keepdims=True
                )
                grad_token = token * (grad_token - delta)
                grad_from = from_state * (grad_from - delta)
                near[h, :, 0:128] += (
                    grad_token[:, 0:128] + grad_token[:, 128:256] + grad_token[:, 256:384]
                )
                near[h, :, 128:384] += grad_token[:, 384:640]
                token_low = grad_token.astype(BF)
                from_low = grad_from.astype(BF)
                grad_q = scale * (
                    nn(token_low, kv_all[m, window, k_cols]) + nn(from_low, state_kv[m, :, sk_cols])
                )
                dqkv[m, own_chunk(qi), :, head(h)] = grad_q.astype(BF)
                grad_kv[m, window, k_cols] += tn(token_low, q)
                grad_kv[m, window, v_cols] += tn(token.astype(BF), d)
                grad_state[m, :, sk_cols] += tn(from_low, q)
                grad_state[m, :, sv_cols] += tn(from_state.astype(BF), d)

        loop(4, attend)
        early[m, :, 0:256] = (scale * grad_kv[m, 0:512, 0:256]).astype(BF)
        early[m, :, 256:512] = grad_kv[m, 0:512, 256:512].astype(BF)
        shifts[m].start()
        for h in range(2):
            low = jnp.concatenate(
                [
                    (scale * grad_state[m, :, h * 256 : h * 256 + TILE]).astype(BF),
                    grad_state[m, :, h * 256 + TILE : (h + 1) * 256].astype(BF),
                ],
                1,
            )
            grad_prior[m, :, head(h)] = nt(low, state_proj[h]).astype(BF)
            part = tn(prior[m, :, head(h)], low)
            g_proj[h] = part if m == 0 else g_proj[h] + part
        there[m].start()
        outs[m].relay()

    for m in range(2):
        there[m].finish()

        def scan(t, grad, m=m):
            b = count - 1 - t
            rows = tile_of(b, 16)
            held[m, rows] = grad.astype(BF)
            forget = jax.nn.sigmoid(bias[...] + slope[...] * across[m, rows].astype(F32))
            return keeps[b, m : m + 1] * (moved[m, rows].astype(F32) + forget * grad)

        lax.fori_loop(0, count, scan, jnp.zeros((16, 256), F32))
        back[m].start()

    row = lax.broadcasted_iota(jnp.int32, (TILE, TILE), 0)
    col = lax.broadcasted_iota(jnp.int32, (TILE, TILE), 1)
    distance = [row - col + TILE, row - col]
    for h in range(2):
        for t in range(BUCKETS):
            total = jnp.zeros((1, TILE), F32)
            for part in range(2):
                d = distance[part]
                inside = d >= STARTS[t]
                if t + 1 < BUCKETS:
                    inside = inside & (d < STARTS[t + 1])
                values = near[h, :, TILE * (part + 1) : TILE * (part + 2)]
                total = total + jnp.sum(jnp.where(inside, values, 0.0), axis=0, keepdims=True)
            if t + 1 == BUCKETS:
                total = total + jnp.sum(near[h, :, 0:TILE], axis=0, keepdims=True)
            sums[t : t + 1] = total
        g_rel[h] = jnp.sum(sums[...], axis=1, keepdims=True)

    for m in range(2):
        out[m] = middle[m] + outs[m].finish()
    for m in range(2):
        back[m].finish()

        def update_tile(t, m=m):
            rows = tile_of(t)
            for h in range(2):
                cols, k_cols, v_cols = head(h), head(h, base=256), head(h, base=512)
                grad = grad_after[m, rows, cols].astype(F32)
                u = update[m, rows, cols]
                inverse = inverse_rms(u)
                unit = u * inverse
                forget = jax.nn.sigmoid(bias[:, cols] + slope[:, cols] * unit)
                gate = grad * (prior[m, rows, cols].astype(F32) - unit) * forget * (1.0 - forget)
                g_bias[:, cols] += jnp.sum(gate, axis=0, keepdims=True)
                g_scale[:, cols] += jnp.sum(gate * unit, axis=0, keepdims=True)
                grad_unit = grad * (1.0 - forget) + gate * slope[:, cols]
                inner = jnp.mean(grad_unit * unit, axis=-1, keepdims=True)
                low = (inverse * (grad_unit - unit * inner)).astype(BF)
                q = state_query[rows, cols]
                probs = jnp.exp(nt(q, qkv[m, :, k_cols]) * scale - update_lse[m, h, rows])
                grad_probs = nt(low, qkv[m, :, v_cols])
                delta = jnp.sum(probs * grad_probs, axis=-1, keepdims=True)
                grad_scores = (probs * (grad_probs - delta)).astype(BF)
                g_query[rows, cols] += scale * nn(grad_scores, qkv[m, :, k_cols])
                grad_kv[m, 512:1024, cols] += tn(grad_scores, q)
                grad_kv[m, 512:1024, head(h, base=256)] += tn(probs.astype(BF), low)

        loop(4, update_tile)
        shifts[m].wait_recv()

        def finish_rows(t, m=m):
            rows = tile_of(t)
            full = grad_kv[m, pl.ds(pl.multiple_of(512 + t * TILE, TILE), TILE)]
            extra = later[m, rows].astype(F32)
            dqkv[m, own_chunk(t), :, 256:512] = (scale * full[:, 0:256] + extra[:, 0:256]).astype(BF)
            dqkv[m, own_chunk(t), :, 512:768] = (full[:, 256:512] + extra[:, 256:512]).astype(BF)

        loop(4, finish_rows)
    for m in range(2):
        outs[m].close()
        shifts[m].wait_send()
        there[m].close()
        back[m].close()


def end_kernel(
    dqkv, w, x, gain, grad_middle, whole, att_rel, whole_gm,
    grad_x, g_qkv, g_out, g_gain,
    terms, mid, into, send, recv,
):
    ring = Ring(send, recv)
    pl.semaphore_wait(pltpu.get_barrier_semaphore(), ring.greet())
    sums = [Reduce(ring, terms.at[m], mid.at[m], into.at[m]) for m in range(2)]
    for m in range(2):

        def columns(n, m=m):
            cols = tile_of(n, 256)
            part = nt(dqkv[m].reshape(512, 768), w[cols]).astype(BF)
            for k in range(4):
                terms[m, k, :, cols] = part[k * TILE : (k + 1) * TILE]

        loop(4, columns)
        sums[m].start()

    def out_rows():
        total = tn(att_rel[0].reshape(512, 256), whole_gm[0].reshape(512, 1024))
        total = total + tn(att_rel[1].reshape(512, 256), whole_gm[1].reshape(512, 1024))
        g_out[...] = total.astype(BF)

    def qkv_rows(n):
        rows = tile_of(n, 256)
        total = tn(whole[0, :, :, rows].reshape(512, 256), dqkv[0].reshape(512, 768))
        total = total + tn(whole[1, :, :, rows].reshape(512, 256), dqkv[1].reshape(512, 768))
        g_qkv[rows] = total.astype(BF)

    out_rows()
    for m in range(2):
        sums[m].relay()
    loop(4, qkv_rows)
    for m in range(2):
        grad_normed = sums[m].finish()
        rows = x[m].astype(F32)
        inverse = inverse_rms(rows)
        unit = rows * inverse
        part = jnp.sum(grad_normed * unit, axis=0, keepdims=True)
        g_gain[...] = part if m == 0 else g_gain[...] + part
        scaled = grad_normed * gain[...]
        inner = jnp.mean(scaled * unit, axis=-1, keepdims=True)
        grad_x[m] = grad_middle[m] + inverse * (scaled - unit * inner)
    for m in range(2):
        sums[m].close()


def call(kernel, name, number, outs, scratch, *args):
    return pl.pallas_call(
        kernel,
        out_shape=tuple(jax.ShapeDtypeStruct(shape, kind) for shape, kind in outs),
        in_specs=[SMEM if a.shape == (BUCKETS, 2) else VMEM for a in args],
        out_specs=tuple(VMEM for _ in outs),
        scratch_shapes=scratch,
        compiler_params=pltpu.CompilerParams(
            collective_id=number, has_side_effects=True, vmem_limit_bytes=LIMIT
        ),
        name=name,
    )(*args)


def sems(*shape):
    return pltpu.SemaphoreType.DMA(shape)


def body(
    tokens_in,
    grad_out,
    flags,
    attn_gain,
    mlp_gain,
    w_qkv,
    w_out,
    rel_bias,
    state_query,
    state_proj,
    forget_bias,
    forget_scale,
    w_up,
    w_down,
):
    micros, rows, width = tokens_in.shape
    block = rows * 4
    local_width = w_qkv.shape[2]
    heads = rel_bias.shape[1]
    states = state_query.shape[0]
    buckets = rel_bias.shape[0]
    count = lax.axis_size("blk")
    w = w_qkv.reshape(width, 3 * local_width)
    attn_row, mlp_row = attn_gain[None], mlp_gain[None]
    bias_row, scale_row = forget_bias[None], forget_scale[None]
    keep_own = (1 - flags[:, 0]).astype(F32)
    keep_rows = jnp.zeros((8, local_width), F32).at[:micros].set(keep_own[:, None])
    closed = jnp.broadcast_to(
        jnp.where(flags == 0, 0.0, MASKED).astype(F32)[:, :, None], (micros, 8, 5 * TILE)
    )
    whole_shape = (micros, 4, rows, width)

    whole, qkv = call(
        front_kernel,
        "front",
        1,
        [(whole_shape, BF), ((micros, block, 3 * local_width), BF)],
        [sems(12), sems(12)],
        tokens_in,
        attn_row,
        w,
    )
    (
        prior,
        across,
        keeps,
        update,
        update_lse,
        state_after,
        kv_all,
        state_kv,
        attended,
        lse,
        table,
        whole_grad,
    ) = call(
        memory_kernel,
        "memory",
        2,
        [
            ((micros, states, local_width), BF),
            ((micros, states, local_width), BF),
            ((count, 8, local_width), F32),
            ((micros, states, local_width), F32),
            ((micros, heads, states, 1), F32),
            ((micros, states, local_width), F32),
            ((micros, 2 * block, 2 * local_width), BF),
            ((micros, states, 2 * local_width), BF),
            ((micros, block, local_width), BF),
            ((micros, heads, block, 1), F32),
            ((heads, TILE, 5 * TILE), F32),
            (whole_shape, BF),
        ],
        [pltpu.VMEM((micros, states, local_width), BF)] * 2
        + [sems(12), sems(12), sems(2), sems(2)]
        + [sems(2, count)] * 4
        + [sems(count)] * 2
        + [sems(4)],
        qkv,
        state_query,
        state_proj,
        bias_row,
        scale_row,
        keep_rows,
        closed,
        rel_bias,
        grad_out,
    )
    att_rel, middle, grad_middle, whole_gm, branch, g_up, g_down, g_mlp_gain = call(
        mlp_kernel,
        "mlp",
        3,
        [
            ((micros, 4, rows, local_width), BF),
            ((micros, rows, width), F32),
            ((micros, rows, width), F32),
            (whole_shape, BF),
            (whole_shape, BF),
            (w_up.shape, BF),
            (w_down.shape, BF),
            ((1, width), F32),
        ],
        [
            pltpu.VMEM(whole_shape, BF),
            pltpu.VMEM(whole_shape, BF),
            pltpu.VMEM((micros, block, w_up.shape[1]), BF),
            pltpu.VMEM((micros, block, w_up.shape[1]), BF),
            pltpu.VMEM(whole_shape, BF),
            pltpu.VMEM((4, 4, rows // 2, width), BF),
            pltpu.VMEM((4, 2, rows, width), BF),
            sems(48),
            sems(48),
        ],
        attended,
        tokens_in,
        grad_out,
        whole_grad,
        w_out,
        w_up,
        w_down,
        mlp_row,
    )

    def summed(values):
        return lax.psum(values.astype(BF), "blk").astype(F32)

    g_up, g_down = summed(g_up), summed(g_down)

    state_shape = (micros, states, local_width)
    dqkv, g_query, g_proj, g_rel, g_bias, g_scale, out = call(
        back_kernel,
        "back",
        4,
        [
            ((micros, 4, rows, 3 * local_width), BF),
            ((states, local_width), F32),
            (state_proj.shape, F32),
            ((heads, buckets, 1), F32),
            ((1, local_width), F32),
            ((1, local_width), F32),
            ((micros, rows, width), F32),
        ],
        [
            pltpu.VMEM((micros, block, local_width), BF),
            pltpu.VMEM((micros, 2 * block, 2 * local_width), F32),
            pltpu.VMEM((micros, states, 2 * local_width), F32),
            pltpu.VMEM((micros, block, 2 * local_width), BF),
            pltpu.VMEM((micros, block, 2 * local_width), BF),
            pltpu.VMEM(state_shape, BF),
            pltpu.VMEM(state_shape, BF),
            pltpu.VMEM(state_shape, BF),
            pltpu.VMEM(state_shape, BF),
            pltpu.VMEM((heads, TILE, 3 * TILE), F32),
            pltpu.VMEM((buckets, TILE), F32),
            pltpu.VMEM((2, 4, rows // 2, width), BF),
            pltpu.VMEM((2, 2, rows, width), BF),
            sems(12),
            sems(12),
            sems(2),
            sems(2),
        ]
        + [sems(2, count)] * 4
        + [sems(4)],
        whole_gm,
        w_out,
        qkv,
        kv_all,
        state_kv,
        lse,
        table,
        closed,
        prior,
        update,
        update_lse,
        state_query,
        state_proj,
        bias_row,
        scale_row,
        across,
        keeps,
        branch,
        middle,
    )
    grad_x, g_qkv, g_out, g_attn_gain = call(
        end_kernel,
        "end",
        5,
        [
            ((micros, rows, width), F32),
            ((width, 3 * local_width), BF),
            (w_out.shape, BF),
            ((1, width), F32),
        ],
        [
            pltpu.VMEM(whole_shape, BF),
            pltpu.VMEM((2, 4, rows // 2, width), BF),
            pltpu.VMEM((2, 2, rows, width), BF),
            sems(12),
            sems(12),
        ],
        dqkv,
        w,
        tokens_in,
        attn_row,
        grad_middle,
        whole,
        att_rel,
        whole_gm,
    )

    def over_head(values):
        for step in (1, 2):
            values = values + lax.ppermute(values, "head", [(i, i ^ step) for i in range(4)])
        return values

    gains = over_head(jnp.concatenate([g_attn_gain, g_mlp_gain], 0).reshape(8, local_width))
    g_rel = jnp.transpose(g_rel[:, :, 0])
    small = jnp.concatenate(
        [g_rel.reshape(1, buckets * heads), jnp.zeros((1, local_width - buckets * heads), F32)], 1
    )
    packed = jnp.concatenate(
        [g_query, gains, g_bias, g_scale, small, jnp.zeros((5, local_width), F32)], 0
    )
    g_qkv, g_out, packed, g_proj = (summed(part) for part in (g_qkv, g_out, packed, g_proj))
    gains = packed[states : states + 8].reshape(2, width)
    return (
        out,
        grad_x,
        state_after[:, None],
        gains[0],
        gains[1],
        g_qkv.reshape(width, 3, local_width),
        g_out,
        packed[states + 10, : buckets * heads].reshape(buckets, heads),
        packed[:states],
        g_proj,
        packed[states + 8],
        packed[states + 9],
        g_up,
        g_down,
    )


def solution(mesh):
    return jax.shard_map(
        body,
        mesh=mesh,
        in_specs=(
            P(None, ("blk", "head"), None),
            P(None, ("blk", "head"), None),
            P(None, "blk"),
            P(),
            P(),
            P(None, None, "head"),
            P("head", None),
            P(None, "head"),
            P(None, "head"),
            P("head", None, None),
            P("head"),
            P("head"),
            P(None, "head"),
            P("head", None),
        ),
        out_specs=(
            P(None, ("blk", "head"), None),
            P(None, ("blk", "head"), None),
            P(None, "blk", None, "head"),
            P(),
            P(),
            P(None, None, "head"),
            P("head", None),
            P(None, "head"),
            P(None, "head"),
            P("head", None, None),
            P("head"),
            P("head"),
            P(None, "head"),
            P("head", None),
        ),
        check_vma=False,
    )
```

```python
import math
import types

import jax
import jax.numpy as jnp
from jax import lax
from jax.experimental import pallas as pl
from jax.experimental.pallas import tpu as pltpu
from jax.sharding import PartitionSpec as P

BUCKETS = 32
MAXDIST = 128
EPSILON = 1e-06
MASKED = -1e30
TILE = 128
MESH = pl.DeviceIdType.MESH
BF = jnp.bfloat16
F32 = jnp.float32
VMEM = pl.BlockSpec(memory_space=pltpu.VMEM)
SMEM = pl.BlockSpec(memory_space=pltpu.SMEM)
LIMIT = 60 * 2**20
ROOT = math.sqrt(2.0 / math.pi)
CUBIC = 0.044715


def bucket_starts():
    exact = BUCKETS // 2
    levels = [
        int(math.ceil(exact * (MAXDIST / exact) ** (t / (BUCKETS - exact))))
        for t in range(1, BUCKETS - exact)
    ]
    return list(range(exact + 1)) + levels


STARTS = bucket_starts()


def nn(a, b):
    return lax.dot_general(a, b, (((1,), (0,)), ((), ())), preferred_element_type=F32)


def nt(a, b):
    return lax.dot_general(a, b, (((1,), (1,)), ((), ())), preferred_element_type=F32)


def tn(a, b):
    return lax.dot_general(a, b, (((0,), (0,)), ((), ())), preferred_element_type=F32)


def inverse_rms(values):
    return lax.rsqrt(jnp.mean(values * values, axis=-1, keepdims=True) + EPSILON)


def tile_of(index, size=TILE):
    return pl.ds(pl.multiple_of(index * size, size), size)


def loop(count, step):
    def run(i, c):
        step(i)
        return c

    lax.fori_loop(0, count, run, 0)


def remote(src, dst, send_sem, recv_sem, device):
    return pltpu.make_async_remote_copy(
        src_ref=src,
        dst_ref=dst,
        send_sem=send_sem,
        recv_sem=recv_sem,
        device_id=device,
        device_id_type=MESH,
    )


class Links:
    def __init__(self, send, recv):
        self.send, self.recv, self.used = send, recv, 0

    def go(self, src, dst, device):
        copy = remote(src, dst, self.send.at[self.used], self.recv.at[self.used], device)
        self.used += 1
        copy.start()
        return copy


class Ring:
    def __init__(self, links, me, device):
        self.links, self.me = links, me
        self.right = device(lax.rem(me + 1, 4))
        self.left = device(lax.rem(me + 3, 4))

    def go(self, src, dst, peer):
        return self.links.go(src, dst, peer)

    def greet(self):
        barrier = pltpu.get_barrier_semaphore()
        for peer in (self.right, self.left):
            pl.semaphore_signal(barrier, inc=1, device_id=peer, device_id_type=MESH)
        return 2

    def chunk(self, k):
        return lax.rem(self.me + k, 4)

    def row_chunk(self, k):
        return tile_of(self.chunk(k))


def head_ring(links):
    return Ring(links, lax.axis_index("head"), lambda i: {"head": i})


def by_rows(buf):
    half = buf.shape[1] // 2

    def piece(k, part=None, offset=0):
        return buf.at[k] if part is None else buf.at[k, part * half : (part + 1) * half]

    return piece


def by_columns(buf, base, rows, chunk):
    half = buf.shape[1] // 2

    def piece(k, part=None, offset=0):
        at = pl.ds(pl.multiple_of(base + chunk(k + offset) * rows, rows), rows)
        return buf.at[at] if part is None else buf.at[at, part * half : (part + 1) * half]

    return piece


class Gather:
    def __init__(self, ring, piece):
        self.ring, self.piece = ring, piece

    def start(self):
        r, p = self.ring, self.piece
        self.a0 = r.go(p(0, 0), p(3, 0, 1), r.right)
        self.b0 = r.go(p(0, 1), p(1, 1, 3), r.left)
        self.a1 = r.go(p(0, 1), p(3, 1, 1), r.right)
        self.b1 = r.go(p(0, 0), p(1, 0, 3), r.left)

    def relay(self):
        r, p = self.ring, self.piece
        self.a0.wait_recv()
        self.a2 = r.go(p(3, 0), p(2, 0, 1), r.right)
        self.b0.wait_recv()
        self.b2 = r.go(p(1, 1), p(2, 1, 3), r.left)

    def finish(self):
        for copy in (self.a1, self.b1, self.a2, self.b2):
            copy.wait_recv()

    def close(self):
        for copy in (self.a0, self.b0, self.a1, self.b1, self.a2, self.b2):
            copy.wait_send()


class Reduce:
    def __init__(self, ring, terms, mid, into):
        self.ring, self.terms, self.mid, self.into = ring, terms, mid, into
        if mid.shape[1] == into.shape[1]:
            half = into.shape[2] // 2
            self.place = lambda i, part: into.at[i, :, part * half : (part + 1) * half]
        else:
            half = into.shape[1] // 2
            self.place = lambda i, part: into.at[i, part * half : (part + 1) * half]

    def start(self):
        r, t = self.ring, self.terms
        self.a0 = r.go(t(2, 0), self.mid.at[0], r.right)
        self.b0 = r.go(t(2, 1), self.mid.at[1], r.left)
        self.a1 = r.go(t(1, 1), self.place(0, 1), r.right)
        self.b1 = r.go(t(3, 0), self.place(1, 0), r.left)

    def relay(self):
        r, t, mid = self.ring, self.terms, self.mid
        self.a0.wait_recv()
        mid[2] = (mid[0].astype(F32) + t(1, 0)[...].astype(F32)).astype(BF)
        self.a2 = r.go(mid.at[2], self.place(0, 0), r.right)
        self.b0.wait_recv()
        mid[3] = (mid[1].astype(F32) + t(3, 1)[...].astype(F32)).astype(BF)
        self.b2 = r.go(mid.at[3], self.place(1, 1), r.left)

    def finish(self):
        for copy in (self.a1, self.b1, self.a2, self.b2):
            copy.wait_recv()
        return (
            self.terms(0)[...].astype(F32)
            + self.into[0].astype(F32)
            + self.into[1].astype(F32)
        )

    def close(self):
        for copy in (self.a0, self.b0, self.a1, self.b1, self.a2, self.b2):
            copy.wait_send()


def block_device(x, z, c):
    return {"blk": (x * 4 + z) * 2 + c}


def block_place():
    place = lax.axis_index("blk")
    return place % 2, (place // 2) % 4, place // 8


class Plane:
    def __init__(self, links):
        c, z, x = block_place()
        self.links = links
        self.peer = block_device(x, z, 1 - c)
        rx = Ring(links, x, lambda i: block_device(i, z, c))
        rz = Ring(links, z, lambda i: block_device(x, i, c))
        self.rings = [rx, rz]
        self.first, self.second = (rx, rz), (rz, rx)
        self.base = c * 512
        self.own = pl.ds(pl.multiple_of(c * 512, 512), 512)
        self.away = pl.ds(pl.multiple_of((1 - c) * 512, 512), 512)
        self.top = [c * 512 + x * 64, c * 512 + 256 + z * 64]
        self.last = [
            pl.ds(pl.multiple_of(self.top[0] + z * 16, 16), 16),
            pl.ds(pl.multiple_of(self.top[1] + x * 16, 16), 16),
        ]

    def greet(self):
        barrier = pltpu.get_barrier_semaphore()
        pl.semaphore_signal(barrier, inc=1, device_id=self.peer, device_id_type=MESH)
        return 1 + sum(ring.greet() for ring in self.rings)


class Steps:
    def advance(self, steps=1):
        for _ in range(steps):
            if self.steps:
                self.steps.pop(0)()


class PlaneReduce(Steps):
    def __init__(self, plane, parts, result, half, mid, into, quarter, small_mid, small_into):
        self.plane, self.parts, self.result, self.half = plane, parts, result, half
        self.quarter = quarter
        first, second = plane.first, plane.second
        self.reduce1 = [
            Reduce(first[i], by_columns(half, i * 256, 64, first[i].chunk), mid.at[i], into.at[i])
            for i in range(2)
        ]
        self.reduce2 = [
            Reduce(
                second[i],
                by_columns(quarter.at[i], 0, 16, second[i].chunk),
                small_mid.at[i],
                small_into.at[i],
            )
            for i in range(2)
        ]
        self.steps = [
            self.cores,
            self.start1,
            lambda: [r.relay() for r in self.reduce1],
            self.start2,
            lambda: [r.relay() for r in self.reduce2],
            self.finish,
        ]

    def cores(self):
        plane = self.plane
        self.swap = plane.links.go(self.parts.at[plane.away], self.half, plane.peer)

    def start1(self):
        self.swap.wait_recv()

        def add(t):
            rows = tile_of(t, 64)
            own = pl.ds(pl.multiple_of(self.plane.base + t * 64, 64), 64)
            self.half[rows] = (
                self.parts[own].astype(F32) + self.half[rows].astype(F32)
            ).astype(BF)

        loop(8, add)
        for r in self.reduce1:
            r.start()

    def start2(self):
        for i, r in enumerate(self.reduce1):
            self.quarter[i] = r.finish().astype(BF)
            self.reduce2[i].start()

    def finish(self):
        for i, r in enumerate(self.reduce2):
            self.result(i, r.finish().astype(BF))

    def close(self):
        self.swap.wait_send()
        for r in self.reduce1 + self.reduce2:
            r.close()


class PlaneGather(Steps):
    def __init__(self, plane, total):
        self.plane, self.total = plane, total
        first, second = plane.first, plane.second
        self.gather1 = [
            Gather(second[i], by_columns(total, plane.top[i], 16, second[i].chunk))
            for i in range(2)
        ]
        self.gather2 = [
            Gather(first[i], by_columns(total, plane.base + i * 256, 64, first[i].chunk))
            for i in range(2)
        ]
        self.steps = [
            lambda: [g.start() for g in self.gather1],
            lambda: [g.relay() for g in self.gather1],
            self.start2,
            lambda: [g.relay() for g in self.gather2],
            self.cores,
            lambda: self.swap.wait_recv(),
        ]

    def start2(self):
        for i, g in enumerate(self.gather1):
            g.finish()
            self.gather2[i].start()

    def cores(self):
        for g in self.gather2:
            g.finish()
        rows = self.total.at[self.plane.own]
        self.swap = self.plane.links.go(rows, rows, self.plane.peer)

    def close(self):
        self.swap.wait_send()
        for g in self.gather1 + self.gather2:
            g.close()


def reduce_scratch(width):
    return dict(
        half=((512, width), BF),
        mid=((2, 4, 64, width // 2), BF),
        into=((2, 2, 64, width), BF),
        quarter=((2, 64, width), BF),
        small_mid=((2, 4, 16, width // 2), BF),
        small_into=((2, 2, 16, width), BF),
    )


class Exchange:
    def __init__(self, source, target, send, recv, local):
        self.count = lax.axis_size("blk")
        self.place = lax.axis_index("blk")
        self.size = source.shape[0] // self.count
        self.source, self.target = source, target
        self.send, self.recv, self.local = send, recv, local

    def part(self, j):
        peer = lax.rem(self.place + j, self.count)
        return remote(
            self.source.at[tile_of(peer, self.size)],
            self.target.at[tile_of(self.place, self.size)],
            self.send.at[j],
            self.recv.at[j],
            {"blk": peer},
        )

    def own(self):
        rows = tile_of(self.place, self.size)
        return pltpu.make_async_copy(self.source.at[rows], self.target.at[rows], self.local)

    def start(self):
        loop(self.count - 1, lambda j: self.part(j + 1).start())
        self.own().start()

    def finish(self):
        self.own().wait()
        loop(self.count - 1, lambda j: self.part(j + 1).wait_recv())

    def close(self):
        loop(self.count - 1, lambda j: self.part(j + 1).wait_send())


def greet_blocks():
    barrier = pltpu.get_barrier_semaphore()
    count, place = lax.axis_size("blk"), lax.axis_index("blk")

    def greet(j):
        pl.semaphore_signal(
            barrier, inc=1, device_id={"blk": lax.rem(place + j + 1, count)}, device_id_type=MESH
        )

    loop(count - 1, greet)
    return count - 1


def closed_row(closed, qi):
    column = lax.broadcasted_iota(jnp.int32, closed.shape, 1) + qi * TILE
    return jnp.where(column < 512, closed, 0.0)


def head(h, size=TILE, base=0):
    return slice(base + h * size, base + (h + 1) * size)


def window_of(qi):
    return pl.ds(pl.multiple_of(qi * TILE, TILE), 5 * TILE)


def split_rows(target, m, cols, part):
    for k in range(4):
        target[m, k, :, cols] = part[k * TILE : (k + 1) * TILE]


def write_table(table, rel):
    row = lax.broadcasted_iota(jnp.int32, (TILE, TILE), 0)
    col = lax.broadcasted_iota(jnp.int32, (TILE, TILE), 1)
    for h in range(2):
        far = jnp.full((TILE, TILE), rel[BUCKETS - 1, h], F32)
        table[h, :, 0:128] = jnp.where(row < col, far, MASKED)
        table[h, :, 128:256] = far
        table[h, :, 256:384] = far
        for shift, at in ((TILE, 384), (0, 512)):
            distance = row - col + shift
            total = jnp.full((TILE, TILE), rel[0, h], F32)
            for t in range(1, BUCKETS):
                total = jnp.where(distance >= STARTS[t], rel[t, h], total)
            table[h, :, at : at + TILE] = jnp.where(distance >= 0, total, MASKED)


def forward_kernel(r):
    scale = TILE**-0.5
    links = Links(r.send, r.recv)
    ring = head_ring(links)
    plane = Plane(links)
    place, count = lax.axis_index("blk"), lax.axis_size("blk")
    both = range(2)
    for m in both:
        rows = r.x[m].astype(F32)
        r.whole.ref[m, 0] = (rows * inverse_rms(rows) * r.attn_gain[...]).astype(BF)
        r.whole_grad[m, 0] = r.g[m]
    pl.semaphore_wait(pltpu.get_barrier_semaphore(), ring.greet() + greet_blocks())
    whole, qkv, kv_all = r.whole.ref, r.qkv.ref, r.kv_all.ref
    prior, across, keeps = r.prior.ref, r.across.ref, r.keeps.ref
    update, stats, state_kv = r.update.ref, r.stats.ref, r.state_kv.ref
    table, att_rel, middle, branch = r.table.ref, r.att_rel.ref, r.middle.ref, r.branch.ref
    gather_x = [Gather(ring, by_rows(whole.at[m])) for m in both]
    gather_g = [Gather(ring, by_rows(r.whole_grad.at[m])) for m in both]
    for m in both:
        gather_x[m].start()

    def tell(j):
        peer = {"blk": lax.rem(place + j, count)}
        return remote(r.own_keep, keeps.at[place], r.s3.at[j], r.r3.at[j], peer)

    loop(count - 1, lambda j: tell(j + 1).start())
    keeps[place] = r.own_keep[...]
    write_table(table, r.rel)
    r.table.put()
    after = {"blk": lax.rem(place + 1, count)}
    shifts = [
        remote(qkv.at[m, :, 256:768], kv_all.at[m, 0:512], r.s0.at[m], r.r0.at[m], after)
        for m in both
    ]
    there = [
        Exchange(r.unit_low.at[m], across.at[m], r.s1.at[m], r.r1.at[m], r.local.at[m])
        for m in both
    ]
    back = [
        Exchange(r.held.at[m], prior.at[m], r.s2.at[m], r.r2.at[m], r.local.at[2 + m])
        for m in both
    ]

    def project(m):
        def columns(n):
            cols = tile_of(n, 256)
            part = nn(whole[m].reshape(512, 1024), r.w[:, cols]).astype(BF)
            for k in range(4):
                qkv[m, ring.row_chunk(k), cols] = part[k * TILE : (k + 1) * TILE]

        loop(3, columns)
        shifts[m].start()
        kv_all[m, 512:1024] = qkv[m, :, 256:768]

    def update_tile(m):
        def step(t):
            rows = tile_of(t)
            for h in range(2):
                scores = nt(r.state_query[rows, head(h)], qkv[m, :, head(h, base=256)]) * scale
                top = jnp.max(scores, axis=-1, keepdims=True)
                raised = jnp.exp(scores - top)
                total = jnp.sum(raised, axis=-1, keepdims=True)
                stats[m, rows, h : h + 1] = top + jnp.log(total)
                u = nn((raised / total).astype(BF), qkv[m, :, head(h, base=512)])
                update[m, rows, head(h)] = u
                r.unit_low[m, rows, head(h)] = (u * inverse_rms(u)).astype(BF)

        return step

    def scan(m):
        def step(b, state):
            rows = tile_of(b, 16)
            u = across[m, rows].astype(F32)
            forget = jax.nn.sigmoid(r.bias[...] + r.slope[...] * u)
            before = keeps[b, m : m + 1] * state
            r.held[m, rows] = before.astype(BF)
            return forget * before + (1.0 - forget) * u

        lax.fori_loop(0, count, step, jnp.zeros((16, 256), F32))

    def state(m):
        def step(t):
            rows = tile_of(t)
            before = prior[m, rows]
            for h in range(2):
                state_kv[m, rows, head(h, 256)] = nn(before[:, head(h)], r.state_proj[h]).astype(BF)
                u = update[m, rows, head(h)]
                u = u * inverse_rms(u)
                forget = jax.nn.sigmoid(r.bias[:, head(h)] + r.slope[:, head(h)] * u)
                r.state_after.ref[m, rows, head(h)] = (
                    forget * before[:, head(h)].astype(F32) + (1.0 - forget) * u
                )

        return step

    def attend(m):
        def step(qi):
            rows, window = tile_of(qi), window_of(qi)
            shut = closed_row(r.closed[m, 0:1], qi)
            for h in range(2):
                q = qkv[m, rows, head(h)]
                token = nt(q, kv_all[m, window, head(h)]) * scale + (table[h] + shut)
                from_state = nt(q, state_kv[m, :, h * 256 : h * 256 + TILE]) * scale
                top = jnp.maximum(
                    jnp.max(token, axis=-1, keepdims=True),
                    jnp.max(from_state, axis=-1, keepdims=True),
                )
                token = jnp.exp(token - top)
                from_state = jnp.exp(from_state - top)
                total = jnp.sum(token, axis=-1, keepdims=True) + jnp.sum(
                    from_state, axis=-1, keepdims=True
                )
                stats[m, rows, 2 + h : 3 + h] = top + jnp.log(total)
                out = nn(token.astype(BF), kv_all[m, window, head(h, base=256)]) + nn(
                    from_state.astype(BF), state_kv[m, :, h * 256 + TILE : (h + 1) * 256]
                )
                att_rel[m, lax.rem(qi + 4 - ring.me, 4), :, head(h)] = (out / total).astype(BF)

        return step

    first = [
        Reduce(ring, by_rows(r.terms.at[m]), r.mids.at[m], r.intos.at[m]) for m in both
    ]
    second = [Gather(ring, by_rows(r.whole_mlp.at[m])) for m in both]
    third = [
        Reduce(ring, by_rows(r.terms.at[m]), r.mids.at[2 + m], r.intos.at[2 + m]) for m in both
    ]
    fourth = [Gather(ring, by_rows(r.whole_gm.at[m])) for m in both]

    def out_terms(m):
        def columns(n):
            cols = tile_of(n, 256)
            part = nn(att_rel[m].reshape(512, 256), r.w_out.ref[:, cols]).astype(BF)
            split_rows(r.terms, m, cols, part)

        loop(4, columns)

    def normalise(m):
        rows = r.x[m].astype(F32) + first[m].finish()
        middle[m] = rows
        r.whole_mlp[m, 0] = (rows * inverse_rms(rows) * r.mlp_gain[...]).astype(BF)

    def hidden(m):
        def columns(n):
            cols = tile_of(n, 256)
            value = nn(r.whole_mlp[m].reshape(512, 1024), r.w_up.ref[:, cols])
            grad_active = nt(r.whole_grad[m].reshape(512, 1024), r.w_down.ref[cols])
            square = value * value
            bent = jnp.tanh(ROOT * value * (1.0 + CUBIC * square))
            r.active[m, :, cols] = (0.5 * value * (1.0 + bent)).astype(BF)
            rise = 0.5 * (1.0 + bent) + 0.5 * value * (1.0 - bent * bent) * ROOT * (
                1.0 + 3.0 * CUBIC * square
            )
            r.grad_hidden[m, :, cols] = (grad_active * rise).astype(BF)

        loop(4, columns)

    def grad_terms(m):
        def columns(n):
            cols = tile_of(n, 256)
            part = nt(r.grad_hidden[m], r.w_up.ref[cols]).astype(BF)
            split_rows(r.terms, m, cols, part)

        loop(4, columns)

    def branch_terms(m):
        def columns(n):
            cols = tile_of(n, 256)
            part = nn(r.active[m], r.w_down.ref[:, cols]).astype(BF)
            split_rows(branch, m, cols, part)

        loop(4, columns)

    def grad_rows(m):
        grad_normed = third[m].finish()
        rows = middle[m]
        inverse = inverse_rms(rows)
        unit = rows * inverse
        part = jnp.sum(grad_normed * unit, axis=0, keepdims=True)
        r.g_gain[...] = part if m == 0 else r.g_gain[...] + part
        scaled = grad_normed * r.mlp_gain[...]
        inner = jnp.mean(scaled * unit, axis=-1, keepdims=True)
        total = r.g[m].astype(F32) + inverse * (scaled - unit * inner)
        r.grad_middle[m] = total
        r.whole_gm[m, 0] = total.astype(BF)

    def up_rows(n):
        rows = tile_of(n, 256)
        total = tn(r.whole_mlp[0, :, :, rows].reshape(512, 256), r.grad_hidden[0])
        total = total + tn(r.whole_mlp[1, :, :, rows].reshape(512, 256), r.grad_hidden[1])
        r.parts[rows, 0:1024] = total.astype(BF)

    def down_rows(n):
        rows = tile_of(n, 256)
        total = tn(r.active[0, :, rows], r.whole_grad[0].reshape(512, 1024))
        total = total + tn(r.active[1, :, rows], r.whole_grad[1].reshape(512, 1024))
        r.parts[rows, 1024:2048] = total.astype(BF)

    def keep_seed(i, rows):
        r.seeds[i] = rows

    weights = PlaneReduce(
        plane, r.parts, keep_seed, r.half, r.mid, r.into, r.quarter, r.small_mid, r.small_into
    )

    gather_x[0].relay()
    gather_x[1].relay()
    gather_x[0].finish()
    project(0)
    loop(4, update_tile(0))
    there[0].start()
    gather_x[1].finish()
    gather_g[0].start()
    gather_g[1].start()
    project(1)
    r.whole.put()
    r.qkv.put()
    loop(4, update_tile(1))
    there[1].start()
    r.update.put()
    gather_g[0].relay()
    loop(count - 1, lambda j: tell(j + 1).wait_recv())
    there[0].finish()
    scan(0)
    back[0].start()
    gather_g[1].relay()
    there[1].finish()
    scan(1)
    back[1].start()
    r.across.put()
    r.keeps.put()
    shifts[0].wait_recv()
    shifts[1].wait_recv()
    r.kv_all.put()
    back[0].finish()
    loop(4, state(0))
    loop(4, attend(0))
    r.w_out.get()
    out_terms(0)
    first[0].start()
    back[1].finish()
    r.prior.put()
    loop(4, state(1))
    r.state_kv.put()
    r.state_after.put()
    loop(2, attend(1))
    first[0].relay()
    loop(2, lambda qi: attend(1)(qi + 2))
    r.stats.put()
    out_terms(1)
    r.att_rel.put()
    first[1].start()
    normalise(0)
    second[0].start()
    first[1].relay()
    second[0].relay()
    normalise(1)
    second[1].start()
    r.middle.put()
    r.w_up.get()
    r.w_down.get()
    gather_g[0].finish()
    second[0].finish()
    hidden(0)
    second[1].relay()
    first[0].close()
    grad_terms(0)
    third[0].start()
    branch_terms(0)
    third[0].relay()
    gather_g[1].finish()
    second[1].finish()
    hidden(1)
    first[1].close()
    grad_terms(1)
    third[1].start()
    grad_rows(0)
    fourth[0].start()
    loop(1, up_rows)
    third[1].relay()
    fourth[0].relay()
    loop(3, lambda n: up_rows(n + 1))
    grad_rows(1)
    fourth[1].start()
    loop(2, down_rows)
    fourth[1].relay()
    loop(2, lambda n: down_rows(n + 2))
    weights.advance()
    branch_terms(1)
    r.branch.put()
    weights.advance(5)
    for m in both:
        fourth[m].finish()
    weights.close()
    for m in both:
        for step in (gather_x, gather_g, second, third, fourth):
            step[m].close()
        shifts[m].wait_send()
        there[m].close()
        back[m].close()
    loop(count - 1, lambda j: tell(j + 1).wait_send())


def backward_kernel(r):
    scale = TILE**-0.5
    links = Links(r.send, r.recv)
    ring = head_ring(links)
    plane = Plane(links)
    opposite = {"head": ring.chunk(2)}
    place, count = lax.axis_index("blk"), lax.axis_size("blk")
    both = range(2)
    r.total_mlp[plane.last[0]] = r.seeds[0]
    r.total_mlp[plane.last[1]] = r.seeds[1]
    barrier = pltpu.get_barrier_semaphore()
    pl.semaphore_signal(barrier, inc=1, device_id=opposite, device_id_type=MESH)
    pl.semaphore_wait(barrier, 1 + ring.greet() + greet_blocks())
    mlp_sum = PlaneGather(plane, r.total_mlp)
    mlp_sum.advance()
    qkv, kv_all, state_kv, stats = r.qkv, r.kv_all, r.state_kv, r.stats
    r.branch.get()
    branch = r.branch.ref
    outs = [Reduce(ring, by_rows(branch.at[m]), r.mids.at[m], r.intos.at[m]) for m in both]
    ends = [
        Reduce(ring, by_rows(branch.at[m]), r.mids.at[2 + m], r.intos.at[2 + m]) for m in both
    ]
    for m in both:
        outs[m].start()
    before = {"blk": lax.rem(place + count - 1, count)}
    shifts = [
        remote(r.early.at[m], r.later.at[m], r.s0.at[m], r.r0.at[m], before) for m in both
    ]
    there = [
        Exchange(r.grad_prior.at[m], r.moved.at[m], r.s1.at[m], r.r1.at[m], r.local.at[m])
        for m in both
    ]
    back = [
        Exchange(r.held.at[m], r.grad_after.at[m], r.s2.at[m], r.r2.at[m], r.local.at[2 + m])
        for m in both
    ]
    for ref in (r.near, r.sums, r.g_query, r.g_bias, r.g_scale, r.grad_kv, r.grad_state):
        ref[...] = jnp.zeros(ref.shape, F32)

    def own_chunk(qi):
        return lax.rem(qi + 4 - ring.me, 4)

    def attention_rows(m):
        part = nt(r.whole_gm[m].reshape(512, 1024), r.w_out[...]).astype(BF)
        for k in range(4):
            r.grad_att[m, ring.row_chunk(k)] = part[k * TILE : (k + 1) * TILE]

    def attend(m):
        def step(qi):
            rows, window = tile_of(qi), window_of(qi)
            shut = closed_row(r.closed[m, 0:1], qi)
            for h in range(2):
                k_cols, v_cols = head(h), head(h, base=256)
                sk_cols = slice(h * 256, h * 256 + TILE)
                sv_cols = slice(h * 256 + TILE, (h + 1) * 256)
                q = qkv[m, rows, head(h)]
                d = r.grad_att[m, rows, head(h)]
                level = stats[m, rows, 2 + h : 3 + h]
                token = jnp.exp(
                    nt(q, kv_all[m, window, k_cols]) * scale + (r.table[h] + shut) - level
                )
                from_state = jnp.exp(nt(q, state_kv[m, :, sk_cols]) * scale - level)
                grad_token = nt(d, kv_all[m, window, v_cols])
                grad_from = nt(d, state_kv[m, :, sv_cols])
                delta = jnp.sum(token * grad_token, axis=-1, keepdims=True) + jnp.sum(
                    from_state * grad_from, axis=-1, keepdims=True
                )
                grad_token = token * (grad_token - delta)
                grad_from = from_state * (grad_from - delta)
                r.near[h, :, 0:128] += (
                    grad_token[:, 0:128] + grad_token[:, 128:256] + grad_token[:, 256:384]
                )
                r.near[h, :, 128:384] += grad_token[:, 384:640]
                token_low = grad_token.astype(BF)
                from_low = grad_from.astype(BF)
                grad_q = scale * (
                    nn(token_low, kv_all[m, window, k_cols]) + nn(from_low, state_kv[m, :, sk_cols])
                )
                r.dqkv[m, own_chunk(qi), :, head(h)] = grad_q.astype(BF)
                r.grad_kv[m, window, k_cols] += tn(token_low, q)
                r.grad_kv[m, window, v_cols] += tn(token.astype(BF), d)
                r.grad_state[m, :, sk_cols] += tn(from_low, q)
                r.grad_state[m, :, sv_cols] += tn(from_state.astype(BF), d)

        return step

    def pass_on(m):
        r.early[m, :, 0:256] = (scale * r.grad_kv[m, 0:512, 0:256]).astype(BF)
        r.early[m, :, 256:512] = r.grad_kv[m, 0:512, 256:512].astype(BF)
        for h in range(2):
            low = jnp.concatenate(
                [
                    (scale * r.grad_state[m, :, h * 256 : h * 256 + TILE]).astype(BF),
                    r.grad_state[m, :, h * 256 + TILE : (h + 1) * 256].astype(BF),
                ],
                1,
            )
            r.grad_prior[m, :, head(h)] = nt(low, r.state_proj.ref[h]).astype(BF)
            part = tn(r.prior.ref[m, :, head(h)], low)
            r.g_proj[h] = part if m == 0 else r.g_proj[h] + part
        there[m].start()
        shifts[m].start()

    def scan(m):
        def step(t, grad):
            b = count - 1 - t
            rows = tile_of(b, 16)
            r.held[m, rows] = grad.astype(BF)
            u = r.across.ref[m, rows].astype(F32)
            forget = jax.nn.sigmoid(r.bias[...] + r.slope[...] * u)
            moved = r.moved[m, rows].astype(F32)
            return r.keeps.ref[b, m : m + 1] * (moved + forget * grad)

        lax.fori_loop(0, count, step, jnp.zeros((16, 256), F32))

    def bucket_sums():
        row = lax.broadcasted_iota(jnp.int32, (TILE, TILE), 0)
        col = lax.broadcasted_iota(jnp.int32, (TILE, TILE), 1)
        distance = [row - col + TILE, row - col]
        for h in range(2):
            for t in range(BUCKETS):
                total = jnp.zeros((1, TILE), F32)
                for part in range(2):
                    d = distance[part]
                    inside = d >= STARTS[t]
                    if t + 1 < BUCKETS:
                        inside = inside & (d < STARTS[t + 1])
                    values = r.near[h, :, TILE * (part + 1) : TILE * (part + 2)]
                    total = total + jnp.sum(
                        jnp.where(inside, values, 0.0), axis=0, keepdims=True
                    )
                if t + 1 == BUCKETS:
                    total = total + jnp.sum(r.near[h, :, 0:TILE], axis=0, keepdims=True)
                r.sums[t : t + 1] = total
            r.g_rel[h] = lax.dot_general(
                jnp.ones((8, TILE), F32),
                r.sums[...],
                (((1,), (1,)), ((), ())),
                precision=lax.Precision.HIGHEST,
                preferred_element_type=F32,
            )

    def update_tile(m):
        def step(t):
            rows = tile_of(t)
            for h in range(2):
                cols, k_cols, v_cols = head(h), head(h, base=256), head(h, base=512)
                grad = r.grad_after[m, rows, cols].astype(F32)
                u = r.update.ref[m, rows, cols]
                inverse = inverse_rms(u)
                unit = u * inverse
                forget = jax.nn.sigmoid(r.bias[:, cols] + r.slope[:, cols] * unit)
                gate = grad * (r.prior.ref[m, rows, cols].astype(F32) - unit)
                gate = gate * forget * (1.0 - forget)
                r.g_bias[:, cols] += jnp.sum(gate, axis=0, keepdims=True)
                r.g_scale[:, cols] += jnp.sum(gate * unit, axis=0, keepdims=True)
                grad_unit = grad * (1.0 - forget) + gate * r.slope[:, cols]
                inner = jnp.mean(grad_unit * unit, axis=-1, keepdims=True)
                low = (inverse * (grad_unit - unit * inner)).astype(BF)
                q = r.state_query.ref[rows, cols]
                probs = jnp.exp(nt(q, qkv[m, :, k_cols]) * scale - stats[m, rows, h : h + 1])
                grad_probs = nt(low, qkv[m, :, v_cols])
                delta = jnp.sum(probs * grad_probs, axis=-1, keepdims=True)
                grad_scores = (probs * (grad_probs - delta)).astype(BF)
                r.g_query[rows, cols] += scale * nn(grad_scores, qkv[m, :, k_cols])
                r.grad_kv[m, 512:1024, cols] += tn(grad_scores, q)
                r.grad_kv[m, 512:1024, head(h, base=256)] += tn(probs.astype(BF), low)

        return step

    def finish_rows(m):
        def step(t):
            rows = tile_of(t)
            full = r.grad_kv[m, pl.ds(pl.multiple_of(512 + t * TILE, TILE), TILE)]
            extra = r.later[m, rows].astype(F32)
            at = own_chunk(t)
            r.dqkv[m, at, :, 256:512] = (scale * full[:, 0:256] + extra[:, 0:256]).astype(BF)
            r.dqkv[m, at, :, 512:768] = (full[:, 256:512] + extra[:, 256:512]).astype(BF)

        return step

    def out_weights(n):
        rows = tile_of(n, 256)
        part = tn(r.att_rel.ref[0].reshape(512, 256), r.whole_gm[0, :, :, rows].reshape(512, 256))
        part = part + tn(
            r.att_rel.ref[1].reshape(512, 256), r.whole_gm[1, :, :, rows].reshape(512, 256)
        )
        r.parts[rows, 768:1024] = part.astype(BF)

    def end_terms(m):
        def columns(n):
            cols = tile_of(n, 256)
            part = nt(r.dqkv[m].reshape(512, 768), r.w.ref[cols]).astype(BF)
            split_rows(branch, m, cols, part)

        loop(4, columns)

    def weight_rows(n):
        rows = slice(n * 256, (n + 1) * 256)
        whole = r.whole.ref
        part = tn(whole[0, :, :, rows].reshape(512, 256), r.dqkv[0].reshape(512, 768))
        part = part + tn(whole[1, :, :, rows].reshape(512, 256), r.dqkv[1].reshape(512, 768))
        r.parts[rows, 0:768] = part.astype(BF)
        product = part * r.w.ref[rows].astype(F32)
        high = product.astype(BF)
        low = (product - high.astype(F32)).astype(BF)
        ones = jnp.ones((8, 768), BF)
        return (nt(ones, high) + nt(ones, low))[0:1] / r.attn_gain[:, rows]

    def end_rows(m):
        grad_normed = ends[m].finish()
        rows = r.x.ref[m].astype(F32)
        inverse = inverse_rms(rows)
        unit = rows * inverse
        scaled = grad_normed * r.attn_gain[...]
        inner = jnp.mean(scaled * unit, axis=-1, keepdims=True)
        r.grad_x.ref[m] = r.grad_middle.ref[m] + inverse * (scaled - unit * inner)

    def give_seed(i, rows):
        r.total[plane.last[i]] = rows

    attention_rows(0)
    loop(2, attend(0))
    mlp_sum.advance()
    outs[0].relay()
    outs[1].relay()
    loop(2, lambda qi: attend(0)(qi + 2))
    mlp_sum.advance()
    r.prior.get()
    r.state_proj.get()
    pass_on(0)
    attention_rows(1)
    loop(2, attend(1))
    mlp_sum.advance()
    loop(2, lambda qi: attend(1)(qi + 2))
    mlp_sum.advance()
    pass_on(1)
    r.across.get()
    r.keeps.get()
    there[0].finish()
    scan(0)
    back[0].start()
    r.att_rel.get()
    loop(4, out_weights)
    mlp_sum.advance()
    there[1].finish()
    scan(1)
    back[1].start()
    bucket_sums()
    r.middle.get()
    for m in both:
        r.out.ref[m] = r.middle.ref[m] + outs[m].finish()
    r.out.put()
    r.update.get()
    r.state_query.get()
    for m in both:
        outs[m].close()
    r.w.get()
    r.whole.get()
    back[0].finish()
    loop(4, update_tile(0))
    shifts[0].wait_recv()
    loop(4, finish_rows(0))
    end_terms(0)
    ends[0].start()
    back[1].finish()
    loop(4, update_tile(1))
    shifts[1].wait_recv()
    loop(4, finish_rows(1))
    ends[0].relay()
    small = [weight_rows(n) for n in range(4)]
    small = small + [r.g_mlp_gain[:, n * 256 : (n + 1) * 256] for n in range(4)]
    small = small + [r.g_bias[...], r.g_scale[...], r.g_rel[0, 0:1], r.g_rel[1, 0:1]]
    r.parts[0:512, 1024:1280] = r.g_query[...].astype(BF)
    r.parts[512:768, 1024:1280] = r.g_proj[...].reshape(256, 256).astype(BF)
    r.parts[768:784, 1024:1280] = jnp.concatenate(small + [jnp.zeros((4, 256), F32)], 0).astype(BF)
    r.parts[784:1024, 1024:1280] = jnp.zeros((240, 256), BF)
    weights = PlaneReduce(
        plane, r.parts, give_seed, r.half, r.mid, r.into, r.quarter, r.small_mid, r.small_into
    )
    spread = PlaneGather(plane, r.total)
    weights.advance()
    end_terms(1)
    ends[1].start()
    weights.advance()
    r.x.get()
    r.grad_middle.get()
    end_rows(0)
    weights.advance()
    ends[1].relay()
    weights.advance(3)
    spread.advance()
    end_rows(1)
    r.grad_x.put()
    spread.advance(5)
    own = r.total.at[768:784, 1024:1280]
    swaps = [
        links.go(own, r.others.at[i], peer)
        for i, peer in enumerate((ring.right, opposite, ring.left))
    ]
    mlp_sum.advance(6)
    mlp_sum.close()
    weights.close()
    spread.close()
    for m in both:
        ends[m].close()
        shifts[m].wait_send()
        there[m].close()
        back[m].close()
    for swap in swaps:
        swap.wait_recv()
    r.gains[...] = r.total[768:784, 1024:1280].astype(F32) + (
        r.others[0].astype(F32) + r.others[1].astype(F32) + r.others[2].astype(F32)
    )
    for swap in swaps:
        swap.wait_send()


class Late:
    def __init__(self, source, ref, sem):
        self.ref = ref
        self.copy = pltpu.make_async_copy(source, ref, sem)
        self.copy.start()
        self.open = True

    def get(self):
        if self.open:
            self.copy.wait()
            self.open = False


class Early:
    def __init__(self, target, ref, sem):
        self.ref = ref
        self.copy = pltpu.make_async_copy(ref, target, sem)
        self.sent = False

    def put(self):
        self.copy.start()
        self.sent = True


def call(kernel, name, number, now, late, small, outs, early, scratch, semaphores):
    anywhere = pl.BlockSpec(memory_space=pl.ANY)
    in_names = list(now) + list(small) + list(late)
    out_names = list(outs) + list(early)
    own = [a.shape for a in late.values()], [a.dtype for a in late.values()]
    buffers = list(zip(*own)) + list(early.values()) + list(scratch.values())

    def run(*refs):
        n, o = len(in_names), len(out_names)
        r = types.SimpleNamespace()
        held = refs[n + o : n + o + len(buffers)]
        rest = refs[n + o + len(buffers) :]
        fetch, store = rest[0], rest[1]
        for key, ref in zip(in_names[: len(now) + len(small)], refs):
            setattr(r, key, ref)
        for i, key in enumerate(late):
            setattr(r, key, Late(refs[len(now) + len(small) + i], held[i], fetch.at[i]))
        for key, ref in zip(outs, refs[n:]):
            setattr(r, key, ref)
        stores = []
        for i, key in enumerate(early):
            result = Early(refs[n + len(outs) + i], held[len(late) + i], store.at[i])
            setattr(r, key, result)
            stores.append(result)
        for key, ref in zip(scratch, held[len(late) + len(early) :]):
            setattr(r, key, ref)
        for key, ref in zip(semaphores, rest[2:]):
            setattr(r, key, ref)
        kernel(r)
        for result in stores:
            if not result.sent:
                result.put()
            result.copy.wait()

    shapes = list(outs.values()) + list(early.values())
    results = pl.pallas_call(
        run,
        out_shape=tuple(jax.ShapeDtypeStruct(shape, kind) for shape, kind in shapes),
        in_specs=[VMEM] * len(now) + [SMEM] * len(small) + [anywhere] * len(late),
        out_specs=tuple([VMEM] * len(outs) + [anywhere] * len(early)),
        scratch_shapes=[pltpu.VMEM(shape, kind) for shape, kind in buffers]
        + [sems(max(1, len(late))), sems(max(1, len(early)))]
        + list(semaphores.values()),
        compiler_params=pltpu.CompilerParams(
            collective_id=number, has_side_effects=True, vmem_limit_bytes=LIMIT
        ),
        name=name,
    )(*now.values(), *small.values(), *late.values())
    return dict(zip(out_names, results))


def sems(*shape):
    return pltpu.SemaphoreType.DMA(shape)


def body(
    tokens_in,
    grad_out,
    flags,
    attn_gain,
    mlp_gain,
    w_qkv,
    w_out,
    rel_bias,
    state_query,
    state_proj,
    forget_bias,
    forget_scale,
    w_up,
    w_down,
):
    micros, rows, width = tokens_in.shape
    block = rows * 4
    local = w_qkv.shape[2]
    heads = rel_bias.shape[1]
    states = state_query.shape[0]
    buckets = rel_bias.shape[0]
    count = lax.axis_size("blk")
    w = w_qkv.reshape(width, 3 * local)
    keep_own = (1 - flags[:, 0]).astype(F32)
    closed = jnp.broadcast_to(
        jnp.where(flags == 0, 0.0, MASKED).astype(F32)[:, :, None], (micros, 8, 5 * TILE)
    )
    own_keep = jnp.broadcast_to(
        jnp.concatenate([keep_own, jnp.zeros((8 - micros,), F32)])[:, None], (8, local)
    )
    whole_shape = ((micros, 4, rows, width), BF)
    state_low = ((micros, states, local), BF)
    state_wide = ((micros, states, local), F32)
    rows_wide = ((micros, rows, width), F32)
    mlp_width = w_up.shape[1] + w_down.shape[1]
    exchange = dict(
        s0=sems(2),
        r0=sems(2),
        s1=sems(2, count),
        r1=sems(2, count),
        s2=sems(2, count),
        r2=sems(2, count),
        local=sems(4),
    )
    gates = dict(bias=forget_bias[None], slope=forget_scale[None])
    f = call(
        forward_kernel,
        "forward",
        1,
        dict(
            x=tokens_in,
            g=grad_out,
            attn_gain=attn_gain[None],
            mlp_gain=mlp_gain[None],
            w=w,
            state_query=state_query,
            state_proj=state_proj,
            own_keep=own_keep,
            closed=closed,
            **gates,
        ),
        dict(w_out=w_out, w_up=w_up, w_down=w_down),
        dict(rel=rel_bias),
        dict(
            grad_middle=rows_wide,
            whole_gm=whole_shape,
            seeds=((2, 16, mlp_width), BF),
            g_gain=((1, width), F32),
        ),
        dict(
            whole=whole_shape,
            qkv=((micros, block, 3 * local), BF),
            kv_all=((micros, 2 * block, 2 * local), BF),
            state_kv=((micros, states, 2 * local), BF),
            prior=state_low,
            across=state_low,
            keeps=((count, 8, local), F32),
            update=state_wide,
            stats=((micros, block, TILE), F32),
            table=((heads, TILE, 5 * TILE), F32),
            state_after=state_wide,
            att_rel=((micros, 4, rows, local), BF),
            middle=rows_wide,
            branch=whole_shape,
        ),
        dict(
            whole_grad=whole_shape,
            unit_low=state_low,
            held=state_low,
            terms=whole_shape,
            whole_mlp=whole_shape,
            active=((micros, block, w_up.shape[1]), BF),
            grad_hidden=((micros, block, w_up.shape[1]), BF),
            mids=((4, 4, rows // 2, width), BF),
            intos=((4, 2, rows, width), BF),
            parts=((width, mlp_width), BF),
            **reduce_scratch(mlp_width),
        ),
        dict(send=sems(104), recv=sems(104), s3=sems(count), r3=sems(count), **exchange),
    )
    b = call(
        backward_kernel,
        "backward",
        2,
        dict(
            whole_gm=f["whole_gm"],
            w_out=w_out,
            qkv=f["qkv"],
            kv_all=f["kv_all"],
            state_kv=f["state_kv"],
            stats=f["stats"],
            table=f["table"],
            closed=closed,
            seeds=f["seeds"],
            attn_gain=attn_gain[None],
            g_mlp_gain=f["g_gain"],
            **gates,
        ),
        dict(
            branch=f["branch"],
            prior=f["prior"],
            state_proj=state_proj,
            across=f["across"],
            keeps=f["keeps"],
            att_rel=f["att_rel"],
            middle=f["middle"],
            update=f["update"],
            state_query=state_query,
            w=w,
            whole=f["whole"],
            x=tokens_in,
            grad_middle=f["grad_middle"],
        ),
        {},
        dict(
            total_mlp=((width, mlp_width), BF),
            total=((width, 1280), BF),
            gains=((16, local), F32),
        ),
        dict(out=rows_wide, grad_x=rows_wide),
        dict(
            dqkv=((micros, 4, rows, 3 * local), BF),
            g_query=((states, local), F32),
            g_proj=(state_proj.shape, F32),
            g_rel=((heads, 8, local), F32),
            g_bias=((1, local), F32),
            g_scale=((1, local), F32),
            grad_att=((micros, block, local), BF),
            grad_kv=((micros, 2 * block, 2 * local), F32),
            grad_state=((micros, states, 2 * local), F32),
            early=((micros, block, 2 * local), BF),
            later=((micros, block, 2 * local), BF),
            grad_prior=state_low,
            moved=state_low,
            held=state_low,
            grad_after=state_low,
            near=((heads, TILE, 3 * TILE), F32),
            sums=((local, TILE), F32),
            mids=((4, 4, rows // 2, width), BF),
            intos=((4, 2, rows, width), BF),
            others=((3, 16, local), BF),
            parts=((width, 1280), BF),
            **reduce_scratch(1280),
        ),
        dict(send=sems(104), recv=sems(104), **exchange),
    )
    total, g_mlp, gains = b["total"], b["total_mlp"], b["gains"]
    g_out = jnp.concatenate(
        [total[n * 256 : (n + 1) * 256, 768:1024] for n in range(4)], 1
    ).astype(F32)
    side = total[:784, 1024:1280].astype(F32)
    return (
        b["out"],
        b["grad_x"],
        f["state_after"][:, None],
        gains[0:4].reshape(width),
        gains[4:8].reshape(width),
        total[:, 0:768].astype(F32).reshape(width, 3, local),
        g_out,
        jnp.transpose(side[778:780, :buckets]),
        side[:512],
        side[512:768].reshape(state_proj.shape),
        side[776],
        side[777],
        g_mlp[:, :1024].astype(F32),
        g_mlp[:, 1024:].astype(F32),
    )


def solution(mesh):
    return jax.shard_map(
        body,
        mesh=mesh,
        in_specs=(
            P(None, ("blk", "head"), None),
            P(None, ("blk", "head"), None),
            P(None, "blk"),
            P(),
            P(),
            P(None, None, "head"),
            P("head", None),
            P(None, "head"),
            P(None, "head"),
            P("head", None, None),
            P("head"),
            P("head"),
            P(None, "head"),
            P("head", None),
        ),
        out_specs=(
            P(None, ("blk", "head"), None),
            P(None, ("blk", "head"), None),
            P(None, "blk", None, "head"),
            P(),
            P(),
            P(None, None, "head"),
            P("head", None),
            P(None, "head"),
            P(None, "head"),
            P("head", None, None),
            P("head"),
            P("head"),
            P(None, "head"),
            P("head", None),
        ),
        check_vma=False,
    )
```

```python
import math
import types

import jax
import jax.numpy as jnp
from jax import lax
from jax.experimental import pallas as pl
from jax.experimental.pallas import tpu as pltpu
from jax.sharding import PartitionSpec as P

BUCKETS = 32
MAXDIST = 128
EPSILON = 1e-06
MASKED = -1e30
TILE = 128
MESH = pl.DeviceIdType.MESH
BF = jnp.bfloat16
F32 = jnp.float32
VMEM = pl.BlockSpec(memory_space=pltpu.VMEM)
SMEM = pl.BlockSpec(memory_space=pltpu.SMEM)
LIMIT = 60 * 2**20
ROOT = math.sqrt(2.0 / math.pi)
CUBIC = 0.044715


def bucket_starts():
    exact = BUCKETS // 2
    levels = [
        int(math.ceil(exact * (MAXDIST / exact) ** (t / (BUCKETS - exact))))
        for t in range(1, BUCKETS - exact)
    ]
    return list(range(exact + 1)) + levels


STARTS = bucket_starts()


def nn(a, b):
    return lax.dot_general(a, b, (((1,), (0,)), ((), ())), preferred_element_type=F32)


def nt(a, b):
    return lax.dot_general(a, b, (((1,), (1,)), ((), ())), preferred_element_type=F32)


def tn(a, b):
    return lax.dot_general(a, b, (((0,), (0,)), ((), ())), preferred_element_type=F32)


def inverse_rms(values):
    return lax.rsqrt(jnp.mean(values * values, axis=-1, keepdims=True) + EPSILON)


def tile_of(index, size=TILE):
    return pl.ds(pl.multiple_of(index * size, size), size)


def loop(count, step):
    def run(i, c):
        step(i)
        return c

    lax.fori_loop(0, count, run, 0)


def remote(src, dst, send_sem, recv_sem, device):
    return pltpu.make_async_remote_copy(
        src_ref=src,
        dst_ref=dst,
        send_sem=send_sem,
        recv_sem=recv_sem,
        device_id=device,
        device_id_type=MESH,
    )


class Links:
    def __init__(self, send, recv):
        self.send, self.recv, self.used = send, recv, 0

    def go(self, src, dst, device):
        copy = remote(src, dst, self.send.at[self.used], self.recv.at[self.used], device)
        self.used += 1
        copy.start()
        return copy


class Ring:
    def __init__(self, links, me, device):
        self.links, self.me = links, me
        self.right = device(lax.rem(me + 1, 4))
        self.left = device(lax.rem(me + 3, 4))
        self.opposite = device(lax.rem(me + 2, 4))

    def go(self, src, dst, peer):
        return self.links.go(src, dst, peer)

    def greet(self):
        barrier = pltpu.get_barrier_semaphore()
        for peer in (self.right, self.left):
            pl.semaphore_signal(barrier, inc=1, device_id=peer, device_id_type=MESH)
        return 2

    def chunk(self, k):
        return lax.rem(self.me + k, 4)

    def row_chunk(self, k):
        return tile_of(self.chunk(k))


def head_ring(links):
    return Ring(links, lax.axis_index("head"), lambda i: {"head": i})


def by_rows(buf):
    half = buf.shape[1] // 2

    def piece(k, part=None, offset=0):
        return buf.at[k] if part is None else buf.at[k, part * half : (part + 1) * half]

    return piece


def by_columns(buf, base, rows, chunk):
    half = buf.shape[1] // 2

    def piece(k, part=None, offset=0):
        at = pl.ds(pl.multiple_of(base + chunk(k + offset) * rows, rows), rows)
        return buf.at[at] if part is None else buf.at[at, part * half : (part + 1) * half]

    return piece


class Gather:
    def __init__(self, ring, piece):
        self.ring, self.piece = ring, piece

    def start(self):
        r, p = self.ring, self.piece
        self.a0 = r.go(p(0, 0), p(3, 0, 1), r.right)
        self.b0 = r.go(p(0, 1), p(1, 1, 3), r.left)
        self.a1 = r.go(p(0, 1), p(3, 1, 1), r.right)
        self.b1 = r.go(p(0, 0), p(1, 0, 3), r.left)

    def relay(self):
        r, p = self.ring, self.piece
        self.a0.wait_recv()
        self.a2 = r.go(p(3, 0), p(2, 0, 1), r.right)
        self.b0.wait_recv()
        self.b2 = r.go(p(1, 1), p(2, 1, 3), r.left)

    def finish(self):
        for copy in (self.a1, self.b1, self.a2, self.b2):
            copy.wait_recv()

    def close(self):
        for copy in (self.a0, self.b0, self.a1, self.b1, self.a2, self.b2):
            copy.wait_send()


class Reduce:
    def __init__(self, ring, terms, mid, into):
        self.ring, self.terms, self.mid, self.into = ring, terms, mid, into
        if mid.shape[1] == into.shape[1]:
            half = into.shape[2] // 2
            self.place = lambda i, part: into.at[i, :, part * half : (part + 1) * half]
        else:
            half = into.shape[1] // 2
            self.place = lambda i, part: into.at[i, part * half : (part + 1) * half]

    def start(self):
        r, t = self.ring, self.terms
        self.a0 = r.go(t(2, 0), self.mid.at[0], r.right)
        self.b0 = r.go(t(2, 1), self.mid.at[1], r.left)
        self.a1 = r.go(t(1, 1), self.place(0, 1), r.right)
        self.b1 = r.go(t(3, 0), self.place(1, 0), r.left)

    def relay(self):
        r, t, mid = self.ring, self.terms, self.mid
        self.a0.wait_recv()
        mid[2] = (mid[0].astype(F32) + t(1, 0)[...].astype(F32)).astype(BF)
        self.a2 = r.go(mid.at[2], self.place(0, 0), r.right)
        self.b0.wait_recv()
        mid[3] = (mid[1].astype(F32) + t(3, 1)[...].astype(F32)).astype(BF)
        self.b2 = r.go(mid.at[3], self.place(1, 1), r.left)

    def finish(self):
        for copy in (self.a1, self.b1, self.a2, self.b2):
            copy.wait_recv()
        return (
            self.terms(0)[...].astype(F32)
            + self.into[0].astype(F32)
            + self.into[1].astype(F32)
        )

    def close(self):
        for copy in (self.a0, self.b0, self.a1, self.b1, self.a2, self.b2):
            copy.wait_send()


def block_device(x, z, c):
    return {"blk": (x * 4 + z) * 2 + c}


def block_place():
    place = lax.axis_index("blk")
    return place % 2, (place // 2) % 4, place // 8


class Plane:
    def __init__(self, links):
        c, z, x = block_place()
        self.links = links
        self.peer = block_device(x, z, 1 - c)
        rx = Ring(links, x, lambda i: block_device(i, z, c))
        rz = Ring(links, z, lambda i: block_device(x, i, c))
        self.rings = [rx, rz]
        self.first, self.second = (rx, rz), (rz, rx)
        self.base = c * 512
        self.own = pl.ds(pl.multiple_of(c * 512, 512), 512)
        self.away = pl.ds(pl.multiple_of((1 - c) * 512, 512), 512)
        self.top = [c * 512 + x * 64, c * 512 + 256 + z * 64]
        self.last = [
            pl.ds(pl.multiple_of(self.top[0] + z * 16, 16), 16),
            pl.ds(pl.multiple_of(self.top[1] + x * 16, 16), 16),
        ]

    def greet(self):
        barrier = pltpu.get_barrier_semaphore()
        pl.semaphore_signal(barrier, inc=1, device_id=self.peer, device_id_type=MESH)
        return 1 + sum(ring.greet() for ring in self.rings)


class Steps:
    def advance(self, steps=1):
        for _ in range(steps):
            if self.steps:
                self.steps.pop(0)()


class PlaneReduce(Steps):
    def __init__(self, plane, parts, result, extra, half, mid, into, quarter, small_into):
        self.plane, self.parts, self.result, self.half = plane, parts, result, half
        self.quarter, self.extra = quarter, extra
        first, second = plane.first, plane.second
        self.reduce1 = [
            Reduce(first[i], by_columns(half, i * 256, 64, first[i].chunk), mid.at[i], into.at[i])
            for i in range(2)
        ]
        self.reduce2 = [
            ReduceDirect(
                second[i], by_columns(quarter.at[i], 0, 16, second[i].chunk), small_into.at[i]
            )
            for i in range(2)
        ]
        self.steps = [
            self.cores,
            self.start1,
            lambda: [r.relay() for r in self.reduce1],
            self.start2,
            self.finish,
        ]

    def cores(self):
        plane = self.plane
        self.swap = plane.links.go(self.parts.at[plane.away], self.half, plane.peer)

    def start1(self):
        self.swap.wait_recv()

        def add(t):
            rows = tile_of(t, 64)
            own = pl.ds(pl.multiple_of(self.plane.base + t * 64, 64), 64)
            self.half[rows] = (
                self.parts[own].astype(F32) + self.half[rows].astype(F32)
            ).astype(BF)

        loop(8, add)
        self.extra()
        for r in self.reduce1:
            r.start()

    def start2(self):
        for i, r in enumerate(self.reduce1):
            self.quarter[i] = r.finish().astype(BF)
            self.reduce2[i].start()

    def finish(self):
        for i, r in enumerate(self.reduce2):
            self.result(i, r.finish().astype(BF))

    def close(self):
        self.swap.wait_send()
        for r in self.reduce1 + self.reduce2:
            r.close()


class PlaneGather(Steps):
    def __init__(self, plane, total):
        self.plane, self.total = plane, total
        first, second = plane.first, plane.second
        self.gather1 = [
            GatherDirect(second[i], by_columns(total, plane.top[i], 16, second[i].chunk))
            for i in range(2)
        ]
        self.gather2 = [
            Gather(first[i], by_columns(total, plane.base + i * 256, 64, first[i].chunk))
            for i in range(2)
        ]
        self.steps = [
            lambda: [g.start() for g in self.gather1],
            self.start2,
            lambda: [g.relay() for g in self.gather2],
            self.cores,
            lambda: self.swap.wait_recv(),
        ]

    def start2(self):
        for i, g in enumerate(self.gather1):
            g.finish()
            self.gather2[i].start()

    def cores(self):
        for g in self.gather2:
            g.finish()
        rows = self.total.at[self.plane.own]
        self.swap = self.plane.links.go(rows, rows, self.plane.peer)

    def close(self):
        self.swap.wait_send()
        for g in self.gather1 + self.gather2:
            g.close()


def reduce_scratch(width):
    return dict(
        half=((512, width), BF),
        mid=((2, 4, 64, width // 2), BF),
        into=((2, 2, 64, width), BF),
        quarter=((2, 64, width), BF),
        small_into=((2, 3, 16, width), BF),
    )


class GatherDirect:
    def __init__(self, ring, piece):
        self.ring, self.piece = ring, piece

    def start(self):
        r, p = self.ring, self.piece
        self.copies = [
            r.go(p(0), p(4 - k, None, k), peer)
            for k, peer in ((1, r.right), (3, r.left), (2, r.opposite))
        ]

    def finish(self):
        for copy in self.copies:
            copy.wait_recv()

    def close(self):
        for copy in self.copies:
            copy.wait_send()


class ReduceDirect:
    def __init__(self, ring, terms, into):
        self.ring, self.terms, self.into = ring, terms, into

    def start(self):
        r, t = self.ring, self.terms
        self.copies = [
            r.go(t(k), self.into.at[k - 1], peer)
            for k, peer in ((1, r.right), (3, r.left), (2, r.opposite))
        ]

    def finish(self):
        for copy in self.copies:
            copy.wait_recv()
        total = self.terms(0)[...].astype(F32)
        for k in range(3):
            total = total + self.into[k].astype(F32)
        return total

    def close(self):
        for copy in self.copies:
            copy.wait_send()


class Exchange:
    def __init__(self, source, target, send, recv, local):
        self.count = lax.axis_size("blk")
        self.place = lax.axis_index("blk")
        self.size = source.shape[0] // self.count
        self.source, self.target = source, target
        self.send, self.recv, self.local = send, recv, local

    def part(self, j):
        peer = lax.rem(self.place + j, self.count)
        return remote(
            self.source.at[tile_of(peer, self.size)],
            self.target.at[tile_of(self.place, self.size)],
            self.send.at[j],
            self.recv.at[j],
            {"blk": peer},
        )

    def own(self):
        rows = tile_of(self.place, self.size)
        return pltpu.make_async_copy(self.source.at[rows], self.target.at[rows], self.local)

    def start(self):
        loop(self.count - 1, lambda j: self.part(j + 1).start())
        self.own().start()

    def finish(self):
        self.own().wait()
        loop(self.count - 1, lambda j: self.part(j + 1).wait_recv())

    def close(self):
        loop(self.count - 1, lambda j: self.part(j + 1).wait_send())


def greet_blocks():
    barrier = pltpu.get_barrier_semaphore()
    count, place = lax.axis_size("blk"), lax.axis_index("blk")

    def greet(j):
        pl.semaphore_signal(
            barrier, inc=1, device_id={"blk": lax.rem(place + j + 1, count)}, device_id_type=MESH
        )

    loop(count - 1, greet)
    return count - 1


def closed_row(flag, qi):
    column = lax.broadcasted_iota(jnp.int32, (1, 5 * TILE), 1) + qi * TILE
    return jnp.where(column < 512, MASKED * flag.astype(F32), 0.0)


def head(h, size=TILE, base=0):
    return slice(base + h * size, base + (h + 1) * size)


def window_of(qi):
    return pl.ds(pl.multiple_of(qi * TILE, TILE), 5 * TILE)


def split_rows(target, m, cols, part):
    for k in range(4):
        target[m, k, :, cols] = part[k * TILE : (k + 1) * TILE]


def write_table(table, rel):
    row = lax.broadcasted_iota(jnp.int32, (TILE, TILE), 0)
    col = lax.broadcasted_iota(jnp.int32, (TILE, TILE), 1)
    for h in range(2):
        far = jnp.full((TILE, TILE), rel[h, BUCKETS - 1], F32)
        table[h, :, 0:128] = jnp.where(row < col, far, MASKED)
        table[h, :, 128:256] = far
        table[h, :, 256:384] = far
        for shift, at in ((TILE, 384), (0, 512)):
            distance = row - col + shift
            total = jnp.full((TILE, TILE), rel[h, 0], F32)
            for t in range(1, BUCKETS):
                total = jnp.where(distance >= STARTS[t], rel[h, t], total)
            table[h, :, at : at + TILE] = jnp.where(distance >= 0, total, MASKED)


def forward_kernel(r):
    scale = TILE**-0.5
    links = Links(r.send, r.recv)
    ring = head_ring(links)
    plane = Plane(links)
    place, count = lax.axis_index("blk"), lax.axis_size("blk")
    both = range(2)

    def norm_rows(m):
        rows = r.x[m].astype(F32)
        r.whole.ref[m, 0] = (rows * inverse_rms(rows) * r.attn_gain[...]).astype(BF)

    norm_rows(0)
    for m in both:
        r.whole_grad[m, 0] = r.g[m]
        keep = 1.0 - r.flags[0, m].astype(F32)
        r.own_keep[m : m + 1] = jnp.full((1, 256), keep, F32)
    r.own_keep[2:8] = jnp.zeros((6, 256), F32)
    pl.semaphore_wait(pltpu.get_barrier_semaphore(), ring.greet() + greet_blocks())
    whole, qkv, kv_all = r.whole.ref, r.qkv.ref, r.kv_all.ref
    prior, across, keeps = r.prior.ref, r.across.ref, r.keeps.ref
    update, stats, state_kv = r.update.ref, r.stats.ref, r.state_kv.ref
    table, att_rel, middle, branch = r.table.ref, r.att_rel.ref, r.middle.ref, r.branch.ref
    gather_x = [Gather(ring, by_rows(whole.at[m])) for m in both]
    gather_g = [Gather(ring, by_rows(r.whole_grad.at[m])) for m in both]
    gather_x[0].start()
    norm_rows(1)

    def tell(j):
        peer = {"blk": lax.rem(place + j, count)}
        return remote(r.own_keep, keeps.at[place], r.s3.at[j], r.r3.at[j], peer)

    loop(count - 1, lambda j: tell(j + 1).start())
    keeps[place] = r.own_keep[...]
    write_table(table, r.rel)
    r.table.put()
    after = {"blk": lax.rem(place + 1, count)}
    shifts = [
        remote(qkv.at[m, :, 256:768], kv_all.at[m, 0:512], r.s0.at[m], r.r0.at[m], after)
        for m in both
    ]
    there = [
        Exchange(r.unit_low.at[m], across.at[m], r.s1.at[m], r.r1.at[m], r.local.at[m])
        for m in both
    ]
    back = [
        Exchange(r.held.at[m], prior.at[m], r.s2.at[m], r.r2.at[m], r.local.at[2 + m])
        for m in both
    ]

    def project(m):
        def columns(n):
            cols = tile_of(n, 256)
            part = nn(whole[m].reshape(512, 1024), r.w[n]).astype(BF)
            for k in range(4):
                qkv[m, ring.row_chunk(k), cols] = part[k * TILE : (k + 1) * TILE]

        loop(3, columns)
        shifts[m].start()
        kv_all[m, 512:1024] = qkv[m, :, 256:768]

    def update_tile(m):
        def step(t):
            rows = tile_of(t)
            for h in range(2):
                scores = nt(r.state_query[rows, head(h)], qkv[m, :, head(h, base=256)]) * scale
                top = jnp.max(scores, axis=-1, keepdims=True)
                raised = jnp.exp(scores - top)
                total = jnp.sum(raised, axis=-1, keepdims=True)
                stats[m, rows, h : h + 1] = top + jnp.log(total)
                u = nn((raised / total).astype(BF), qkv[m, :, head(h, base=512)])
                update[m, rows, head(h)] = u
                r.unit_low[m, rows, head(h)] = (u * inverse_rms(u)).astype(BF)

        return step

    def scan(m):
        def step(b, state):
            rows = tile_of(b, 16)
            u = across[m, rows].astype(F32)
            forget = jax.nn.sigmoid(r.bias[...] + r.slope[...] * u)
            before = keeps[b, m : m + 1] * state
            r.held[m, rows] = before.astype(BF)
            return forget * before + (1.0 - forget) * u

        lax.fori_loop(0, count, step, jnp.zeros((16, 256), F32))

    def state(m):
        def step(t):
            rows = tile_of(t)
            before = prior[m, rows]
            for h in range(2):
                state_kv[m, rows, head(h, 256)] = nn(before[:, head(h)], r.state_proj[h]).astype(BF)
                u = update[m, rows, head(h)]
                u = u * inverse_rms(u)
                forget = jax.nn.sigmoid(r.bias[:, head(h)] + r.slope[:, head(h)] * u)
                r.state_after.ref[m, rows, head(h)] = (
                    forget * before[:, head(h)].astype(F32) + (1.0 - forget) * u
                )

        return step

    def attend(m):
        def step(qi):
            rows, window = tile_of(qi), window_of(qi)
            shut = closed_row(r.flags[0, m], qi)
            for h in range(2):
                q = qkv[m, rows, head(h)]
                token = nt(q, kv_all[m, window, head(h)]) * scale + (table[h] + shut)
                from_state = nt(q, state_kv[m, :, h * 256 : h * 256 + TILE]) * scale
                top = jnp.maximum(
                    jnp.max(token, axis=-1, keepdims=True),
                    jnp.max(from_state, axis=-1, keepdims=True),
                )
                token = jnp.exp(token - top)
                from_state = jnp.exp(from_state - top)
                total = jnp.sum(token, axis=-1, keepdims=True) + jnp.sum(
                    from_state, axis=-1, keepdims=True
                )
                stats[m, rows, 2 + h : 3 + h] = top + jnp.log(total)
                out = nn(token.astype(BF), kv_all[m, window, head(h, base=256)]) + nn(
                    from_state.astype(BF), state_kv[m, :, h * 256 + TILE : (h + 1) * 256]
                )
                att_rel[m, lax.rem(qi + 4 - ring.me, 4), :, head(h)] = (out / total).astype(BF)

        return step

    first = [
        Reduce(ring, by_rows(r.terms.at[m]), r.mids.at[m], r.intos.at[m]) for m in both
    ]
    second = [Gather(ring, by_rows(r.whole_mlp.at[m])) for m in both]
    third = [
        Reduce(ring, by_rows(r.terms.at[m]), r.mids.at[2 + m], r.intos.at[2 + m]) for m in both
    ]
    fourth = Gather(ring, by_rows(r.gm0))

    def out_terms(m):
        def columns(n):
            cols = tile_of(n, 256)
            part = nn(att_rel[m].reshape(512, 256), r.w_out.ref[:, cols]).astype(BF)
            split_rows(r.terms, m, cols, part)

        loop(4, columns)

    def normalise(m):
        rows = r.x[m].astype(F32) + first[m].finish()
        middle[m] = rows
        r.whole_mlp[m, 0] = (rows * inverse_rms(rows) * r.mlp_gain[...]).astype(BF)

    def hidden(m):
        def columns(n):
            cols = tile_of(n, 256)
            value = nn(r.whole_mlp[m].reshape(512, 1024), r.w_up.ref[:, cols])
            grad_active = nt(r.whole_grad[m].reshape(512, 1024), r.w_down.ref[cols])
            square = value * value
            bent = jnp.tanh(ROOT * value * (1.0 + CUBIC * square))
            r.active[m, :, cols] = (0.5 * value * (1.0 + bent)).astype(BF)
            rise = 0.5 * (1.0 + bent) + 0.5 * value * (1.0 - bent * bent) * ROOT * (
                1.0 + 3.0 * CUBIC * square
            )
            r.grad_hidden[m, :, cols] = (grad_active * rise).astype(BF)

        return columns

    def grad_terms(m):
        def columns(n):
            cols = tile_of(n, 256)
            part = nt(r.grad_hidden[m], r.w_up.ref[cols]).astype(BF)
            split_rows(r.terms, m, cols, part)

        loop(4, columns)

    def branch_terms(m):
        def columns(n):
            cols = tile_of(n, 256)
            part = nn(r.active[m], r.w_down.ref[:, cols]).astype(BF)
            split_rows(branch, m, cols, part)

        loop(4, columns)

    def grad_rows(m):
        grad_normed = third[m].finish()
        rows = middle[m]
        inverse = inverse_rms(rows)
        unit = rows * inverse
        part = jnp.sum(grad_normed * unit, axis=0, keepdims=True)
        r.g_gain[...] = part if m == 0 else r.g_gain[...] + part
        scaled = grad_normed * r.mlp_gain[...]
        inner = jnp.mean(scaled * unit, axis=-1, keepdims=True)
        total = r.g[m].astype(F32) + inverse * (scaled - unit * inner)
        r.grad_middle[m] = total
        if m == 0:
            r.gm0[0] = total.astype(BF)

    def up_rows(n):
        rows = tile_of(n, 256)
        total = tn(r.whole_mlp[0, :, :, rows].reshape(512, 256), r.grad_hidden[0])
        total = total + tn(r.whole_mlp[1, :, :, rows].reshape(512, 256), r.grad_hidden[1])
        r.parts[rows, 0:1024] = total.astype(BF)

    def down_rows(n):
        rows = tile_of(n, 256)
        total = tn(r.active[0, :, rows], r.whole_grad[0].reshape(512, 1024))
        total = total + tn(r.active[1, :, rows], r.whole_grad[1].reshape(512, 1024))
        r.parts[rows, 1024:2048] = total.astype(BF)

    def keep_seed(i, rows):
        r.seeds[i] = rows

    weights = PlaneReduce(
        plane, r.parts, keep_seed, lambda: None, r.half, r.mid, r.into, r.quarter, r.small_into
    )

    gather_x[0].relay()
    gather_x[1].start()
    gather_x[0].finish()
    project(0)
    gather_x[1].relay()
    loop(4, update_tile(0))
    there[0].start()
    gather_x[1].finish()
    gather_g[0].start()
    project(1)
    r.whole.put()
    r.qkv.put()
    loop(4, update_tile(1))
    there[1].start()
    r.update.put()
    gather_g[0].relay()
    gather_g[1].start()
    loop(count - 1, lambda j: tell(j + 1).wait_recv())
    there[0].finish()
    scan(0)
    back[0].start()
    there[1].finish()
    scan(1)
    back[1].start()
    gather_g[1].relay()
    r.across.put()
    r.keeps.put()
    shifts[0].wait_recv()
    shifts[1].wait_recv()
    r.kv_all.put()
    back[0].finish()
    loop(4, state(0))
    loop(4, attend(0))
    r.w_out.get()
    out_terms(0)
    first[0].start()
    back[1].finish()
    r.prior.put()
    loop(4, state(1))
    r.state_kv.put()
    r.state_after.put()
    loop(1, attend(1))
    first[0].relay()
    loop(3, lambda qi: attend(1)(qi + 1))
    r.stats.put()
    out_terms(1)
    r.att_rel.put()
    first[1].start()
    normalise(0)
    second[0].start()
    first[1].relay()
    second[0].relay()
    r.w_up.get()
    r.w_down.get()
    gather_g[0].finish()
    gather_g[1].finish()
    normalise(1)
    second[1].start()
    r.middle.put()
    second[0].finish()
    loop(2, hidden(0))
    second[1].relay()
    loop(2, lambda n: hidden(0)(n + 2))
    first[0].close()
    grad_terms(0)
    third[0].start()
    second[1].finish()
    loop(2, hidden(1))
    third[0].relay()
    loop(2, lambda n: hidden(1)(n + 2))
    first[1].close()
    grad_terms(1)
    third[1].start()
    loop(4, up_rows)
    grad_rows(0)
    fourth.start()
    third[1].relay()
    loop(4, down_rows)
    weights.advance()
    fourth.relay()
    branch_terms(0)
    weights.advance()
    branch_terms(1)
    r.branch.put()
    weights.advance()
    grad_rows(1)
    weights.advance(2)
    fourth.finish()
    weights.close()
    fourth.close()
    for m in both:
        for step in (gather_x, gather_g, second, third):
            step[m].close()
        shifts[m].wait_send()
        there[m].close()
        back[m].close()
    loop(count - 1, lambda j: tell(j + 1).wait_send())


def backward_kernel(r):
    scale = TILE**-0.5
    links = Links(r.send, r.recv)
    ring = head_ring(links)
    plane = Plane(links)
    place, count = lax.axis_index("blk"), lax.axis_size("blk")
    both = range(2)
    r.total_mlp[plane.last[0]] = r.seeds[0]
    r.total_mlp[plane.last[1]] = r.seeds[1]
    gm = [r.gm0, r.gm1]
    r.gm1[0] = r.grad_middle[1].astype(BF)
    core = place % 2
    others = [
        {"head": ring.chunk(k), "blk": place - core + c} for k in range(1, 4) for c in range(2)
    ]
    barrier = pltpu.get_barrier_semaphore()
    for device in others:
        pl.semaphore_signal(barrier, inc=1, device_id=device, device_id_type=MESH)
    pl.semaphore_wait(barrier, len(others) + greet_blocks())
    fourth = Gather(ring, by_rows(r.gm1))
    fourth.start()
    mlp_sum = PlaneGather(plane, r.total_mlp)
    mlp_sum.advance()
    qkv, kv_all, state_kv, stats = r.qkv, r.kv_all, r.state_kv, r.stats
    r.branch.get()
    branch = r.branch.ref
    outs = [Reduce(ring, by_rows(branch.at[m]), r.mids.at[m], r.intos.at[m]) for m in both]
    ends = [
        Reduce(ring, by_rows(branch.at[m]), r.mids.at[2 + m], r.intos.at[2 + m]) for m in both
    ]
    before = {"blk": lax.rem(place + count - 1, count)}
    shifts = [
        remote(r.early.at[m], r.later.at[m], r.s0.at[m], r.r0.at[m], before) for m in both
    ]
    there = [
        Exchange(r.grad_prior.at[m], r.moved.at[m], r.s1.at[m], r.r1.at[m], r.local.at[m])
        for m in both
    ]
    back = [
        Exchange(r.held.at[m], r.grad_after.at[m], r.s2.at[m], r.r2.at[m], r.local.at[2 + m])
        for m in both
    ]
    for ref in (r.near, r.sums, r.g_query, r.g_bias, r.g_scale, r.grad_kv, r.grad_state):
        ref[...] = jnp.zeros(ref.shape, F32)

    def own_chunk(qi):
        return lax.rem(qi + 4 - ring.me, 4)

    def attention_rows(m):
        part = nt(gm[m][...].reshape(512, 1024), r.w_out[...]).astype(BF)
        for k in range(4):
            r.grad_att[m, ring.row_chunk(k)] = part[k * TILE : (k + 1) * TILE]

    def attend(m):
        def step(qi):
            rows, window = tile_of(qi), window_of(qi)
            shut = closed_row(r.flags[0, m], qi)
            for h in range(2):
                k_cols, v_cols = head(h), head(h, base=256)
                sk_cols = slice(h * 256, h * 256 + TILE)
                sv_cols = slice(h * 256 + TILE, (h + 1) * 256)
                q = qkv[m, rows, head(h)]
                d = r.grad_att[m, rows, head(h)]
                level = stats[m, rows, 2 + h : 3 + h]
                token = jnp.exp(
                    nt(q, kv_all[m, window, k_cols]) * scale + (r.table[h] + shut) - level
                )
                from_state = jnp.exp(nt(q, state_kv[m, :, sk_cols]) * scale - level)
                grad_token = nt(d, kv_all[m, window, v_cols])
                grad_from = nt(d, state_kv[m, :, sv_cols])
                delta = jnp.sum(token * grad_token, axis=-1, keepdims=True) + jnp.sum(
                    from_state * grad_from, axis=-1, keepdims=True
                )
                grad_token = token * (grad_token - delta)
                grad_from = from_state * (grad_from - delta)
                r.near[h, :, 0:128] += (
                    grad_token[:, 0:128] + grad_token[:, 128:256] + grad_token[:, 256:384]
                )
                r.near[h, :, 128:384] += grad_token[:, 384:640]
                token_low = grad_token.astype(BF)
                from_low = grad_from.astype(BF)
                grad_q = scale * (
                    nn(token_low, kv_all[m, window, k_cols]) + nn(from_low, state_kv[m, :, sk_cols])
                )
                r.dqkv[m, own_chunk(qi), :, head(h)] = grad_q.astype(BF)
                r.grad_kv[m, window, k_cols] += tn(token_low, q)
                r.grad_kv[m, window, v_cols] += tn(token.astype(BF), d)
                r.grad_state[m, :, sk_cols] += tn(from_low, q)
                r.grad_state[m, :, sv_cols] += tn(from_state.astype(BF), d)

        return step

    def pass_on(m):
        r.early[m, :, 0:256] = (scale * r.grad_kv[m, 0:512, 0:256]).astype(BF)
        r.early[m, :, 256:512] = r.grad_kv[m, 0:512, 256:512].astype(BF)
        for h in range(2):
            low = jnp.concatenate(
                [
                    (scale * r.grad_state[m, :, h * 256 : h * 256 + TILE]).astype(BF),
                    r.grad_state[m, :, h * 256 + TILE : (h + 1) * 256].astype(BF),
                ],
                1,
            )
            r.grad_prior[m, :, head(h)] = nt(low, r.state_proj.ref[h]).astype(BF)
            part = tn(r.prior.ref[m, :, head(h)], low)
            r.g_proj[h] = part if m == 0 else r.g_proj[h] + part
        there[m].start()
        shifts[m].start()

    def scan(m):
        def step(t, grad):
            b = count - 1 - t
            rows = tile_of(b, 16)
            r.held[m, rows] = grad.astype(BF)
            u = r.across.ref[m, rows].astype(F32)
            forget = jax.nn.sigmoid(r.bias[...] + r.slope[...] * u)
            moved = r.moved[m, rows].astype(F32)
            return r.keeps.ref[b, m : m + 1] * (moved + forget * grad)

        lax.fori_loop(0, count, step, jnp.zeros((16, 256), F32))

    def bucket_sums():
        row = lax.broadcasted_iota(jnp.int32, (TILE, TILE), 0)
        col = lax.broadcasted_iota(jnp.int32, (TILE, TILE), 1)
        distance = [row - col + TILE, row - col]
        for h in range(2):
            for t in range(BUCKETS):
                total = jnp.zeros((1, TILE), F32)
                for part in range(2):
                    d = distance[part]
                    inside = d >= STARTS[t]
                    if t + 1 < BUCKETS:
                        inside = inside & (d < STARTS[t + 1])
                    values = r.near[h, :, TILE * (part + 1) : TILE * (part + 2)]
                    total = total + jnp.sum(
                        jnp.where(inside, values, 0.0), axis=0, keepdims=True
                    )
                if t + 1 == BUCKETS:
                    total = total + jnp.sum(r.near[h, :, 0:TILE], axis=0, keepdims=True)
                r.sums[t : t + 1] = total
            r.g_rel[h] = lax.dot_general(
                jnp.ones((8, TILE), F32),
                r.sums[...],
                (((1,), (1,)), ((), ())),
                precision=lax.Precision.HIGHEST,
                preferred_element_type=F32,
            )

    def update_tile(m):
        def step(t):
            rows = tile_of(t)
            for h in range(2):
                cols, k_cols, v_cols = head(h), head(h, base=256), head(h, base=512)
                grad = r.grad_after[m, rows, cols].astype(F32)
                u = r.update.ref[m, rows, cols]
                inverse = inverse_rms(u)
                unit = u * inverse
                forget = jax.nn.sigmoid(r.bias[:, cols] + r.slope[:, cols] * unit)
                gate = grad * (r.prior.ref[m, rows, cols].astype(F32) - unit)
                gate = gate * forget * (1.0 - forget)
                r.g_bias[:, cols] += jnp.sum(gate, axis=0, keepdims=True)
                r.g_scale[:, cols] += jnp.sum(gate * unit, axis=0, keepdims=True)
                grad_unit = grad * (1.0 - forget) + gate * r.slope[:, cols]
                inner = jnp.mean(grad_unit * unit, axis=-1, keepdims=True)
                low = (inverse * (grad_unit - unit * inner)).astype(BF)
                q = r.state_query.ref[rows, cols]
                probs = jnp.exp(nt(q, qkv[m, :, k_cols]) * scale - stats[m, rows, h : h + 1])
                grad_probs = nt(low, qkv[m, :, v_cols])
                delta = jnp.sum(probs * grad_probs, axis=-1, keepdims=True)
                grad_scores = (probs * (grad_probs - delta)).astype(BF)
                r.g_query[rows, cols] += scale * nn(grad_scores, qkv[m, :, k_cols])
                r.grad_kv[m, 512:1024, cols] += tn(grad_scores, q)
                r.grad_kv[m, 512:1024, head(h, base=256)] += tn(probs.astype(BF), low)

        return step

    def finish_rows(m):
        def step(t):
            rows = tile_of(t)
            full = r.grad_kv[m, pl.ds(pl.multiple_of(512 + t * TILE, TILE), TILE)]
            extra = r.later[m, rows].astype(F32)
            at = own_chunk(t)
            r.dqkv[m, at, :, 256:512] = (scale * full[:, 0:256] + extra[:, 0:256]).astype(BF)
            r.dqkv[m, at, :, 512:768] = (full[:, 256:512] + extra[:, 256:512]).astype(BF)

        return step

    def out_weights(n):
        rows = tile_of(n, 256)
        part = tn(r.att_rel.ref[0].reshape(512, 256), gm[0][:, :, rows].reshape(512, 256))
        part = part + tn(
            r.att_rel.ref[1].reshape(512, 256), gm[1][:, :, rows].reshape(512, 256)
        )
        r.parts[rows, 768:1024] = part.astype(BF)

    def end_terms(m):
        def columns(n):
            cols = tile_of(n, 256)
            part = nt(r.dqkv[m, :, :, 0:256].reshape(512, 256), r.w.ref[0, cols])
            for p in (1, 2):
                some = r.dqkv[m, :, :, p * 256 : (p + 1) * 256].reshape(512, 256)
                part = part + nt(some, r.w.ref[p, cols])
            part = part.astype(BF)
            split_rows(branch, m, cols, part)

        loop(4, columns)

    def weight_rows(n):
        rows = slice(n * 256, (n + 1) * 256)
        whole = r.whole.ref
        part = tn(whole[0, :, :, rows].reshape(512, 256), r.dqkv[0].reshape(512, 768))
        part = part + tn(whole[1, :, :, rows].reshape(512, 256), r.dqkv[1].reshape(512, 768))
        r.parts[rows, 0:768] = part.astype(BF)
        product = part * jnp.concatenate([r.w.ref[p, rows] for p in range(3)], 1).astype(F32)
        high = product.astype(BF)
        low = (product - high.astype(F32)).astype(BF)
        ones = jnp.ones((8, 768), BF)
        return (nt(ones, high) + nt(ones, low))[0:1] / r.attn_gain[:, rows]

    def end_rows(m):
        grad_normed = ends[m].finish()
        rows = r.x.ref[m].astype(F32)
        inverse = inverse_rms(rows)
        unit = rows * inverse
        scaled = grad_normed * r.attn_gain[...]
        inner = jnp.mean(scaled * unit, axis=-1, keepdims=True)
        r.grad_x.ref[m] = r.grad_middle[m] + inverse * (scaled - unit * inner)

    def give_seed(i, rows):
        r.total[plane.last[i]] = rows

    def share(i):
        k, c = i // 2 + 1, i % 2
        slot = (3 - k) * 2 + core
        return remote(
            r.parts.at[768:784, 1024:1280],
            r.others.at[slot],
            r.s3.at[i],
            r.r3.at[slot],
            others[i],
        )

    def got(i):
        return remote(
            r.parts.at[768:784, 1024:1280], r.others.at[i], r.s3.at[i], r.r3.at[i], others[i]
        )

    def add_gains():
        for i in range(6):
            got(i).wait_recv()
        total = r.others[0].astype(F32)
        for i in range(1, 6):
            total = total + r.others[i].astype(F32)
        row = lax.broadcasted_iota(jnp.int32, (16, 256), 0)
        total = jnp.where(row < 8, total, 0.0) * core.astype(F32)
        at = slice(256, 272), slice(1024, 1280)
        r.half[at] = (r.half[at].astype(F32) + total).astype(BF)

    attention_rows(0)
    fourth.relay()
    loop(1, attend(0))
    mlp_sum.advance()
    loop(2, lambda qi: attend(0)(qi + 1))
    mlp_sum.advance()
    loop(1, lambda qi: attend(0)(qi + 3))
    r.prior.get()
    r.state_proj.get()
    pass_on(0)
    fourth.finish()
    attention_rows(1)
    outs[0].start()
    loop(2, attend(1))
    mlp_sum.advance()
    outs[0].relay()
    outs[1].start()
    loop(2, lambda qi: attend(1)(qi + 2))
    pass_on(1)
    outs[1].relay()
    r.across.get()
    r.keeps.get()
    there[0].finish()
    scan(0)
    back[0].start()
    r.att_rel.get()
    loop(4, out_weights)
    bucket_sums()
    there[1].finish()
    scan(1)
    back[1].start()
    mlp_sum.advance()
    r.middle.get()
    for m in both:
        r.out.ref[m] = r.middle.ref[m] + outs[m].finish()
    r.out.put()
    r.update.get()
    r.state_query.get()
    for m in both:
        outs[m].close()
    r.w.get()
    r.whole.get()
    back[0].finish()
    loop(4, update_tile(0))
    shifts[0].wait_recv()
    loop(4, finish_rows(0))
    end_terms(0)
    ends[0].start()
    back[1].finish()
    loop(4, update_tile(1))
    shifts[1].wait_recv()
    loop(4, finish_rows(1))
    ends[0].relay()
    small = [weight_rows(n) for n in range(4)]
    small = small + [r.g_mlp_gain[:, n * 256 : (n + 1) * 256] for n in range(4)]
    small = small + [r.g_bias[...], r.g_scale[...], r.g_rel[0, 0:1], r.g_rel[1, 0:1]]
    r.parts[0:512, 1024:1280] = r.g_query[...].astype(BF)
    r.parts[512:768, 1024:1280] = r.g_proj[...].reshape(256, 256).astype(BF)
    r.parts[768:784, 1024:1280] = jnp.concatenate(small + [jnp.zeros((4, 256), F32)], 0).astype(BF)
    r.parts[784:1024, 1024:1280] = jnp.zeros((240, 256), BF)
    weights = PlaneReduce(
        plane, r.parts, give_seed, add_gains, r.half, r.mid, r.into, r.quarter, r.small_into
    )
    spread = PlaneGather(plane, r.total)
    weights.advance()
    for i in range(6):
        share(i).start()
    end_terms(1)
    ends[1].start()
    weights.advance()
    r.x.get()
    end_rows(0)
    weights.advance()
    ends[1].relay()
    weights.advance(2)
    spread.advance(2)
    end_rows(1)
    r.grad_x.put()
    spread.advance(3)
    mlp_sum.close()
    weights.close()
    spread.close()
    fourth.close()
    for i in range(6):
        share(i).wait_send()
    for m in both:
        ends[m].close()
        shifts[m].wait_send()
        there[m].close()
        back[m].close()


class Late:
    def __init__(self, source, ref, sem):
        self.ref = ref
        self.copy = pltpu.make_async_copy(source, ref, sem)
        self.copy.start()
        self.open = True

    def get(self):
        if self.open:
            self.copy.wait()
            self.open = False


class Early:
    def __init__(self, target, ref, sem):
        self.ref = ref
        self.copy = pltpu.make_async_copy(ref, target, sem)
        self.sent = False

    def put(self):
        self.copy.start()
        self.sent = True


def call(kernel, name, number, now, late, small, outs, early, scratch, semaphores):
    anywhere = pl.BlockSpec(memory_space=pl.ANY)
    in_names = list(now) + list(small) + list(late)
    out_names = list(outs) + list(early)
    own = [a.shape for a in late.values()], [a.dtype for a in late.values()]
    buffers = list(zip(*own)) + list(early.values()) + list(scratch.values())

    def run(*refs):
        n, o = len(in_names), len(out_names)
        r = types.SimpleNamespace()
        held = refs[n + o : n + o + len(buffers)]
        rest = refs[n + o + len(buffers) :]
        fetch, store = rest[0], rest[1]
        for key, ref in zip(in_names[: len(now) + len(small)], refs):
            setattr(r, key, ref)
        for i, key in enumerate(late):
            setattr(r, key, Late(refs[len(now) + len(small) + i], held[i], fetch.at[i]))
        for key, ref in zip(outs, refs[n:]):
            setattr(r, key, ref)
        stores = []
        for i, key in enumerate(early):
            result = Early(refs[n + len(outs) + i], held[len(late) + i], store.at[i])
            setattr(r, key, result)
            stores.append(result)
        for key, ref in zip(scratch, held[len(late) + len(early) :]):
            setattr(r, key, ref)
        for key, ref in zip(semaphores, rest[2:]):
            setattr(r, key, ref)
        kernel(r)
        for result in stores:
            if not result.sent:
                result.put()
            result.copy.wait()

    shapes = list(outs.values()) + list(early.values())
    results = pl.pallas_call(
        run,
        out_shape=tuple(jax.ShapeDtypeStruct(shape, kind) for shape, kind in shapes),
        in_specs=[VMEM] * len(now) + [SMEM] * len(small) + [anywhere] * len(late),
        out_specs=tuple([VMEM] * len(outs) + [anywhere] * len(early)),
        scratch_shapes=[pltpu.VMEM(shape, kind) for shape, kind in buffers]
        + [sems(max(1, len(late))), sems(max(1, len(early)))]
        + list(semaphores.values()),
        compiler_params=pltpu.CompilerParams(
            collective_id=number, has_side_effects=True, vmem_limit_bytes=LIMIT
        ),
        name=name,
    )(*now.values(), *small.values(), *late.values())
    return dict(zip(out_names, results))


def finish_kernel(total, g_mlp, out, grad_x, state, *refs):
    results, (wide, low, pieces, rows_in, states_in, fetch, store) = refs[:11], refs[11:]
    places = [rows_in.at[0], rows_in.at[1], states_in]
    taken = [
        pltpu.make_async_copy(a, b, fetch.at[8 + i])
        for i, (a, b) in enumerate(zip((out, grad_x, state), places))
    ]
    passed = [
        pltpu.make_async_copy(a, b, store.at[i])
        for i, (a, b) in enumerate(zip(places, results[:3]))
    ]
    g_up, g_down, g_qkv, g_out, g_query, g_proj, gains, others = results[3:]
    loads = []
    for n in range(4):
        rows = slice(n * 256, (n + 1) * 256)
        loads.append(pltpu.make_async_copy(g_mlp.at[rows], low.at[rows], fetch.at[n]))
        loads.append(pltpu.make_async_copy(total.at[rows], pieces.at[rows], fetch.at[4 + n]))
    for copy in loads + taken:
        copy.start()
    stores = []

    def put(value, at, target):
        wide[at] = value.astype(F32)
        copy = pltpu.make_async_copy(wide.at[at], target, store.at[3 + len(stores)])
        copy.start()
        stores.append(copy)

    for n in range(4):
        rows = slice(n * 256, (n + 1) * 256)
        loads[2 * n].wait()
        put(low[rows, 0:1024], (rows, slice(0, 1024)), g_up.at[rows])
        put(low[rows, 1024:2048], (rows, slice(1024, 2048)), g_down.at[rows])
        loads[2 * n + 1].wait()
        for p in range(3):
            cols = slice(p * 256, (p + 1) * 256)
            put(pieces[rows, cols], (rows, slice(2048 + p * 256, 2304 + p * 256)), g_qkv.at[p, rows])
        put(pieces[rows, 768:1024], (rows, slice(2816, 3072)), g_out.at[:, rows])
    put(pieces[0:512, 1024:1280], (slice(0, 512), slice(3072, 3328)), g_query)
    put(pieces[512:768, 1024:1280], (slice(512, 768), slice(3072, 3328)), g_proj)
    for into, copy in zip(taken, passed):
        into.wait()
        copy.start()
    small = pieces[768:784, 1024:1280].astype(F32)
    gains[...] = small[0:8]
    others[...] = small[8:16]
    for copy in stores + passed:
        copy.wait()


def sems(*shape):
    return pltpu.SemaphoreType.DMA(shape)


def body(
    tokens_in,
    grad_out,
    flags,
    attn_gain,
    mlp_gain,
    w_qkv,
    w_out,
    rel_bias,
    state_query,
    state_proj,
    forget_bias,
    forget_scale,
    w_up,
    w_down,
):
    micros, rows, width = tokens_in.shape
    block = rows * 4
    local = w_qkv.shape[2]
    heads = rel_bias.shape[1]
    states = state_query.shape[0]
    buckets = rel_bias.shape[0]
    count = lax.axis_size("blk")
    w = jnp.transpose(w_qkv, (1, 0, 2))
    small = dict(flags=jnp.transpose(flags))
    whole_shape = ((micros, 4, rows, width), BF)
    state_low = ((micros, states, local), BF)
    state_wide = ((micros, states, local), F32)
    rows_wide = ((micros, rows, width), F32)
    mlp_width = w_up.shape[1] + w_down.shape[1]
    exchange = dict(
        s0=sems(2),
        r0=sems(2),
        s1=sems(2, count),
        r1=sems(2, count),
        s2=sems(2, count),
        r2=sems(2, count),
        local=sems(4),
    )
    gates = dict(bias=forget_bias[None], slope=forget_scale[None])
    f = call(
        forward_kernel,
        "forward",
        1,
        dict(
            x=tokens_in,
            g=grad_out,
            attn_gain=attn_gain[None],
            mlp_gain=mlp_gain[None],
            w=w,
            state_query=state_query,
            state_proj=state_proj,
            **gates,
        ),
        dict(w_out=w_out, w_up=w_up, w_down=w_down),
        dict(rel=jnp.transpose(rel_bias), **small),
        dict(
            grad_middle=rows_wide,
            gm0=((4, rows, width), BF),
            seeds=((2, 16, mlp_width), BF),
            g_gain=((1, width), F32),
        ),
        dict(
            whole=whole_shape,
            qkv=((micros, block, 3 * local), BF),
            kv_all=((micros, 2 * block, 2 * local), BF),
            state_kv=((micros, states, 2 * local), BF),
            prior=state_low,
            across=state_low,
            keeps=((count, 8, local), F32),
            update=state_wide,
            stats=((micros, block, TILE), F32),
            table=((heads, TILE, 5 * TILE), F32),
            state_after=state_wide,
            att_rel=((micros, 4, rows, local), BF),
            middle=rows_wide,
            branch=whole_shape,
        ),
        dict(
            whole_grad=whole_shape,
            own_keep=((8, local), F32),
            unit_low=state_low,
            held=state_low,
            terms=whole_shape,
            whole_mlp=whole_shape,
            active=((micros, block, w_up.shape[1]), BF),
            grad_hidden=((micros, block, w_up.shape[1]), BF),
            mids=((4, 4, rows // 2, width), BF),
            intos=((4, 2, rows, width), BF),
            parts=((width, mlp_width), BF),
            **reduce_scratch(mlp_width),
        ),
        dict(send=sems(104), recv=sems(104), s3=sems(count), r3=sems(count), **exchange),
    )
    b = call(
        backward_kernel,
        "backward",
        2,
        dict(
            gm0=f["gm0"],
            grad_middle=f["grad_middle"],
            w_out=w_out,
            qkv=f["qkv"],
            kv_all=f["kv_all"],
            state_kv=f["state_kv"],
            stats=f["stats"],
            table=f["table"],
            seeds=f["seeds"],
            attn_gain=attn_gain[None],
            g_mlp_gain=f["g_gain"],
            **gates,
        ),
        dict(
            branch=f["branch"],
            prior=f["prior"],
            state_proj=state_proj,
            across=f["across"],
            keeps=f["keeps"],
            att_rel=f["att_rel"],
            middle=f["middle"],
            update=f["update"],
            state_query=state_query,
            w=w,
            whole=f["whole"],
            x=tokens_in,
        ),
        small,
        dict(
            total_mlp=((width, mlp_width), BF),
            total=((width, 1280), BF),
        ),
        dict(out=rows_wide, grad_x=rows_wide),
        dict(
            dqkv=((micros, 4, rows, 3 * local), BF),
            g_query=((states, local), F32),
            g_proj=(state_proj.shape, F32),
            g_rel=((heads, 8, local), F32),
            g_bias=((1, local), F32),
            g_scale=((1, local), F32),
            grad_att=((micros, block, local), BF),
            grad_kv=((micros, 2 * block, 2 * local), F32),
            grad_state=((micros, states, 2 * local), F32),
            early=((micros, block, 2 * local), BF),
            later=((micros, block, 2 * local), BF),
            grad_prior=state_low,
            moved=state_low,
            held=state_low,
            grad_after=state_low,
            near=((heads, TILE, 3 * TILE), F32),
            sums=((local, TILE), F32),
            mids=((4, 4, rows // 2, width), BF),
            intos=((4, 2, rows, width), BF),
            others=((6, 16, local), BF),
            gm1=((4, rows, width), BF),
            parts=((width, 1280), BF),
            **reduce_scratch(1280),
        ),
        dict(send=sems(104), recv=sems(104), s3=sems(6), r3=sems(6), **exchange),
    )
    results = [
        rows_wide[0],
        rows_wide[0],
        state_wide[0],
        w_up.shape,
        w_down.shape,
        w.shape,
        w_out.shape,
        state_query.shape,
        (heads * state_proj.shape[1], local),
        (8, local),
        (8, local),
    ]
    anywhere = pl.BlockSpec(memory_space=pl.ANY)
    out, grad_x, state_after, g_up, g_down, g_qkv, g_out, g_query, g_proj, gains, others = (
        pl.pallas_call(
            finish_kernel,
            out_shape=tuple(jax.ShapeDtypeStruct(shape, F32) for shape in results),
            in_specs=[anywhere] * 5,
            out_specs=tuple([anywhere] * 9 + [VMEM] * 2),
            scratch_shapes=[
                pltpu.VMEM((width, 3328), F32),
                pltpu.VMEM((width, mlp_width), BF),
                pltpu.VMEM((width, 1280), BF),
                pltpu.VMEM((2,) + rows_wide[0], F32),
                pltpu.VMEM(state_wide[0], F32),
                sems(11),
                sems(32),
            ],
            compiler_params=pltpu.CompilerParams(vmem_limit_bytes=LIMIT),
            name="finish",
        )(b["total"], b["total_mlp"], b["out"], b["grad_x"], f["state_after"])
    )
    return (
        out,
        grad_x,
        state_after[:, None],
        gains[0:4].reshape(width),
        gains[4:8].reshape(width),
        jnp.transpose(g_qkv, (1, 0, 2)),
        g_out,
        jnp.transpose(others[2:4, :buckets]),
        g_query,
        g_proj.reshape(state_proj.shape),
        others[0],
        others[1],
        g_up,
        g_down,
    )


def solution(mesh):
    return jax.shard_map(
        body,
        mesh=mesh,
        in_specs=(
            P(None, ("blk", "head"), None),
            P(None, ("blk", "head"), None),
            P(None, "blk"),
            P(),
            P(),
            P(None, None, "head"),
            P("head", None),
            P(None, "head"),
            P(None, "head"),
            P("head", None, None),
            P("head"),
            P("head"),
            P(None, "head"),
            P("head", None),
        ),
        out_specs=(
            P(None, ("blk", "head"), None),
            P(None, ("blk", "head"), None),
            P(None, "blk", None, "head"),
            P(),
            P(),
            P(None, None, "head"),
            P("head", None),
            P(None, "head"),
            P(None, "head"),
            P("head", None, None),
            P("head"),
            P("head"),
            P(None, "head"),
            P("head", None),
        ),
        check_vma=False,
    )
```

```python
import math
import types

import jax
import jax.numpy as jnp
from jax import lax
from jax.experimental import pallas as pl
from jax.experimental.pallas import tpu as pltpu
from jax.sharding import PartitionSpec as P

BUCKETS = 32
MAXDIST = 128
EPSILON = 1e-06
MASKED = -1e30
TILE = 128
MESH = pl.DeviceIdType.MESH
BF = jnp.bfloat16
F32 = jnp.float32
VMEM = pl.BlockSpec(memory_space=pltpu.VMEM)
SMEM = pl.BlockSpec(memory_space=pltpu.SMEM)
LIMIT = 60 * 2**20
ROOT = math.sqrt(2.0 / math.pi)
CUBIC = 0.044715


def bucket_starts():
    exact = BUCKETS // 2
    levels = [
        int(math.ceil(exact * (MAXDIST / exact) ** (t / (BUCKETS - exact))))
        for t in range(1, BUCKETS - exact)
    ]
    return list(range(exact + 1)) + levels


STARTS = bucket_starts()


def nn(a, b):
    return lax.dot_general(a, b, (((1,), (0,)), ((), ())), preferred_element_type=F32)


def nt(a, b):
    return lax.dot_general(a, b, (((1,), (1,)), ((), ())), preferred_element_type=F32)


def tn(a, b):
    return lax.dot_general(a, b, (((0,), (0,)), ((), ())), preferred_element_type=F32)


def inverse_rms(values):
    return lax.rsqrt(jnp.mean(values * values, axis=-1, keepdims=True) + EPSILON)


def tile_of(index, size=TILE):
    return pl.ds(pl.multiple_of(index * size, size), size)


def loop(count, step):
    def run(i, c):
        step(i)
        return c

    lax.fori_loop(0, count, run, 0)


def remote(src, dst, send_sem, recv_sem, device):
    return pltpu.make_async_remote_copy(
        src_ref=src,
        dst_ref=dst,
        send_sem=send_sem,
        recv_sem=recv_sem,
        device_id=device,
        device_id_type=MESH,
    )


class Links:
    def __init__(self, send, recv):
        self.send, self.recv, self.used = send, recv, 0

    def go(self, src, dst, device):
        copy = remote(src, dst, self.send.at[self.used], self.recv.at[self.used], device)
        self.used += 1
        copy.start()
        return copy


class Ring:
    def __init__(self, links, me, device):
        self.links, self.me = links, me
        self.right = device(lax.rem(me + 1, 4))
        self.left = device(lax.rem(me + 3, 4))
        self.opposite = device(lax.rem(me + 2, 4))

    def go(self, src, dst, peer):
        return self.links.go(src, dst, peer)

    def greet(self):
        barrier = pltpu.get_barrier_semaphore()
        for peer in (self.right, self.left):
            pl.semaphore_signal(barrier, inc=1, device_id=peer, device_id_type=MESH)
        return 2

    def chunk(self, k):
        return lax.rem(self.me + k, 4)

    def row_chunk(self, k):
        return tile_of(self.chunk(k))


def head_ring(links):
    return Ring(links, lax.axis_index("head"), lambda i: {"head": i})


def by_rows(buf):
    half = buf.shape[1] // 2

    def piece(k, part=None, offset=0):
        return buf.at[k] if part is None else buf.at[k, part * half : (part + 1) * half]

    return piece


def by_columns(buf, base, rows, chunk):
    half = buf.shape[1] // 2

    def piece(k, part=None, offset=0):
        at = pl.ds(pl.multiple_of(base + chunk(k + offset) * rows, rows), rows)
        return buf.at[at] if part is None else buf.at[at, part * half : (part + 1) * half]

    return piece


class Gather:
    def __init__(self, ring, piece):
        self.ring, self.piece = ring, piece

    def start(self):
        r, p = self.ring, self.piece
        self.a0 = r.go(p(0, 0), p(3, 0, 1), r.right)
        self.b0 = r.go(p(0, 1), p(1, 1, 3), r.left)
        self.a1 = r.go(p(0, 1), p(3, 1, 1), r.right)
        self.b1 = r.go(p(0, 0), p(1, 0, 3), r.left)

    def relay(self):
        r, p = self.ring, self.piece
        self.a0.wait_recv()
        self.a2 = r.go(p(3, 0), p(2, 0, 1), r.right)
        self.b0.wait_recv()
        self.b2 = r.go(p(1, 1), p(2, 1, 3), r.left)

    def finish(self):
        for copy in (self.a1, self.b1, self.a2, self.b2):
            copy.wait_recv()

    def close(self):
        for copy in (self.a0, self.b0, self.a1, self.b1, self.a2, self.b2):
            copy.wait_send()


class Reduce:
    def __init__(self, ring, terms, mid, into):
        self.ring, self.terms, self.mid, self.into = ring, terms, mid, into
        if mid.shape[1] == into.shape[1]:
            half = into.shape[2] // 2
            self.place = lambda i, part: into.at[i, :, part * half : (part + 1) * half]
        else:
            half = into.shape[1] // 2
            self.place = lambda i, part: into.at[i, part * half : (part + 1) * half]

    def start(self):
        r, t = self.ring, self.terms
        self.a0 = r.go(t(2, 0), self.mid.at[0], r.right)
        self.b0 = r.go(t(2, 1), self.mid.at[1], r.left)
        self.a1 = r.go(t(1, 1), self.place(0, 1), r.right)
        self.b1 = r.go(t(3, 0), self.place(1, 0), r.left)

    def relay(self):
        r, t, mid = self.ring, self.terms, self.mid
        self.a0.wait_recv()
        mid[2] = (mid[0].astype(F32) + t(1, 0)[...].astype(F32)).astype(BF)
        self.a2 = r.go(mid.at[2], self.place(0, 0), r.right)
        self.b0.wait_recv()
        mid[3] = (mid[1].astype(F32) + t(3, 1)[...].astype(F32)).astype(BF)
        self.b2 = r.go(mid.at[3], self.place(1, 1), r.left)

    def finish(self):
        for copy in (self.a1, self.b1, self.a2, self.b2):
            copy.wait_recv()
        return (
            self.terms(0)[...].astype(F32)
            + self.into[0].astype(F32)
            + self.into[1].astype(F32)
        )

    def close(self):
        for copy in (self.a0, self.b0, self.a1, self.b1, self.a2, self.b2):
            copy.wait_send()


def block_device(x, z, c):
    return {"blk": (x * 4 + z) * 2 + c}


def block_place():
    place = lax.axis_index("blk")
    return place % 2, (place // 2) % 4, place // 8


class Plane:
    def __init__(self, links):
        c, z, x = block_place()
        self.links = links
        self.peer = block_device(x, z, 1 - c)
        rx = Ring(links, x, lambda i: block_device(i, z, c))
        rz = Ring(links, z, lambda i: block_device(x, i, c))
        self.rings = [rx, rz]
        self.first, self.second = (rx, rz), (rz, rx)
        self.base = c * 512
        self.own = pl.ds(pl.multiple_of(c * 512, 512), 512)
        self.away = pl.ds(pl.multiple_of((1 - c) * 512, 512), 512)
        self.top = [c * 512 + x * 64, c * 512 + 256 + z * 64]
        self.last = [
            pl.ds(pl.multiple_of(self.top[0] + z * 16, 16), 16),
            pl.ds(pl.multiple_of(self.top[1] + x * 16, 16), 16),
        ]

    def greet(self):
        barrier = pltpu.get_barrier_semaphore()
        pl.semaphore_signal(barrier, inc=1, device_id=self.peer, device_id_type=MESH)
        return 1 + sum(ring.greet() for ring in self.rings)


class Steps:
    def advance(self, steps=1):
        for _ in range(steps):
            if self.steps:
                self.steps.pop(0)()


class CoreSum:
    def __init__(self, plane, parts, half):
        self.plane, self.parts, self.half = plane, parts, half

    def start(self):
        plane = self.plane
        self.swap = plane.links.go(self.parts.at[plane.away], self.half, plane.peer)

    def finish(self):
        self.swap.wait_recv()

        def add(t):
            rows = tile_of(t, 64)
            own = pl.ds(pl.multiple_of(self.plane.base + t * 64, 64), 64)
            self.half[rows] = (
                self.parts[own].astype(F32) + self.half[rows].astype(F32)
            ).astype(BF)

        loop(8, add)

    def close(self):
        self.swap.wait_send()


class PlaneReduce(Steps):
    def __init__(self, plane, half, total, mid, into, quarter, small_into):
        self.plane, self.half, self.total, self.quarter = plane, half, total, quarter
        first, second = plane.first, plane.second
        self.reduce1 = [
            Reduce(first[i], by_columns(half, i * 256, 64, first[i].chunk), mid.at[i], into.at[i])
            for i in range(2)
        ]
        self.reduce2 = [
            ReduceDirect(
                second[i], by_columns(quarter.at[i], 0, 16, second[i].chunk), small_into.at[i]
            )
            for i in range(2)
        ]
        self.steps = [
            lambda: [r.start() for r in self.reduce1],
            lambda: [r.relay() for r in self.reduce1],
            self.start2,
            self.finish,
        ]

    def start2(self):
        for i, r in enumerate(self.reduce1):
            self.quarter[i] = r.finish().astype(BF)
            self.reduce2[i].start()

    def finish(self):
        for i, r in enumerate(self.reduce2):
            self.total[self.plane.last[i]] = r.finish().astype(BF)

    def close(self):
        for r in self.reduce1 + self.reduce2:
            r.close()


class PlaneGather(Steps):
    def __init__(self, plane, total):
        self.plane, self.total = plane, total
        first, second = plane.first, plane.second
        self.gather1 = [
            GatherDirect(second[i], by_columns(total, plane.top[i], 16, second[i].chunk))
            for i in range(2)
        ]
        self.gather2 = [
            Gather(first[i], by_columns(total, plane.base + i * 256, 64, first[i].chunk))
            for i in range(2)
        ]
        self.steps = [
            lambda: [g.start() for g in self.gather1],
            self.start2,
            lambda: [g.relay() for g in self.gather2],
            self.cores,
            lambda: self.swap.wait_recv(),
        ]

    def start2(self):
        for i, g in enumerate(self.gather1):
            g.finish()
            self.gather2[i].start()

    def cores(self):
        for g in self.gather2:
            g.finish()
        rows = self.total.at[self.plane.own]
        self.swap = self.plane.links.go(rows, rows, self.plane.peer)

    def close(self):
        self.swap.wait_send()
        for g in self.gather1 + self.gather2:
            g.close()


def reduce_scratch(name, width):
    return {
        name + "mid": ((2, 4, 64, width // 2), BF),
        name + "into": ((2, 2, 64, width), BF),
        name + "quarter": ((2, 64, width), BF),
        name + "small": ((2, 3, 16, width), BF),
    }


class GatherDirect:
    def __init__(self, ring, piece):
        self.ring, self.piece = ring, piece

    def start(self):
        r, p = self.ring, self.piece
        self.copies = [
            r.go(p(0), p(4 - k, None, k), peer)
            for k, peer in ((1, r.right), (3, r.left), (2, r.opposite))
        ]

    def finish(self):
        for copy in self.copies:
            copy.wait_recv()

    def close(self):
        for copy in self.copies:
            copy.wait_send()


class ReduceDirect:
    def __init__(self, ring, terms, into):
        self.ring, self.terms, self.into = ring, terms, into

    def start(self):
        r, t = self.ring, self.terms
        self.copies = [
            r.go(t(k), self.into.at[k - 1], peer)
            for k, peer in ((1, r.right), (3, r.left), (2, r.opposite))
        ]

    def finish(self):
        for copy in self.copies:
            copy.wait_recv()
        total = self.terms(0)[...].astype(F32)
        for k in range(3):
            total = total + self.into[k].astype(F32)
        return total

    def close(self):
        for copy in self.copies:
            copy.wait_send()


class Exchange:
    def __init__(self, source, target, send, recv, local):
        self.count = lax.axis_size("blk")
        self.place = lax.axis_index("blk")
        self.size = source.shape[0] // self.count
        self.source, self.target = source, target
        self.send, self.recv, self.local = send, recv, local

    def part(self, j):
        peer = lax.rem(self.place + j, self.count)
        return remote(
            self.source.at[tile_of(peer, self.size)],
            self.target.at[tile_of(self.place, self.size)],
            self.send.at[j],
            self.recv.at[j],
            {"blk": peer},
        )

    def own(self):
        rows = tile_of(self.place, self.size)
        return pltpu.make_async_copy(self.source.at[rows], self.target.at[rows], self.local)

    def start(self):
        loop(self.count - 1, lambda j: self.part(j + 1).start())
        self.own().start()

    def finish(self):
        self.own().wait()
        loop(self.count - 1, lambda j: self.part(j + 1).wait_recv())

    def close(self):
        loop(self.count - 1, lambda j: self.part(j + 1).wait_send())


def greet_blocks():
    barrier = pltpu.get_barrier_semaphore()
    count, place = lax.axis_size("blk"), lax.axis_index("blk")

    def greet(j):
        pl.semaphore_signal(
            barrier, inc=1, device_id={"blk": lax.rem(place + j + 1, count)}, device_id_type=MESH
        )

    loop(count - 1, greet)
    return count - 1


def closed_row(flag, qi):
    column = lax.broadcasted_iota(jnp.int32, (1, 5 * TILE), 1) + qi * TILE
    return jnp.where(column < 512, MASKED * flag.astype(F32), 0.0)


def head(h, size=TILE, base=0):
    return slice(base + h * size, base + (h + 1) * size)


def window_of(qi):
    return pl.ds(pl.multiple_of(qi * TILE, TILE), 5 * TILE)


def split_rows(target, m, cols, part):
    for k in range(4):
        target[m, k, :, cols] = part[k * TILE : (k + 1) * TILE]


def write_table(table, rel):
    row = lax.broadcasted_iota(jnp.int32, (TILE, TILE), 0)
    col = lax.broadcasted_iota(jnp.int32, (TILE, TILE), 1)
    for h in range(2):
        far = jnp.full((TILE, TILE), rel[h, BUCKETS - 1], F32)
        table[h, :, 0:128] = jnp.where(row < col, far, MASKED)
        table[h, :, 128:256] = far
        table[h, :, 256:384] = far
        for shift, at in ((TILE, 384), (0, 512)):
            distance = row - col + shift
            total = jnp.full((TILE, TILE), rel[h, 0], F32)
            for t in range(1, BUCKETS):
                total = jnp.where(distance >= STARTS[t], rel[h, t], total)
            table[h, :, at : at + TILE] = jnp.where(distance >= 0, total, MASKED)


def forward_kernel(r):
    scale = TILE**-0.5
    links = Links(r.send, r.recv)
    ring = head_ring(links)
    plane = Plane(links)
    place, count = lax.axis_index("blk"), lax.axis_size("blk")
    both = range(2)

    def norm_rows(m):
        rows = r.x[m].astype(F32)
        r.whole.ref[m, 0] = (rows * inverse_rms(rows) * r.attn_gain[...]).astype(BF)

    norm_rows(0)
    for m in both:
        keep = 1.0 - r.flags[0, m].astype(F32)
        r.own_keep[m : m + 1] = jnp.full((1, 256), keep, F32)
    r.own_keep[2:8] = jnp.zeros((6, 256), F32)
    pl.semaphore_wait(pltpu.get_barrier_semaphore(), ring.greet() + greet_blocks())
    whole, qkv, kv_all = r.whole.ref, r.qkv.ref, r.kv_all.ref
    prior, across, keeps = r.prior.ref, r.across.ref, r.keeps.ref
    update, stats, state_kv = r.update.ref, r.stats.ref, r.state_kv.ref
    table, att_rel, middle, branch = r.table.ref, r.att_rel.ref, r.middle.ref, r.branch.ref
    gather_x = [Gather(ring, by_rows(whole.at[m])) for m in both]
    gather_g = [Gather(ring, by_rows(r.whole_grad.at[m])) for m in both]
    gather_x[0].start()
    norm_rows(1)

    def tell(j):
        peer = {"blk": lax.rem(place + j, count)}
        return remote(r.own_keep, keeps.at[place], r.s3.at[j], r.r3.at[j], peer)

    loop(count - 1, lambda j: tell(j + 1).start())
    keeps[place] = r.own_keep[...]
    write_table(table, r.rel)
    r.table.put()
    after = {"blk": lax.rem(place + 1, count)}
    shifts = [
        remote(qkv.at[m, :, 256:768], kv_all.at[m, 0:512], r.s0.at[m], r.r0.at[m], after)
        for m in both
    ]
    there = [
        Exchange(r.unit_low.at[m], across.at[m], r.s1.at[m], r.r1.at[m], r.local.at[m])
        for m in both
    ]
    back = [
        Exchange(r.held.at[m], prior.at[m], r.s2.at[m], r.r2.at[m], r.local.at[2 + m])
        for m in both
    ]

    def project(m):
        def columns(n):
            cols = tile_of(n, 256)
            part = nn(whole[m].reshape(512, 1024), r.w.ref[n]).astype(BF)
            for k in range(4):
                qkv[m, ring.row_chunk(k), cols] = part[k * TILE : (k + 1) * TILE]

        loop(3, columns)
        shifts[m].start()
        kv_all[m, 512:1024] = qkv[m, :, 256:768]

    def update_tile(m):
        def step(t):
            rows = tile_of(t)
            for h in range(2):
                scores = nt(r.state_query.ref[rows, head(h)], qkv[m, :, head(h, base=256)]) * scale
                top = jnp.max(scores, axis=-1, keepdims=True)
                raised = jnp.exp(scores - top)
                total = jnp.sum(raised, axis=-1, keepdims=True)
                stats[m, rows, h : h + 1] = top + jnp.log(total)
                u = nn(raised.astype(BF), qkv[m, :, head(h, base=512)]) / total
                update[m, rows, head(h)] = u
                r.unit_low[m, rows, head(h)] = (u * inverse_rms(u)).astype(BF)

        return step

    def scan(m):
        def step(b, state):
            rows = tile_of(b, 16)
            u = across[m, rows].astype(F32)
            forget = jax.nn.sigmoid(r.bias[...] + r.slope[...] * u)
            before = keeps[b, m : m + 1] * state
            r.held[m, rows] = before.astype(BF)
            return forget * before + (1.0 - forget) * u

        lax.fori_loop(0, count, step, jnp.zeros((16, 256), F32))

    def state(m):
        def step(t):
            rows = tile_of(t)
            before = prior[m, rows]
            for h in range(2):
                state_kv[m, rows, head(h, 256)] = nn(before[:, head(h)], r.state_proj.ref[h]).astype(BF)
                u = update[m, rows, head(h)]
                u = u * inverse_rms(u)
                forget = jax.nn.sigmoid(r.bias[:, head(h)] + r.slope[:, head(h)] * u)
                r.state_after.ref[m, rows, head(h)] = (
                    forget * before[:, head(h)].astype(F32) + (1.0 - forget) * u
                )

        return step

    def attend(m):
        def step(qi):
            rows, window = tile_of(qi), window_of(qi)
            shut = closed_row(r.flags[0, m], qi)
            for h in range(2):
                q = qkv[m, rows, head(h)]
                token = nt(q, kv_all[m, window, head(h)]) * scale + (table[h] + shut)
                from_state = nt(q, state_kv[m, :, h * 256 : h * 256 + TILE]) * scale
                top = jnp.maximum(
                    jnp.max(token, axis=-1, keepdims=True),
                    jnp.max(from_state, axis=-1, keepdims=True),
                )
                token = jnp.exp(token - top)
                from_state = jnp.exp(from_state - top)
                total = jnp.sum(token, axis=-1, keepdims=True) + jnp.sum(
                    from_state, axis=-1, keepdims=True
                )
                stats[m, rows, 2 + h : 3 + h] = top + jnp.log(total)
                out = nn(token.astype(BF), kv_all[m, window, head(h, base=256)]) + nn(
                    from_state.astype(BF), state_kv[m, :, h * 256 + TILE : (h + 1) * 256]
                )
                att_rel[m, lax.rem(qi + 4 - ring.me, 4), :, head(h)] = (out / total).astype(BF)

        return step

    first = [
        Reduce(ring, by_rows(r.terms.at[m]), r.mids.at[m], r.intos.at[m]) for m in both
    ]
    second = [Gather(ring, by_rows(r.whole_mlp.at[m])) for m in both]
    third = [
        Reduce(ring, by_rows(r.terms.at[m]), r.mids.at[2 + m], r.intos.at[2 + m]) for m in both
    ]
    fourth = Gather(ring, by_rows(r.gm0))

    def out_terms(m):
        def columns(n):
            cols = tile_of(n, 256)
            part = nn(att_rel[m].reshape(512, 256), r.w_out.ref[:, cols]).astype(BF)
            split_rows(r.terms, m, cols, part)

        loop(4, columns)

    def normalise(m):
        rows = r.x[m].astype(F32) + first[m].finish()
        middle[m] = rows
        r.whole_mlp[m, 0] = (rows * inverse_rms(rows) * r.mlp_gain[...]).astype(BF)

    def hidden(m):
        def columns(n):
            cols = tile_of(n, 256)
            value = nn(r.whole_mlp[m].reshape(512, 1024), r.w_up.ref[:, cols])
            grad_active = nt(r.whole_grad[m].reshape(512, 1024), r.w_down.ref[cols])
            square = value * value
            bent = jnp.tanh(ROOT * value * (1.0 + CUBIC * square))
            r.active[m, :, cols] = (0.5 * value * (1.0 + bent)).astype(BF)
            rise = 0.5 * (1.0 + bent) + 0.5 * value * (1.0 - bent * bent) * ROOT * (
                1.0 + 3.0 * CUBIC * square
            )
            r.grad_hidden[m, :, cols] = (grad_active * rise).astype(BF)

        return columns

    def grad_terms(m):
        def columns(n):
            cols = tile_of(n, 256)
            part = nt(r.grad_hidden[m], r.w_up.ref[cols]).astype(BF)
            split_rows(r.terms, m, cols, part)

        loop(4, columns)

    def branch_terms(m):
        def columns(n):
            cols = tile_of(n, 256)
            part = nn(r.active[m], r.w_down.ref[:, cols]).astype(BF)
            split_rows(branch, m, cols, part)

        loop(4, columns)

    def grad_rows(m):
        grad_normed = third[m].finish()
        rows = middle[m]
        inverse = inverse_rms(rows)
        unit = rows * inverse
        part = jnp.sum(grad_normed * unit, axis=0, keepdims=True)
        r.g_gain[...] = part if m == 0 else r.g_gain[...] + part
        scaled = grad_normed * r.mlp_gain[...]
        inner = jnp.mean(scaled * unit, axis=-1, keepdims=True)
        total = r.g.ref[m].astype(F32) + inverse * (scaled - unit * inner)
        r.grad_middle[m] = total
        if m == 0:
            r.gm0[0] = total.astype(BF)

    def up_rows(n):
        rows = tile_of(n, 256)
        total = tn(r.whole_mlp[0, :, :, rows].reshape(512, 256), r.grad_hidden[0])
        total = total + tn(r.whole_mlp[1, :, :, rows].reshape(512, 256), r.grad_hidden[1])
        r.parts[rows, 0:1024] = total.astype(BF)

    def down_rows(n):
        rows = tile_of(n, 256)
        total = tn(r.active[0, :, rows], r.whole_grad[0].reshape(512, 1024))
        total = total + tn(r.active[1, :, rows], r.whole_grad[1].reshape(512, 1024))
        r.parts[rows, 1024:2048] = total.astype(BF)

    cores = CoreSum(plane, r.parts, r.half)

    gather_x[0].relay()
    gather_x[1].start()
    r.w.get()
    gather_x[0].finish()
    project(0)
    gather_x[1].relay()
    r.state_query.get()
    loop(4, update_tile(0))
    there[0].start()
    gather_x[1].finish()
    r.g.get()
    for m in both:
        r.whole_grad[m, 0] = r.g.ref[m]
    gather_g[0].start()
    project(1)
    r.whole.put()
    r.qkv.put()
    loop(4, update_tile(1))
    there[1].start()
    r.update.put()
    gather_g[0].relay()
    gather_g[1].start()
    loop(count - 1, lambda j: tell(j + 1).wait_recv())
    there[0].finish()
    scan(0)
    back[0].start()
    there[1].finish()
    scan(1)
    back[1].start()
    gather_g[1].relay()
    r.across.put()
    r.keeps.put()
    shifts[0].wait_recv()
    shifts[1].wait_recv()
    r.kv_all.put()
    r.state_proj.get()
    back[0].finish()
    loop(4, state(0))
    loop(4, attend(0))
    r.w_out.get()
    out_terms(0)
    first[0].start()
    back[1].finish()
    r.prior.put()
    loop(4, state(1))
    r.state_kv.put()
    r.state_after.put()
    loop(1, attend(1))
    first[0].relay()
    loop(3, lambda qi: attend(1)(qi + 1))
    r.stats.put()
    out_terms(1)
    r.att_rel.put()
    first[1].start()
    normalise(0)
    second[0].start()
    first[1].relay()
    second[0].relay()
    r.w_up.get()
    r.w_down.get()
    gather_g[0].finish()
    gather_g[1].finish()
    normalise(1)
    second[1].start()
    r.middle.put()
    second[0].finish()
    loop(2, hidden(0))
    second[1].relay()
    loop(2, lambda n: hidden(0)(n + 2))
    first[0].close()
    grad_terms(0)
    third[0].start()
    second[1].finish()
    loop(2, hidden(1))
    third[0].relay()
    loop(2, lambda n: hidden(1)(n + 2))
    first[1].close()
    grad_terms(1)
    third[1].start()
    loop(4, up_rows)
    grad_rows(0)
    fourth.start()
    third[1].relay()
    loop(4, down_rows)
    cores.start()
    fourth.relay()
    branch_terms(0)
    branch_terms(1)
    r.branch.put()
    cores.finish()
    grad_rows(1)
    fourth.finish()
    cores.close()
    fourth.close()
    for m in both:
        for step in (gather_x, gather_g, second, third):
            step[m].close()
        shifts[m].wait_send()
        there[m].close()
        back[m].close()
    loop(count - 1, lambda j: tell(j + 1).wait_send())


def backward_kernel(r):
    scale = TILE**-0.5
    links = Links(r.send, r.recv)
    ring = head_ring(links)
    plane = Plane(links)
    place, count = lax.axis_index("blk"), lax.axis_size("blk")
    both = range(2)
    gm = [r.gm0, r.gm1]
    r.gm1[0] = r.grad_middle[1].astype(BF)
    core = place % 2
    others = [
        {"head": ring.chunk(k), "blk": place - core + c} for k in range(1, 4) for c in range(2)
    ]
    barrier = pltpu.get_barrier_semaphore()
    for device in others:
        pl.semaphore_signal(barrier, inc=1, device_id=device, device_id_type=MESH)
    pl.semaphore_wait(barrier, len(others) + greet_blocks())
    fourth = Gather(ring, by_rows(r.gm1))
    fourth.start()
    mlp_sum = PlaneReduce(
        plane, r.half, r.total_mlp, r.mlp_mid, r.mlp_into, r.mlp_quarter, r.mlp_small
    )
    mlp_all = PlaneGather(plane, r.total_mlp)
    mlp_sum.advance()
    qkv, kv_all, state_kv, stats = r.qkv.ref, r.kv_all.ref, r.state_kv.ref, r.stats.ref
    r.branch.get()
    branch = r.branch.ref
    outs = [Reduce(ring, by_rows(branch.at[m]), r.mids.at[m], r.intos.at[m]) for m in both]
    ends = [
        Reduce(ring, by_rows(branch.at[m]), r.mids.at[2 + m], r.intos.at[2 + m]) for m in both
    ]
    before = {"blk": lax.rem(place + count - 1, count)}
    shifts = [
        remote(r.early.at[m], r.later.at[m], r.s0.at[m], r.r0.at[m], before) for m in both
    ]
    there = [
        Exchange(r.grad_prior.at[m], r.moved.at[m], r.s1.at[m], r.r1.at[m], r.local.at[m])
        for m in both
    ]
    back = [
        Exchange(r.held.at[m], r.grad_after.at[m], r.s2.at[m], r.r2.at[m], r.local.at[2 + m])
        for m in both
    ]
    for ref in (r.near, r.sums, r.g_query, r.g_bias, r.g_scale, r.grad_kv, r.grad_state):
        ref[...] = jnp.zeros(ref.shape, F32)

    def own_chunk(qi):
        return lax.rem(qi + 4 - ring.me, 4)

    def attention_rows(m):
        part = nt(gm[m][...].reshape(512, 1024), r.w_out[...]).astype(BF)
        for k in range(4):
            r.grad_att[m, ring.row_chunk(k)] = part[k * TILE : (k + 1) * TILE]

    def attend(m):
        def step(qi):
            rows, window = tile_of(qi), window_of(qi)
            shut = closed_row(r.flags[0, m], qi)
            for h in range(2):
                k_cols, v_cols = head(h), head(h, base=256)
                sk_cols = slice(h * 256, h * 256 + TILE)
                sv_cols = slice(h * 256 + TILE, (h + 1) * 256)
                q = qkv[m, rows, head(h)]
                d = r.grad_att[m, rows, head(h)]
                level = stats[m, rows, 2 + h : 3 + h]
                token = jnp.exp(
                    nt(q, kv_all[m, window, k_cols]) * scale + (r.table.ref[h] + shut) - level
                )
                from_state = jnp.exp(nt(q, state_kv[m, :, sk_cols]) * scale - level)
                grad_token = nt(d, kv_all[m, window, v_cols])
                grad_from = nt(d, state_kv[m, :, sv_cols])
                delta = jnp.sum(token * grad_token, axis=-1, keepdims=True) + jnp.sum(
                    from_state * grad_from, axis=-1, keepdims=True
                )
                grad_token = token * (grad_token - delta)
                grad_from = from_state * (grad_from - delta)
                r.near[h, :, 0:128] += (
                    grad_token[:, 0:128] + grad_token[:, 128:256] + grad_token[:, 256:384]
                )
                r.near[h, :, 128:384] += grad_token[:, 384:640]
                token_low = grad_token.astype(BF)
                from_low = grad_from.astype(BF)
                grad_q = scale * (
                    nn(token_low, kv_all[m, window, k_cols]) + nn(from_low, state_kv[m, :, sk_cols])
                )
                r.dqkv[m, own_chunk(qi), :, head(h)] = grad_q.astype(BF)
                r.grad_kv[m, window, k_cols] += tn(token_low, q)
                r.grad_kv[m, window, v_cols] += tn(token.astype(BF), d)
                r.grad_state[m, :, sk_cols] += tn(from_low, q)
                r.grad_state[m, :, sv_cols] += tn(from_state.astype(BF), d)

        return step

    def pass_on(m):
        r.early[m, :, 0:256] = (scale * r.grad_kv[m, 0:512, 0:256]).astype(BF)
        r.early[m, :, 256:512] = r.grad_kv[m, 0:512, 256:512].astype(BF)
        for h in range(2):
            low = jnp.concatenate(
                [
                    (scale * r.grad_state[m, :, h * 256 : h * 256 + TILE]).astype(BF),
                    r.grad_state[m, :, h * 256 + TILE : (h + 1) * 256].astype(BF),
                ],
                1,
            )
            r.grad_prior[m, :, head(h)] = nt(low, r.state_proj.ref[h]).astype(BF)
            part = tn(r.prior.ref[m, :, head(h)], low)
            r.g_proj[h] = part if m == 0 else r.g_proj[h] + part
        there[m].start()
        shifts[m].start()

    def scan(m):
        def step(t, grad):
            b = count - 1 - t
            rows = tile_of(b, 16)
            r.held[m, rows] = grad.astype(BF)
            u = r.across.ref[m, rows].astype(F32)
            forget = jax.nn.sigmoid(r.bias[...] + r.slope[...] * u)
            moved = r.moved[m, rows].astype(F32)
            return r.keeps.ref[b, m : m + 1] * (moved + forget * grad)

        lax.fori_loop(0, count, step, jnp.zeros((16, 256), F32))

    def bucket_sums():
        row = lax.broadcasted_iota(jnp.int32, (TILE, TILE), 0)
        col = lax.broadcasted_iota(jnp.int32, (TILE, TILE), 1)
        distance = [row - col + TILE, row - col]
        for h in range(2):
            for t in range(BUCKETS):
                total = jnp.zeros((1, TILE), F32)
                for part in range(2):
                    d = distance[part]
                    inside = d >= STARTS[t]
                    if t + 1 < BUCKETS:
                        inside = inside & (d < STARTS[t + 1])
                    values = r.near[h, :, TILE * (part + 1) : TILE * (part + 2)]
                    total = total + jnp.sum(
                        jnp.where(inside, values, 0.0), axis=0, keepdims=True
                    )
                if t + 1 == BUCKETS:
                    total = total + jnp.sum(r.near[h, :, 0:TILE], axis=0, keepdims=True)
                r.sums[t : t + 1] = total
            r.g_rel[h] = lax.dot_general(
                jnp.ones((8, TILE), F32),
                r.sums[...],
                (((1,), (1,)), ((), ())),
                precision=lax.Precision.HIGHEST,
                preferred_element_type=F32,
            )

    def update_tile(m):
        def step(t):
            rows = tile_of(t)
            for h in range(2):
                cols, k_cols, v_cols = head(h), head(h, base=256), head(h, base=512)
                grad = r.grad_after[m, rows, cols].astype(F32)
                u = r.update.ref[m, rows, cols]
                inverse = inverse_rms(u)
                unit = u * inverse
                forget = jax.nn.sigmoid(r.bias[:, cols] + r.slope[:, cols] * unit)
                gate = grad * (r.prior.ref[m, rows, cols].astype(F32) - unit)
                gate = gate * forget * (1.0 - forget)
                r.g_bias[:, cols] += jnp.sum(gate, axis=0, keepdims=True)
                r.g_scale[:, cols] += jnp.sum(gate * unit, axis=0, keepdims=True)
                grad_unit = grad * (1.0 - forget) + gate * r.slope[:, cols]
                inner = jnp.mean(grad_unit * unit, axis=-1, keepdims=True)
                low = (inverse * (grad_unit - unit * inner)).astype(BF)
                q = r.state_query.ref[rows, cols]
                probs = jnp.exp(nt(q, qkv[m, :, k_cols]) * scale - stats[m, rows, h : h + 1])
                grad_probs = nt(low, qkv[m, :, v_cols])
                delta = jnp.sum(probs * grad_probs, axis=-1, keepdims=True)
                grad_scores = (probs * (grad_probs - delta)).astype(BF)
                r.g_query[rows, cols] += scale * nn(grad_scores, qkv[m, :, k_cols])
                r.grad_kv[m, 512:1024, cols] += tn(grad_scores, q)
                r.grad_kv[m, 512:1024, head(h, base=256)] += tn(probs.astype(BF), low)

        return step

    def finish_rows(m):
        def step(t):
            rows = tile_of(t)
            full = r.grad_kv[m, pl.ds(pl.multiple_of(512 + t * TILE, TILE), TILE)]
            extra = r.later[m, rows].astype(F32)
            at = own_chunk(t)
            r.dqkv[m, at, :, 256:512] = (scale * full[:, 0:256] + extra[:, 0:256]).astype(BF)
            r.dqkv[m, at, :, 512:768] = (full[:, 256:512] + extra[:, 256:512]).astype(BF)

        return step

    ones = jnp.ones((8, 256), BF)

    def gain_row(part, p, rows):
        product = part * r.w.ref[p, rows].astype(F32)
        high = product.astype(BF)
        low = (product - high.astype(F32)).astype(BF)
        return (nt(ones, high) + nt(ones, low))[0:1]

    def weight_part(p, rows):
        whole, cols = r.whole.ref, slice(p * 256, (p + 1) * 256)
        part = tn(whole[0, :, :, rows].reshape(512, 256), r.dqkv[0, :, :, cols].reshape(512, 256))
        return part + tn(
            whole[1, :, :, rows].reshape(512, 256), r.dqkv[1, :, :, cols].reshape(512, 256)
        )

    def early_weights(n):
        rows = slice(n * 256, (n + 1) * 256)
        part = tn(r.att_rel.ref[0].reshape(512, 256), gm[0][:, :, rows].reshape(512, 256))
        part = part + tn(r.att_rel.ref[1].reshape(512, 256), gm[1][:, :, rows].reshape(512, 256))
        r.parts_a[rows, 256:512] = part.astype(BF)
        part = weight_part(0, rows)
        r.parts_a[rows, 0:256] = part.astype(BF)
        return gain_row(part, 0, rows)

    def end_terms(m):
        def columns(n):
            cols = tile_of(n, 256)
            part = nt(r.dqkv[m, :, :, 0:256].reshape(512, 256), r.w.ref[0, cols])
            for p in (1, 2):
                some = r.dqkv[m, :, :, p * 256 : (p + 1) * 256].reshape(512, 256)
                part = part + nt(some, r.w.ref[p, cols])
            part = part.astype(BF)
            split_rows(branch, m, cols, part)

        loop(4, columns)

    def late_weights(n):
        rows = slice(n * 256, (n + 1) * 256)
        total = gains[n]
        for p in (1, 2):
            part = weight_part(p, rows)
            r.parts_b[rows, (p - 1) * 256 : p * 256] = part.astype(BF)
            total = total + gain_row(part, p, rows)
        return total / r.attn_gain[:, rows]

    def end_rows(m):
        grad_normed = ends[m].finish()
        rows = r.x.ref[m].astype(F32)
        inverse = inverse_rms(rows)
        unit = rows * inverse
        scaled = grad_normed * r.attn_gain[...]
        inner = jnp.mean(scaled * unit, axis=-1, keepdims=True)
        r.grad_x.ref[m] = r.grad_middle[m] + inverse * (scaled - unit * inner)

    def share(i):
        k, c = i // 2 + 1, i % 2
        slot = (3 - k) * 2 + core
        return remote(
            r.parts_b.at[768:784, 512:768],
            r.others.at[slot],
            r.s3.at[i],
            r.r3.at[slot],
            others[i],
        )

    def got(i):
        return remote(
            r.parts_b.at[768:784, 512:768], r.others.at[i], r.s3.at[i], r.r3.at[i], others[i]
        )

    def add_gains():
        for i in range(6):
            got(i).wait_recv()
        total = r.others[0].astype(F32)
        for i in range(1, 6):
            total = total + r.others[i].astype(F32)
        row = lax.broadcasted_iota(jnp.int32, (16, 256), 0)
        total = jnp.where(row < 8, total, 0.0) * core.astype(F32)
        at = slice(256, 272), slice(512, 768)
        r.half_b[at] = (r.half_b[at].astype(F32) + total).astype(BF)

    core_a = CoreSum(plane, r.parts_a, r.half_a)
    sum_a = PlaneReduce(plane, r.half_a, r.total_a, r.a_mid, r.a_into, r.a_quarter, r.a_small)
    all_a = PlaneGather(plane, r.total_a)
    core_b = CoreSum(plane, r.parts_b, r.half_b)
    sum_b = PlaneReduce(plane, r.half_b, r.total_b, r.b_mid, r.b_into, r.b_quarter, r.b_small)
    all_b = PlaneGather(plane, r.total_b)

    attention_rows(0)
    fourth.relay()
    for part in (r.qkv, r.kv_all, r.state_kv, r.stats, r.table):
        part.get()
    loop(1, attend(0))
    mlp_sum.advance()
    loop(2, lambda qi: attend(0)(qi + 1))
    mlp_sum.advance()
    loop(1, lambda qi: attend(0)(qi + 3))
    r.prior.get()
    r.state_proj.get()
    pass_on(0)
    mlp_sum.advance()
    mlp_all.advance()
    fourth.finish()
    attention_rows(1)
    r.branch.get()
    outs[0].start()
    loop(1, attend(1))
    mlp_all.advance()
    loop(2, lambda qi: attend(1)(qi + 1))
    outs[0].relay()
    outs[1].start()
    mlp_all.advance()
    loop(1, lambda qi: attend(1)(qi + 3))
    pass_on(1)
    outs[1].relay()
    r.across.get()
    r.keeps.get()
    there[0].finish()
    scan(0)
    back[0].start()
    r.att_rel.get()
    r.w.get()
    r.whole.get()
    gains = [early_weights(n) for n in range(4)]
    mlp_all.advance()
    core_a.start()
    there[1].finish()
    scan(1)
    back[1].start()
    bucket_sums()
    core_a.finish()
    sum_a.advance()
    r.middle.get()
    for m in both:
        r.out.ref[m] = r.middle.ref[m] + outs[m].finish()
    r.out.put()
    r.update.get()
    r.state_query.get()
    for m in both:
        outs[m].close()
    mlp_all.advance()
    back[0].finish()
    loop(2, update_tile(0))
    sum_a.advance()
    loop(2, lambda t: update_tile(0)(t + 2))
    shifts[0].wait_recv()
    loop(4, finish_rows(0))
    sum_a.advance()
    end_terms(0)
    ends[0].start()
    sum_a.advance()
    all_a.advance()
    back[1].finish()
    loop(2, update_tile(1))
    all_a.advance()
    loop(2, lambda t: update_tile(1)(t + 2))
    shifts[1].wait_recv()
    loop(4, finish_rows(1))
    ends[0].relay()
    all_a.advance()
    small = [late_weights(n) for n in range(4)]
    small = small + [r.g_mlp_gain[:, n * 256 : (n + 1) * 256] for n in range(4)]
    small = small + [r.g_bias[...], r.g_scale[...], r.g_rel[0, 0:1], r.g_rel[1, 0:1]]
    r.parts_b[0:512, 512:768] = r.g_query[...].astype(BF)
    r.parts_b[512:768, 512:768] = r.g_proj[...].reshape(256, 256).astype(BF)
    r.parts_b[768:784, 512:768] = jnp.concatenate(small + [jnp.zeros((4, 256), F32)], 0).astype(BF)
    r.parts_b[784:1024, 512:768] = jnp.zeros((240, 256), BF)
    core_b.start()
    for i in range(6):
        share(i).start()
    all_a.advance()
    end_terms(1)
    ends[1].start()
    core_b.finish()
    add_gains()
    sum_b.advance()
    r.x.get()
    end_rows(0)
    sum_b.advance()
    ends[1].relay()
    sum_b.advance(2)
    all_b.advance(2)
    end_rows(1)
    r.grad_x.put()
    all_b.advance()
    all_a.advance()
    all_b.advance(2)
    for step in (mlp_sum, mlp_all, core_a, sum_a, all_a, core_b, sum_b, all_b, fourth):
        step.close()
    for i in range(6):
        share(i).wait_send()
    for m in both:
        ends[m].close()
        shifts[m].wait_send()
        there[m].close()
        back[m].close()


class Late:
    def __init__(self, source, ref, sem):
        self.ref = ref
        self.copy = pltpu.make_async_copy(source, ref, sem)
        self.copy.start()
        self.open = True

    def get(self):
        if self.open:
            self.copy.wait()
            self.open = False


class Early:
    def __init__(self, target, ref, sem):
        self.ref = ref
        self.copy = pltpu.make_async_copy(ref, target, sem)
        self.sent = False

    def put(self):
        self.copy.start()
        self.sent = True


def call(kernel, name, number, now, late, small, outs, early, scratch, semaphores):
    anywhere = pl.BlockSpec(memory_space=pl.ANY)
    in_names = list(now) + list(small) + list(late)
    out_names = list(outs) + list(early)
    own = [a.shape for a in late.values()], [a.dtype for a in late.values()]
    buffers = list(zip(*own)) + list(early.values()) + list(scratch.values())

    def run(*refs):
        n, o = len(in_names), len(out_names)
        r = types.SimpleNamespace()
        held = refs[n + o : n + o + len(buffers)]
        rest = refs[n + o + len(buffers) :]
        fetch, store = rest[0], rest[1]
        for key, ref in zip(in_names[: len(now) + len(small)], refs):
            setattr(r, key, ref)
        for i, key in enumerate(late):
            setattr(r, key, Late(refs[len(now) + len(small) + i], held[i], fetch.at[i]))
        for key, ref in zip(outs, refs[n:]):
            setattr(r, key, ref)
        stores = []
        for i, key in enumerate(early):
            result = Early(refs[n + len(outs) + i], held[len(late) + i], store.at[i])
            setattr(r, key, result)
            stores.append(result)
        for key, ref in zip(scratch, held[len(late) + len(early) :]):
            setattr(r, key, ref)
        for key, ref in zip(semaphores, rest[2:]):
            setattr(r, key, ref)
        kernel(r)
        for result in stores:
            if not result.sent:
                result.put()
            result.copy.wait()

    shapes = list(outs.values()) + list(early.values())
    results = pl.pallas_call(
        run,
        out_shape=tuple(jax.ShapeDtypeStruct(shape, kind) for shape, kind in shapes),
        in_specs=[VMEM] * len(now) + [SMEM] * len(small) + [anywhere] * len(late),
        out_specs=tuple([VMEM] * len(outs) + [anywhere] * len(early)),
        scratch_shapes=[pltpu.VMEM(shape, kind) for shape, kind in buffers]
        + [sems(max(1, len(late))), sems(max(1, len(early)))]
        + list(semaphores.values()),
        compiler_params=pltpu.CompilerParams(
            collective_id=number, has_side_effects=True, vmem_limit_bytes=LIMIT
        ),
        name=name,
    )(*now.values(), *small.values(), *late.values())
    return dict(zip(out_names, results))


def finish_kernel(total_a, total_b, g_mlp, out, grad_x, state, *refs):
    results, (wide, low, some_a, some_b, rows_in, states_in, fetch, store) = refs[:14], refs[14:]
    places = [rows_in.at[0], rows_in.at[1], states_in]
    taken = [
        pltpu.make_async_copy(a, b, fetch.at[12 + i])
        for i, (a, b) in enumerate(zip((out, grad_x, state), places))
    ]
    passed = [
        pltpu.make_async_copy(a, b, store.at[i])
        for i, (a, b) in enumerate(zip(places, results[:3]))
    ]
    g_up, g_down, g_qkv, g_out, g_query, g_proj = results[3:9]
    attn_gain, mlp_gain, bias, slope, rel = results[9:]
    loads = []
    for n in range(4):
        rows = slice(n * 256, (n + 1) * 256)
        loads.append(
            [
                pltpu.make_async_copy(a.at[rows], b.at[rows], fetch.at[3 * n + i])
                for i, (a, b) in enumerate(((g_mlp, low), (total_a, some_a), (total_b, some_b)))
            ]
        )
    for copy in sum(loads, []) + taken:
        copy.start()
    stores = []

    def put(value, at, target):
        wide[at] = value.astype(F32)
        copy = pltpu.make_async_copy(wide.at[at], target, store.at[3 + len(stores)])
        copy.start()
        stores.append(copy)

    for n in range(4):
        rows = slice(n * 256, (n + 1) * 256)
        for copy in loads[n]:
            copy.wait()
        put(low[rows, 0:1024], (rows, slice(0, 1024)), g_up.at[rows])
        put(low[rows, 1024:2048], (rows, slice(1024, 2048)), g_down.at[rows])
        put(some_a[rows, 0:256], (rows, slice(2048, 2304)), g_qkv.at[0, rows])
        put(some_b[rows, 0:256], (rows, slice(2304, 2560)), g_qkv.at[1, rows])
        put(some_b[rows, 256:512], (rows, slice(2560, 2816)), g_qkv.at[2, rows])
        put(some_a[rows, 256:512], (rows, slice(2816, 3072)), g_out.at[:, rows])
    put(some_b[0:512, 512:768], (slice(0, 512), slice(3072, 3328)), g_query)
    put(some_b[512:768, 512:768], (slice(512, 768), slice(3072, 3328)), g_proj)
    for into, copy in zip(taken, passed):
        into.wait()
        copy.start()
    small = some_b[768:784, 512:768].astype(F32)
    attn_gain[...] = jnp.concatenate([small[n : n + 1] for n in range(4)], 1)
    mlp_gain[...] = jnp.concatenate([small[n : n + 1] for n in range(4, 8)], 1)
    bias[...] = small[8:9]
    slope[...] = small[9:10]
    rel[...] = small[10:12, 0:BUCKETS]
    for copy in stores + passed:
        copy.wait()


def sems(*shape):
    return pltpu.SemaphoreType.DMA(shape)


def body(
    tokens_in,
    grad_out,
    flags,
    attn_gain,
    mlp_gain,
    w_qkv,
    w_out,
    rel_bias,
    state_query,
    state_proj,
    forget_bias,
    forget_scale,
    w_up,
    w_down,
):
    micros, rows, width = tokens_in.shape
    block = rows * 4
    local = w_qkv.shape[2]
    heads = rel_bias.shape[1]
    states = state_query.shape[0]
    buckets = rel_bias.shape[0]
    count = lax.axis_size("blk")
    w = jnp.transpose(w_qkv, (1, 0, 2))
    small = dict(flags=jnp.transpose(flags))
    whole_shape = ((micros, 4, rows, width), BF)
    state_low = ((micros, states, local), BF)
    state_wide = ((micros, states, local), F32)
    rows_wide = ((micros, rows, width), F32)
    mlp_width = w_up.shape[1] + w_down.shape[1]
    exchange = dict(
        s0=sems(2),
        r0=sems(2),
        s1=sems(2, count),
        r1=sems(2, count),
        s2=sems(2, count),
        r2=sems(2, count),
        local=sems(4),
    )
    gates = dict(bias=forget_bias[None], slope=forget_scale[None])
    f = call(
        forward_kernel,
        "forward",
        1,
        dict(
            x=tokens_in,
            attn_gain=attn_gain[None],
            mlp_gain=mlp_gain[None],
            **gates,
        ),
        dict(
            w=w,
            state_query=state_query,
            g=grad_out,
            state_proj=state_proj,
            w_out=w_out,
            w_up=w_up,
            w_down=w_down,
        ),
        dict(rel=jnp.transpose(rel_bias), **small),
        dict(
            grad_middle=rows_wide,
            gm0=((4, rows, width), BF),
            half=((512, mlp_width), BF),
            g_gain=((1, width), F32),
        ),
        dict(
            whole=whole_shape,
            qkv=((micros, block, 3 * local), BF),
            kv_all=((micros, 2 * block, 2 * local), BF),
            state_kv=((micros, states, 2 * local), BF),
            prior=state_low,
            across=state_low,
            keeps=((count, 8, local), F32),
            update=state_wide,
            stats=((micros, block, TILE), F32),
            table=((heads, TILE, 5 * TILE), F32),
            state_after=state_wide,
            att_rel=((micros, 4, rows, local), BF),
            middle=rows_wide,
            branch=whole_shape,
        ),
        dict(
            whole_grad=whole_shape,
            own_keep=((8, local), F32),
            unit_low=state_low,
            held=state_low,
            terms=whole_shape,
            whole_mlp=whole_shape,
            active=((micros, block, w_up.shape[1]), BF),
            grad_hidden=((micros, block, w_up.shape[1]), BF),
            mids=((4, 4, rows // 2, width), BF),
            intos=((4, 2, rows, width), BF),
            parts=((width, mlp_width), BF),
        ),
        dict(send=sems(80), recv=sems(80), s3=sems(count), r3=sems(count), **exchange),
    )
    b = call(
        backward_kernel,
        "backward",
        2,
        dict(
            gm0=f["gm0"],
            grad_middle=f["grad_middle"],
            w_out=w_out,
            half=f["half"],
            attn_gain=attn_gain[None],
            g_mlp_gain=f["g_gain"],
            **gates,
        ),
        dict(
            qkv=f["qkv"],
            kv_all=f["kv_all"],
            state_kv=f["state_kv"],
            stats=f["stats"],
            table=f["table"],
            branch=f["branch"],
            prior=f["prior"],
            state_proj=state_proj,
            across=f["across"],
            keeps=f["keeps"],
            att_rel=f["att_rel"],
            middle=f["middle"],
            update=f["update"],
            state_query=state_query,
            w=w,
            whole=f["whole"],
            x=tokens_in,
        ),
        small,
        dict(
            total_mlp=((width, mlp_width), BF),
            total_a=((width, 512), BF),
            total_b=((width, 768), BF),
        ),
        dict(out=rows_wide, grad_x=rows_wide),
        dict(
            dqkv=((micros, 4, rows, 3 * local), BF),
            g_query=((states, local), F32),
            g_proj=(state_proj.shape, F32),
            g_rel=((heads, 8, local), F32),
            g_bias=((1, local), F32),
            g_scale=((1, local), F32),
            grad_att=((micros, block, local), BF),
            grad_kv=((micros, 2 * block, 2 * local), F32),
            grad_state=((micros, states, 2 * local), F32),
            early=((micros, block, 2 * local), BF),
            later=((micros, block, 2 * local), BF),
            grad_prior=state_low,
            moved=state_low,
            held=state_low,
            grad_after=state_low,
            near=((heads, TILE, 3 * TILE), F32),
            sums=((local, TILE), F32),
            mids=((4, 4, rows // 2, width), BF),
            intos=((4, 2, rows, width), BF),
            others=((6, 16, local), BF),
            gm1=((4, rows, width), BF),
            parts_a=((width, 512), BF),
            half_a=((512, 512), BF),
            parts_b=((width, 768), BF),
            half_b=((512, 768), BF),
            **reduce_scratch("mlp_", mlp_width),
            **reduce_scratch("a_", 512),
            **reduce_scratch("b_", 768),
        ),
        dict(send=sems(150), recv=sems(150), s3=sems(6), r3=sems(6), **exchange),
    )
    results = [
        rows_wide[0],
        rows_wide[0],
        state_wide[0],
        w_up.shape,
        w_down.shape,
        w.shape,
        w_out.shape,
        state_query.shape,
        (heads * state_proj.shape[1], local),
        (1, width),
        (1, width),
        (1, local),
        (1, local),
        (heads, buckets),
    ]
    anywhere = pl.BlockSpec(memory_space=pl.ANY)
    values = pl.pallas_call(
        finish_kernel,
        out_shape=tuple(jax.ShapeDtypeStruct(shape, F32) for shape in results),
        in_specs=[anywhere] * 6,
        out_specs=tuple([anywhere] * 9 + [VMEM] * 5),
        scratch_shapes=[
            pltpu.VMEM((width, 3328), F32),
            pltpu.VMEM((width, mlp_width), BF),
            pltpu.VMEM((width, 512), BF),
            pltpu.VMEM((width, 768), BF),
            pltpu.VMEM((2,) + rows_wide[0], F32),
            pltpu.VMEM(state_wide[0], F32),
            sems(15),
            sems(32),
        ],
        compiler_params=pltpu.CompilerParams(vmem_limit_bytes=LIMIT),
        name="finish",
    )(b["total_a"], b["total_b"], b["total_mlp"], b["out"], b["grad_x"], f["state_after"])
    out, grad_x, state_after, g_up, g_down, g_qkv, g_out, g_query, g_proj = values[:9]
    g_attn_gain, g_mlp_gain, g_bias, g_scale, g_rel = values[9:]
    return (
        out,
        grad_x,
        state_after[:, None],
        g_attn_gain[0],
        g_mlp_gain[0],
        jnp.transpose(g_qkv, (1, 0, 2)),
        g_out,
        jnp.transpose(g_rel),
        g_query,
        g_proj.reshape(state_proj.shape),
        g_bias[0],
        g_scale[0],
        g_up,
        g_down,
    )


def solution(mesh):
    return jax.shard_map(
        body,
        mesh=mesh,
        in_specs=(
            P(None, ("blk", "head"), None),
            P(None, ("blk", "head"), None),
            P(None, "blk"),
            P(),
            P(),
            P(None, None, "head"),
            P("head", None),
            P(None, "head"),
            P(None, "head"),
            P("head", None, None),
            P("head"),
            P("head"),
            P(None, "head"),
            P("head", None),
        ),
        out_specs=(
            P(None, ("blk", "head"), None),
            P(None, ("blk", "head"), None),
            P(None, "blk", None, "head"),
            P(),
            P(),
            P(None, None, "head"),
            P("head", None),
            P(None, "head"),
            P(None, "head"),
            P("head", None, None),
            P("head"),
            P("head"),
            P(None, "head"),
            P("head", None),
        ),
        check_vma=False,
    )
```

```python
import math
import types

import jax
import jax.numpy as jnp
from jax import lax
from jax.experimental import pallas as pl
from jax.experimental.pallas import tpu as pltpu
from jax.sharding import PartitionSpec as P

BUCKETS = 32
MAXDIST = 128
EPSILON = 1e-06
MASKED = -1e30
TILE = 128
MESH = pl.DeviceIdType.MESH
BF = jnp.bfloat16
F32 = jnp.float32
VMEM = pl.BlockSpec(memory_space=pltpu.VMEM)
SMEM = pl.BlockSpec(memory_space=pltpu.SMEM)
LIMIT = 60 * 2**20
ROOT = math.sqrt(2.0 / math.pi)
CUBIC = 0.044715


def bucket_starts():
    exact = BUCKETS // 2
    levels = [
        int(math.ceil(exact * (MAXDIST / exact) ** (t / (BUCKETS - exact))))
        for t in range(1, BUCKETS - exact)
    ]
    return list(range(exact + 1)) + levels


STARTS = bucket_starts()


def nn(a, b):
    return lax.dot_general(a, b, (((1,), (0,)), ((), ())), preferred_element_type=F32)


def nt(a, b):
    return lax.dot_general(a, b, (((1,), (1,)), ((), ())), preferred_element_type=F32)


def tn(a, b):
    return lax.dot_general(a, b, (((0,), (0,)), ((), ())), preferred_element_type=F32)


def inverse_rms(values):
    return lax.rsqrt(jnp.mean(values * values, axis=-1, keepdims=True) + EPSILON)


def tile_of(index, size=TILE):
    return pl.ds(pl.multiple_of(index * size, size), size)


def loop(count, step):
    def run(i, c):
        step(i)
        return c

    lax.fori_loop(0, count, run, 0)


def remote(src, dst, send_sem, recv_sem, device):
    return pltpu.make_async_remote_copy(
        src_ref=src,
        dst_ref=dst,
        send_sem=send_sem,
        recv_sem=recv_sem,
        device_id=device,
        device_id_type=MESH,
    )


class Links:
    def __init__(self, send, recv):
        self.send, self.recv, self.used = send, recv, 0

    def go(self, src, dst, device):
        copy = remote(src, dst, self.send.at[self.used], self.recv.at[self.used], device)
        self.used += 1
        copy.start()
        return copy


class Ring:
    def __init__(self, links, me, device):
        self.links, self.me = links, me
        self.right = device(lax.rem(me + 1, 4))
        self.left = device(lax.rem(me + 3, 4))
        self.opposite = device(lax.rem(me + 2, 4))

    def go(self, src, dst, peer):
        return self.links.go(src, dst, peer)

    def greet(self):
        barrier = pltpu.get_barrier_semaphore()
        for peer in (self.right, self.left):
            pl.semaphore_signal(barrier, inc=1, device_id=peer, device_id_type=MESH)
        return 2

    def chunk(self, k):
        return lax.rem(self.me + k, 4)

    def row_chunk(self, k):
        return tile_of(self.chunk(k))


def head_ring(links):
    return Ring(links, lax.axis_index("head"), lambda i: {"head": i})


def by_rows(buf):
    half = buf.shape[1] // 2

    def piece(k, part=None, offset=0):
        return buf.at[k] if part is None else buf.at[k, part * half : (part + 1) * half]

    return piece


def by_columns(buf, base, rows, chunk):
    half = buf.shape[1] // 2

    def piece(k, part=None, offset=0):
        at = pl.ds(pl.multiple_of(base + chunk(k + offset) * rows, rows), rows)
        return buf.at[at] if part is None else buf.at[at, part * half : (part + 1) * half]

    return piece


class Gather:
    def __init__(self, ring, piece):
        self.ring, self.piece = ring, piece

    def start(self):
        r, p = self.ring, self.piece
        self.a0 = r.go(p(0, 0), p(3, 0, 1), r.right)
        self.b0 = r.go(p(0, 1), p(1, 1, 3), r.left)
        self.a1 = r.go(p(0, 1), p(3, 1, 1), r.right)
        self.b1 = r.go(p(0, 0), p(1, 0, 3), r.left)

    def relay(self):
        r, p = self.ring, self.piece
        self.a0.wait_recv()
        self.a2 = r.go(p(3, 0), p(2, 0, 1), r.right)
        self.b0.wait_recv()
        self.b2 = r.go(p(1, 1), p(2, 1, 3), r.left)

    def finish(self):
        for copy in (self.a1, self.b1, self.a2, self.b2):
            copy.wait_recv()

    def close(self):
        for copy in (self.a0, self.b0, self.a1, self.b1, self.a2, self.b2):
            copy.wait_send()


class Reduce:
    def __init__(self, ring, terms, mid, into):
        self.ring, self.terms, self.mid, self.into = ring, terms, mid, into
        if mid.shape[1] == into.shape[1]:
            half = into.shape[2] // 2
            self.place = lambda i, part: into.at[i, :, part * half : (part + 1) * half]
        else:
            half = into.shape[1] // 2
            self.place = lambda i, part: into.at[i, part * half : (part + 1) * half]

    def start(self):
        r, t = self.ring, self.terms
        self.a0 = r.go(t(2, 0), self.mid.at[0], r.right)
        self.b0 = r.go(t(2, 1), self.mid.at[1], r.left)
        self.a1 = r.go(t(1, 1), self.place(0, 1), r.right)
        self.b1 = r.go(t(3, 0), self.place(1, 0), r.left)

    def relay(self):
        r, t, mid = self.ring, self.terms, self.mid
        self.a0.wait_recv()
        mid[2] = (mid[0].astype(F32) + t(1, 0)[...].astype(F32)).astype(BF)
        self.a2 = r.go(mid.at[2], self.place(0, 0), r.right)
        self.b0.wait_recv()
        mid[3] = (mid[1].astype(F32) + t(3, 1)[...].astype(F32)).astype(BF)
        self.b2 = r.go(mid.at[3], self.place(1, 1), r.left)

    def finish(self):
        for copy in (self.a1, self.b1, self.a2, self.b2):
            copy.wait_recv()
        return (
            self.terms(0)[...].astype(F32)
            + self.into[0].astype(F32)
            + self.into[1].astype(F32)
        )

    def close(self):
        for copy in (self.a0, self.b0, self.a1, self.b1, self.a2, self.b2):
            copy.wait_send()


def block_device(x, z, c):
    return {"blk": (x * 4 + z) * 2 + c}


def block_place():
    place = lax.axis_index("blk")
    return place % 2, (place // 2) % 4, place // 8


class Plane:
    def __init__(self, links):
        c, z, x = block_place()
        self.links = links
        self.peer = block_device(x, z, 1 - c)
        rx = Ring(links, x, lambda i: block_device(i, z, c))
        rz = Ring(links, z, lambda i: block_device(x, i, c))
        self.rings = [rx, rz]
        self.first, self.second = (rx, rz), (rz, rx)
        self.base = c * 512
        self.own = pl.ds(pl.multiple_of(c * 512, 512), 512)
        self.away = pl.ds(pl.multiple_of((1 - c) * 512, 512), 512)
        self.top = [c * 512 + x * 64, c * 512 + 256 + z * 64]
        self.last = [
            pl.ds(pl.multiple_of(self.top[0] + z * 16, 16), 16),
            pl.ds(pl.multiple_of(self.top[1] + x * 16, 16), 16),
        ]

    def greet(self):
        barrier = pltpu.get_barrier_semaphore()
        pl.semaphore_signal(barrier, inc=1, device_id=self.peer, device_id_type=MESH)
        return 1 + sum(ring.greet() for ring in self.rings)


class Steps:
    def advance(self, steps=1):
        for _ in range(steps):
            if self.steps:
                self.steps.pop(0)()


class CoreSum:
    def __init__(self, plane, parts, half):
        self.plane, self.parts, self.half = plane, parts, half

    def start(self):
        plane = self.plane
        self.swap = plane.links.go(self.parts.at[plane.away], self.half, plane.peer)

    def finish(self):
        self.swap.wait_recv()

        def add(t):
            rows = tile_of(t, 64)
            own = pl.ds(pl.multiple_of(self.plane.base + t * 64, 64), 64)
            self.half[rows] = (
                self.parts[own].astype(F32) + self.half[rows].astype(F32)
            ).astype(BF)

        loop(8, add)

    def close(self):
        self.swap.wait_send()


class PlaneReduce(Steps):
    def __init__(self, plane, half, total, mid, into, quarter, small_into):
        self.plane, self.half, self.total, self.quarter = plane, half, total, quarter
        first, second = plane.first, plane.second
        self.reduce1 = [
            Reduce(first[i], by_columns(half, i * 256, 64, first[i].chunk), mid.at[i], into.at[i])
            for i in range(2)
        ]
        self.reduce2 = [
            ReduceDirect(
                second[i], by_columns(quarter.at[i], 0, 16, second[i].chunk), small_into.at[i]
            )
            for i in range(2)
        ]
        self.steps = [
            lambda: [r.start() for r in self.reduce1],
            lambda: [r.relay() for r in self.reduce1],
            self.start2,
            self.finish,
        ]

    def start2(self):
        for i, r in enumerate(self.reduce1):
            self.quarter[i] = r.finish().astype(BF)
            self.reduce2[i].start()

    def finish(self):
        for i, r in enumerate(self.reduce2):
            self.total[self.plane.last[i]] = r.finish().astype(BF)

    def close(self):
        for r in self.reduce1 + self.reduce2:
            r.close()


class PlaneGather(Steps):
    def __init__(self, plane, total):
        self.plane, self.total = plane, total
        first, second = plane.first, plane.second
        self.gather1 = [
            GatherDirect(second[i], by_columns(total, plane.top[i], 16, second[i].chunk))
            for i in range(2)
        ]
        self.gather2 = [
            Gather(first[i], by_columns(total, plane.base + i * 256, 64, first[i].chunk))
            for i in range(2)
        ]
        self.steps = [
            lambda: [g.start() for g in self.gather1],
            self.start2,
            lambda: [g.relay() for g in self.gather2],
            self.cores,
            lambda: self.swap.wait_recv(),
        ]

    def start2(self):
        for i, g in enumerate(self.gather1):
            g.finish()
            self.gather2[i].start()

    def cores(self):
        for g in self.gather2:
            g.finish()
        rows = self.total.at[self.plane.own]
        self.swap = self.plane.links.go(rows, rows, self.plane.peer)

    def close(self):
        self.swap.wait_send()
        for g in self.gather1 + self.gather2:
            g.close()


def reduce_scratch(name, width):
    return {
        name + "mid": ((2, 4, 64, width // 2), BF),
        name + "into": ((2, 2, 64, width), BF),
        name + "quarter": ((2, 64, width), BF),
        name + "small": ((2, 3, 16, width), BF),
    }


class GatherDirect:
    def __init__(self, ring, piece):
        self.ring, self.piece = ring, piece

    def start(self):
        r, p = self.ring, self.piece
        self.copies = [
            r.go(p(0), p(4 - k, None, k), peer)
            for k, peer in ((1, r.right), (3, r.left), (2, r.opposite))
        ]

    def finish(self):
        for copy in self.copies:
            copy.wait_recv()

    def close(self):
        for copy in self.copies:
            copy.wait_send()


class ReduceDirect:
    def __init__(self, ring, terms, into):
        self.ring, self.terms, self.into = ring, terms, into

    def start(self):
        r, t = self.ring, self.terms
        self.copies = [
            r.go(t(k), self.into.at[k - 1], peer)
            for k, peer in ((1, r.right), (3, r.left), (2, r.opposite))
        ]

    def finish(self):
        for copy in self.copies:
            copy.wait_recv()
        total = self.terms(0)[...].astype(F32)
        for k in range(3):
            total = total + self.into[k].astype(F32)
        return total

    def close(self):
        for copy in self.copies:
            copy.wait_send()


class Exchange:
    def __init__(self, source, target, send, recv, local):
        self.count = lax.axis_size("blk")
        self.place = lax.axis_index("blk")
        self.size = source.shape[0] // self.count
        self.source, self.target = source, target
        self.send, self.recv, self.local = send, recv, local

    def part(self, j):
        peer = lax.rem(self.place + j, self.count)
        return remote(
            self.source.at[tile_of(peer, self.size)],
            self.target.at[tile_of(self.place, self.size)],
            self.send.at[j],
            self.recv.at[j],
            {"blk": peer},
        )

    def own(self):
        rows = tile_of(self.place, self.size)
        return pltpu.make_async_copy(self.source.at[rows], self.target.at[rows], self.local)

    def start(self):
        loop(self.count - 1, lambda j: self.part(j + 1).start())
        self.own().start()

    def finish(self):
        self.own().wait()
        loop(self.count - 1, lambda j: self.part(j + 1).wait_recv())

    def close(self):
        loop(self.count - 1, lambda j: self.part(j + 1).wait_send())


def greet_blocks():
    barrier = pltpu.get_barrier_semaphore()
    count, place = lax.axis_size("blk"), lax.axis_index("blk")

    def greet(j):
        pl.semaphore_signal(
            barrier, inc=1, device_id={"blk": lax.rem(place + j + 1, count)}, device_id_type=MESH
        )

    loop(count - 1, greet)
    return count - 1


def closed_row(flag, qi):
    column = lax.broadcasted_iota(jnp.int32, (1, 5 * TILE), 1) + qi * TILE
    return jnp.where(column < 512, MASKED * flag.astype(F32), 0.0)


def head(h, size=TILE, base=0):
    return slice(base + h * size, base + (h + 1) * size)


def window_of(qi):
    return pl.ds(pl.multiple_of(qi * TILE, TILE), 5 * TILE)


def split_rows(target, m, cols, part):
    for k in range(4):
        target[m, k, :, cols] = part[k * TILE : (k + 1) * TILE]


def write_table(table, rel):
    row = lax.broadcasted_iota(jnp.int32, (TILE, TILE), 0)
    col = lax.broadcasted_iota(jnp.int32, (TILE, TILE), 1)
    for h in range(2):
        far = jnp.full((TILE, TILE), rel[h, BUCKETS - 1], F32)
        table[h, :, 0:128] = jnp.where(row < col, far, MASKED)
        table[h, :, 128:256] = far
        table[h, :, 256:384] = far
        for shift, at in ((TILE, 384), (0, 512)):
            distance = row - col + shift
            total = jnp.full((TILE, TILE), rel[h, 0], F32)
            for t in range(1, BUCKETS):
                total = jnp.where(distance >= STARTS[t], rel[h, t], total)
            table[h, :, at : at + TILE] = jnp.where(distance >= 0, total, MASKED)


def forward_kernel(r):
    scale = TILE**-0.5
    links = Links(r.send, r.recv)
    ring = head_ring(links)
    place, count = lax.axis_index("blk"), lax.axis_size("blk")
    both = range(2)

    def norm_rows(m):
        rows = r.x[m].astype(F32)
        r.whole.ref[m, 0] = (rows * inverse_rms(rows) * r.attn_gain[...]).astype(BF)

    norm_rows(0)
    for m in both:
        keep = 1.0 - r.flags[0, m].astype(F32)
        r.own_keep[m : m + 1] = jnp.full((1, 256), keep, F32)
    r.own_keep[2:8] = jnp.zeros((6, 256), F32)
    pl.semaphore_wait(pltpu.get_barrier_semaphore(), ring.greet() + greet_blocks())
    whole, qkv, kv_all = r.whole.ref, r.qkv.ref, r.kv_all.ref
    prior, across, keeps = r.prior.ref, r.across.ref, r.keeps.ref
    update, stats, state_kv = r.update.ref, r.stats.ref, r.state_kv.ref
    table, att_rel, middle, branch = r.table.ref, r.att_rel.ref, r.middle.ref, r.branch.ref
    gather_x = [Gather(ring, by_rows(whole.at[m])) for m in both]
    gather_g = [Gather(ring, by_rows(r.whole_grad.at[m])) for m in both]
    gather_x[0].start()
    norm_rows(1)

    def tell(j):
        peer = {"blk": lax.rem(place + j, count)}
        return remote(r.own_keep, keeps.at[place], r.s3.at[j], r.r3.at[j], peer)

    loop(count - 1, lambda j: tell(j + 1).start())
    keeps[place] = r.own_keep[...]
    write_table(table, r.rel)
    r.table.put()
    after = {"blk": lax.rem(place + 1, count)}
    shifts = [
        remote(qkv.at[m, :, 256:768], kv_all.at[m, 0:512], r.s0.at[m], r.r0.at[m], after)
        for m in both
    ]
    there = [
        Exchange(r.unit_low.at[m], across.at[m], r.s1.at[m], r.r1.at[m], r.local.at[m])
        for m in both
    ]
    back = [
        Exchange(r.held.at[m], prior.at[m], r.s2.at[m], r.r2.at[m], r.local.at[2 + m])
        for m in both
    ]

    def project(m):
        def columns(n):
            cols = tile_of(n, 256)
            part = nn(whole[m].reshape(512, 1024), r.w.ref[n]).astype(BF)
            for k in range(4):
                qkv[m, ring.row_chunk(k), cols] = part[k * TILE : (k + 1) * TILE]

        loop(3, columns)
        shifts[m].start()
        kv_all[m, 512:1024] = qkv[m, :, 256:768]

    def update_tile(m):
        def step(t):
            rows = tile_of(t)
            for h in range(2):
                scores = nt(r.state_query.ref[rows, head(h)], qkv[m, :, head(h, base=256)]) * scale
                top = jnp.max(scores, axis=-1, keepdims=True)
                raised = jnp.exp(scores - top)
                total = jnp.sum(raised, axis=-1, keepdims=True)
                stats[m, rows, h : h + 1] = top + jnp.log(total)
                u = nn(raised.astype(BF), qkv[m, :, head(h, base=512)]) / total
                update[m, rows, head(h)] = u
                r.unit_low[m, rows, head(h)] = (u * inverse_rms(u)).astype(BF)

        return step

    def scan(m):
        def step(b, state):
            rows = tile_of(b, 16)
            u = across[m, rows].astype(F32)
            forget = jax.nn.sigmoid(r.bias[...] + r.slope[...] * u)
            before = keeps[b, m : m + 1] * state
            r.held[m, rows] = before.astype(BF)
            return forget * before + (1.0 - forget) * u

        lax.fori_loop(0, count, step, jnp.zeros((16, 256), F32))

    def state(m):
        def step(t):
            rows = tile_of(t)
            before = prior[m, rows]
            for h in range(2):
                state_kv[m, rows, head(h, 256)] = nn(before[:, head(h)], r.state_proj.ref[h]).astype(BF)
                u = update[m, rows, head(h)]
                u = u * inverse_rms(u)
                forget = jax.nn.sigmoid(r.bias[:, head(h)] + r.slope[:, head(h)] * u)
                r.state_after.ref[m, rows, head(h)] = (
                    forget * before[:, head(h)].astype(F32) + (1.0 - forget) * u
                )

        return step

    def attend(m):
        def step(qi):
            rows, window = tile_of(qi), window_of(qi)
            shut = closed_row(r.flags[0, m], qi)
            for h in range(2):
                q = qkv[m, rows, head(h)]
                token = nt(q, kv_all[m, window, head(h)]) * scale + (table[h] + shut)
                from_state = nt(q, state_kv[m, :, h * 256 : h * 256 + TILE]) * scale
                top = jnp.maximum(
                    jnp.max(token, axis=-1, keepdims=True),
                    jnp.max(from_state, axis=-1, keepdims=True),
                )
                token = jnp.exp(token - top)
                from_state = jnp.exp(from_state - top)
                total = jnp.sum(token, axis=-1, keepdims=True) + jnp.sum(
                    from_state, axis=-1, keepdims=True
                )
                stats[m, rows, 2 + h : 3 + h] = top + jnp.log(total)
                out = nn(token.astype(BF), kv_all[m, window, head(h, base=256)]) + nn(
                    from_state.astype(BF), state_kv[m, :, h * 256 + TILE : (h + 1) * 256]
                )
                att_rel[m, lax.rem(qi + 4 - ring.me, 4), :, head(h)] = (out / total).astype(BF)

        return step

    first = [
        Reduce(ring, by_rows(r.terms.at[m]), r.mids.at[m], r.intos.at[m]) for m in both
    ]
    second = [Gather(ring, by_rows(r.whole_mlp.at[m])) for m in both]
    third = [
        Reduce(ring, by_rows(r.terms.at[m]), r.mids.at[2 + m], r.intos.at[2 + m]) for m in both
    ]
    fourth = Gather(ring, by_rows(r.gm0))

    def out_terms(m):
        def columns(n):
            cols = tile_of(n, 256)
            part = nn(att_rel[m].reshape(512, 256), r.w_out.ref[:, cols]).astype(BF)
            split_rows(r.terms, m, cols, part)

        loop(4, columns)

    def normalise(m):
        rows = r.x[m].astype(F32) + first[m].finish()
        middle[m] = rows
        r.whole_mlp[m, 0] = (rows * inverse_rms(rows) * r.mlp_gain[...]).astype(BF)

    def hidden(m):
        def columns(n):
            cols = tile_of(n, 256)
            value = nn(r.whole_mlp[m].reshape(512, 1024), r.w_up.ref[:, cols])
            grad_active = nt(r.whole_grad[m].reshape(512, 1024), r.w_down.ref[cols])
            square = value * value
            bent = jnp.tanh(ROOT * value * (1.0 + CUBIC * square))
            r.active[m, :, cols] = (0.5 * value * (1.0 + bent)).astype(BF)
            rise = 0.5 * (1.0 + bent) + 0.5 * value * (1.0 - bent * bent) * ROOT * (
                1.0 + 3.0 * CUBIC * square
            )
            r.grad_hidden[m, :, cols] = (grad_active * rise).astype(BF)

        return columns

    def grad_terms(m):
        def columns(n):
            cols = tile_of(n, 256)
            part = nt(r.grad_hidden[m], r.w_up.ref[cols]).astype(BF)
            split_rows(r.terms, m, cols, part)

        loop(4, columns)

    def branch_terms(m):
        def columns(n):
            cols = tile_of(n, 256)
            part = nn(r.active[m], r.w_down.ref[:, cols]).astype(BF)
            split_rows(branch, m, cols, part)

        loop(4, columns)

    def grad_rows(m):
        grad_normed = third[m].finish()
        rows = middle[m]
        inverse = inverse_rms(rows)
        unit = rows * inverse
        part = jnp.sum(grad_normed * unit, axis=0, keepdims=True)
        r.g_gain[...] = part if m == 0 else r.g_gain[...] + part
        scaled = grad_normed * r.mlp_gain[...]
        inner = jnp.mean(scaled * unit, axis=-1, keepdims=True)
        total = r.g.ref[m].astype(F32) + inverse * (scaled - unit * inner)
        r.grad_middle[m] = total
        if m == 0:
            r.gm0[0] = total.astype(BF)

    def up_rows(n):
        rows = tile_of(n, 256)
        total = tn(r.whole_mlp[0, :, :, rows].reshape(512, 256), r.grad_hidden[0])
        total = total + tn(r.whole_mlp[1, :, :, rows].reshape(512, 256), r.grad_hidden[1])
        r.parts.ref[rows, 0:1024] = total.astype(BF)

    def down_rows(n):
        rows = tile_of(n, 256)
        total = tn(r.active[0, :, rows], r.whole_grad[0].reshape(512, 1024))
        total = total + tn(r.active[1, :, rows], r.whole_grad[1].reshape(512, 1024))
        r.parts.ref[rows, 1024:2048] = total.astype(BF)

    gather_x[0].relay()
    gather_x[1].start()
    r.w.get()
    gather_x[0].finish()
    project(0)
    gather_x[1].relay()
    r.state_query.get()
    loop(4, update_tile(0))
    there[0].start()
    gather_x[1].finish()
    r.g.get()
    for m in both:
        r.whole_grad[m, 0] = r.g.ref[m]
    gather_g[0].start()
    project(1)
    r.whole.put()
    r.qkv.put()
    loop(4, update_tile(1))
    there[1].start()
    r.update.put()
    gather_g[0].relay()
    gather_g[1].start()
    loop(count - 1, lambda j: tell(j + 1).wait_recv())
    there[0].finish()
    scan(0)
    back[0].start()
    there[1].finish()
    scan(1)
    back[1].start()
    gather_g[1].relay()
    r.across.put()
    r.keeps.put()
    shifts[0].wait_recv()
    shifts[1].wait_recv()
    r.kv_all.put()
    r.state_proj.get()
    back[0].finish()
    loop(4, state(0))
    loop(4, attend(0))
    r.w_out.get()
    out_terms(0)
    first[0].start()
    back[1].finish()
    r.prior.put()
    loop(4, state(1))
    r.state_kv.put()
    r.state_after.put()
    loop(1, attend(1))
    first[0].relay()
    loop(3, lambda qi: attend(1)(qi + 1))
    r.stats.put()
    out_terms(1)
    r.att_rel.put()
    first[1].start()
    normalise(0)
    second[0].start()
    first[1].relay()
    second[0].relay()
    r.w_up.get()
    r.w_down.get()
    gather_g[0].finish()
    gather_g[1].finish()
    normalise(1)
    second[1].start()
    r.middle.put()
    second[0].finish()
    loop(2, hidden(0))
    second[1].relay()
    loop(2, lambda n: hidden(0)(n + 2))
    first[0].close()
    grad_terms(0)
    third[0].start()
    second[1].finish()
    loop(2, hidden(1))
    third[0].relay()
    loop(2, lambda n: hidden(1)(n + 2))
    first[1].close()
    grad_terms(1)
    third[1].start()
    loop(4, up_rows)
    grad_rows(0)
    fourth.start()
    third[1].relay()
    loop(4, down_rows)
    r.parts.put()
    fourth.relay()
    branch_terms(0)
    branch_terms(1)
    r.branch.put()
    grad_rows(1)
    fourth.finish()
    fourth.close()
    for m in both:
        for step in (gather_x, gather_g, second, third):
            step[m].close()
        shifts[m].wait_send()
        there[m].close()
        back[m].close()
    loop(count - 1, lambda j: tell(j + 1).wait_send())


def backward_kernel(r):
    scale = TILE**-0.5
    links = Links(r.send, r.recv)
    ring = head_ring(links)
    plane = Plane(links)
    place, count = lax.axis_index("blk"), lax.axis_size("blk")
    both = range(2)
    gm = [r.gm0, r.gm1]
    r.gm1[0] = r.grad_middle[1].astype(BF)
    core = place % 2
    others = [
        {"head": ring.chunk(k), "blk": place - core + c} for k in range(1, 4) for c in range(2)
    ]
    barrier = pltpu.get_barrier_semaphore()
    for device in others:
        pl.semaphore_signal(barrier, inc=1, device_id=device, device_id_type=MESH)
    pl.semaphore_wait(barrier, len(others) + greet_blocks())
    fourth = Gather(ring, by_rows(r.gm1))
    fourth.start()
    qkv, kv_all, state_kv, stats = r.qkv.ref, r.kv_all.ref, r.state_kv.ref, r.stats.ref
    r.branch.get()
    branch = r.branch.ref
    outs = [Reduce(ring, by_rows(branch.at[m]), r.mids.at[m], r.intos.at[m]) for m in both]
    ends = [
        Reduce(ring, by_rows(branch.at[m]), r.mids.at[2 + m], r.intos.at[2 + m]) for m in both
    ]
    before = {"blk": lax.rem(place + count - 1, count)}
    shifts = [
        remote(r.early.at[m], r.later.at[m], r.s0.at[m], r.r0.at[m], before) for m in both
    ]
    there = [
        Exchange(r.grad_prior.at[m], r.moved.at[m], r.s1.at[m], r.r1.at[m], r.local.at[m])
        for m in both
    ]
    back = [
        Exchange(r.held.at[m], r.grad_after.at[m], r.s2.at[m], r.r2.at[m], r.local.at[2 + m])
        for m in both
    ]
    for ref in (r.near, r.sums, r.g_query, r.g_bias, r.g_scale, r.grad_kv, r.grad_state):
        ref[...] = jnp.zeros(ref.shape, F32)

    def own_chunk(qi):
        return lax.rem(qi + 4 - ring.me, 4)

    def attention_rows(m):
        part = nt(gm[m][...].reshape(512, 1024), r.w_out[...]).astype(BF)
        for k in range(4):
            r.grad_att[m, ring.row_chunk(k)] = part[k * TILE : (k + 1) * TILE]

    def attend(m):
        def step(qi):
            rows, window = tile_of(qi), window_of(qi)
            shut = closed_row(r.flags[0, m], qi)
            for h in range(2):
                k_cols, v_cols = head(h), head(h, base=256)
                sk_cols = slice(h * 256, h * 256 + TILE)
                sv_cols = slice(h * 256 + TILE, (h + 1) * 256)
                q = qkv[m, rows, head(h)]
                d = r.grad_att[m, rows, head(h)]
                level = stats[m, rows, 2 + h : 3 + h]
                token = jnp.exp(
                    nt(q, kv_all[m, window, k_cols]) * scale + (r.table.ref[h] + shut) - level
                )
                from_state = jnp.exp(nt(q, state_kv[m, :, sk_cols]) * scale - level)
                grad_token = nt(d, kv_all[m, window, v_cols])
                grad_from = nt(d, state_kv[m, :, sv_cols])
                delta = jnp.sum(token * grad_token, axis=-1, keepdims=True) + jnp.sum(
                    from_state * grad_from, axis=-1, keepdims=True
                )
                grad_token = token * (grad_token - delta)
                grad_from = from_state * (grad_from - delta)
                r.near[h, :, 0:128] += (
                    grad_token[:, 0:128] + grad_token[:, 128:256] + grad_token[:, 256:384]
                )
                r.near[h, :, 128:384] += grad_token[:, 384:640]
                token_low = grad_token.astype(BF)
                from_low = grad_from.astype(BF)
                grad_q = scale * (
                    nn(token_low, kv_all[m, window, k_cols]) + nn(from_low, state_kv[m, :, sk_cols])
                )
                r.dqkv[m, own_chunk(qi), :, head(h)] = grad_q.astype(BF)
                r.grad_kv[m, window, k_cols] += tn(token_low, q)
                r.grad_kv[m, window, v_cols] += tn(token.astype(BF), d)
                r.grad_state[m, :, sk_cols] += tn(from_low, q)
                r.grad_state[m, :, sv_cols] += tn(from_state.astype(BF), d)

        return step

    def pass_on(m):
        r.early[m, :, 0:256] = (scale * r.grad_kv[m, 0:512, 0:256]).astype(BF)
        r.early[m, :, 256:512] = r.grad_kv[m, 0:512, 256:512].astype(BF)
        for h in range(2):
            low = jnp.concatenate(
                [
                    (scale * r.grad_state[m, :, h * 256 : h * 256 + TILE]).astype(BF),
                    r.grad_state[m, :, h * 256 + TILE : (h + 1) * 256].astype(BF),
                ],
                1,
            )
            r.grad_prior[m, :, head(h)] = nt(low, r.state_proj.ref[h]).astype(BF)
            part = tn(r.prior.ref[m, :, head(h)], low)
            r.g_proj[h] = part if m == 0 else r.g_proj[h] + part
        there[m].start()
        shifts[m].start()

    def scan(m):
        def step(t, grad):
            b = count - 1 - t
            rows = tile_of(b, 16)
            r.held[m, rows] = grad.astype(BF)
            u = r.across.ref[m, rows].astype(F32)
            forget = jax.nn.sigmoid(r.bias[...] + r.slope[...] * u)
            moved = r.moved[m, rows].astype(F32)
            return r.keeps.ref[b, m : m + 1] * (moved + forget * grad)

        lax.fori_loop(0, count, step, jnp.zeros((16, 256), F32))

    def bucket_sums():
        row = lax.broadcasted_iota(jnp.int32, (TILE, TILE), 0)
        col = lax.broadcasted_iota(jnp.int32, (TILE, TILE), 1)
        distance = [row - col + TILE, row - col]
        for h in range(2):
            for t in range(BUCKETS):
                total = jnp.zeros((1, TILE), F32)
                for part in range(2):
                    d = distance[part]
                    inside = d >= STARTS[t]
                    if t + 1 < BUCKETS:
                        inside = inside & (d < STARTS[t + 1])
                    values = r.near[h, :, TILE * (part + 1) : TILE * (part + 2)]
                    total = total + jnp.sum(
                        jnp.where(inside, values, 0.0), axis=0, keepdims=True
                    )
                if t + 1 == BUCKETS:
                    total = total + jnp.sum(r.near[h, :, 0:TILE], axis=0, keepdims=True)
                r.sums[t : t + 1] = total
            r.g_rel[h] = lax.dot_general(
                jnp.ones((8, TILE), F32),
                r.sums[...],
                (((1,), (1,)), ((), ())),
                precision=lax.Precision.HIGHEST,
                preferred_element_type=F32,
            )

    def update_tile(m):
        def step(t):
            rows = tile_of(t)
            for h in range(2):
                cols, k_cols, v_cols = head(h), head(h, base=256), head(h, base=512)
                grad = r.grad_after[m, rows, cols].astype(F32)
                u = r.update.ref[m, rows, cols]
                inverse = inverse_rms(u)
                unit = u * inverse
                forget = jax.nn.sigmoid(r.bias[:, cols] + r.slope[:, cols] * unit)
                gate = grad * (r.prior.ref[m, rows, cols].astype(F32) - unit)
                gate = gate * forget * (1.0 - forget)
                r.g_bias[:, cols] += jnp.sum(gate, axis=0, keepdims=True)
                r.g_scale[:, cols] += jnp.sum(gate * unit, axis=0, keepdims=True)
                grad_unit = grad * (1.0 - forget) + gate * r.slope[:, cols]
                inner = jnp.mean(grad_unit * unit, axis=-1, keepdims=True)
                low = (inverse * (grad_unit - unit * inner)).astype(BF)
                q = r.state_query.ref[rows, cols]
                probs = jnp.exp(nt(q, qkv[m, :, k_cols]) * scale - stats[m, rows, h : h + 1])
                grad_probs = nt(low, qkv[m, :, v_cols])
                delta = jnp.sum(probs * grad_probs, axis=-1, keepdims=True)
                grad_scores = (probs * (grad_probs - delta)).astype(BF)
                r.g_query[rows, cols] += scale * nn(grad_scores, qkv[m, :, k_cols])
                r.grad_kv[m, 512:1024, cols] += tn(grad_scores, q)
                r.grad_kv[m, 512:1024, head(h, base=256)] += tn(probs.astype(BF), low)

        return step

    def finish_rows(m):
        def step(t):
            rows = tile_of(t)
            full = r.grad_kv[m, pl.ds(pl.multiple_of(512 + t * TILE, TILE), TILE)]
            extra = r.later[m, rows].astype(F32)
            at = own_chunk(t)
            r.dqkv[m, at, :, 256:512] = (scale * full[:, 0:256] + extra[:, 0:256]).astype(BF)
            r.dqkv[m, at, :, 512:768] = (full[:, 256:512] + extra[:, 256:512]).astype(BF)

        return step

    ones = jnp.ones((8, 256), BF)

    def gain_row(part, p, rows):
        product = part * r.w.ref[p, rows].astype(F32)
        high = product.astype(BF)
        low = (product - high.astype(F32)).astype(BF)
        return (nt(ones, high) + nt(ones, low))[0:1]

    def weight_part(p, rows):
        whole, cols = r.whole.ref, slice(p * 256, (p + 1) * 256)
        part = tn(whole[0, :, :, rows].reshape(512, 256), r.dqkv[0, :, :, cols].reshape(512, 256))
        return part + tn(
            whole[1, :, :, rows].reshape(512, 256), r.dqkv[1, :, :, cols].reshape(512, 256)
        )

    def early_weights(n):
        rows = slice(n * 256, (n + 1) * 256)
        part = tn(r.att_rel.ref[0].reshape(512, 256), gm[0][:, :, rows].reshape(512, 256))
        part = part + tn(r.att_rel.ref[1].reshape(512, 256), gm[1][:, :, rows].reshape(512, 256))
        r.parts_a[rows, 256:512] = part.astype(BF)
        part = weight_part(0, rows)
        r.parts_a[rows, 0:256] = part.astype(BF)
        return gain_row(part, 0, rows)

    def end_terms(m):
        def columns(n):
            cols = tile_of(n, 256)
            part = nt(r.dqkv[m, :, :, 0:256].reshape(512, 256), r.w.ref[0, cols])
            for p in (1, 2):
                some = r.dqkv[m, :, :, p * 256 : (p + 1) * 256].reshape(512, 256)
                part = part + nt(some, r.w.ref[p, cols])
            part = part.astype(BF)
            split_rows(branch, m, cols, part)

        loop(4, columns)

    def late_weights(n):
        rows = slice(n * 256, (n + 1) * 256)
        total = gains[n]
        for p in (1, 2):
            part = weight_part(p, rows)
            r.parts_b[rows, (p - 1) * 256 : p * 256] = part.astype(BF)
            total = total + gain_row(part, p, rows)
        return total / r.attn_gain[:, rows]

    def end_rows(m):
        grad_normed = ends[m].finish()
        rows = r.x.ref[m].astype(F32)
        inverse = inverse_rms(rows)
        unit = rows * inverse
        scaled = grad_normed * r.attn_gain[...]
        inner = jnp.mean(scaled * unit, axis=-1, keepdims=True)
        r.grad_x.ref[m] = r.grad_middle[m] + inverse * (scaled - unit * inner)

    def share(i):
        k, c = i // 2 + 1, i % 2
        slot = (3 - k) * 2 + core
        return remote(
            r.parts_b.at[768:784, 512:768],
            r.others.at[slot],
            r.s3.at[i],
            r.r3.at[slot],
            others[i],
        )

    def got(i):
        return remote(
            r.parts_b.at[768:784, 512:768], r.others.at[i], r.s3.at[i], r.r3.at[i], others[i]
        )

    def add_gains():
        for i in range(6):
            got(i).wait_recv()
        total = r.others[0].astype(F32)
        for i in range(1, 6):
            total = total + r.others[i].astype(F32)
        row = lax.broadcasted_iota(jnp.int32, (16, 256), 0)
        total = jnp.where(row < 8, total, 0.0) * core.astype(F32)
        at = slice(256, 272), slice(512, 768)
        r.half_b[at] = (r.half_b[at].astype(F32) + total).astype(BF)

    core_a = CoreSum(plane, r.parts_a, r.half_a)
    sum_a = PlaneReduce(plane, r.half_a, r.total_a, r.a_mid, r.a_into, r.a_quarter, r.a_small)
    all_a = PlaneGather(plane, r.total_a)
    core_b = CoreSum(plane, r.parts_b, r.half_b)
    sum_b = PlaneReduce(plane, r.half_b, r.total_b, r.b_mid, r.b_into, r.b_quarter, r.b_small)
    all_b = PlaneGather(plane, r.total_b)

    attention_rows(0)
    fourth.relay()
    for part in (r.qkv, r.kv_all, r.state_kv, r.stats, r.table):
        part.get()
    loop(1, attend(0))
    loop(2, lambda qi: attend(0)(qi + 1))
    loop(1, lambda qi: attend(0)(qi + 3))
    r.prior.get()
    r.state_proj.get()
    pass_on(0)
    fourth.finish()
    attention_rows(1)
    r.branch.get()
    outs[0].start()
    loop(1, attend(1))
    loop(2, lambda qi: attend(1)(qi + 1))
    outs[0].relay()
    outs[1].start()
    loop(1, lambda qi: attend(1)(qi + 3))
    pass_on(1)
    outs[1].relay()
    r.across.get()
    r.keeps.get()
    there[0].finish()
    scan(0)
    back[0].start()
    r.att_rel.get()
    r.w.get()
    r.whole.get()
    gains = [early_weights(n) for n in range(4)]
    core_a.start()
    there[1].finish()
    scan(1)
    back[1].start()
    bucket_sums()
    core_a.finish()
    sum_a.advance()
    r.middle.get()
    for m in both:
        r.out.ref[m] = r.middle.ref[m] + outs[m].finish()
    r.out.put()
    r.update.get()
    r.state_query.get()
    for m in both:
        outs[m].close()
    back[0].finish()
    loop(2, update_tile(0))
    sum_a.advance()
    loop(2, lambda t: update_tile(0)(t + 2))
    shifts[0].wait_recv()
    loop(4, finish_rows(0))
    sum_a.advance()
    end_terms(0)
    ends[0].start()
    sum_a.advance()
    all_a.advance()
    back[1].finish()
    loop(2, update_tile(1))
    all_a.advance()
    loop(2, lambda t: update_tile(1)(t + 2))
    shifts[1].wait_recv()
    loop(4, finish_rows(1))
    ends[0].relay()
    all_a.advance()
    small = [late_weights(n) for n in range(4)]
    small = small + [r.g_mlp_gain[:, n * 256 : (n + 1) * 256] for n in range(4)]
    small = small + [r.g_bias[...], r.g_scale[...], r.g_rel[0, 0:1], r.g_rel[1, 0:1]]
    r.parts_b[0:512, 512:768] = r.g_query[...].astype(BF)
    r.parts_b[512:768, 512:768] = r.g_proj[...].reshape(256, 256).astype(BF)
    r.parts_b[768:784, 512:768] = jnp.concatenate(small + [jnp.zeros((4, 256), F32)], 0).astype(BF)
    r.parts_b[784:1024, 512:768] = jnp.zeros((240, 256), BF)
    core_b.start()
    for i in range(6):
        share(i).start()
    all_a.advance()
    end_terms(1)
    ends[1].start()
    core_b.finish()
    add_gains()
    sum_b.advance()
    r.x.get()
    end_rows(0)
    sum_b.advance()
    ends[1].relay()
    sum_b.advance(2)
    all_b.advance(2)
    end_rows(1)
    r.grad_x.put()
    all_b.advance()
    all_a.advance()
    all_b.advance(2)
    for step in (core_a, sum_a, all_a, core_b, sum_b, all_b, fourth):
        step.close()
    for i in range(6):
        share(i).wait_send()
    for m in both:
        ends[m].close()
        shifts[m].wait_send()
        there[m].close()
        back[m].close()


class Late:
    def __init__(self, source, ref, sem):
        self.ref = ref
        self.copy = pltpu.make_async_copy(source, ref, sem)
        self.copy.start()
        self.open = True

    def get(self):
        if self.open:
            self.copy.wait()
            self.open = False


class Early:
    def __init__(self, target, ref, sem):
        self.ref = ref
        self.copy = pltpu.make_async_copy(ref, target, sem)
        self.sent = False

    def put(self):
        self.copy.start()
        self.sent = True


def call(kernel, name, number, now, late, small, outs, early, scratch, semaphores):
    anywhere = pl.BlockSpec(memory_space=pl.ANY)
    in_names = list(now) + list(small) + list(late)
    out_names = list(outs) + list(early)
    own = [a.shape for a in late.values()], [a.dtype for a in late.values()]
    buffers = list(zip(*own)) + list(early.values()) + list(scratch.values())

    def run(*refs):
        n, o = len(in_names), len(out_names)
        r = types.SimpleNamespace()
        held = refs[n + o : n + o + len(buffers)]
        rest = refs[n + o + len(buffers) :]
        fetch, store = rest[0], rest[1]
        for key, ref in zip(in_names[: len(now) + len(small)], refs):
            setattr(r, key, ref)
        for i, key in enumerate(late):
            setattr(r, key, Late(refs[len(now) + len(small) + i], held[i], fetch.at[i]))
        for key, ref in zip(outs, refs[n:]):
            setattr(r, key, ref)
        stores = []
        for i, key in enumerate(early):
            result = Early(refs[n + len(outs) + i], held[len(late) + i], store.at[i])
            setattr(r, key, result)
            stores.append(result)
        for key, ref in zip(scratch, held[len(late) + len(early) :]):
            setattr(r, key, ref)
        for key, ref in zip(semaphores, rest[2:]):
            setattr(r, key, ref)
        kernel(r)
        for result in stores:
            if not result.sent:
                result.put()
            result.copy.wait()

    shapes = list(outs.values()) + list(early.values())
    results = pl.pallas_call(
        run,
        out_shape=tuple(jax.ShapeDtypeStruct(shape, kind) for shape, kind in shapes),
        in_specs=[VMEM] * len(now) + [SMEM] * len(small) + [anywhere] * len(late),
        out_specs=tuple([VMEM] * len(outs) + [anywhere] * len(early)),
        scratch_shapes=[pltpu.VMEM(shape, kind) for shape, kind in buffers]
        + [sems(max(1, len(late))), sems(max(1, len(early)))]
        + list(semaphores.values()),
        compiler_params=pltpu.CompilerParams(
            collective_id=number, has_side_effects=True, vmem_limit_bytes=LIMIT
        ),
        name=name,
    )(*now.values(), *small.values(), *late.values())
    return dict(zip(out_names, results))


def finish_kernel(total_a, total_b, g_mlp, out, grad_x, state, *refs):
    results, (wide, low, some_a, some_b, rows_in, states_in, fetch, store) = refs[:14], refs[14:]
    places = [rows_in.at[0], rows_in.at[1], states_in]
    taken = [
        pltpu.make_async_copy(a, b, fetch.at[12 + i])
        for i, (a, b) in enumerate(zip((out, grad_x, state), places))
    ]
    passed = [
        pltpu.make_async_copy(a, b, store.at[i])
        for i, (a, b) in enumerate(zip(places, results[:3]))
    ]
    g_up, g_down, g_qkv, g_out, g_query, g_proj = results[3:9]
    attn_gain, mlp_gain, bias, slope, rel = results[9:]
    loads = []
    for n in range(4):
        rows = slice(n * 256, (n + 1) * 256)
        loads.append(
            [
                pltpu.make_async_copy(a.at[rows], b.at[rows], fetch.at[3 * n + i])
                for i, (a, b) in enumerate(((g_mlp, low), (total_a, some_a), (total_b, some_b)))
            ]
        )
    for copy in sum(loads, []) + taken:
        copy.start()
    stores = []

    def put(value, at, target):
        wide[at] = value.astype(F32)
        copy = pltpu.make_async_copy(wide.at[at], target, store.at[3 + len(stores)])
        copy.start()
        stores.append(copy)

    for n in range(4):
        rows = slice(n * 256, (n + 1) * 256)
        for copy in loads[n]:
            copy.wait()
        put(low[rows, 0:1024], (rows, slice(0, 1024)), g_up.at[rows])
        put(low[rows, 1024:2048], (rows, slice(1024, 2048)), g_down.at[rows])
        put(some_a[rows, 0:256], (rows, slice(2048, 2304)), g_qkv.at[0, rows])
        put(some_b[rows, 0:256], (rows, slice(2304, 2560)), g_qkv.at[1, rows])
        put(some_b[rows, 256:512], (rows, slice(2560, 2816)), g_qkv.at[2, rows])
        put(some_a[rows, 256:512], (rows, slice(2816, 3072)), g_out.at[:, rows])
    put(some_b[0:512, 512:768], (slice(0, 512), slice(3072, 3328)), g_query)
    put(some_b[512:768, 512:768], (slice(512, 768), slice(3072, 3328)), g_proj)
    for into, copy in zip(taken, passed):
        into.wait()
        copy.start()
    small = some_b[768:784, 512:768].astype(F32)
    attn_gain[...] = jnp.concatenate([small[n : n + 1] for n in range(4)], 1)
    mlp_gain[...] = jnp.concatenate([small[n : n + 1] for n in range(4, 8)], 1)
    bias[...] = small[8:9]
    slope[...] = small[9:10]
    rel[...] = small[8:16]
    for copy in stores + passed:
        copy.wait()


def sems(*shape):
    return pltpu.SemaphoreType.DMA(shape)


def body(
    tokens_in,
    grad_out,
    flags,
    attn_gain,
    mlp_gain,
    w_qkv,
    w_out,
    rel_bias,
    state_query,
    state_proj,
    forget_bias,
    forget_scale,
    w_up,
    w_down,
):
    micros, rows, width = tokens_in.shape
    block = rows * 4
    local = w_qkv.shape[2]
    heads = rel_bias.shape[1]
    states = state_query.shape[0]
    buckets = rel_bias.shape[0]
    count = lax.axis_size("blk")
    w = jnp.transpose(w_qkv, (1, 0, 2))
    small = dict(flags=jnp.transpose(flags))
    whole_shape = ((micros, 4, rows, width), BF)
    state_low = ((micros, states, local), BF)
    state_wide = ((micros, states, local), F32)
    rows_wide = ((micros, rows, width), F32)
    mlp_width = w_up.shape[1] + w_down.shape[1]
    exchange = dict(
        s0=sems(2),
        r0=sems(2),
        s1=sems(2, count),
        r1=sems(2, count),
        s2=sems(2, count),
        r2=sems(2, count),
        local=sems(4),
    )
    gates = dict(bias=forget_bias[None], slope=forget_scale[None])
    f = call(
        forward_kernel,
        "forward",
        1,
        dict(
            x=tokens_in,
            attn_gain=attn_gain[None],
            mlp_gain=mlp_gain[None],
            **gates,
        ),
        dict(
            w=w,
            state_query=state_query,
            g=grad_out,
            state_proj=state_proj,
            w_out=w_out,
            w_up=w_up,
            w_down=w_down,
        ),
        dict(rel=jnp.transpose(rel_bias), **small),
        dict(
            grad_middle=rows_wide,
            gm0=((4, rows, width), BF),
            g_gain=((1, width), F32),
        ),
        dict(
            whole=whole_shape,
            qkv=((micros, block, 3 * local), BF),
            kv_all=((micros, 2 * block, 2 * local), BF),
            state_kv=((micros, states, 2 * local), BF),
            prior=state_low,
            across=state_low,
            keeps=((count, 8, local), F32),
            update=state_wide,
            stats=((micros, block, TILE), F32),
            table=((heads, TILE, 5 * TILE), F32),
            state_after=state_wide,
            att_rel=((micros, 4, rows, local), BF),
            middle=rows_wide,
            branch=whole_shape,
            parts=((width, mlp_width), BF),
        ),
        dict(
            whole_grad=whole_shape,
            own_keep=((8, local), F32),
            unit_low=state_low,
            held=state_low,
            terms=whole_shape,
            whole_mlp=whole_shape,
            active=((micros, block, w_up.shape[1]), BF),
            grad_hidden=((micros, block, w_up.shape[1]), BF),
            mids=((4, 4, rows // 2, width), BF),
            intos=((4, 2, rows, width), BF),
        ),
        dict(send=sems(80), recv=sems(80), s3=sems(count), r3=sems(count), **exchange),
    )
    g_mlp = lax.psum(f["parts"], "blk")
    b = call(
        backward_kernel,
        "backward",
        2,
        dict(
            gm0=f["gm0"],
            grad_middle=f["grad_middle"],
            w_out=w_out,
            attn_gain=attn_gain[None],
            g_mlp_gain=f["g_gain"],
            **gates,
        ),
        dict(
            qkv=f["qkv"],
            kv_all=f["kv_all"],
            state_kv=f["state_kv"],
            stats=f["stats"],
            table=f["table"],
            branch=f["branch"],
            prior=f["prior"],
            state_proj=state_proj,
            across=f["across"],
            keeps=f["keeps"],
            att_rel=f["att_rel"],
            middle=f["middle"],
            update=f["update"],
            state_query=state_query,
            w=w,
            whole=f["whole"],
            x=tokens_in,
        ),
        small,
        dict(
            total_a=((width, 512), BF),
            total_b=((width, 768), BF),
        ),
        dict(out=rows_wide, grad_x=rows_wide),
        dict(
            dqkv=((micros, 4, rows, 3 * local), BF),
            g_query=((states, local), F32),
            g_proj=(state_proj.shape, F32),
            g_rel=((heads, 8, local), F32),
            g_bias=((1, local), F32),
            g_scale=((1, local), F32),
            grad_att=((micros, block, local), BF),
            grad_kv=((micros, 2 * block, 2 * local), F32),
            grad_state=((micros, states, 2 * local), F32),
            early=((micros, block, 2 * local), BF),
            later=((micros, block, 2 * local), BF),
            grad_prior=state_low,
            moved=state_low,
            held=state_low,
            grad_after=state_low,
            near=((heads, TILE, 3 * TILE), F32),
            sums=((local, TILE), F32),
            mids=((4, 4, rows // 2, width), BF),
            intos=((4, 2, rows, width), BF),
            others=((6, 16, local), BF),
            gm1=((4, rows, width), BF),
            parts_a=((width, 512), BF),
            half_a=((512, 512), BF),
            parts_b=((width, 768), BF),
            half_b=((512, 768), BF),
            **reduce_scratch("a_", 512),
            **reduce_scratch("b_", 768),
        ),
        dict(send=sems(150), recv=sems(150), s3=sems(6), r3=sems(6), **exchange),
    )
    results = [
        rows_wide[0],
        rows_wide[0],
        state_wide[0],
        w_up.shape,
        w_down.shape,
        w.shape,
        w_out.shape,
        state_query.shape,
        (heads * state_proj.shape[1], local),
        (1, width),
        (1, width),
        (1, local),
        (1, local),
        (8, local),
    ]
    anywhere = pl.BlockSpec(memory_space=pl.ANY)
    values = pl.pallas_call(
        finish_kernel,
        out_shape=tuple(jax.ShapeDtypeStruct(shape, F32) for shape in results),
        in_specs=[anywhere] * 6,
        out_specs=tuple([anywhere] * 9 + [VMEM] * 5),
        scratch_shapes=[
            pltpu.VMEM((width, 3328), F32),
            pltpu.VMEM((width, mlp_width), BF),
            pltpu.VMEM((width, 512), BF),
            pltpu.VMEM((width, 768), BF),
            pltpu.VMEM((2,) + rows_wide[0], F32),
            pltpu.VMEM(state_wide[0], F32),
            sems(15),
            sems(32),
        ],
        compiler_params=pltpu.CompilerParams(vmem_limit_bytes=LIMIT),
        name="finish",
    )(b["total_a"], b["total_b"], g_mlp, b["out"], b["grad_x"], f["state_after"])
    out, grad_x, state_after, g_up, g_down, g_qkv, g_out, g_query, g_proj = values[:9]
    g_attn_gain, g_mlp_gain, g_bias, g_scale, g_rel = values[9:]
    return (
        out,
        grad_x,
        state_after[:, None],
        g_attn_gain[0],
        g_mlp_gain[0],
        jnp.transpose(g_qkv, (1, 0, 2)),
        g_out,
        jnp.transpose(g_rel[2:4, :buckets]),
        g_query,
        g_proj.reshape(state_proj.shape),
        g_bias[0],
        g_scale[0],
        g_up,
        g_down,
    )


def solution(mesh):
    return jax.shard_map(
        body,
        mesh=mesh,
        in_specs=(
            P(None, ("blk", "head"), None),
            P(None, ("blk", "head"), None),
            P(None, "blk"),
            P(),
            P(),
            P(None, None, "head"),
            P("head", None),
            P(None, "head"),
            P(None, "head"),
            P("head", None, None),
            P("head"),
            P("head"),
            P(None, "head"),
            P("head", None),
        ),
        out_specs=(
            P(None, ("blk", "head"), None),
            P(None, ("blk", "head"), None),
            P(None, "blk", None, "head"),
            P(),
            P(),
            P(None, None, "head"),
            P("head", None),
            P(None, "head"),
            P(None, "head"),
            P("head", None, None),
            P("head"),
            P("head"),
            P(None, "head"),
            P("head", None),
        ),
        check_vma=False,
    )
```

```python
import math
import types

import jax
import jax.numpy as jnp
from jax import lax
from jax.experimental import pallas as pl
from jax.experimental.pallas import tpu as pltpu
from jax.sharding import PartitionSpec as P

BUCKETS = 32
MAXDIST = 128
EPSILON = 1e-06
MASKED = -1e30
TILE = 128
MESH = pl.DeviceIdType.MESH
BF = jnp.bfloat16
F32 = jnp.float32
VMEM = pl.BlockSpec(memory_space=pltpu.VMEM)
SMEM = pl.BlockSpec(memory_space=pltpu.SMEM)
LIMIT = 60 * 2**20
ROOT = math.sqrt(2.0 / math.pi)
CUBIC = 0.044715


def bucket_starts():
    exact = BUCKETS // 2
    levels = [
        int(math.ceil(exact * (MAXDIST / exact) ** (t / (BUCKETS - exact))))
        for t in range(1, BUCKETS - exact)
    ]
    return list(range(exact + 1)) + levels


STARTS = bucket_starts()


def nn(a, b):
    return lax.dot_general(a, b, (((1,), (0,)), ((), ())), preferred_element_type=F32)


def nt(a, b):
    return lax.dot_general(a, b, (((1,), (1,)), ((), ())), preferred_element_type=F32)


def tn(a, b):
    return lax.dot_general(a, b, (((0,), (0,)), ((), ())), preferred_element_type=F32)


def inverse_rms(values):
    return lax.rsqrt(jnp.mean(values * values, axis=-1, keepdims=True) + EPSILON)


def tile_of(index, size=TILE):
    return pl.ds(pl.multiple_of(index * size, size), size)


def loop(count, step, after=None, action=None):
    def run(i, c):
        step(i)
        return c

    if after is not None:
        lax.fori_loop(0, after + 1, run, 0)
        action()
    lax.fori_loop(0 if after is None else after + 1, count, run, 0)


def remote(src, dst, send_sem, recv_sem, device):
    return pltpu.make_async_remote_copy(
        src_ref=src,
        dst_ref=dst,
        send_sem=send_sem,
        recv_sem=recv_sem,
        device_id=device,
        device_id_type=MESH,
    )


class Links:
    def __init__(self, send, recv):
        self.send, self.recv, self.used = send, recv, 0

    def go(self, src, dst, device):
        copy = remote(src, dst, self.send.at[self.used], self.recv.at[self.used], device)
        self.used += 1
        copy.start()
        return copy


class Ring:
    def __init__(self, links, me, device):
        self.links, self.me = links, me
        self.right = device(lax.rem(me + 1, 4))
        self.left = device(lax.rem(me + 3, 4))
        self.opposite = device(lax.rem(me + 2, 4))

    def go(self, src, dst, peer):
        return self.links.go(src, dst, peer)

    def greet(self):
        barrier = pltpu.get_barrier_semaphore()
        for peer in (self.right, self.left):
            pl.semaphore_signal(barrier, inc=1, device_id=peer, device_id_type=MESH)
        return 2

    def chunk(self, k):
        return lax.rem(self.me + k, 4)

    def row_chunk(self, k):
        return tile_of(self.chunk(k))


def head_ring(links):
    return Ring(links, lax.axis_index("head"), lambda i: {"head": i})


def by_rows(buf):
    half = buf.shape[1] // 2

    def piece(k, part=None, offset=0):
        return buf.at[k] if part is None else buf.at[k, part * half : (part + 1) * half]

    return piece


def by_columns(buf, base, rows, chunk):
    half = buf.shape[1] // 2
    starts = [pl.multiple_of(base + chunk(k) * rows, rows) for k in range(4)]

    def piece(k, part=None, offset=0):
        at = pl.ds(starts[(k + offset) % 4], rows)
        return buf.at[at] if part is None else buf.at[at, part * half : (part + 1) * half]

    return piece


class Gather:
    def __init__(self, ring, piece):
        self.ring, self.piece = ring, piece

    def start(self):
        r, p = self.ring, self.piece
        self.a0 = r.go(p(0, 0), p(3, 0, 1), r.right)
        self.b0 = r.go(p(0, 1), p(1, 1, 3), r.left)
        self.a1 = r.go(p(0, 1), p(3, 1, 1), r.right)
        self.b1 = r.go(p(0, 0), p(1, 0, 3), r.left)

    def relay(self):
        r, p = self.ring, self.piece
        self.a0.wait_recv()
        self.a2 = r.go(p(3, 0), p(2, 0, 1), r.right)
        self.b0.wait_recv()
        self.b2 = r.go(p(1, 1), p(2, 1, 3), r.left)

    def finish(self):
        for copy in (self.a1, self.b1, self.a2, self.b2):
            copy.wait_recv()

    def close(self):
        for copy in (self.a0, self.b0, self.a1, self.b1, self.a2, self.b2):
            copy.wait_send()


class Reduce:
    def __init__(self, ring, terms, mid, into):
        self.ring, self.terms, self.mid, self.into = ring, terms, mid, into
        if mid.shape[1] == into.shape[1]:
            half = into.shape[2] // 2
            self.place = lambda i, part: into.at[i, :, part * half : (part + 1) * half]
        else:
            half = into.shape[1] // 2
            self.place = lambda i, part: into.at[i, part * half : (part + 1) * half]

    def start(self):
        r, t = self.ring, self.terms
        self.a0 = r.go(t(2, 0), self.mid.at[0], r.right)
        self.b0 = r.go(t(2, 1), self.mid.at[1], r.left)
        self.a1 = r.go(t(1, 1), self.place(0, 1), r.right)
        self.b1 = r.go(t(3, 0), self.place(1, 0), r.left)

    def relay(self):
        r, t, mid = self.ring, self.terms, self.mid
        self.a0.wait_recv()
        mid[2] = (mid[0].astype(F32) + t(1, 0)[...].astype(F32)).astype(BF)
        self.a2 = r.go(mid.at[2], self.place(0, 0), r.right)
        self.b0.wait_recv()
        mid[3] = (mid[1].astype(F32) + t(3, 1)[...].astype(F32)).astype(BF)
        self.b2 = r.go(mid.at[3], self.place(1, 1), r.left)

    def finish(self):
        for copy in (self.a1, self.b1, self.a2, self.b2):
            copy.wait_recv()
        return (
            self.terms(0)[...].astype(F32)
            + self.into[0].astype(F32)
            + self.into[1].astype(F32)
        )

    def close(self):
        for copy in (self.a0, self.b0, self.a1, self.b1, self.a2, self.b2):
            copy.wait_send()


def block_device(x, z, c):
    return {"blk": (x * 4 + z) * 2 + c}


def block_place():
    place = lax.axis_index("blk")
    return place % 2, (place // 2) % 4, place // 8


class Plane:
    def __init__(self, links):
        c, z, x = block_place()
        self.links = links
        self.peer = block_device(x, z, 1 - c)
        rx = Ring(links, x, lambda i: block_device(i, z, c))
        rz = Ring(links, z, lambda i: block_device(x, i, c))
        self.rings = [rx, rz]
        self.first, self.second = (rx, rz), (rz, rx)
        self.base = c * 512
        self.own = pl.ds(pl.multiple_of(c * 512, 512), 512)
        self.away = pl.ds(pl.multiple_of((1 - c) * 512, 512), 512)
        self.top = [c * 512 + x * 64, c * 512 + 256 + z * 64]
        self.last = [
            pl.ds(pl.multiple_of(self.top[0] + z * 16, 16), 16),
            pl.ds(pl.multiple_of(self.top[1] + x * 16, 16), 16),
        ]

    def greet(self):
        barrier = pltpu.get_barrier_semaphore()
        pl.semaphore_signal(barrier, inc=1, device_id=self.peer, device_id_type=MESH)
        return 1 + sum(ring.greet() for ring in self.rings)


class Steps:
    def advance(self, steps=1):
        for _ in range(steps):
            if self.steps:
                self.steps.pop(0)()


class CoreSum:
    def __init__(self, plane, parts, half):
        self.plane, self.parts, self.half = plane, parts, half

    def start(self):
        plane = self.plane
        self.swap = plane.links.go(self.parts.at[plane.away], self.half, plane.peer)

    def finish(self):
        self.swap.wait_recv()

        def add(t):
            rows = tile_of(t, 64)
            own = pl.ds(pl.multiple_of(self.plane.base + t * 64, 64), 64)
            self.half[rows] = (
                self.parts[own].astype(F32) + self.half[rows].astype(F32)
            ).astype(BF)

        loop(8, add)

    def close(self):
        self.swap.wait_send()


class PlaneReduce(Steps):
    def __init__(self, plane, half, total, mid, into, quarter, small_into):
        self.plane, self.half, self.total, self.quarter = plane, half, total, quarter
        first, second = plane.first, plane.second
        self.reduce1 = [
            Reduce(first[i], by_columns(half, i * 256, 64, first[i].chunk), mid.at[i], into.at[i])
            for i in range(2)
        ]
        self.reduce2 = [
            ReduceDirect(
                second[i], by_columns(quarter.at[i], 0, 16, second[i].chunk), small_into.at[i]
            )
            for i in range(2)
        ]
        self.steps = [
            lambda: [r.start() for r in self.reduce1],
            lambda: [r.relay() for r in self.reduce1],
            self.start2,
            self.finish,
        ]

    def start2(self):
        for i, r in enumerate(self.reduce1):
            self.quarter[i] = r.finish().astype(BF)
            self.reduce2[i].start()

    def finish(self):
        for i, r in enumerate(self.reduce2):
            self.total[self.plane.last[i]] = r.finish().astype(BF)

    def close(self):
        for r in self.reduce1 + self.reduce2:
            r.close()


class PlaneGather(Steps):
    def __init__(self, plane, total):
        self.plane, self.total = plane, total
        first, second = plane.first, plane.second
        self.gather1 = [
            GatherDirect(second[i], by_columns(total, plane.top[i], 16, second[i].chunk))
            for i in range(2)
        ]
        self.gather2 = [
            Gather(first[i], by_columns(total, plane.base + i * 256, 64, first[i].chunk))
            for i in range(2)
        ]
        self.steps = [
            lambda: [g.start() for g in self.gather1],
            self.start2,
            lambda: [g.relay() for g in self.gather2],
            self.cores,
            lambda: self.swap.wait_recv(),
        ]

    def start2(self):
        for i, g in enumerate(self.gather1):
            g.finish()
            self.gather2[i].start()

    def cores(self):
        for g in self.gather2:
            g.finish()
        rows = self.total.at[self.plane.own]
        self.swap = self.plane.links.go(rows, rows, self.plane.peer)

    def close(self):
        self.swap.wait_send()
        for g in self.gather1 + self.gather2:
            g.close()


def reduce_scratch(name, width):
    return {
        name + "mid": ((2, 4, 64, width // 2), BF),
        name + "into": ((2, 2, 64, width), BF),
        name + "quarter": ((2, 64, width), BF),
        name + "small": ((2, 3, 16, width), BF),
    }


class GatherDirect:
    def __init__(self, ring, piece):
        self.ring, self.piece = ring, piece

    def start(self):
        r, p = self.ring, self.piece
        self.copies = [
            r.go(p(0), p(4 - k, None, k), peer)
            for k, peer in ((1, r.right), (3, r.left), (2, r.opposite))
        ]

    def finish(self):
        for copy in self.copies:
            copy.wait_recv()

    def close(self):
        for copy in self.copies:
            copy.wait_send()


class ReduceDirect:
    def __init__(self, ring, terms, into):
        self.ring, self.terms, self.into = ring, terms, into

    def start(self):
        r, t = self.ring, self.terms
        self.copies = [
            r.go(t(k), self.into.at[k - 1], peer)
            for k, peer in ((1, r.right), (3, r.left), (2, r.opposite))
        ]

    def finish(self):
        for copy in self.copies:
            copy.wait_recv()
        total = self.terms(0)[...].astype(F32)
        for k in range(3):
            total = total + self.into[k].astype(F32)
        return total

    def close(self):
        for copy in self.copies:
            copy.wait_send()


class Exchange:
    def __init__(self, source, target, send, recv, local):
        self.count = lax.axis_size("blk")
        self.place = lax.axis_index("blk")
        self.size = source.shape[0] // self.count
        self.source, self.target = source, target
        self.send, self.recv, self.local = send, recv, local

    def part(self, j):
        peer = lax.rem(self.place + j, self.count)
        return remote(
            self.source.at[tile_of(peer, self.size)],
            self.target.at[tile_of(self.place, self.size)],
            self.send.at[j],
            self.recv.at[j],
            {"blk": peer},
        )

    def own(self):
        rows = tile_of(self.place, self.size)
        return pltpu.make_async_copy(self.source.at[rows], self.target.at[rows], self.local)

    def start(self):
        loop(self.count - 1, lambda j: self.part(j + 1).start())
        self.own().start()

    def finish(self):
        self.own().wait()
        loop(self.count - 1, lambda j: self.part(j + 1).wait_recv())

    def close(self):
        loop(self.count - 1, lambda j: self.part(j + 1).wait_send())


def greet_blocks():
    barrier = pltpu.get_barrier_semaphore()
    count, place = lax.axis_size("blk"), lax.axis_index("blk")

    def greet(j):
        pl.semaphore_signal(
            barrier, inc=1, device_id={"blk": lax.rem(place + j + 1, count)}, device_id_type=MESH
        )

    loop(count - 1, greet)
    return count - 1


def closed_row(flag, qi):
    column = lax.broadcasted_iota(jnp.int32, (1, 5 * TILE), 1) + qi * TILE
    return jnp.where(column < 512, MASKED * flag.astype(F32), 0.0)


def head(h, size=TILE, base=0):
    return slice(base + h * size, base + (h + 1) * size)


def window_of(qi):
    return pl.ds(pl.multiple_of(qi * TILE, TILE), 5 * TILE)


def split_rows(target, m, cols, part):
    for k in range(4):
        target[m, k, :, cols] = part[k * TILE : (k + 1) * TILE]


def write_table(table, rel):
    row = lax.broadcasted_iota(jnp.int32, (TILE, TILE), 0)
    col = lax.broadcasted_iota(jnp.int32, (TILE, TILE), 1)

    def per_head(h):
        far = jnp.full((TILE, TILE), rel[h, BUCKETS - 1], F32)
        table[h, :, 0:128] = jnp.where(row < col, far, MASKED)
        table[h, :, 128:256] = far
        table[h, :, 256:384] = far
        for shift, at in ((TILE, 384), (0, 512)):
            distance = row - col + shift
            total = jnp.full((TILE, TILE), rel[h, 0], F32)
            for t in range(1, BUCKETS):
                total = jnp.where(distance >= STARTS[t], rel[h, t], total)
            table[h, :, at : at + TILE] = jnp.where(distance >= 0, total, MASKED)

    loop(2, per_head)


def forward_kernel(r):
    scale = TILE**-0.5
    links = Links(r.send, r.recv)
    ring = head_ring(links)
    plane = Plane(links)
    place, count = lax.axis_index("blk"), lax.axis_size("blk")
    both = range(2)

    def norm_rows(m):
        rows = r.x[m].astype(F32)
        r.whole.ref[m, 0] = (rows * inverse_rms(rows) * r.attn_gain[...]).astype(BF)

    norm_rows(0)
    for m in both:
        keep = 1.0 - r.flags[0, m].astype(F32)
        r.own_keep[m : m + 1] = jnp.full((1, 256), keep, F32)
    r.own_keep[2:8] = jnp.zeros((6, 256), F32)
    pl.semaphore_wait(pltpu.get_barrier_semaphore(), ring.greet() + greet_blocks())
    whole, qkv, kv_all = r.whole.ref, r.qkv.ref, r.kv_all.ref
    prior, across, keeps = r.prior.ref, r.across.ref, r.keeps.ref
    update, stats, state_kv = r.update.ref, r.stats.ref, r.state_kv.ref
    table, att_rel, middle, branch = r.table.ref, r.att_rel.ref, r.middle.ref, r.branch.ref
    gather_x = [Gather(ring, by_rows(whole.at[m])) for m in both]
    gather_g = [Gather(ring, by_rows(r.whole_grad.at[m])) for m in both]
    gather_x[0].start()
    norm_rows(1)

    def tell(j):
        peer = {"blk": lax.rem(place + j, count)}
        return remote(r.own_keep, keeps.at[place], r.s3.at[j], r.r3.at[j], peer)

    loop(count - 1, lambda j: tell(j + 1).start())
    keeps[place] = r.own_keep[...]
    write_table(table, r.rel)
    r.table.put()
    after = {"blk": lax.rem(place + 1, count)}
    shifts = [
        remote(qkv.at[m, :, 256:768], kv_all.at[m, 0:512], r.s0.at[m], r.r0.at[m], after)
        for m in both
    ]
    there = [
        Exchange(r.unit_low.at[m], across.at[m], r.s1.at[m], r.r1.at[m], r.local.at[m])
        for m in both
    ]
    back = [
        Exchange(r.held.at[m], prior.at[m], r.s2.at[m], r.r2.at[m], r.local.at[2 + m])
        for m in both
    ]

    def project(m):
        def columns(n):
            cols = tile_of(n, 256)
            part = nn(whole[m].reshape(512, 1024), r.w.ref[n]).astype(BF)
            for k in range(4):
                qkv[m, ring.row_chunk(k), cols] = part[k * TILE : (k + 1) * TILE]

        loop(3, columns)
        shifts[m].start()
        kv_all[m, 512:1024] = qkv[m, :, 256:768]

    def update_tile(m):
        def step(t):
            rows = tile_of(t)
            for h in range(2):
                scores = nt(r.state_query.ref[rows, head(h)], qkv[m, :, head(h, base=256)]) * scale
                top = jnp.max(scores, axis=-1, keepdims=True)
                raised = jnp.exp(scores - top)
                total = jnp.sum(raised, axis=-1, keepdims=True)
                stats[m, rows, h : h + 1] = top + jnp.log(total)
                u = nn(raised.astype(BF), qkv[m, :, head(h, base=512)]) / total
                update[m, rows, head(h)] = u
                r.unit_low[m, rows, head(h)] = (u * inverse_rms(u)).astype(BF)

        return step

    def scan(m):
        def step(b, state):
            rows = tile_of(b, 16)
            u = across[m, rows].astype(F32)
            forget = jax.nn.sigmoid(r.bias[...] + r.slope[...] * u)
            before = keeps[b, m : m + 1] * state
            r.held[m, rows] = before.astype(BF)
            return forget * before + (1.0 - forget) * u

        lax.fori_loop(0, count, step, jnp.zeros((16, 256), F32))

    def state(m):
        def step(t):
            rows = tile_of(t)
            before = prior[m, rows]
            for h in range(2):
                state_kv[m, rows, head(h, 256)] = nn(before[:, head(h)], r.state_proj.ref[h]).astype(BF)
                u = update[m, rows, head(h)]
                u = u * inverse_rms(u)
                forget = jax.nn.sigmoid(r.bias[:, head(h)] + r.slope[:, head(h)] * u)
                r.state_after.ref[m, rows, head(h)] = (
                    forget * before[:, head(h)].astype(F32) + (1.0 - forget) * u
                )

        return step

    def attend(m):
        def step(qi):
            rows, window = tile_of(qi), window_of(qi)
            shut = closed_row(r.flags[0, m], qi)
            for h in range(2):
                q = qkv[m, rows, head(h)]
                token = nt(q, kv_all[m, window, head(h)]) * scale + (table[h] + shut)
                from_state = nt(q, state_kv[m, :, h * 256 : h * 256 + TILE]) * scale
                top = jnp.maximum(
                    jnp.max(token, axis=-1, keepdims=True),
                    jnp.max(from_state, axis=-1, keepdims=True),
                )
                token = jnp.exp(token - top)
                from_state = jnp.exp(from_state - top)
                total = jnp.sum(token, axis=-1, keepdims=True) + jnp.sum(
                    from_state, axis=-1, keepdims=True
                )
                stats[m, rows, 2 + h : 3 + h] = top + jnp.log(total)
                out = nn(token.astype(BF), kv_all[m, window, head(h, base=256)]) + nn(
                    from_state.astype(BF), state_kv[m, :, h * 256 + TILE : (h + 1) * 256]
                )
                att_rel[m, lax.rem(qi + 4 - ring.me, 4), :, head(h)] = (out / total).astype(BF)

        return step

    first = [
        Reduce(ring, by_rows(r.terms.at[m]), r.mids.at[m], r.intos.at[m]) for m in both
    ]
    second = [Gather(ring, by_rows(r.whole_mlp.at[m])) for m in both]
    third = [
        Reduce(ring, by_rows(r.terms.at[m]), r.mids.at[2 + m], r.intos.at[2 + m]) for m in both
    ]
    fourth = Gather(ring, by_rows(r.gm0))

    def out_terms(m):
        def columns(n):
            cols = tile_of(n, 256)
            part = nn(att_rel[m].reshape(512, 256), r.w_out.ref[:, cols]).astype(BF)
            split_rows(r.terms, m, cols, part)

        loop(4, columns)

    def normalise(m):
        rows = r.x[m].astype(F32) + first[m].finish()
        middle[m] = rows
        r.whole_mlp[m, 0] = (rows * inverse_rms(rows) * r.mlp_gain[...]).astype(BF)

    def hidden(m):
        def columns(n):
            cols = tile_of(n, 256)
            value = nn(r.whole_mlp[m].reshape(512, 1024), r.w_up.ref[:, cols])
            grad_active = nt(r.whole_grad[m].reshape(512, 1024), r.w_down.ref[cols])
            square = value * value
            bent = jnp.tanh(ROOT * value * (1.0 + CUBIC * square))
            r.active[m, :, cols] = (0.5 * value * (1.0 + bent)).astype(BF)
            rise = 0.5 * (1.0 + bent) + 0.5 * value * (1.0 - bent * bent) * ROOT * (
                1.0 + 3.0 * CUBIC * square
            )
            r.grad_hidden[m, :, cols] = (grad_active * rise).astype(BF)

        return columns

    def grad_terms(m):
        def columns(n):
            cols = tile_of(n, 256)
            part = nt(r.grad_hidden[m], r.w_up.ref[cols]).astype(BF)
            split_rows(r.terms, m, cols, part)

        loop(4, columns)

    def branch_terms(m):
        def columns(n):
            cols = tile_of(n, 256)
            part = nn(r.active[m], r.w_down.ref[:, cols]).astype(BF)
            split_rows(branch, m, cols, part)

        loop(4, columns)

    def grad_rows(m):
        grad_normed = third[m].finish()
        rows = middle[m]
        inverse = inverse_rms(rows)
        unit = rows * inverse
        part = jnp.sum(grad_normed * unit, axis=0, keepdims=True)
        r.g_gain[...] = part if m == 0 else r.g_gain[...] + part
        scaled = grad_normed * r.mlp_gain[...]
        inner = jnp.mean(scaled * unit, axis=-1, keepdims=True)
        total = r.g.ref[m].astype(F32) + inverse * (scaled - unit * inner)
        r.grad_middle[m] = total
        if m == 0:
            r.gm0[0] = total.astype(BF)

    def up_rows(n):
        rows = tile_of(n, 256)
        total = tn(r.whole_mlp[0, :, :, rows].reshape(512, 256), r.grad_hidden[0])
        total = total + tn(r.whole_mlp[1, :, :, rows].reshape(512, 256), r.grad_hidden[1])
        r.parts[rows, 0:1024] = total.astype(BF)

    def down_rows(n):
        rows = tile_of(n, 256)
        total = tn(r.active[0, :, rows], r.whole_grad[0].reshape(512, 1024))
        total = total + tn(r.active[1, :, rows], r.whole_grad[1].reshape(512, 1024))
        r.parts[rows, 1024:2048] = total.astype(BF)

    cores = CoreSum(plane, r.parts, r.half)

    gather_x[0].relay()
    gather_x[1].start()
    r.w.get()
    gather_x[0].finish()
    project(0)
    gather_x[1].relay()
    r.state_query.get()
    loop(4, update_tile(0))
    there[0].start()
    gather_x[1].finish()
    r.g.get()
    for m in both:
        r.whole_grad[m, 0] = r.g.ref[m]
    gather_g[0].start()
    project(1)
    r.whole.put()
    r.qkv.put()
    loop(4, update_tile(1))
    there[1].start()
    r.update.put()
    gather_g[0].relay()
    gather_g[1].start()
    loop(count - 1, lambda j: tell(j + 1).wait_recv())
    there[0].finish()
    scan(0)
    back[0].start()
    there[1].finish()
    scan(1)
    back[1].start()
    gather_g[1].relay()
    r.across.put()
    r.keeps.put()
    shifts[0].wait_recv()
    shifts[1].wait_recv()
    r.kv_all.put()
    r.state_proj.get()
    back[0].finish()
    loop(4, state(0))
    loop(4, attend(0))
    r.w_out.get()
    out_terms(0)
    first[0].start()
    back[1].finish()
    r.prior.put()
    loop(4, state(1))
    r.state_kv.put()
    r.state_after.put()
    loop(4, attend(1), 0, first[0].relay)
    r.stats.put()
    out_terms(1)
    r.att_rel.put()
    first[1].start()
    normalise(0)
    second[0].start()
    first[1].relay()
    second[0].relay()
    r.w_up.get()
    r.w_down.get()
    gather_g[0].finish()
    gather_g[1].finish()
    normalise(1)
    second[1].start()
    r.middle.put()
    second[0].finish()
    loop(4, hidden(0), 1, second[1].relay)
    first[0].close()
    grad_terms(0)
    third[0].start()
    second[1].finish()
    loop(4, hidden(1), 1, third[0].relay)
    first[1].close()
    grad_terms(1)
    third[1].start()
    loop(4, up_rows)
    grad_rows(0)
    fourth.start()
    third[1].relay()
    loop(4, down_rows)
    cores.start()
    fourth.relay()
    branch_terms(0)
    branch_terms(1)
    r.branch.put()
    cores.finish()
    grad_rows(1)
    fourth.finish()
    cores.close()
    fourth.close()
    for m in both:
        for step in (gather_x, gather_g, second, third):
            step[m].close()
        shifts[m].wait_send()
        there[m].close()
        back[m].close()
    loop(count - 1, lambda j: tell(j + 1).wait_send())


def backward_kernel(r):
    scale = TILE**-0.5
    links = Links(r.send, r.recv)
    ring = head_ring(links)
    plane = Plane(links)
    place, count = lax.axis_index("blk"), lax.axis_size("blk")
    both = range(2)
    gm = [r.gm0, r.gm1]
    r.gm1[0] = r.grad_middle[1].astype(BF)
    core = place % 2
    others = [
        {"head": ring.chunk(k), "blk": place - core + c} for k in range(1, 4) for c in range(2)
    ]
    barrier = pltpu.get_barrier_semaphore()
    for device in others:
        pl.semaphore_signal(barrier, inc=1, device_id=device, device_id_type=MESH)
    pl.semaphore_wait(barrier, len(others) + greet_blocks())
    fourth = Gather(ring, by_rows(r.gm1))
    fourth.start()
    mlp_sum = PlaneReduce(
        plane, r.half, r.total_mlp, r.mlp_mid, r.mlp_into, r.mlp_quarter, r.mlp_small
    )
    mlp_all = PlaneGather(plane, r.total_mlp)
    mlp_sum.advance()
    qkv, kv_all, state_kv, stats = r.qkv.ref, r.kv_all.ref, r.state_kv.ref, r.stats.ref
    r.branch.get()
    branch = r.branch.ref
    outs = [Reduce(ring, by_rows(branch.at[m]), r.mids.at[m], r.intos.at[m]) for m in both]
    ends = [
        Reduce(ring, by_rows(branch.at[m]), r.mids.at[2 + m], r.intos.at[2 + m]) for m in both
    ]
    before = {"blk": lax.rem(place + count - 1, count)}
    shifts = [
        remote(r.early.at[m], r.later.at[m], r.s0.at[m], r.r0.at[m], before) for m in both
    ]
    there = [
        Exchange(r.grad_prior.at[m], r.moved.at[m], r.s1.at[m], r.r1.at[m], r.local.at[m])
        for m in both
    ]
    back = [
        Exchange(r.held.at[m], r.grad_after.at[m], r.s2.at[m], r.r2.at[m], r.local.at[2 + m])
        for m in both
    ]
    for ref in (r.near, r.sums, r.g_query, r.g_bias, r.g_scale, r.grad_kv, r.grad_state):
        ref[...] = jnp.zeros(ref.shape, F32)

    def own_chunk(qi):
        return lax.rem(qi + 4 - ring.me, 4)

    def attention_rows(m):
        part = nt(gm[m][...].reshape(512, 1024), r.w_out[...]).astype(BF)
        for k in range(4):
            r.grad_att[m, ring.row_chunk(k)] = part[k * TILE : (k + 1) * TILE]

    def attend(m):
        def step(qi):
            rows, window = tile_of(qi), window_of(qi)
            shut = closed_row(r.flags[0, m], qi)
            for h in range(2):
                k_cols, v_cols = head(h), head(h, base=256)
                sk_cols = slice(h * 256, h * 256 + TILE)
                sv_cols = slice(h * 256 + TILE, (h + 1) * 256)
                q = qkv[m, rows, head(h)]
                d = r.grad_att[m, rows, head(h)]
                level = stats[m, rows, 2 + h : 3 + h]
                token = jnp.exp(
                    nt(q, kv_all[m, window, k_cols]) * scale + (r.table.ref[h] + shut) - level
                )
                from_state = jnp.exp(nt(q, state_kv[m, :, sk_cols]) * scale - level)
                grad_token = nt(d, kv_all[m, window, v_cols])
                grad_from = nt(d, state_kv[m, :, sv_cols])
                delta = jnp.sum(token * grad_token, axis=-1, keepdims=True) + jnp.sum(
                    from_state * grad_from, axis=-1, keepdims=True
                )
                grad_token = token * (grad_token - delta)
                grad_from = from_state * (grad_from - delta)
                r.near[h, :, 0:128] += (
                    grad_token[:, 0:128] + grad_token[:, 128:256] + grad_token[:, 256:384]
                )
                r.near[h, :, 128:384] += grad_token[:, 384:640]
                token_low = grad_token.astype(BF)
                from_low = grad_from.astype(BF)
                grad_q = scale * (
                    nn(token_low, kv_all[m, window, k_cols]) + nn(from_low, state_kv[m, :, sk_cols])
                )
                r.dqkv[m, own_chunk(qi), :, head(h)] = grad_q.astype(BF)
                r.grad_kv[m, window, k_cols] += tn(token_low, q)
                r.grad_kv[m, window, v_cols] += tn(token.astype(BF), d)
                r.grad_state[m, :, sk_cols] += tn(from_low, q)
                r.grad_state[m, :, sv_cols] += tn(from_state.astype(BF), d)

        return step

    def pass_on(m):
        r.early[m, :, 0:256] = (scale * r.grad_kv[m, 0:512, 0:256]).astype(BF)
        r.early[m, :, 256:512] = r.grad_kv[m, 0:512, 256:512].astype(BF)
        for h in range(2):
            low = jnp.concatenate(
                [
                    (scale * r.grad_state[m, :, h * 256 : h * 256 + TILE]).astype(BF),
                    r.grad_state[m, :, h * 256 + TILE : (h + 1) * 256].astype(BF),
                ],
                1,
            )
            r.grad_prior[m, :, head(h)] = nt(low, r.state_proj.ref[h]).astype(BF)
            part = tn(r.prior.ref[m, :, head(h)], low)
            r.g_proj[h] = part if m == 0 else r.g_proj[h] + part
        there[m].start()
        shifts[m].start()

    def scan(m):
        def step(t, grad):
            b = count - 1 - t
            rows = tile_of(b, 16)
            r.held[m, rows] = grad.astype(BF)
            u = r.across.ref[m, rows].astype(F32)
            forget = jax.nn.sigmoid(r.bias[...] + r.slope[...] * u)
            moved = r.moved[m, rows].astype(F32)
            return r.keeps.ref[b, m : m + 1] * (moved + forget * grad)

        lax.fori_loop(0, count, step, jnp.zeros((16, 256), F32))

    def bucket_sums():
        row = lax.broadcasted_iota(jnp.int32, (TILE, TILE), 0)
        col = lax.broadcasted_iota(jnp.int32, (TILE, TILE), 1)
        distance = [row - col + TILE, row - col]

        def per_head(h):
            for t in range(BUCKETS):
                total = jnp.zeros((1, TILE), F32)
                for part in range(2):
                    d = distance[part]
                    inside = d >= STARTS[t]
                    if t + 1 < BUCKETS:
                        inside = inside & (d < STARTS[t + 1])
                    values = r.near[h, :, TILE * (part + 1) : TILE * (part + 2)]
                    total = total + jnp.sum(
                        jnp.where(inside, values, 0.0), axis=0, keepdims=True
                    )
                if t + 1 == BUCKETS:
                    total = total + jnp.sum(r.near[h, :, 0:TILE], axis=0, keepdims=True)
                r.sums[t : t + 1] = total
            r.g_rel[h] = lax.dot_general(
                jnp.ones((8, TILE), F32),
                r.sums[...],
                (((1,), (1,)), ((), ())),
                precision=lax.Precision.HIGHEST,
                preferred_element_type=F32,
            )

        loop(2, per_head)

    def update_tile(m):
        def step(t):
            rows = tile_of(t)
            for h in range(2):
                cols, k_cols, v_cols = head(h), head(h, base=256), head(h, base=512)
                grad = r.grad_after[m, rows, cols].astype(F32)
                u = r.update.ref[m, rows, cols]
                inverse = inverse_rms(u)
                unit = u * inverse
                forget = jax.nn.sigmoid(r.bias[:, cols] + r.slope[:, cols] * unit)
                gate = grad * (r.prior.ref[m, rows, cols].astype(F32) - unit)
                gate = gate * forget * (1.0 - forget)
                r.g_bias[:, cols] += jnp.sum(gate, axis=0, keepdims=True)
                r.g_scale[:, cols] += jnp.sum(gate * unit, axis=0, keepdims=True)
                grad_unit = grad * (1.0 - forget) + gate * r.slope[:, cols]
                inner = jnp.mean(grad_unit * unit, axis=-1, keepdims=True)
                low = (inverse * (grad_unit - unit * inner)).astype(BF)
                q = r.state_query.ref[rows, cols]
                probs = jnp.exp(nt(q, qkv[m, :, k_cols]) * scale - stats[m, rows, h : h + 1])
                grad_probs = nt(low, qkv[m, :, v_cols])
                delta = jnp.sum(probs * grad_probs, axis=-1, keepdims=True)
                grad_scores = (probs * (grad_probs - delta)).astype(BF)
                r.g_query[rows, cols] += scale * nn(grad_scores, qkv[m, :, k_cols])
                r.grad_kv[m, 512:1024, cols] += tn(grad_scores, q)
                r.grad_kv[m, 512:1024, head(h, base=256)] += tn(probs.astype(BF), low)

        return step

    def finish_rows(m):
        def step(t):
            rows = tile_of(t)
            full = r.grad_kv[m, pl.ds(pl.multiple_of(512 + t * TILE, TILE), TILE)]
            extra = r.later[m, rows].astype(F32)
            at = own_chunk(t)
            r.dqkv[m, at, :, 256:512] = (scale * full[:, 0:256] + extra[:, 0:256]).astype(BF)
            r.dqkv[m, at, :, 512:768] = (full[:, 256:512] + extra[:, 256:512]).astype(BF)

        return step

    ones = jnp.ones((8, 256), BF)

    def gain_row(part, p, rows):
        product = part * r.w.ref[p, rows].astype(F32)
        high = product.astype(BF)
        low = (product - high.astype(F32)).astype(BF)
        return (nt(ones, high) + nt(ones, low))[0:1]

    def weight_part(p, rows):
        whole, cols = r.whole.ref, slice(p * 256, (p + 1) * 256)
        part = tn(whole[0, :, :, rows].reshape(512, 256), r.dqkv[0, :, :, cols].reshape(512, 256))
        return part + tn(
            whole[1, :, :, rows].reshape(512, 256), r.dqkv[1, :, :, cols].reshape(512, 256)
        )

    def early_weights(n):
        rows = tile_of(n, 256)
        part = tn(r.att_rel.ref[0].reshape(512, 256), gm[0][:, :, rows].reshape(512, 256))
        part = part + tn(r.att_rel.ref[1].reshape(512, 256), gm[1][:, :, rows].reshape(512, 256))
        r.parts_a[rows, 256:512] = part.astype(BF)
        part = weight_part(0, rows)
        r.parts_a[rows, 0:256] = part.astype(BF)
        r.small[pl.ds(n, 1)] = gain_row(part, 0, rows)

    def end_terms(m):
        def columns(n):
            cols = tile_of(n, 256)
            part = nt(r.dqkv[m, :, :, 0:256].reshape(512, 256), r.w.ref[0, cols])
            for p in (1, 2):
                some = r.dqkv[m, :, :, p * 256 : (p + 1) * 256].reshape(512, 256)
                part = part + nt(some, r.w.ref[p, cols])
            part = part.astype(BF)
            split_rows(branch, m, cols, part)

        loop(4, columns)

    def late_weights(n):
        rows = tile_of(n, 256)
        total = r.small[pl.ds(n, 1)]
        for p in (1, 2):
            part = weight_part(p, rows)
            r.parts_b[rows, (p - 1) * 256 : p * 256] = part.astype(BF)
            total = total + gain_row(part, p, rows)
        r.small[pl.ds(n, 1)] = total / r.attn_gain[:, rows]

    def end_rows(m):
        grad_normed = ends[m].finish()
        rows = r.x.ref[m].astype(F32)
        inverse = inverse_rms(rows)
        unit = rows * inverse
        scaled = grad_normed * r.attn_gain[...]
        inner = jnp.mean(scaled * unit, axis=-1, keepdims=True)
        r.grad_x.ref[m] = r.grad_middle[m] + inverse * (scaled - unit * inner)

    def share(i):
        k, c = i // 2 + 1, i % 2
        slot = (3 - k) * 2 + core
        return remote(
            r.parts_b.at[768:784, 512:768],
            r.others.at[slot],
            r.s3.at[i],
            r.r3.at[slot],
            others[i],
        )

    def got(i):
        return remote(
            r.parts_b.at[768:784, 512:768], r.others.at[i], r.s3.at[i], r.r3.at[i], others[i]
        )

    def add_gains():
        for i in range(6):
            got(i).wait_recv()
        total = r.others[0].astype(F32)
        for i in range(1, 6):
            total = total + r.others[i].astype(F32)
        row = lax.broadcasted_iota(jnp.int32, (16, 256), 0)
        total = jnp.where(row < 8, total, 0.0) * core.astype(F32)
        at = slice(256, 272), slice(512, 768)
        r.half_b[at] = (r.half_b[at].astype(F32) + total).astype(BF)

    core_a = CoreSum(plane, r.parts_a, r.half_a)
    sum_a = PlaneReduce(plane, r.half_a, r.total_a, r.a_mid, r.a_into, r.a_quarter, r.a_small)
    all_a = PlaneGather(plane, r.total_a)
    core_b = CoreSum(plane, r.parts_b, r.half_b)
    sum_b = PlaneReduce(plane, r.half_b, r.total_b, r.b_mid, r.b_into, r.b_quarter, r.b_small)
    all_b = PlaneGather(plane, r.total_b)

    attention_rows(0)
    fourth.relay()
    for part in (r.qkv, r.kv_all, r.state_kv, r.stats, r.table):
        part.get()
    loop(4, attend(0), 1, mlp_sum.advance)
    r.prior.get()
    r.state_proj.get()
    pass_on(0)
    mlp_sum.advance()
    fourth.finish()
    attention_rows(1)
    r.branch.get()
    outs[0].start()

    def second_stage():
        mlp_sum.advance()
        mlp_all.advance()

        outs[0].relay()
        outs[1].start()

    loop(4, attend(1), 1, second_stage)
    pass_on(1)
    mlp_all.advance()
    outs[1].relay()
    r.across.get()
    r.keeps.get()
    there[0].finish()
    scan(0)
    back[0].start()
    mlp_all.advance()
    r.att_rel.get()
    r.w.get()
    r.whole.get()
    loop(4, early_weights)
    core_a.start()
    there[1].finish()
    scan(1)
    back[1].start()
    mlp_all.advance()
    bucket_sums()
    core_a.finish()
    r.middle.get()
    for m in both:
        r.out.ref[m] = r.middle.ref[m] + outs[m].finish()
    r.out.put()
    r.update.get()
    r.state_query.get()
    for m in both:
        outs[m].close()
    back[0].finish()
    loop(4, update_tile(0))
    shifts[0].wait_recv()
    loop(4, finish_rows(0))
    end_terms(0)
    ends[0].start()
    mlp_all.advance()
    back[1].finish()
    sum_a.advance()
    loop(4, update_tile(1))
    sum_a.advance()
    shifts[1].wait_recv()
    loop(4, finish_rows(1))
    ends[0].relay()
    sum_a.advance()
    loop(4, late_weights)
    for n in range(4):
        r.small[4 + n : 5 + n] = r.g_mlp_gain[:, n * 256 : (n + 1) * 256]
    r.small[8:9] = r.g_bias[...]
    r.small[9:10] = r.g_scale[...]
    r.small[10:11] = r.g_rel[0, 0:1]
    r.small[11:12] = r.g_rel[1, 0:1]
    r.small[12:16] = jnp.zeros((4, 256), F32)
    r.parts_b[0:512, 512:768] = r.g_query[...].astype(BF)
    r.parts_b[512:768, 512:768] = r.g_proj[...].reshape(256, 256).astype(BF)
    r.parts_b[768:784, 512:768] = r.small[...].astype(BF)
    r.parts_b[784:1024, 512:768] = jnp.zeros((240, 256), BF)
    core_b.start()
    for i in range(6):
        share(i).start()
    sum_a.advance()
    all_a.advance()
    end_terms(1)
    ends[1].start()
    core_b.finish()
    add_gains()
    sum_b.advance()
    all_a.advance()
    r.x.get()
    end_rows(0)
    sum_b.advance()
    ends[1].relay()
    all_a.advance()
    sum_b.advance(2)
    all_b.advance()
    all_a.advance()
    all_b.advance()
    end_rows(1)
    r.grad_x.put()
    all_b.advance()
    all_a.advance()
    all_b.advance(2)
    for step in (mlp_sum, mlp_all, core_a, sum_a, all_a, core_b, sum_b, all_b, fourth):
        step.close()
    for i in range(6):
        share(i).wait_send()
    for m in both:
        ends[m].close()
        shifts[m].wait_send()
        there[m].close()
        back[m].close()


class Late:
    def __init__(self, source, ref, sem):
        self.ref = ref
        self.copy = pltpu.make_async_copy(source, ref, sem)
        self.copy.start()
        self.open = True

    def get(self):
        if self.open:
            self.copy.wait()
            self.open = False


class Early:
    def __init__(self, target, ref, sem):
        self.ref = ref
        self.copy = pltpu.make_async_copy(ref, target, sem)
        self.sent = False

    def put(self):
        self.copy.start()
        self.sent = True


def call(kernel, name, number, now, late, small, outs, early, scratch, semaphores):
    anywhere = pl.BlockSpec(memory_space=pl.ANY)
    in_names = list(now) + list(small) + list(late)
    out_names = list(outs) + list(early)
    own = [a.shape for a in late.values()], [a.dtype for a in late.values()]
    buffers = list(zip(*own)) + list(early.values()) + list(scratch.values())

    def run(*refs):
        n, o = len(in_names), len(out_names)
        r = types.SimpleNamespace()
        held = refs[n + o : n + o + len(buffers)]
        rest = refs[n + o + len(buffers) :]
        fetch, store = rest[0], rest[1]
        for key, ref in zip(in_names[: len(now) + len(small)], refs):
            setattr(r, key, ref)
        for i, key in enumerate(late):
            setattr(r, key, Late(refs[len(now) + len(small) + i], held[i], fetch.at[i]))
        for key, ref in zip(outs, refs[n:]):
            setattr(r, key, ref)
        stores = []
        for i, key in enumerate(early):
            result = Early(refs[n + len(outs) + i], held[len(late) + i], store.at[i])
            setattr(r, key, result)
            stores.append(result)
        for key, ref in zip(scratch, held[len(late) + len(early) :]):
            setattr(r, key, ref)
        for key, ref in zip(semaphores, rest[2:]):
            setattr(r, key, ref)
        kernel(r)
        for result in stores:
            if not result.sent:
                result.put()
            result.copy.wait()

    shapes = list(outs.values()) + list(early.values())
    results = pl.pallas_call(
        run,
        out_shape=tuple(jax.ShapeDtypeStruct(shape, kind) for shape, kind in shapes),
        in_specs=[VMEM] * len(now) + [SMEM] * len(small) + [anywhere] * len(late),
        out_specs=tuple([VMEM] * len(outs) + [anywhere] * len(early)),
        scratch_shapes=[pltpu.VMEM(shape, kind) for shape, kind in buffers]
        + [sems(max(1, len(late))), sems(max(1, len(early)))]
        + list(semaphores.values()),
        compiler_params=pltpu.CompilerParams(
            collective_id=number, has_side_effects=True, vmem_limit_bytes=LIMIT
        ),
        name=name,
    )(*now.values(), *small.values(), *late.values())
    return dict(zip(out_names, results))


def finish_kernel(total_a, total_b, g_mlp, out, grad_x, state, *refs):
    results, (wide, low, some_a, some_b, rows_in, states_in, fetch, store) = refs[:14], refs[14:]
    places = [rows_in.at[0], rows_in.at[1], states_in]
    taken = [
        pltpu.make_async_copy(a, b, fetch.at[12 + i])
        for i, (a, b) in enumerate(zip((out, grad_x, state), places))
    ]
    passed = [
        pltpu.make_async_copy(a, b, store.at[i])
        for i, (a, b) in enumerate(zip(places, results[:3]))
    ]
    g_up, g_down, g_qkv, g_out, g_query, g_proj = results[3:9]
    attn_gain, mlp_gain, bias, slope, rel = results[9:]
    loads = []
    for n in range(4):
        rows = slice(n * 256, (n + 1) * 256)
        loads.append(
            [
                pltpu.make_async_copy(a.at[rows], b.at[rows], fetch.at[3 * n + i])
                for i, (a, b) in enumerate(((g_mlp, low), (total_a, some_a), (total_b, some_b)))
            ]
        )
    for copy in sum(loads, []) + taken:
        copy.start()
    stores = []

    def put(value, at, target):
        wide[at] = value.astype(F32)
        copy = pltpu.make_async_copy(wide.at[at], target, store.at[3 + len(stores)])
        copy.start()
        stores.append(copy)

    for n in range(4):
        rows = slice(n * 256, (n + 1) * 256)
        for copy in loads[n]:
            copy.wait()
        put(low[rows, 0:1024], (rows, slice(0, 1024)), g_up.at[rows])
        put(low[rows, 1024:2048], (rows, slice(1024, 2048)), g_down.at[rows])
        put(some_a[rows, 0:256], (rows, slice(2048, 2304)), g_qkv.at[0, rows])
        put(some_b[rows, 0:256], (rows, slice(2304, 2560)), g_qkv.at[1, rows])
        put(some_b[rows, 256:512], (rows, slice(2560, 2816)), g_qkv.at[2, rows])
        put(some_a[rows, 256:512], (rows, slice(2816, 3072)), g_out.at[:, rows])
    put(some_b[0:512, 512:768], (slice(0, 512), slice(3072, 3328)), g_query)
    put(some_b[512:768, 512:768], (slice(512, 768), slice(3072, 3328)), g_proj)
    for into, copy in zip(taken, passed):
        into.wait()
        copy.start()
    small = some_b[768:784, 512:768].astype(F32)
    attn_gain[...] = jnp.concatenate([small[n : n + 1] for n in range(4)], 1)
    mlp_gain[...] = jnp.concatenate([small[n : n + 1] for n in range(4, 8)], 1)
    bias[...] = small[8:9]
    slope[...] = small[9:10]
    rel[...] = small[10:12, 0:BUCKETS]
    for copy in stores + passed:
        copy.wait()


def sems(*shape):
    return pltpu.SemaphoreType.DMA(shape)


def body(
    tokens_in,
    grad_out,
    flags,
    attn_gain,
    mlp_gain,
    w_qkv,
    w_out,
    rel_bias,
    state_query,
    state_proj,
    forget_bias,
    forget_scale,
    w_up,
    w_down,
):
    micros, rows, width = tokens_in.shape
    block = rows * 4
    local = w_qkv.shape[2]
    heads = rel_bias.shape[1]
    states = state_query.shape[0]
    buckets = rel_bias.shape[0]
    count = lax.axis_size("blk")
    w = jnp.transpose(w_qkv, (1, 0, 2))
    small = dict(flags=jnp.transpose(flags))
    whole_shape = ((micros, 4, rows, width), BF)
    state_low = ((micros, states, local), BF)
    state_wide = ((micros, states, local), F32)
    rows_wide = ((micros, rows, width), F32)
    mlp_width = w_up.shape[1] + w_down.shape[1]
    exchange = dict(
        s0=sems(2),
        r0=sems(2),
        s1=sems(2, count),
        r1=sems(2, count),
        s2=sems(2, count),
        r2=sems(2, count),
        local=sems(4),
    )
    gates = dict(bias=forget_bias[None], slope=forget_scale[None])
    f = call(
        forward_kernel,
        "forward",
        1,
        dict(
            x=tokens_in,
            attn_gain=attn_gain[None],
            mlp_gain=mlp_gain[None],
            **gates,
        ),
        dict(
            w=w,
            state_query=state_query,
            g=grad_out,
            state_proj=state_proj,
            w_out=w_out,
            w_up=w_up,
            w_down=w_down,
        ),
        dict(rel=jnp.transpose(rel_bias), **small),
        dict(
            grad_middle=rows_wide,
            gm0=((4, rows, width), BF),
            half=((512, mlp_width), BF),
            g_gain=((1, width), F32),
        ),
        dict(
            whole=whole_shape,
            qkv=((micros, block, 3 * local), BF),
            kv_all=((micros, 2 * block, 2 * local), BF),
            state_kv=((micros, states, 2 * local), BF),
            prior=state_low,
            across=state_low,
            keeps=((count, 8, local), F32),
            update=state_wide,
            stats=((micros, block, TILE), F32),
            table=((heads, TILE, 5 * TILE), F32),
            state_after=state_wide,
            att_rel=((micros, 4, rows, local), BF),
            middle=rows_wide,
            branch=whole_shape,
        ),
        dict(
            whole_grad=whole_shape,
            own_keep=((8, local), F32),
            unit_low=state_low,
            held=state_low,
            terms=whole_shape,
            whole_mlp=whole_shape,
            active=((micros, block, w_up.shape[1]), BF),
            grad_hidden=((micros, block, w_up.shape[1]), BF),
            mids=((4, 4, rows // 2, width), BF),
            intos=((4, 2, rows, width), BF),
            parts=((width, mlp_width), BF),
        ),
        dict(send=sems(80), recv=sems(80), s3=sems(count), r3=sems(count), **exchange),
    )
    b = call(
        backward_kernel,
        "backward",
        2,
        dict(
            gm0=f["gm0"],
            grad_middle=f["grad_middle"],
            w_out=w_out,
            half=f["half"],
            attn_gain=attn_gain[None],
            g_mlp_gain=f["g_gain"],
            **gates,
        ),
        dict(
            qkv=f["qkv"],
            kv_all=f["kv_all"],
            state_kv=f["state_kv"],
            stats=f["stats"],
            table=f["table"],
            branch=f["branch"],
            prior=f["prior"],
            state_proj=state_proj,
            across=f["across"],
            keeps=f["keeps"],
            att_rel=f["att_rel"],
            middle=f["middle"],
            update=f["update"],
            state_query=state_query,
            w=w,
            whole=f["whole"],
            x=tokens_in,
        ),
        small,
        dict(
            total_mlp=((width, mlp_width), BF),
            total_a=((width, 512), BF),
            total_b=((width, 768), BF),
        ),
        dict(out=rows_wide, grad_x=rows_wide),
        dict(
            dqkv=((micros, 4, rows, 3 * local), BF),
            g_query=((states, local), F32),
            g_proj=(state_proj.shape, F32),
            g_rel=((heads, 8, local), F32),
            g_bias=((1, local), F32),
            g_scale=((1, local), F32),
            grad_att=((micros, block, local), BF),
            grad_kv=((micros, 2 * block, 2 * local), F32),
            grad_state=((micros, states, 2 * local), F32),
            early=((micros, block, 2 * local), BF),
            later=((micros, block, 2 * local), BF),
            grad_prior=state_low,
            moved=state_low,
            held=state_low,
            grad_after=state_low,
            near=((heads, TILE, 3 * TILE), F32),
            sums=((local, TILE), F32),
            mids=((4, 4, rows // 2, width), BF),
            intos=((4, 2, rows, width), BF),
            others=((6, 16, local), BF),
            small=((16, local), F32),
            gm1=((4, rows, width), BF),
            parts_a=((width, 512), BF),
            half_a=((512, 512), BF),
            parts_b=((width, 768), BF),
            half_b=((512, 768), BF),
            **reduce_scratch("mlp_", mlp_width),
            **reduce_scratch("a_", 512),
            **reduce_scratch("b_", 768),
        ),
        dict(send=sems(150), recv=sems(150), s3=sems(6), r3=sems(6), **exchange),
    )
    results = [
        rows_wide[0],
        rows_wide[0],
        state_wide[0],
        w_up.shape,
        w_down.shape,
        w.shape,
        w_out.shape,
        state_query.shape,
        (heads * state_proj.shape[1], local),
        (1, width),
        (1, width),
        (1, local),
        (1, local),
        (heads, buckets),
    ]
    anywhere = pl.BlockSpec(memory_space=pl.ANY)
    values = pl.pallas_call(
        finish_kernel,
        out_shape=tuple(jax.ShapeDtypeStruct(shape, F32) for shape in results),
        in_specs=[anywhere] * 6,
        out_specs=tuple([anywhere] * 9 + [VMEM] * 5),
        scratch_shapes=[
            pltpu.VMEM((width, 3328), F32),
            pltpu.VMEM((width, mlp_width), BF),
            pltpu.VMEM((width, 512), BF),
            pltpu.VMEM((width, 768), BF),
            pltpu.VMEM((2,) + rows_wide[0], F32),
            pltpu.VMEM(state_wide[0], F32),
            sems(15),
            sems(32),
        ],
        compiler_params=pltpu.CompilerParams(vmem_limit_bytes=LIMIT),
        name="finish",
    )(b["total_a"], b["total_b"], b["total_mlp"], b["out"], b["grad_x"], f["state_after"])
    out, grad_x, state_after, g_up, g_down, g_qkv, g_out, g_query, g_proj = values[:9]
    g_attn_gain, g_mlp_gain, g_bias, g_scale, g_rel = values[9:]
    return (
        out,
        grad_x,
        state_after[:, None],
        g_attn_gain[0],
        g_mlp_gain[0],
        jnp.transpose(g_qkv, (1, 0, 2)),
        g_out,
        jnp.transpose(g_rel),
        g_query,
        g_proj.reshape(state_proj.shape),
        g_bias[0],
        g_scale[0],
        g_up,
        g_down,
    )


def solution(mesh):
    return jax.shard_map(
        body,
        mesh=mesh,
        in_specs=(
            P(None, ("blk", "head"), None),
            P(None, ("blk", "head"), None),
            P(None, "blk"),
            P(),
            P(),
            P(None, None, "head"),
            P("head", None),
            P(None, "head"),
            P(None, "head"),
            P("head", None, None),
            P("head"),
            P("head"),
            P(None, "head"),
            P("head", None),
        ),
        out_specs=(
            P(None, ("blk", "head"), None),
            P(None, ("blk", "head"), None),
            P(None, "blk", None, "head"),
            P(),
            P(),
            P(None, None, "head"),
            P("head", None),
            P(None, "head"),
            P(None, "head"),
            P("head", None, None),
            P("head"),
            P("head"),
            P(None, "head"),
            P("head", None),
        ),
        check_vma=False,
    )
```

```python
import math
import types

import jax
import jax.numpy as jnp
from jax import lax
from jax.experimental import pallas as pl
from jax.experimental.pallas import tpu as pltpu
from jax.sharding import PartitionSpec as P

BUCKETS = 32
MAXDIST = 128
EPSILON = 1e-06
MASKED = -1e30
TILE = 128
MESH = pl.DeviceIdType.MESH
BF = jnp.bfloat16
F32 = jnp.float32
VMEM = pl.BlockSpec(memory_space=pltpu.VMEM)
SMEM = pl.BlockSpec(memory_space=pltpu.SMEM)
LIMIT = 60 * 2**20
ROOT = math.sqrt(2.0 / math.pi)
CUBIC = 0.044715


def bucket_starts():
    exact = BUCKETS // 2
    levels = [
        int(math.ceil(exact * (MAXDIST / exact) ** (t / (BUCKETS - exact))))
        for t in range(1, BUCKETS - exact)
    ]
    return list(range(exact + 1)) + levels


STARTS = bucket_starts()


def nn(a, b):
    return lax.dot_general(a, b, (((1,), (0,)), ((), ())), preferred_element_type=F32)


def nt(a, b):
    return lax.dot_general(a, b, (((1,), (1,)), ((), ())), preferred_element_type=F32)


def tn(a, b):
    return lax.dot_general(a, b, (((0,), (0,)), ((), ())), preferred_element_type=F32)


def inverse_rms(values):
    return lax.rsqrt(jnp.mean(values * values, axis=-1, keepdims=True) + EPSILON)


def tile_of(index, size=TILE):
    return pl.ds(pl.multiple_of(index * size, size), size)


def loop(count, step, after=None, action=None):
    def run(i, c):
        step(i)
        return c

    if after is not None:
        lax.fori_loop(0, after + 1, run, 0)
        action()
    lax.fori_loop(0 if after is None else after + 1, count, run, 0)


def remote(src, dst, send_sem, recv_sem, device):
    return pltpu.make_async_remote_copy(
        src_ref=src,
        dst_ref=dst,
        send_sem=send_sem,
        recv_sem=recv_sem,
        device_id=device,
        device_id_type=MESH,
    )


class Links:
    def __init__(self, send, recv):
        self.send, self.recv, self.used = send, recv, 0

    def go(self, src, dst, device):
        copy = remote(src, dst, self.send.at[self.used], self.recv.at[self.used], device)
        self.used += 1
        copy.start()
        return copy


class Ring:
    def __init__(self, links, me, device):
        self.links, self.me = links, me
        self.right = device(lax.rem(me + 1, 4))
        self.left = device(lax.rem(me + 3, 4))
        self.opposite = device(lax.rem(me + 2, 4))

    def go(self, src, dst, peer):
        return self.links.go(src, dst, peer)

    def greet(self):
        barrier = pltpu.get_barrier_semaphore()
        for peer in (self.right, self.left):
            pl.semaphore_signal(barrier, inc=1, device_id=peer, device_id_type=MESH)
        return 2

    def chunk(self, k):
        return lax.rem(self.me + k, 4)

    def row_chunk(self, k):
        return tile_of(self.chunk(k))


def head_ring(links):
    return Ring(links, lax.axis_index("head"), lambda i: {"head": i})


def by_rows(buf):
    half = buf.shape[1] // 2

    def piece(k, part=None, offset=0):
        return buf.at[k] if part is None else buf.at[k, part * half : (part + 1) * half]

    return piece


def by_columns(buf, base, rows, chunk):
    half = buf.shape[1] // 2
    starts = [pl.multiple_of(base + chunk(k) * rows, rows) for k in range(4)]

    def piece(k, part=None, offset=0):
        at = pl.ds(starts[(k + offset) % 4], rows)
        return buf.at[at] if part is None else buf.at[at, part * half : (part + 1) * half]

    return piece


class Gather:
    def __init__(self, ring, piece):
        self.ring, self.piece = ring, piece

    def start(self):
        r, p = self.ring, self.piece
        self.a0 = r.go(p(0, 0), p(3, 0, 1), r.right)
        self.b0 = r.go(p(0, 1), p(1, 1, 3), r.left)
        self.a1 = r.go(p(0, 1), p(3, 1, 1), r.right)
        self.b1 = r.go(p(0, 0), p(1, 0, 3), r.left)

    def relay(self):
        r, p = self.ring, self.piece
        self.a0.wait_recv()
        self.a2 = r.go(p(3, 0), p(2, 0, 1), r.right)
        self.b0.wait_recv()
        self.b2 = r.go(p(1, 1), p(2, 1, 3), r.left)

    def finish(self):
        for copy in (self.a1, self.b1, self.a2, self.b2):
            copy.wait_recv()

    def close(self):
        for copy in (self.a0, self.b0, self.a1, self.b1, self.a2, self.b2):
            copy.wait_send()


class Reduce:
    def __init__(self, ring, terms, mid, into):
        self.ring, self.terms, self.mid, self.into = ring, terms, mid, into
        if mid.shape[1] == into.shape[1]:
            half = into.shape[2] // 2
            self.place = lambda i, part: into.at[i, :, part * half : (part + 1) * half]
        else:
            half = into.shape[1] // 2
            self.place = lambda i, part: into.at[i, part * half : (part + 1) * half]

    def start(self):
        r, t = self.ring, self.terms
        self.a0 = r.go(t(2, 0), self.mid.at[0], r.right)
        self.b0 = r.go(t(2, 1), self.mid.at[1], r.left)
        self.a1 = r.go(t(1, 1), self.place(0, 1), r.right)
        self.b1 = r.go(t(3, 0), self.place(1, 0), r.left)

    def relay(self):
        r, t, mid = self.ring, self.terms, self.mid
        self.a0.wait_recv()
        mid[2] = (mid[0].astype(F32) + t(1, 0)[...].astype(F32)).astype(BF)
        self.a2 = r.go(mid.at[2], self.place(0, 0), r.right)
        self.b0.wait_recv()
        mid[3] = (mid[1].astype(F32) + t(3, 1)[...].astype(F32)).astype(BF)
        self.b2 = r.go(mid.at[3], self.place(1, 1), r.left)

    def finish(self):
        for copy in (self.a1, self.b1, self.a2, self.b2):
            copy.wait_recv()
        return (
            self.terms(0)[...].astype(F32)
            + self.into[0].astype(F32)
            + self.into[1].astype(F32)
        )

    def close(self):
        for copy in (self.a0, self.b0, self.a1, self.b1, self.a2, self.b2):
            copy.wait_send()


def block_device(x, z, c):
    return {"blk": (x * 4 + z) * 2 + c}


def block_place():
    place = lax.axis_index("blk")
    return place % 2, (place // 2) % 4, place // 8


class Plane:
    def __init__(self, links):
        c, z, x = block_place()
        self.links = links
        self.peer = block_device(x, z, 1 - c)
        rx = Ring(links, x, lambda i: block_device(i, z, c))
        rz = Ring(links, z, lambda i: block_device(x, i, c))
        self.rings = [rx, rz]
        self.first, self.second = (rx, rz), (rz, rx)
        self.base = c * 512
        self.own = pl.ds(pl.multiple_of(c * 512, 512), 512)
        self.away = pl.ds(pl.multiple_of((1 - c) * 512, 512), 512)
        self.top = [c * 512 + x * 64, c * 512 + 256 + z * 64]
        self.last = [
            pl.ds(pl.multiple_of(self.top[0] + z * 16, 16), 16),
            pl.ds(pl.multiple_of(self.top[1] + x * 16, 16), 16),
        ]

    def greet(self):
        barrier = pltpu.get_barrier_semaphore()
        pl.semaphore_signal(barrier, inc=1, device_id=self.peer, device_id_type=MESH)
        return 1 + sum(ring.greet() for ring in self.rings)


class Steps:
    def advance(self, steps=1):
        for _ in range(steps):
            if self.steps:
                self.steps.pop(0)()


class CoreSum:
    def __init__(self, plane, parts, half):
        self.plane, self.parts, self.half = plane, parts, half

    def start(self):
        plane = self.plane
        self.swap = plane.links.go(self.parts.at[plane.away], self.half, plane.peer)

    def finish(self):
        self.swap.wait_recv()

        def add(t):
            rows = tile_of(t, 64)
            own = pl.ds(pl.multiple_of(self.plane.base + t * 64, 64), 64)
            self.half[rows] = (
                self.parts[own].astype(F32) + self.half[rows].astype(F32)
            ).astype(BF)

        loop(8, add)

    def close(self):
        self.swap.wait_send()


class PlaneReduce(Steps):
    def __init__(self, plane, half, total, mid, into, quarter, small_into):
        self.plane, self.half, self.total, self.quarter = plane, half, total, quarter
        first, second = plane.first, plane.second
        self.reduce1 = [
            Reduce(first[i], by_columns(half, i * 256, 64, first[i].chunk), mid.at[i], into.at[i])
            for i in range(2)
        ]
        self.reduce2 = [
            ReduceDirect(
                second[i], by_columns(quarter.at[i], 0, 16, second[i].chunk), small_into.at[i]
            )
            for i in range(2)
        ]
        self.steps = [
            lambda: [r.start() for r in self.reduce1],
            lambda: [r.relay() for r in self.reduce1],
            self.start2,
            self.finish,
        ]

    def start2(self):
        for i, r in enumerate(self.reduce1):
            self.quarter[i] = r.finish().astype(BF)
            self.reduce2[i].start()

    def finish(self):
        for i, r in enumerate(self.reduce2):
            self.total[self.plane.last[i]] = r.finish().astype(BF)

    def close(self):
        for r in self.reduce1 + self.reduce2:
            r.close()


class PlaneGather(Steps):
    def __init__(self, plane, total):
        self.plane, self.total = plane, total
        first, second = plane.first, plane.second
        self.gather1 = [
            GatherDirect(second[i], by_columns(total, plane.top[i], 16, second[i].chunk))
            for i in range(2)
        ]
        self.gather2 = [
            Gather(first[i], by_columns(total, plane.base + i * 256, 64, first[i].chunk))
            for i in range(2)
        ]
        self.steps = [
            lambda: [g.start() for g in self.gather1],
            self.start2,
            lambda: [g.relay() for g in self.gather2],
            self.cores,
            lambda: self.swap.wait_recv(),
        ]

    def start2(self):
        for i, g in enumerate(self.gather1):
            g.finish()
            self.gather2[i].start()

    def cores(self):
        for g in self.gather2:
            g.finish()
        rows = self.total.at[self.plane.own]
        self.swap = self.plane.links.go(rows, rows, self.plane.peer)

    def close(self):
        self.swap.wait_send()
        for g in self.gather1 + self.gather2:
            g.close()


def reduce_scratch(name, width):
    return {
        name + "mid": ((2, 4, 64, width // 2), BF),
        name + "into": ((2, 2, 64, width), BF),
        name + "quarter": ((2, 64, width), BF),
        name + "small": ((2, 3, 16, width), BF),
    }


class GatherDirect:
    def __init__(self, ring, piece):
        self.ring, self.piece = ring, piece

    def start(self):
        r, p = self.ring, self.piece
        self.copies = [
            r.go(p(0), p(4 - k, None, k), peer)
            for k, peer in ((1, r.right), (3, r.left), (2, r.opposite))
        ]

    def finish(self):
        for copy in self.copies:
            copy.wait_recv()

    def close(self):
        for copy in self.copies:
            copy.wait_send()


class ReduceDirect:
    def __init__(self, ring, terms, into):
        self.ring, self.terms, self.into = ring, terms, into

    def start(self):
        r, t = self.ring, self.terms
        self.copies = [
            r.go(t(k), self.into.at[k - 1], peer)
            for k, peer in ((1, r.right), (3, r.left), (2, r.opposite))
        ]

    def finish(self):
        for copy in self.copies:
            copy.wait_recv()
        total = self.terms(0)[...].astype(F32)
        for k in range(3):
            total = total + self.into[k].astype(F32)
        return total

    def close(self):
        for copy in self.copies:
            copy.wait_send()


class Exchange:
    def __init__(self, source, target, send, recv, local):
        self.count = lax.axis_size("blk")
        self.place = lax.axis_index("blk")
        self.size = source.shape[0] // self.count
        self.source, self.target = source, target
        self.send, self.recv, self.local = send, recv, local

    def part(self, j):
        peer = lax.rem(self.place + j, self.count)
        return remote(
            self.source.at[tile_of(peer, self.size)],
            self.target.at[tile_of(self.place, self.size)],
            self.send.at[j],
            self.recv.at[j],
            {"blk": peer},
        )

    def own(self):
        rows = tile_of(self.place, self.size)
        return pltpu.make_async_copy(self.source.at[rows], self.target.at[rows], self.local)

    def start(self):
        loop(self.count - 1, lambda j: self.part(j + 1).start())
        self.own().start()

    def finish(self):
        self.own().wait()
        loop(self.count - 1, lambda j: self.part(j + 1).wait_recv())

    def close(self):
        loop(self.count - 1, lambda j: self.part(j + 1).wait_send())


def greet_blocks():
    barrier = pltpu.get_barrier_semaphore()
    count, place = lax.axis_size("blk"), lax.axis_index("blk")

    def greet(j):
        pl.semaphore_signal(
            barrier, inc=1, device_id={"blk": lax.rem(place + j + 1, count)}, device_id_type=MESH
        )

    loop(count - 1, greet)
    return count - 1


def closed_row(flag, qi):
    column = lax.broadcasted_iota(jnp.int32, (1, 5 * TILE), 1) + qi * TILE
    return jnp.where(column < 512, MASKED * flag.astype(F32), 0.0)


def head(h, size=TILE, base=0):
    return slice(base + h * size, base + (h + 1) * size)


def window_of(qi):
    return pl.ds(pl.multiple_of(qi * TILE, TILE), 5 * TILE)


def split_rows(target, m, cols, part):
    for k in range(4):
        target[m, k, :, cols] = part[k * TILE : (k + 1) * TILE]


def write_table(table, rel):
    row = lax.broadcasted_iota(jnp.int32, (TILE, TILE), 0)
    col = lax.broadcasted_iota(jnp.int32, (TILE, TILE), 1)

    def per_head(h):
        far = jnp.full((TILE, TILE), rel[h, BUCKETS - 1], F32)
        table[h, :, 0:128] = jnp.where(row < col, far, MASKED)
        table[h, :, 128:256] = far
        table[h, :, 256:384] = far
        for shift, at in ((TILE, 384), (0, 512)):
            distance = row - col + shift
            total = jnp.full((TILE, TILE), rel[h, 0], F32)
            for t in range(1, BUCKETS):
                total = jnp.where(distance >= STARTS[t], rel[h, t], total)
            table[h, :, at : at + TILE] = jnp.where(distance >= 0, total, MASKED)

    loop(2, per_head)


def forward_kernel(r):
    scale = TILE**-0.5
    links = Links(r.send, r.recv)
    ring = head_ring(links)
    plane = Plane(links)
    place, count = lax.axis_index("blk"), lax.axis_size("blk")
    both = range(2)

    def norm_rows(m):
        rows = r.x[m].astype(F32)
        r.whole.ref[m, 0] = (rows * inverse_rms(rows) * r.attn_gain[...]).astype(BF)

    norm_rows(0)
    for m in both:
        keep = 1.0 - r.flags[0, m].astype(F32)
        r.own_keep[m : m + 1] = jnp.full((1, 256), keep, F32)
    r.own_keep[2:8] = jnp.zeros((6, 256), F32)
    pl.semaphore_wait(pltpu.get_barrier_semaphore(), ring.greet() + greet_blocks())
    whole, qkv, kv_all = r.whole.ref, r.qkv.ref, r.kv_all.ref
    prior, across, keeps = r.prior.ref, r.across.ref, r.keeps.ref
    update, stats, state_kv = r.update.ref, r.stats.ref, r.state_kv.ref
    table, att_rel, middle, branch = r.table.ref, r.att_rel.ref, r.middle.ref, r.branch.ref
    gather_x = [Gather(ring, by_rows(whole.at[m])) for m in both]
    gather_g = [Gather(ring, by_rows(r.whole_grad.at[m])) for m in both]
    gather_x[0].start()
    norm_rows(1)

    def tell(j):
        peer = {"blk": lax.rem(place + j, count)}
        return remote(r.own_keep, keeps.at[place], r.s3.at[j], r.r3.at[j], peer)

    loop(count - 1, lambda j: tell(j + 1).start())
    keeps[place] = r.own_keep[...]
    write_table(table, r.rel)
    r.table.put()
    after = {"blk": lax.rem(place + 1, count)}
    shifts = [
        remote(qkv.at[m, :, 256:768], kv_all.at[m, 0:512], r.s0.at[m], r.r0.at[m], after)
        for m in both
    ]
    there = [
        Exchange(r.unit_low.at[m], across.at[m], r.s1.at[m], r.r1.at[m], r.local.at[m])
        for m in both
    ]
    back = [
        Exchange(r.held.at[m], prior.at[m], r.s2.at[m], r.r2.at[m], r.local.at[2 + m])
        for m in both
    ]

    def project(m):
        def columns(n):
            cols = tile_of(n, 256)
            part = nn(whole[m].reshape(512, 1024), r.w.ref[n]).astype(BF)
            for k in range(4):
                qkv[m, ring.row_chunk(k), cols] = part[k * TILE : (k + 1) * TILE]

        loop(3, columns)
        shifts[m].start()
        kv_all[m, 512:1024] = qkv[m, :, 256:768]

    def update_tile(m):
        def step(t):
            rows = tile_of(t)
            for h in range(2):
                scores = nt(r.state_query.ref[rows, head(h)], qkv[m, :, head(h, base=256)]) * scale
                top = jnp.max(scores, axis=-1, keepdims=True)
                raised = jnp.exp(scores - top)
                total = jnp.sum(raised, axis=-1, keepdims=True)
                stats[m, rows, h : h + 1] = top + jnp.log(total)
                u = nn(raised.astype(BF), qkv[m, :, head(h, base=512)]) / total
                update[m, rows, head(h)] = u
                r.unit_low[m, rows, head(h)] = (u * inverse_rms(u)).astype(BF)

        return step

    def scan(m):
        def step(b, state):
            rows = tile_of(b, 16)
            u = across[m, rows].astype(F32)
            forget = jax.nn.sigmoid(r.bias[...] + r.slope[...] * u)
            before = keeps[b, m : m + 1] * state
            r.held[m, rows] = before.astype(BF)
            return forget * before + (1.0 - forget) * u

        lax.fori_loop(0, count, step, jnp.zeros((16, 256), F32))

    def state(m):
        def step(t):
            rows = tile_of(t)
            before = prior[m, rows]
            for h in range(2):
                state_kv[m, rows, head(h, 256)] = nn(before[:, head(h)], r.state_proj.ref[h]).astype(BF)
                u = update[m, rows, head(h)]
                u = u * inverse_rms(u)
                forget = jax.nn.sigmoid(r.bias[:, head(h)] + r.slope[:, head(h)] * u)
                r.state_after.ref[m, rows, head(h)] = (
                    forget * before[:, head(h)].astype(F32) + (1.0 - forget) * u
                )

        return step

    def attend(m):
        def step(qi):
            rows, window = tile_of(qi), window_of(qi)
            shut = closed_row(r.flags[0, m], qi)
            for h in range(2):
                q = qkv[m, rows, head(h)]
                token = nt(q, kv_all[m, window, head(h)]) * scale + (table[h] + shut)
                from_state = nt(q, state_kv[m, :, h * 256 : h * 256 + TILE]) * scale
                top = jnp.maximum(
                    jnp.max(token, axis=-1, keepdims=True),
                    jnp.max(from_state, axis=-1, keepdims=True),
                )
                token = jnp.exp(token - top)
                from_state = jnp.exp(from_state - top)
                total = jnp.sum(token, axis=-1, keepdims=True) + jnp.sum(
                    from_state, axis=-1, keepdims=True
                )
                stats[m, rows, 2 + h : 3 + h] = top + jnp.log(total)
                out = nn(token.astype(BF), kv_all[m, window, head(h, base=256)]) + nn(
                    from_state.astype(BF), state_kv[m, :, h * 256 + TILE : (h + 1) * 256]
                )
                att_rel[m, lax.rem(qi + 4 - ring.me, 4), :, head(h)] = (out / total).astype(BF)

        return step

    first = [
        Reduce(ring, by_rows(r.terms.at[m]), r.mids.at[m], r.intos.at[m]) for m in both
    ]
    second = [Gather(ring, by_rows(r.whole_mlp.at[m])) for m in both]
    third = [
        Reduce(ring, by_rows(r.terms.at[m]), r.mids.at[2 + m], r.intos.at[2 + m]) for m in both
    ]
    fourth = Gather(ring, by_rows(r.gm0))

    def out_terms(m):
        def columns(n):
            cols = tile_of(n, 256)
            part = nn(att_rel[m].reshape(512, 256), r.w_out.ref[:, cols]).astype(BF)
            split_rows(r.terms, m, cols, part)

        loop(4, columns)

    def normalise(m):
        rows = r.x[m].astype(F32) + first[m].finish()
        middle[m] = rows
        r.whole_mlp[m, 0] = (rows * inverse_rms(rows) * r.mlp_gain[...]).astype(BF)

    def hidden(m):
        def columns(n):
            cols = tile_of(n, 256)
            value = nn(r.whole_mlp[m].reshape(512, 1024), r.w_up.ref[:, cols])
            grad_active = nt(r.whole_grad[m].reshape(512, 1024), r.w_down.ref[cols])
            square = value * value
            bent = jnp.tanh(ROOT * value * (1.0 + CUBIC * square))
            r.active[m, :, cols] = (0.5 * value * (1.0 + bent)).astype(BF)
            rise = 0.5 * (1.0 + bent) + 0.5 * value * (1.0 - bent * bent) * ROOT * (
                1.0 + 3.0 * CUBIC * square
            )
            r.grad_hidden[m, :, cols] = (grad_active * rise).astype(BF)

        return columns

    def grad_terms(m):
        def columns(n):
            cols = tile_of(n, 256)
            part = nt(r.grad_hidden[m], r.w_up.ref[cols]).astype(BF)
            split_rows(r.terms, m, cols, part)

        loop(4, columns)

    def branch_terms(m):
        def columns(n):
            cols = tile_of(n, 256)
            part = nn(r.active[m], r.w_down.ref[:, cols]).astype(BF)
            split_rows(branch, m, cols, part)

        loop(4, columns)

    def grad_rows(m):
        grad_normed = third[m].finish()
        rows = middle[m]
        inverse = inverse_rms(rows)
        unit = rows * inverse
        part = jnp.sum(grad_normed * unit, axis=0, keepdims=True)
        r.g_gain[...] = part if m == 0 else r.g_gain[...] + part
        scaled = grad_normed * r.mlp_gain[...]
        inner = jnp.mean(scaled * unit, axis=-1, keepdims=True)
        total = r.g.ref[m].astype(F32) + inverse * (scaled - unit * inner)
        r.grad_middle[m] = total
        if m == 0:
            r.gm0[0] = total.astype(BF)

    def up_rows(n):
        rows = tile_of(n, 256)
        total = tn(r.whole_mlp[0, :, :, rows].reshape(512, 256), r.grad_hidden[0])
        total = total + tn(r.whole_mlp[1, :, :, rows].reshape(512, 256), r.grad_hidden[1])
        r.parts[rows, 0:1024] = total.astype(BF)

    def down_rows(n):
        rows = tile_of(n, 256)
        total = tn(r.active[0, :, rows], r.whole_grad[0].reshape(512, 1024))
        total = total + tn(r.active[1, :, rows], r.whole_grad[1].reshape(512, 1024))
        r.parts[rows, 1024:2048] = total.astype(BF)

    cores = CoreSum(plane, r.parts, r.half.ref)

    gather_x[0].relay()
    gather_x[1].start()
    r.w.get()
    gather_x[0].finish()
    project(0)
    gather_x[1].relay()
    r.state_query.get()
    loop(4, update_tile(0))
    there[0].start()
    gather_x[1].finish()
    r.g.get()
    for m in both:
        r.whole_grad[m, 0] = r.g.ref[m]
    gather_g[0].start()
    project(1)
    r.whole.put()
    r.qkv.put()
    loop(4, update_tile(1))
    there[1].start()
    r.update.put()
    gather_g[0].relay()
    gather_g[1].start()
    loop(count - 1, lambda j: tell(j + 1).wait_recv())
    there[0].finish()
    scan(0)
    back[0].start()
    there[1].finish()
    scan(1)
    back[1].start()
    gather_g[1].relay()
    r.across.put()
    r.keeps.put()
    shifts[0].wait_recv()
    shifts[1].wait_recv()
    r.kv_all.put()
    r.state_proj.get()
    back[0].finish()
    loop(4, state(0))
    loop(4, attend(0))
    r.w_out.get()
    out_terms(0)
    first[0].start()
    back[1].finish()
    r.prior.put()
    loop(4, state(1))
    r.state_kv.put()
    r.state_after.put()
    loop(4, attend(1), 0, first[0].relay)
    r.stats.put()
    out_terms(1)
    r.att_rel.put()
    first[1].start()
    normalise(0)
    second[0].start()
    first[1].relay()
    second[0].relay()
    r.w_up.get()
    r.w_down.get()
    gather_g[0].finish()
    gather_g[1].finish()
    normalise(1)
    second[1].start()
    r.middle.put()
    second[0].finish()
    loop(4, hidden(0), 1, second[1].relay)
    first[0].close()
    grad_terms(0)
    third[0].start()
    second[1].finish()
    loop(4, hidden(1), 1, third[0].relay)
    first[1].close()
    grad_terms(1)
    third[1].start()
    loop(4, up_rows)
    grad_rows(0)
    fourth.start()
    third[1].relay()
    loop(4, down_rows)
    cores.start()
    fourth.relay()
    branch_terms(0)
    branch_terms(1)
    r.branch.put()
    cores.finish()
    r.half.put()
    grad_rows(1)
    fourth.finish()
    cores.close()
    fourth.close()
    for m in both:
        for step in (gather_x, gather_g, second, third):
            step[m].close()
        shifts[m].wait_send()
        there[m].close()
        back[m].close()
    loop(count - 1, lambda j: tell(j + 1).wait_send())


def backward_kernel(r):
    scale = TILE**-0.5
    links = Links(r.send, r.recv)
    ring = head_ring(links)
    plane = Plane(links)
    place, count = lax.axis_index("blk"), lax.axis_size("blk")
    both = range(2)
    gm = [r.gm0, r.gm1]
    r.gm1[0] = r.grad_middle[1].astype(BF)
    core = place % 2
    others = [
        {"head": ring.chunk(k), "blk": place - core + c} for k in range(1, 4) for c in range(2)
    ]
    barrier = pltpu.get_barrier_semaphore()
    for device in others:
        pl.semaphore_signal(barrier, inc=1, device_id=device, device_id_type=MESH)
    pl.semaphore_wait(barrier, len(others) + greet_blocks())
    fourth = Gather(ring, by_rows(r.gm1))
    fourth.start()
    mlp_sum = PlaneReduce(
        plane, r.half.ref, r.total_mlp.ref, r.mlp_mid, r.mlp_into, r.mlp_quarter, r.mlp_small
    )
    mlp_all = PlaneGather(plane, r.total_mlp.ref)
    qkv, kv_all, state_kv, stats = r.qkv.ref, r.kv_all.ref, r.state_kv.ref, r.stats.ref
    r.branch.get()
    branch = r.branch.ref
    outs = [Reduce(ring, by_rows(branch.at[m]), r.mids.at[m], r.intos.at[m]) for m in both]
    ends = [
        Reduce(ring, by_rows(branch.at[m]), r.mids.at[2 + m], r.intos.at[2 + m]) for m in both
    ]
    before = {"blk": lax.rem(place + count - 1, count)}
    shifts = [
        remote(r.early.at[m], r.later.at[m], r.s0.at[m], r.r0.at[m], before) for m in both
    ]
    there = [
        Exchange(r.grad_prior.at[m], r.moved.at[m], r.s1.at[m], r.r1.at[m], r.local.at[m])
        for m in both
    ]
    back = [
        Exchange(r.held.at[m], r.grad_after.at[m], r.s2.at[m], r.r2.at[m], r.local.at[2 + m])
        for m in both
    ]
    for ref in (r.near, r.sums, r.g_query, r.g_bias, r.g_scale, r.grad_kv, r.grad_state):
        ref[...] = jnp.zeros(ref.shape, F32)

    def own_chunk(qi):
        return lax.rem(qi + 4 - ring.me, 4)

    def attention_rows(m):
        part = nt(gm[m][...].reshape(512, 1024), r.w_out[...]).astype(BF)
        for k in range(4):
            r.grad_att[m, ring.row_chunk(k)] = part[k * TILE : (k + 1) * TILE]

    def attend(m):
        def step(qi):
            rows, window = tile_of(qi), window_of(qi)
            shut = closed_row(r.flags[0, m], qi)
            for h in range(2):
                k_cols, v_cols = head(h), head(h, base=256)
                sk_cols = slice(h * 256, h * 256 + TILE)
                sv_cols = slice(h * 256 + TILE, (h + 1) * 256)
                q = qkv[m, rows, head(h)]
                d = r.grad_att[m, rows, head(h)]
                level = stats[m, rows, 2 + h : 3 + h]
                token = jnp.exp(
                    nt(q, kv_all[m, window, k_cols]) * scale + (r.table.ref[h] + shut) - level
                )
                from_state = jnp.exp(nt(q, state_kv[m, :, sk_cols]) * scale - level)
                grad_token = nt(d, kv_all[m, window, v_cols])
                grad_from = nt(d, state_kv[m, :, sv_cols])
                delta = jnp.sum(token * grad_token, axis=-1, keepdims=True) + jnp.sum(
                    from_state * grad_from, axis=-1, keepdims=True
                )
                grad_token = token * (grad_token - delta)
                grad_from = from_state * (grad_from - delta)
                r.near[h, :, 0:128] += (
                    grad_token[:, 0:128] + grad_token[:, 128:256] + grad_token[:, 256:384]
                )
                r.near[h, :, 128:384] += grad_token[:, 384:640]
                token_low = grad_token.astype(BF)
                from_low = grad_from.astype(BF)
                grad_q = scale * (
                    nn(token_low, kv_all[m, window, k_cols]) + nn(from_low, state_kv[m, :, sk_cols])
                )
                r.dqkv[m, own_chunk(qi), :, head(h)] = grad_q.astype(BF)
                r.grad_kv[m, window, k_cols] += tn(token_low, q)
                r.grad_kv[m, window, v_cols] += tn(token.astype(BF), d)
                r.grad_state[m, :, sk_cols] += tn(from_low, q)
                r.grad_state[m, :, sv_cols] += tn(from_state.astype(BF), d)

        return step

    def pass_on(m):
        r.early[m, :, 0:256] = (scale * r.grad_kv[m, 0:512, 0:256]).astype(BF)
        r.early[m, :, 256:512] = r.grad_kv[m, 0:512, 256:512].astype(BF)
        for h in range(2):
            low = jnp.concatenate(
                [
                    (scale * r.grad_state[m, :, h * 256 : h * 256 + TILE]).astype(BF),
                    r.grad_state[m, :, h * 256 + TILE : (h + 1) * 256].astype(BF),
                ],
                1,
            )
            r.grad_prior[m, :, head(h)] = nt(low, r.state_proj.ref[h]).astype(BF)
            part = tn(r.prior.ref[m, :, head(h)], low)
            r.g_proj[h] = part if m == 0 else r.g_proj[h] + part
        there[m].start()
        shifts[m].start()

    def scan(m):
        def step(t, grad):
            b = count - 1 - t
            rows = tile_of(b, 16)
            r.held[m, rows] = grad.astype(BF)
            u = r.across.ref[m, rows].astype(F32)
            forget = jax.nn.sigmoid(r.bias[...] + r.slope[...] * u)
            moved = r.moved[m, rows].astype(F32)
            return r.keeps.ref[b, m : m + 1] * (moved + forget * grad)

        lax.fori_loop(0, count, step, jnp.zeros((16, 256), F32))

    def bucket_sums():
        row = lax.broadcasted_iota(jnp.int32, (TILE, TILE), 0)
        col = lax.broadcasted_iota(jnp.int32, (TILE, TILE), 1)
        distance = [row - col + TILE, row - col]

        def per_head(h):
            for t in range(BUCKETS):
                total = jnp.zeros((1, TILE), F32)
                for part in range(2):
                    d = distance[part]
                    inside = d >= STARTS[t]
                    if t + 1 < BUCKETS:
                        inside = inside & (d < STARTS[t + 1])
                    values = r.near[h, :, TILE * (part + 1) : TILE * (part + 2)]
                    total = total + jnp.sum(
                        jnp.where(inside, values, 0.0), axis=0, keepdims=True
                    )
                if t + 1 == BUCKETS:
                    total = total + jnp.sum(r.near[h, :, 0:TILE], axis=0, keepdims=True)
                r.sums[t : t + 1] = total
            r.g_rel[h] = lax.dot_general(
                jnp.ones((8, TILE), F32),
                r.sums[...],
                (((1,), (1,)), ((), ())),
                precision=lax.Precision.HIGHEST,
                preferred_element_type=F32,
            )

        loop(2, per_head)

    def update_tile(m):
        def step(t):
            rows = tile_of(t)
            for h in range(2):
                cols, k_cols, v_cols = head(h), head(h, base=256), head(h, base=512)
                grad = r.grad_after[m, rows, cols].astype(F32)
                u = r.update.ref[m, rows, cols]
                inverse = inverse_rms(u)
                unit = u * inverse
                forget = jax.nn.sigmoid(r.bias[:, cols] + r.slope[:, cols] * unit)
                gate = grad * (r.prior.ref[m, rows, cols].astype(F32) - unit)
                gate = gate * forget * (1.0 - forget)
                r.g_bias[:, cols] += jnp.sum(gate, axis=0, keepdims=True)
                r.g_scale[:, cols] += jnp.sum(gate * unit, axis=0, keepdims=True)
                grad_unit = grad * (1.0 - forget) + gate * r.slope[:, cols]
                inner = jnp.mean(grad_unit * unit, axis=-1, keepdims=True)
                low = (inverse * (grad_unit - unit * inner)).astype(BF)
                q = r.state_query.ref[rows, cols]
                probs = jnp.exp(nt(q, qkv[m, :, k_cols]) * scale - stats[m, rows, h : h + 1])
                grad_probs = nt(low, qkv[m, :, v_cols])
                delta = jnp.sum(probs * grad_probs, axis=-1, keepdims=True)
                grad_scores = (probs * (grad_probs - delta)).astype(BF)
                r.g_query[rows, cols] += scale * nn(grad_scores, qkv[m, :, k_cols])
                r.grad_kv[m, 512:1024, cols] += tn(grad_scores, q)
                r.grad_kv[m, 512:1024, head(h, base=256)] += tn(probs.astype(BF), low)

        return step

    def finish_rows(m):
        def step(t):
            rows = tile_of(t)
            full = r.grad_kv[m, pl.ds(pl.multiple_of(512 + t * TILE, TILE), TILE)]
            extra = r.later[m, rows].astype(F32)
            at = own_chunk(t)
            r.dqkv[m, at, :, 256:512] = (scale * full[:, 0:256] + extra[:, 0:256]).astype(BF)
            r.dqkv[m, at, :, 512:768] = (full[:, 256:512] + extra[:, 256:512]).astype(BF)

        return step

    ones = jnp.ones((8, 256), BF)

    def gain_row(part, p, rows):
        product = part * r.w.ref[p, rows].astype(F32)
        high = product.astype(BF)
        low = (product - high.astype(F32)).astype(BF)
        return (nt(ones, high) + nt(ones, low))[0:1]

    def weight_part(p, rows):
        whole, cols = r.whole.ref, slice(p * 256, (p + 1) * 256)
        part = tn(whole[0, :, :, rows].reshape(512, 256), r.dqkv[0, :, :, cols].reshape(512, 256))
        return part + tn(
            whole[1, :, :, rows].reshape(512, 256), r.dqkv[1, :, :, cols].reshape(512, 256)
        )

    def early_weights(n):
        rows = tile_of(n, 256)
        part = tn(r.att_rel.ref[0].reshape(512, 256), gm[0][:, :, rows].reshape(512, 256))
        part = part + tn(r.att_rel.ref[1].reshape(512, 256), gm[1][:, :, rows].reshape(512, 256))
        r.parts_a[rows, 256:512] = part.astype(BF)
        part = weight_part(0, rows)
        r.parts_a[rows, 0:256] = part.astype(BF)
        r.small[pl.ds(n, 1)] = gain_row(part, 0, rows)

    def end_terms(m):
        def columns(n):
            cols = tile_of(n, 256)
            part = nt(r.dqkv[m, :, :, 0:256].reshape(512, 256), r.w.ref[0, cols])
            for p in (1, 2):
                some = r.dqkv[m, :, :, p * 256 : (p + 1) * 256].reshape(512, 256)
                part = part + nt(some, r.w.ref[p, cols])
            part = part.astype(BF)
            split_rows(branch, m, cols, part)

        loop(4, columns)

    def late_weights(n):
        rows = tile_of(n, 256)
        total = r.small[pl.ds(n, 1)]
        for p in (1, 2):
            part = weight_part(p, rows)
            r.parts_b[rows, (p - 1) * 256 : p * 256] = part.astype(BF)
            total = total + gain_row(part, p, rows)
        r.small[pl.ds(n, 1)] = total / r.attn_gain[:, rows]

    def end_rows(m):
        grad_normed = ends[m].finish()
        rows = r.x.ref[m].astype(F32)
        inverse = inverse_rms(rows)
        unit = rows * inverse
        scaled = grad_normed * r.attn_gain[...]
        inner = jnp.mean(scaled * unit, axis=-1, keepdims=True)
        r.grad_x.ref[m] = r.grad_middle[m] + inverse * (scaled - unit * inner)

    def share(i):
        k, c = i // 2 + 1, i % 2
        slot = (3 - k) * 2 + core
        return remote(
            r.parts_b.at[768:784, 512:768],
            r.others.at[slot],
            r.s3.at[i],
            r.r3.at[slot],
            others[i],
        )

    def got(i):
        return remote(
            r.parts_b.at[768:784, 512:768], r.others.at[i], r.s3.at[i], r.r3.at[i], others[i]
        )

    def add_gains():
        for i in range(6):
            got(i).wait_recv()
        total = r.others[0].astype(F32)
        for i in range(1, 6):
            total = total + r.others[i].astype(F32)
        row = lax.broadcasted_iota(jnp.int32, (16, 256), 0)
        total = jnp.where(row < 8, total, 0.0) * core.astype(F32)
        at = slice(256, 272), slice(512, 768)
        r.half_b[at] = (r.half_b[at].astype(F32) + total).astype(BF)

    core_a = CoreSum(plane, r.parts_a, r.half_a)
    sum_a = PlaneReduce(plane, r.half_a, r.total_a, r.a_mid, r.a_into, r.a_quarter, r.a_small)
    all_a = PlaneGather(plane, r.total_a)
    core_b = CoreSum(plane, r.parts_b, r.half_b)
    sum_b = PlaneReduce(plane, r.half_b, r.total_b, r.b_mid, r.b_into, r.b_quarter, r.b_small)
    all_b = PlaneGather(plane, r.total_b)

    attention_rows(0)
    fourth.relay()
    for part in (r.half, r.qkv, r.kv_all, r.state_kv, r.stats, r.table):
        part.get()
    mlp_sum.advance()
    loop(4, attend(0))
    r.prior.get()
    r.state_proj.get()
    pass_on(0)
    mlp_sum.advance()
    fourth.finish()
    attention_rows(1)
    r.branch.get()
    outs[0].start()

    def between():
        mlp_sum.advance()
        outs[0].relay()
        outs[1].start()

    loop(4, attend(1), 1, between)
    pass_on(1)
    outs[1].relay()
    r.across.get()
    r.keeps.get()
    there[0].finish()
    scan(0)
    back[0].start()
    mlp_sum.advance()
    r.att_rel.get()
    r.w.get()
    r.whole.get()
    loop(4, early_weights)
    core_a.start()
    there[1].finish()
    scan(1)
    back[1].start()
    bucket_sums()
    core_a.finish()
    r.middle.get()
    for m in both:
        r.out.ref[m] = r.middle.ref[m] + outs[m].finish()
    r.out.put()
    r.update.get()
    r.state_query.get()
    for m in both:
        outs[m].close()
    back[0].finish()
    mlp_all.advance()
    loop(4, update_tile(0))
    shifts[0].wait_recv()
    loop(4, finish_rows(0))
    end_terms(0)
    ends[0].start()
    back[1].finish()
    mlp_all.advance()
    loop(4, update_tile(1))
    shifts[1].wait_recv()
    loop(4, finish_rows(1))
    ends[0].relay()
    mlp_all.advance()
    loop(4, late_weights)
    for n in range(4):
        r.small[4 + n : 5 + n] = r.g_mlp_gain[:, n * 256 : (n + 1) * 256]
    r.small[8:9] = r.g_bias[...]
    r.small[9:10] = r.g_scale[...]
    r.small[10:11] = r.g_rel[0, 0:1]
    r.small[11:12] = r.g_rel[1, 0:1]
    r.small[12:16] = jnp.zeros((4, 256), F32)
    r.parts_b[0:512, 512:768] = r.g_query[...].astype(BF)
    r.parts_b[512:768, 512:768] = r.g_proj[...].reshape(256, 256).astype(BF)
    r.parts_b[768:784, 512:768] = r.small[...].astype(BF)
    r.parts_b[784:1024, 512:768] = jnp.zeros((240, 256), BF)
    core_b.start()
    for i in range(6):
        share(i).start()
    sum_a.advance()
    mlp_all.advance()
    end_terms(1)
    ends[1].start()
    core_b.finish()
    add_gains()
    sum_b.advance()
    sum_a.advance()
    r.x.get()
    end_rows(0)
    sum_b.advance()
    ends[1].relay()
    mlp_all.advance()
    r.total_mlp.put()
    sum_a.advance()
    sum_b.advance()
    sum_a.advance()
    all_a.advance()
    sum_b.advance()
    all_b.advance()
    all_a.advance()
    all_b.advance()
    end_rows(1)
    r.grad_x.put()
    all_a.advance()
    all_b.advance()
    all_a.advance()
    all_b.advance()
    all_a.advance()
    all_b.advance()
    for step in (mlp_sum, mlp_all, core_a, sum_a, all_a, core_b, sum_b, all_b, fourth):
        step.close()
    for i in range(6):
        share(i).wait_send()
    for m in both:
        ends[m].close()
        shifts[m].wait_send()
        there[m].close()
        back[m].close()


class Late:
    def __init__(self, source, ref, sem):
        self.ref = ref
        self.copy = pltpu.make_async_copy(source, ref, sem)
        self.copy.start()
        self.open = True

    def get(self):
        if self.open:
            self.copy.wait()
            self.open = False


class Early:
    def __init__(self, target, ref, sem):
        self.ref = ref
        self.copy = pltpu.make_async_copy(ref, target, sem)
        self.sent = False

    def put(self):
        self.copy.start()
        self.sent = True


def call(kernel, name, number, now, late, small, outs, early, scratch, semaphores):
    anywhere = pl.BlockSpec(memory_space=pl.ANY)
    in_names = list(now) + list(small) + list(late)
    out_names = list(outs) + list(early)
    own = [a.shape for a in late.values()], [a.dtype for a in late.values()]
    buffers = list(zip(*own)) + list(early.values()) + list(scratch.values())

    def run(*refs):
        n, o = len(in_names), len(out_names)
        r = types.SimpleNamespace()
        held = refs[n + o : n + o + len(buffers)]
        rest = refs[n + o + len(buffers) :]
        fetch, store = rest[0], rest[1]
        for key, ref in zip(in_names[: len(now) + len(small)], refs):
            setattr(r, key, ref)
        for i, key in enumerate(late):
            setattr(r, key, Late(refs[len(now) + len(small) + i], held[i], fetch.at[i]))
        for key, ref in zip(outs, refs[n:]):
            setattr(r, key, ref)
        stores = []
        for i, key in enumerate(early):
            result = Early(refs[n + len(outs) + i], held[len(late) + i], store.at[i])
            setattr(r, key, result)
            stores.append(result)
        for key, ref in zip(scratch, held[len(late) + len(early) :]):
            setattr(r, key, ref)
        for key, ref in zip(semaphores, rest[2:]):
            setattr(r, key, ref)
        kernel(r)
        for result in stores:
            if not result.sent:
                result.put()
            result.copy.wait()

    shapes = list(outs.values()) + list(early.values())
    results = pl.pallas_call(
        run,
        out_shape=tuple(jax.ShapeDtypeStruct(shape, kind) for shape, kind in shapes),
        in_specs=[VMEM] * len(now) + [SMEM] * len(small) + [anywhere] * len(late),
        out_specs=tuple([VMEM] * len(outs) + [anywhere] * len(early)),
        scratch_shapes=[pltpu.VMEM(shape, kind) for shape, kind in buffers]
        + [sems(max(1, len(late))), sems(max(1, len(early)))]
        + list(semaphores.values()),
        compiler_params=pltpu.CompilerParams(
            collective_id=number, has_side_effects=True, vmem_limit_bytes=LIMIT
        ),
        name=name,
    )(*now.values(), *small.values(), *late.values())
    return dict(zip(out_names, results))


def finish_kernel(total_a, total_b, g_mlp, out, grad_x, state, *refs):
    results, (wide, low, some_a, some_b, rows_in, states_in, fetch, store) = refs[:14], refs[14:]
    places = [rows_in.at[0], rows_in.at[1], states_in]
    taken = [
        pltpu.make_async_copy(a, b, fetch.at[12 + i])
        for i, (a, b) in enumerate(zip((out, grad_x, state), places))
    ]
    passed = [
        pltpu.make_async_copy(a, b, store.at[i])
        for i, (a, b) in enumerate(zip(places, results[:3]))
    ]
    g_up, g_down, g_qkv, g_out, g_query, g_proj = results[3:9]
    attn_gain, mlp_gain, bias, slope, rel = results[9:]
    loads = []
    for n in range(4):
        rows = slice(n * 256, (n + 1) * 256)
        loads.append(
            [
                pltpu.make_async_copy(a.at[rows], b.at[rows], fetch.at[3 * n + i])
                for i, (a, b) in enumerate(((g_mlp, low), (total_a, some_a), (total_b, some_b)))
            ]
        )
    for copy in sum(loads, []) + taken:
        copy.start()
    stores = []

    def put(value, at, target):
        wide[at] = value.astype(F32)
        copy = pltpu.make_async_copy(wide.at[at], target, store.at[3 + len(stores)])
        copy.start()
        stores.append(copy)

    for n in range(4):
        rows = slice(n * 256, (n + 1) * 256)
        for copy in loads[n]:
            copy.wait()
        put(low[rows, 0:1024], (rows, slice(0, 1024)), g_up.at[rows])
        put(low[rows, 1024:2048], (rows, slice(1024, 2048)), g_down.at[rows])
        put(some_a[rows, 0:256], (rows, slice(2048, 2304)), g_qkv.at[0, rows])
        put(some_b[rows, 0:256], (rows, slice(2304, 2560)), g_qkv.at[1, rows])
        put(some_b[rows, 256:512], (rows, slice(2560, 2816)), g_qkv.at[2, rows])
        put(some_a[rows, 256:512], (rows, slice(2816, 3072)), g_out.at[:, rows])
    put(some_b[0:512, 512:768], (slice(0, 512), slice(3072, 3328)), g_query)
    put(some_b[512:768, 512:768], (slice(512, 768), slice(3072, 3328)), g_proj)
    for into, copy in zip(taken, passed):
        into.wait()
        copy.start()
    small = some_b[768:784, 512:768].astype(F32)
    attn_gain[...] = jnp.concatenate([small[n : n + 1] for n in range(4)], 1)
    mlp_gain[...] = jnp.concatenate([small[n : n + 1] for n in range(4, 8)], 1)
    bias[...] = small[8:9]
    slope[...] = small[9:10]
    rel[...] = small[10:12, 0:BUCKETS]
    for copy in stores + passed:
        copy.wait()


def sems(*shape):
    return pltpu.SemaphoreType.DMA(shape)


def body(
    tokens_in,
    grad_out,
    flags,
    attn_gain,
    mlp_gain,
    w_qkv,
    w_out,
    rel_bias,
    state_query,
    state_proj,
    forget_bias,
    forget_scale,
    w_up,
    w_down,
):
    micros, rows, width = tokens_in.shape
    block = rows * 4
    local = w_qkv.shape[2]
    heads = rel_bias.shape[1]
    states = state_query.shape[0]
    buckets = rel_bias.shape[0]
    count = lax.axis_size("blk")
    w = jnp.transpose(w_qkv, (1, 0, 2))
    small = dict(flags=jnp.transpose(flags))
    whole_shape = ((micros, 4, rows, width), BF)
    state_low = ((micros, states, local), BF)
    state_wide = ((micros, states, local), F32)
    rows_wide = ((micros, rows, width), F32)
    mlp_width = w_up.shape[1] + w_down.shape[1]
    exchange = dict(
        s0=sems(2),
        r0=sems(2),
        s1=sems(2, count),
        r1=sems(2, count),
        s2=sems(2, count),
        r2=sems(2, count),
        local=sems(4),
    )
    gates = dict(bias=forget_bias[None], slope=forget_scale[None])
    f = call(
        forward_kernel,
        "forward",
        1,
        dict(
            x=tokens_in,
            attn_gain=attn_gain[None],
            mlp_gain=mlp_gain[None],
            **gates,
        ),
        dict(
            w=w,
            state_query=state_query,
            g=grad_out,
            state_proj=state_proj,
            w_out=w_out,
            w_up=w_up,
            w_down=w_down,
        ),
        dict(rel=jnp.transpose(rel_bias), **small),
        dict(
            grad_middle=rows_wide,
            gm0=((4, rows, width), BF),
            g_gain=((1, width), F32),
        ),
        dict(
            whole=whole_shape,
            qkv=((micros, block, 3 * local), BF),
            kv_all=((micros, 2 * block, 2 * local), BF),
            state_kv=((micros, states, 2 * local), BF),
            prior=state_low,
            across=state_low,
            keeps=((count, 8, local), F32),
            update=state_wide,
            stats=((micros, block, TILE), F32),
            table=((heads, TILE, 5 * TILE), F32),
            state_after=state_wide,
            att_rel=((micros, 4, rows, local), BF),
            middle=rows_wide,
            branch=whole_shape,
            half=((512, mlp_width), BF),
        ),
        dict(
            whole_grad=whole_shape,
            own_keep=((8, local), F32),
            unit_low=state_low,
            held=state_low,
            terms=whole_shape,
            whole_mlp=whole_shape,
            active=((micros, block, w_up.shape[1]), BF),
            grad_hidden=((micros, block, w_up.shape[1]), BF),
            mids=((4, 4, rows // 2, width), BF),
            intos=((4, 2, rows, width), BF),
            parts=((width, mlp_width), BF),
        ),
        dict(send=sems(80), recv=sems(80), s3=sems(count), r3=sems(count), **exchange),
    )
    b = call(
        backward_kernel,
        "backward",
        2,
        dict(
            gm0=f["gm0"],
            grad_middle=f["grad_middle"],
            w_out=w_out,
            attn_gain=attn_gain[None],
            g_mlp_gain=f["g_gain"],
            **gates,
        ),
        dict(
            half=f["half"],
            qkv=f["qkv"],
            kv_all=f["kv_all"],
            state_kv=f["state_kv"],
            stats=f["stats"],
            table=f["table"],
            branch=f["branch"],
            prior=f["prior"],
            state_proj=state_proj,
            across=f["across"],
            keeps=f["keeps"],
            att_rel=f["att_rel"],
            middle=f["middle"],
            update=f["update"],
            state_query=state_query,
            w=w,
            whole=f["whole"],
            x=tokens_in,
        ),
        small,
        dict(
            total_a=((width, 512), BF),
            total_b=((width, 768), BF),
        ),
        dict(out=rows_wide, grad_x=rows_wide, total_mlp=((width, mlp_width), BF)),
        dict(
            dqkv=((micros, 4, rows, 3 * local), BF),
            g_query=((states, local), F32),
            g_proj=(state_proj.shape, F32),
            g_rel=((heads, 8, local), F32),
            g_bias=((1, local), F32),
            g_scale=((1, local), F32),
            grad_att=((micros, block, local), BF),
            grad_kv=((micros, 2 * block, 2 * local), F32),
            grad_state=((micros, states, 2 * local), F32),
            early=((micros, block, 2 * local), BF),
            later=((micros, block, 2 * local), BF),
            grad_prior=state_low,
            moved=state_low,
            held=state_low,
            grad_after=state_low,
            near=((heads, TILE, 3 * TILE), F32),
            sums=((local, TILE), F32),
            mids=((4, 4, rows // 2, width), BF),
            intos=((4, 2, rows, width), BF),
            others=((6, 16, local), BF),
            small=((16, local), F32),
            gm1=((4, rows, width), BF),
            parts_a=((width, 512), BF),
            half_a=((512, 512), BF),
            parts_b=((width, 768), BF),
            half_b=((512, 768), BF),
            **reduce_scratch("mlp_", mlp_width),
            **reduce_scratch("a_", 512),
            **reduce_scratch("b_", 768),
        ),
        dict(send=sems(150), recv=sems(150), s3=sems(6), r3=sems(6), **exchange),
    )
    results = [
        rows_wide[0],
        rows_wide[0],
        state_wide[0],
        w_up.shape,
        w_down.shape,
        w.shape,
        w_out.shape,
        state_query.shape,
        (heads * state_proj.shape[1], local),
        (1, width),
        (1, width),
        (1, local),
        (1, local),
        (heads, buckets),
    ]
    anywhere = pl.BlockSpec(memory_space=pl.ANY)
    values = pl.pallas_call(
        finish_kernel,
        out_shape=tuple(jax.ShapeDtypeStruct(shape, F32) for shape in results),
        in_specs=[anywhere] * 6,
        out_specs=tuple([anywhere] * 9 + [VMEM] * 5),
        scratch_shapes=[
            pltpu.VMEM((width, 3328), F32),
            pltpu.VMEM((width, mlp_width), BF),
            pltpu.VMEM((width, 512), BF),
            pltpu.VMEM((width, 768), BF),
            pltpu.VMEM((2,) + rows_wide[0], F32),
            pltpu.VMEM(state_wide[0], F32),
            sems(15),
            sems(32),
        ],
        compiler_params=pltpu.CompilerParams(vmem_limit_bytes=LIMIT),
        name="finish",
    )(b["total_a"], b["total_b"], b["total_mlp"], b["out"], b["grad_x"], f["state_after"])
    out, grad_x, state_after, g_up, g_down, g_qkv, g_out, g_query, g_proj = values[:9]
    g_attn_gain, g_mlp_gain, g_bias, g_scale, g_rel = values[9:]
    return (
        out,
        grad_x,
        state_after[:, None],
        g_attn_gain[0],
        g_mlp_gain[0],
        jnp.transpose(g_qkv, (1, 0, 2)),
        g_out,
        jnp.transpose(g_rel),
        g_query,
        g_proj.reshape(state_proj.shape),
        g_bias[0],
        g_scale[0],
        g_up,
        g_down,
    )


def solution(mesh):
    return jax.shard_map(
        body,
        mesh=mesh,
        in_specs=(
            P(None, ("blk", "head"), None),
            P(None, ("blk", "head"), None),
            P(None, "blk"),
            P(),
            P(),
            P(None, None, "head"),
            P("head", None),
            P(None, "head"),
            P(None, "head"),
            P("head", None, None),
            P("head"),
            P("head"),
            P(None, "head"),
            P("head", None),
        ),
        out_specs=(
            P(None, ("blk", "head"), None),
            P(None, ("blk", "head"), None),
            P(None, "blk", None, "head"),
            P(),
            P(),
            P(None, None, "head"),
            P("head", None),
            P(None, "head"),
            P(None, "head"),
            P("head", None, None),
            P("head"),
            P("head"),
            P(None, "head"),
            P("head", None),
        ),
        check_vma=False,
    )
```

```python
import math
import types

import jax
import jax.numpy as jnp
from jax import lax
from jax.experimental import pallas as pl
from jax.experimental.pallas import tpu as pltpu
from jax.sharding import PartitionSpec as P

BUCKETS = 32
MAXDIST = 128
EPSILON = 1e-06
MASKED = -1e30
TILE = 128
MESH = pl.DeviceIdType.MESH
BF = jnp.bfloat16
F32 = jnp.float32
VMEM = pl.BlockSpec(memory_space=pltpu.VMEM)
SMEM = pl.BlockSpec(memory_space=pltpu.SMEM)
LIMIT = 60 * 2**20
ROOT = math.sqrt(2.0 / math.pi)
CUBIC = 0.044715


def bucket_starts():
    exact = BUCKETS // 2
    levels = [
        int(math.ceil(exact * (MAXDIST / exact) ** (t / (BUCKETS - exact))))
        for t in range(1, BUCKETS - exact)
    ]
    return list(range(exact + 1)) + levels


STARTS = bucket_starts()


def nn(a, b):
    return lax.dot_general(a, b, (((1,), (0,)), ((), ())), preferred_element_type=F32)


def nt(a, b):
    return lax.dot_general(a, b, (((1,), (1,)), ((), ())), preferred_element_type=F32)


def tn(a, b):
    return lax.dot_general(a, b, (((0,), (0,)), ((), ())), preferred_element_type=F32)


def inverse_rms(values):
    return lax.rsqrt(jnp.mean(values * values, axis=-1, keepdims=True) + EPSILON)


def tile_of(index, size=TILE):
    return pl.ds(pl.multiple_of(index * size, size), size)


def loop(count, step, after=None, action=None):
    def run(i, c):
        step(i)
        return c

    if after is not None:
        lax.fori_loop(0, after + 1, run, 0)
        action()
    lax.fori_loop(0 if after is None else after + 1, count, run, 0)


def remote(src, dst, send_sem, recv_sem, device):
    return pltpu.make_async_remote_copy(
        src_ref=src,
        dst_ref=dst,
        send_sem=send_sem,
        recv_sem=recv_sem,
        device_id=device,
        device_id_type=MESH,
    )


class Links:
    def __init__(self, send, recv):
        self.send, self.recv, self.used = send, recv, 0

    def go(self, src, dst, device):
        copy = remote(src, dst, self.send.at[self.used], self.recv.at[self.used], device)
        self.used += 1
        copy.start()
        return copy


class Ring:
    def __init__(self, links, me, device):
        self.links, self.me = links, me
        self.right = device(lax.rem(me + 1, 4))
        self.left = device(lax.rem(me + 3, 4))
        self.opposite = device(lax.rem(me + 2, 4))

    def go(self, src, dst, peer):
        return self.links.go(src, dst, peer)

    def greet(self):
        barrier = pltpu.get_barrier_semaphore()
        for peer in (self.right, self.left):
            pl.semaphore_signal(barrier, inc=1, device_id=peer, device_id_type=MESH)
        return 2

    def chunk(self, k):
        return lax.rem(self.me + k, 4)

    def row_chunk(self, k):
        return tile_of(self.chunk(k))


def head_ring(links):
    return Ring(links, lax.axis_index("head"), lambda i: {"head": i})


def by_rows(buf):
    half = buf.shape[1] // 2

    def piece(k, part=None, offset=0):
        return buf.at[k] if part is None else buf.at[k, part * half : (part + 1) * half]

    return piece


def by_columns(buf, base, rows, chunk):
    half = buf.shape[1] // 2
    starts = [pl.multiple_of(base + chunk(k) * rows, rows) for k in range(4)]

    def piece(k, part=None, offset=0):
        at = pl.ds(starts[(k + offset) % 4], rows)
        return buf.at[at] if part is None else buf.at[at, part * half : (part + 1) * half]

    return piece


class Gather:
    def __init__(self, ring, piece):
        self.ring, self.piece = ring, piece

    def start(self):
        r, p = self.ring, self.piece
        self.a0 = r.go(p(0, 0), p(3, 0, 1), r.right)
        self.b0 = r.go(p(0, 1), p(1, 1, 3), r.left)
        self.a1 = r.go(p(0, 1), p(3, 1, 1), r.right)
        self.b1 = r.go(p(0, 0), p(1, 0, 3), r.left)

    def relay(self):
        r, p = self.ring, self.piece
        self.a0.wait_recv()
        self.a2 = r.go(p(3, 0), p(2, 0, 1), r.right)
        self.b0.wait_recv()
        self.b2 = r.go(p(1, 1), p(2, 1, 3), r.left)

    def finish(self):
        for copy in (self.a1, self.b1, self.a2, self.b2):
            copy.wait_recv()

    def close(self):
        for copy in (self.a0, self.b0, self.a1, self.b1, self.a2, self.b2):
            copy.wait_send()


class Reduce:
    def __init__(self, ring, terms, mid, into):
        self.ring, self.terms, self.mid, self.into = ring, terms, mid, into
        if mid.shape[1] == into.shape[1]:
            half = into.shape[2] // 2
            self.place = lambda i, part: into.at[i, :, part * half : (part + 1) * half]
        else:
            half = into.shape[1] // 2
            self.place = lambda i, part: into.at[i, part * half : (part + 1) * half]

    def start(self):
        r, t = self.ring, self.terms
        self.a0 = r.go(t(2, 0), self.mid.at[0], r.right)
        self.b0 = r.go(t(2, 1), self.mid.at[1], r.left)
        self.a1 = r.go(t(1, 1), self.place(0, 1), r.right)
        self.b1 = r.go(t(3, 0), self.place(1, 0), r.left)

    def relay(self):
        r, t, mid = self.ring, self.terms, self.mid
        self.a0.wait_recv()
        mid[2] = (mid[0].astype(F32) + t(1, 0)[...].astype(F32)).astype(BF)
        self.a2 = r.go(mid.at[2], self.place(0, 0), r.right)
        self.b0.wait_recv()
        mid[3] = (mid[1].astype(F32) + t(3, 1)[...].astype(F32)).astype(BF)
        self.b2 = r.go(mid.at[3], self.place(1, 1), r.left)

    def finish(self):
        for copy in (self.a1, self.b1, self.a2, self.b2):
            copy.wait_recv()
        return (
            self.terms(0)[...].astype(F32)
            + self.into[0].astype(F32)
            + self.into[1].astype(F32)
        )

    def close(self):
        for copy in (self.a0, self.b0, self.a1, self.b1, self.a2, self.b2):
            copy.wait_send()


def block_device(x, z, c):
    return {"blk": (x * 4 + z) * 2 + c}


def block_place():
    place = lax.axis_index("blk")
    return place % 2, (place // 2) % 4, place // 8


class Plane:
    def __init__(self, links):
        c, z, x = block_place()
        self.links = links
        self.peer = block_device(x, z, 1 - c)
        rx = Ring(links, x, lambda i: block_device(i, z, c))
        rz = Ring(links, z, lambda i: block_device(x, i, c))
        self.rings = [rx, rz]
        self.first, self.second = (rx, rz), (rz, rx)
        self.base = c * 512
        self.own = pl.ds(pl.multiple_of(c * 512, 512), 512)
        self.away = pl.ds(pl.multiple_of((1 - c) * 512, 512), 512)
        self.top = [c * 512 + x * 64, c * 512 + 256 + z * 64]
        self.last = [
            pl.ds(pl.multiple_of(self.top[0] + z * 16, 16), 16),
            pl.ds(pl.multiple_of(self.top[1] + x * 16, 16), 16),
        ]

    def greet(self):
        barrier = pltpu.get_barrier_semaphore()
        pl.semaphore_signal(barrier, inc=1, device_id=self.peer, device_id_type=MESH)
        return 1 + sum(ring.greet() for ring in self.rings)


class Steps:
    def advance(self, steps=1):
        for _ in range(steps):
            if self.steps:
                self.steps.pop(0)()


class CoreSum:
    def __init__(self, plane, parts, half):
        self.plane, self.parts, self.half = plane, parts, half

    def start(self):
        plane = self.plane
        self.swap = plane.links.go(self.parts.at[plane.away], self.half, plane.peer)

    def finish(self):
        self.swap.wait_recv()

        def add(t):
            rows = tile_of(t, 64)
            own = pl.ds(pl.multiple_of(self.plane.base + t * 64, 64), 64)
            self.half[rows] = (
                self.parts[own].astype(F32) + self.half[rows].astype(F32)
            ).astype(BF)

        loop(8, add)

    def close(self):
        self.swap.wait_send()


class PlaneReduce(Steps):
    def __init__(self, plane, half, total, mid, into, quarter, small_into):
        self.plane, self.half, self.total, self.quarter = plane, half, total, quarter
        first, second = plane.first, plane.second
        self.reduce1 = [
            Reduce(first[i], by_columns(half, i * 256, 64, first[i].chunk), mid.at[i], into.at[i])
            for i in range(2)
        ]
        self.reduce2 = [
            ReduceDirect(
                second[i], by_columns(quarter.at[i], 0, 16, second[i].chunk), small_into.at[i]
            )
            for i in range(2)
        ]
        self.steps = [
            lambda: [r.start() for r in self.reduce1],
            lambda: [r.relay() for r in self.reduce1],
            self.start2,
            self.finish,
        ]

    def start2(self):
        for i, r in enumerate(self.reduce1):
            self.quarter[i] = r.finish().astype(BF)
            self.reduce2[i].start()

    def finish(self):
        for i, r in enumerate(self.reduce2):
            self.total[self.plane.last[i]] = r.finish().astype(BF)

    def close(self):
        for r in self.reduce1 + self.reduce2:
            r.close()


class PlaneGather(Steps):
    def __init__(self, plane, total):
        self.plane, self.total = plane, total
        first, second = plane.first, plane.second
        self.gather1 = [
            GatherDirect(second[i], by_columns(total, plane.top[i], 16, second[i].chunk))
            for i in range(2)
        ]
        self.gather2 = [
            Gather(first[i], by_columns(total, plane.base + i * 256, 64, first[i].chunk))
            for i in range(2)
        ]
        self.steps = [
            lambda: [g.start() for g in self.gather1],
            self.start2,
            lambda: [g.relay() for g in self.gather2],
            self.cores,
            lambda: self.swap.wait_recv(),
        ]

    def start2(self):
        for i, g in enumerate(self.gather1):
            g.finish()
            self.gather2[i].start()

    def cores(self):
        for g in self.gather2:
            g.finish()
        rows = self.total.at[self.plane.own]
        self.swap = self.plane.links.go(rows, rows, self.plane.peer)

    def close(self):
        self.swap.wait_send()
        for g in self.gather1 + self.gather2:
            g.close()


def reduce_scratch(name, width):
    return {
        name + "mid": ((2, 4, 64, width // 2), BF),
        name + "into": ((2, 2, 64, width), BF),
        name + "quarter": ((2, 64, width), BF),
        name + "small": ((2, 3, 16, width), BF),
    }


class GatherDirect:
    def __init__(self, ring, piece):
        self.ring, self.piece = ring, piece

    def start(self):
        r, p = self.ring, self.piece
        self.copies = [
            r.go(p(0), p(4 - k, None, k), peer)
            for k, peer in ((1, r.right), (3, r.left), (2, r.opposite))
        ]

    def finish(self):
        for copy in self.copies:
            copy.wait_recv()

    def close(self):
        for copy in self.copies:
            copy.wait_send()


class ReduceDirect:
    def __init__(self, ring, terms, into):
        self.ring, self.terms, self.into = ring, terms, into

    def start(self):
        r, t = self.ring, self.terms
        self.copies = [
            r.go(t(k), self.into.at[k - 1], peer)
            for k, peer in ((1, r.right), (3, r.left), (2, r.opposite))
        ]

    def finish(self):
        for copy in self.copies:
            copy.wait_recv()
        total = self.terms(0)[...].astype(F32)
        for k in range(3):
            total = total + self.into[k].astype(F32)
        return total

    def close(self):
        for copy in self.copies:
            copy.wait_send()


class Exchange:
    def __init__(self, source, target, send, recv, local):
        self.count = lax.axis_size("blk")
        self.place = lax.axis_index("blk")
        self.size = source.shape[0] // self.count
        self.source, self.target = source, target
        self.send, self.recv, self.local = send, recv, local

    def part(self, j):
        peer = lax.rem(self.place + j, self.count)
        return remote(
            self.source.at[tile_of(peer, self.size)],
            self.target.at[tile_of(self.place, self.size)],
            self.send,
            self.recv,
            {"blk": peer},
        )

    def all(self):
        rows = slice(0, (self.count - 1) * self.size)
        return remote(
            self.source.at[rows],
            self.target.at[rows],
            self.send,
            self.recv,
            {"blk": lax.rem(self.place + 1, self.count)},
        )

    def own(self):
        rows = tile_of(self.place, self.size)
        return pltpu.make_async_copy(self.source.at[rows], self.target.at[rows], self.local)

    def start(self):
        loop(self.count - 1, lambda j: self.part(j + 1).start())
        self.own().start()

    def finish(self):
        self.own().wait()
        self.all().wait_recv()

    def close(self):
        self.all().wait_send()


def greet_blocks():
    barrier = pltpu.get_barrier_semaphore()
    count, place = lax.axis_size("blk"), lax.axis_index("blk")

    def greet(j):
        pl.semaphore_signal(
            barrier, inc=1, device_id={"blk": lax.rem(place + j + 1, count)}, device_id_type=MESH
        )

    loop(count - 1, greet)
    return count - 1


def closed_row(flag, qi):
    column = lax.broadcasted_iota(jnp.int32, (1, 5 * TILE), 1) + qi * TILE
    return jnp.where(column < 512, MASKED * flag.astype(F32), 0.0)


def head(h, size=TILE, base=0):
    return slice(base + h * size, base + (h + 1) * size)


def window_of(qi):
    return pl.ds(pl.multiple_of(qi * TILE, TILE), 5 * TILE)


def split_rows(target, m, cols, part):
    for k in range(4):
        target[m, k, :, cols] = part[k * TILE : (k + 1) * TILE]


def write_table(table, rel):
    row = lax.broadcasted_iota(jnp.int32, (TILE, TILE), 0)
    col = lax.broadcasted_iota(jnp.int32, (TILE, TILE), 1)

    def per_head(h):
        far = jnp.full((TILE, TILE), rel[h, BUCKETS - 1], F32)
        table[h, :, 0:128] = jnp.where(row < col, far, MASKED)
        table[h, :, 128:256] = far
        table[h, :, 256:384] = far
        for shift, at in ((TILE, 384), (0, 512)):
            distance = row - col + shift
            total = jnp.full((TILE, TILE), rel[h, 0], F32)
            for t in range(1, BUCKETS):
                total = jnp.where(distance >= STARTS[t], rel[h, t], total)
            table[h, :, at : at + TILE] = jnp.where(distance >= 0, total, MASKED)

    loop(2, per_head)


def forward_kernel(r):
    scale = TILE**-0.5
    links = Links(r.send, r.recv)
    ring = head_ring(links)
    plane = Plane(links)
    place, count = lax.axis_index("blk"), lax.axis_size("blk")
    both = range(2)

    def norm_rows(m):
        rows = r.x[m].astype(F32)
        r.whole.ref[m, 0] = (rows * inverse_rms(rows) * r.attn_gain[...]).astype(BF)

    greeted = ring.greet() + greet_blocks()
    norm_rows(0)
    for m in both:
        keep = 1.0 - r.flags[0, m].astype(F32)
        r.own_keep[0, m : m + 1] = jnp.full((1, 256), keep, F32)
    r.own_keep[0, 2:8] = jnp.zeros((6, 256), F32)
    pl.semaphore_wait(pltpu.get_barrier_semaphore(), greeted)
    whole, qkv, kv_all = r.whole.ref, r.qkv.ref, r.kv_all.ref
    prior, across, keeps = r.prior.ref, r.across.ref, r.keeps.ref
    update, stats, state_kv = r.update.ref, r.stats.ref, r.state_kv.ref
    table, att_rel, middle, branch = r.table.ref, r.att_rel.ref, r.middle.ref, r.branch.ref
    gather_x = [Gather(ring, by_rows(whole.at[m])) for m in both]
    gather_g = [Gather(ring, by_rows(r.whole_grad.at[m])) for m in both]
    gather_x[0].start()
    norm_rows(1)

    def tell(j):
        peer = {"blk": lax.rem(place + j, count)}
        return remote(r.own_keep.at[0], keeps.at[place], r.s3.at[0], r.r3.at[0], peer)

    def tell_all():
        peer = {"blk": lax.rem(place + 1, count)}
        rows = slice(0, count - 1)
        return remote(r.own_keep.at[rows], keeps.at[rows], r.s3.at[0], r.r3.at[0], peer)

    loop(count - 1, lambda j: tell(j + 1).start())
    keeps[place] = r.own_keep[0]
    write_table(table, r.rel)
    r.table.put()
    after = {"blk": lax.rem(place + 1, count)}
    shifts = [
        remote(qkv.at[m, :, 256:768], kv_all.at[m, 0:512], r.s0.at[m], r.r0.at[m], after)
        for m in both
    ]
    there = [
        Exchange(r.unit_low.at[m], across.at[m], r.s1.at[m], r.r1.at[m], r.local.at[m])
        for m in both
    ]
    back = [
        Exchange(r.held.at[m], prior.at[m], r.s2.at[m], r.r2.at[m], r.local.at[2 + m])
        for m in both
    ]

    def project(m):
        def columns(n):
            cols = tile_of(n, 256)
            part = nn(whole[m].reshape(512, 1024), r.w.ref[n]).astype(BF)
            for k in range(4):
                qkv[m, ring.row_chunk(k), cols] = part[k * TILE : (k + 1) * TILE]

        loop(3, columns)
        shifts[m].start()
        kv_all[m, 512:1024] = qkv[m, :, 256:768]

    def update_tile(m):
        def step(t):
            rows = tile_of(t)
            for h in range(2):
                scores = nt(r.state_query.ref[rows, head(h)], qkv[m, :, head(h, base=256)]) * scale
                top = jnp.max(scores, axis=-1, keepdims=True)
                raised = jnp.exp(scores - top)
                total = jnp.sum(raised, axis=-1, keepdims=True)
                stats[m, rows, h : h + 1] = top + jnp.log(total)
                u = nn(raised.astype(BF), qkv[m, :, head(h, base=512)]) / total
                update[m, rows, head(h)] = u
                r.unit_low[m, rows, head(h)] = (u * inverse_rms(u)).astype(BF)

        return step

    def scan(m):
        def step(b, state):
            rows = tile_of(b, 16)
            u = across[m, rows].astype(F32)
            forget = jax.nn.sigmoid(r.bias[...] + r.slope[...] * u)
            before = keeps[b, m : m + 1] * state
            r.held[m, rows] = before.astype(BF)
            return forget * before + (1.0 - forget) * u

        lax.fori_loop(0, count, step, jnp.zeros((16, 256), F32))

    def state(m):
        def step(t):
            rows = tile_of(t)
            before = prior[m, rows]
            for h in range(2):
                state_kv[m, rows, head(h, 256)] = nn(before[:, head(h)], r.state_proj.ref[h]).astype(BF)
                u = update[m, rows, head(h)]
                u = u * inverse_rms(u)
                forget = jax.nn.sigmoid(r.bias[:, head(h)] + r.slope[:, head(h)] * u)
                r.state_after.ref[m, rows, head(h)] = (
                    forget * before[:, head(h)].astype(F32) + (1.0 - forget) * u
                )

        return step

    def attend(m):
        def step(qi):
            rows, window = tile_of(qi), window_of(qi)
            shut = closed_row(r.flags[0, m], qi)
            for h in range(2):
                q = qkv[m, rows, head(h)]
                token = nt(q, kv_all[m, window, head(h)]) * scale + (table[h] + shut)
                from_state = nt(q, state_kv[m, :, h * 256 : h * 256 + TILE]) * scale
                top = jnp.maximum(
                    jnp.max(token, axis=-1, keepdims=True),
                    jnp.max(from_state, axis=-1, keepdims=True),
                )
                token = jnp.exp(token - top)
                from_state = jnp.exp(from_state - top)
                total = jnp.sum(token, axis=-1, keepdims=True) + jnp.sum(
                    from_state, axis=-1, keepdims=True
                )
                stats[m, rows, 2 + h : 3 + h] = top + jnp.log(total)
                out = nn(token.astype(BF), kv_all[m, window, head(h, base=256)]) + nn(
                    from_state.astype(BF), state_kv[m, :, h * 256 + TILE : (h + 1) * 256]
                )
                att_rel[m, lax.rem(qi + 4 - ring.me, 4), :, head(h)] = (out / total).astype(BF)

        return step

    first = [
        Reduce(ring, by_rows(r.terms.at[m]), r.mids.at[m], r.intos.at[m]) for m in both
    ]
    second = [Gather(ring, by_rows(r.whole_mlp.at[m])) for m in both]
    third = [
        Reduce(ring, by_rows(r.terms.at[m]), r.mids.at[2 + m], r.intos.at[2 + m]) for m in both
    ]
    fourth = Gather(ring, by_rows(r.gm0))

    def out_terms(m):
        def columns(n):
            cols = tile_of(n, 256)
            part = nn(att_rel[m].reshape(512, 256), r.w_out.ref[:, cols]).astype(BF)
            split_rows(r.terms, m, cols, part)

        loop(4, columns)

    def normalise(m):
        rows = r.x[m].astype(F32) + first[m].finish()
        middle[m] = rows
        r.whole_mlp[m, 0] = (rows * inverse_rms(rows) * r.mlp_gain[...]).astype(BF)

    def hidden(m):
        def columns(n):
            cols = tile_of(n, 256)
            value = nn(r.whole_mlp[m].reshape(512, 1024), r.w_up.ref[:, cols])
            grad_active = nt(r.whole_grad[m].reshape(512, 1024), r.w_down.ref[cols])
            square = value * value
            bent = jnp.tanh(ROOT * value * (1.0 + CUBIC * square))
            r.active[m, :, cols] = (0.5 * value * (1.0 + bent)).astype(BF)
            rise = 0.5 * (1.0 + bent) + 0.5 * value * (1.0 - bent * bent) * ROOT * (
                1.0 + 3.0 * CUBIC * square
            )
            r.grad_hidden[m, :, cols] = (grad_active * rise).astype(BF)

        return columns

    def grad_terms(m):
        def columns(n):
            cols = tile_of(n, 256)
            part = nt(r.grad_hidden[m], r.w_up.ref[cols]).astype(BF)
            split_rows(r.terms, m, cols, part)

        loop(4, columns)

    def branch_terms(m):
        def columns(n):
            cols = tile_of(n, 256)
            part = nn(r.active[m], r.w_down.ref[:, cols]).astype(BF)
            split_rows(branch, m, cols, part)

        loop(4, columns)

    def grad_rows(m):
        grad_normed = third[m].finish()
        rows = middle[m]
        inverse = inverse_rms(rows)
        unit = rows * inverse
        part = jnp.sum(grad_normed * unit, axis=0, keepdims=True)
        r.g_gain[...] = part if m == 0 else r.g_gain[...] + part
        scaled = grad_normed * r.mlp_gain[...]
        inner = jnp.mean(scaled * unit, axis=-1, keepdims=True)
        total = r.g.ref[m].astype(F32) + inverse * (scaled - unit * inner)
        r.grad_middle[m] = total
        if m == 0:
            r.gm0[0] = total.astype(BF)

    def up_rows(n):
        rows = tile_of(n, 256)
        total = tn(r.whole_mlp[0, :, :, rows].reshape(512, 256), r.grad_hidden[0])
        total = total + tn(r.whole_mlp[1, :, :, rows].reshape(512, 256), r.grad_hidden[1])
        r.parts[rows, 0:1024] = total.astype(BF)

    def down_rows(n):
        rows = tile_of(n, 256)
        total = tn(r.active[0, :, rows], r.whole_grad[0].reshape(512, 1024))
        total = total + tn(r.active[1, :, rows], r.whole_grad[1].reshape(512, 1024))
        r.parts[rows, 1024:2048] = total.astype(BF)

    cores = CoreSum(plane, r.parts, r.half.ref)

    gather_x[0].relay()
    gather_x[1].start()
    r.w.get()
    gather_x[0].finish()
    project(0)
    gather_x[1].relay()
    r.state_query.get()
    loop(4, update_tile(0))
    there[0].start()
    gather_x[1].finish()
    r.g.get()
    for m in both:
        r.whole_grad[m, 0] = r.g.ref[m]
    gather_g[0].start()
    project(1)
    r.whole.put()
    r.qkv.put()
    loop(4, update_tile(1))
    there[1].start()
    r.update.put()
    gather_g[0].relay()
    gather_g[1].start()
    tell_all().wait_recv()
    there[0].finish()
    scan(0)
    back[0].start()
    there[1].finish()
    scan(1)
    back[1].start()
    gather_g[1].relay()
    r.across.put()
    r.keeps.put()
    shifts[0].wait_recv()
    shifts[1].wait_recv()
    r.kv_all.put()
    r.state_proj.get()
    back[0].finish()
    loop(4, state(0))
    loop(4, attend(0))
    r.w_out.get()
    out_terms(0)
    first[0].start()
    back[1].finish()
    r.prior.put()
    loop(4, state(1))
    r.state_kv.put()
    r.state_after.put()
    loop(4, attend(1), 0, first[0].relay)
    r.stats.put()
    out_terms(1)
    r.att_rel.put()
    first[1].start()
    normalise(0)
    second[0].start()
    first[1].relay()
    second[0].relay()
    r.w_up.get()
    r.w_down.get()
    gather_g[0].finish()
    gather_g[1].finish()
    normalise(1)
    second[1].start()
    r.middle.put()
    second[0].finish()
    loop(4, hidden(0), 1, second[1].relay)
    first[0].close()
    grad_terms(0)
    third[0].start()
    second[1].finish()
    loop(4, hidden(1), 1, third[0].relay)
    first[1].close()
    grad_terms(1)
    third[1].start()
    loop(4, up_rows)
    grad_rows(0)
    fourth.start()
    third[1].relay()
    loop(4, down_rows)
    cores.start()
    fourth.relay()
    branch_terms(0)
    branch_terms(1)
    r.branch.put()
    cores.finish()
    r.half.put()
    grad_rows(1)
    fourth.finish()
    cores.close()
    fourth.close()
    for m in both:
        for step in (gather_x, gather_g, second, third):
            step[m].close()
        shifts[m].wait_send()
        there[m].close()
        back[m].close()
    tell_all().wait_send()


def backward_kernel(r):
    scale = TILE**-0.5
    links = Links(r.send, r.recv)
    ring = head_ring(links)
    plane = Plane(links)
    place, count = lax.axis_index("blk"), lax.axis_size("blk")
    both = range(2)
    gm = [r.gm0, r.gm1]
    core = place % 2
    others = [
        {"head": ring.chunk(k), "blk": place - core + c} for k in range(1, 4) for c in range(2)
    ]
    barrier = pltpu.get_barrier_semaphore()
    for device in others:
        pl.semaphore_signal(barrier, inc=1, device_id=device, device_id_type=MESH)
    greeted = len(others) + greet_blocks()
    r.gm1[0] = r.grad_middle[1].astype(BF)
    pl.semaphore_wait(barrier, greeted)
    fourth = Gather(ring, by_rows(r.gm1))
    fourth.start()
    mlp_sum = PlaneReduce(
        plane, r.half.ref, r.total_mlp.ref, r.mlp_mid, r.mlp_into, r.mlp_quarter, r.mlp_small
    )
    mlp_all = PlaneGather(plane, r.total_mlp.ref)
    qkv, kv_all, state_kv, stats = r.qkv.ref, r.kv_all.ref, r.state_kv.ref, r.stats.ref
    r.branch.get()
    branch = r.branch.ref
    outs = [Reduce(ring, by_rows(branch.at[m]), r.mids.at[m], r.intos.at[m]) for m in both]
    ends = [
        Reduce(ring, by_rows(branch.at[m]), r.mids.at[2 + m], r.intos.at[2 + m]) for m in both
    ]
    before = {"blk": lax.rem(place + count - 1, count)}
    shifts = [
        remote(r.early.at[m], r.later.at[m], r.s0.at[m], r.r0.at[m], before) for m in both
    ]
    there = [
        Exchange(r.grad_prior.at[m], r.moved.at[m], r.s1.at[m], r.r1.at[m], r.local.at[m])
        for m in both
    ]
    back = [
        Exchange(r.held.at[m], r.grad_after.at[m], r.s2.at[m], r.r2.at[m], r.local.at[2 + m])
        for m in both
    ]
    for ref in (r.near, r.sums, r.g_query, r.g_bias, r.g_scale, r.grad_kv, r.grad_state):
        ref[...] = jnp.zeros(ref.shape, F32)

    def own_chunk(qi):
        return lax.rem(qi + 4 - ring.me, 4)

    def attention_rows(m):
        part = nt(gm[m][...].reshape(512, 1024), r.w_out[...]).astype(BF)
        for k in range(4):
            r.grad_att[m, ring.row_chunk(k)] = part[k * TILE : (k + 1) * TILE]

    def attend(m):
        def step(qi):
            rows, window = tile_of(qi), window_of(qi)
            shut = closed_row(r.flags[0, m], qi)
            for h in range(2):
                k_cols, v_cols = head(h), head(h, base=256)
                sk_cols = slice(h * 256, h * 256 + TILE)
                sv_cols = slice(h * 256 + TILE, (h + 1) * 256)
                q = qkv[m, rows, head(h)]
                d = r.grad_att[m, rows, head(h)]
                level = stats[m, rows, 2 + h : 3 + h]
                token = jnp.exp(
                    nt(q, kv_all[m, window, k_cols]) * scale + (r.table.ref[h] + shut) - level
                )
                from_state = jnp.exp(nt(q, state_kv[m, :, sk_cols]) * scale - level)
                grad_token = nt(d, kv_all[m, window, v_cols])
                grad_from = nt(d, state_kv[m, :, sv_cols])
                delta = jnp.sum(token * grad_token, axis=-1, keepdims=True) + jnp.sum(
                    from_state * grad_from, axis=-1, keepdims=True
                )
                grad_token = token * (grad_token - delta)
                grad_from = from_state * (grad_from - delta)
                r.near[h, :, 0:128] += (
                    grad_token[:, 0:128] + grad_token[:, 128:256] + grad_token[:, 256:384]
                )
                r.near[h, :, 128:384] += grad_token[:, 384:640]
                token_low = grad_token.astype(BF)
                from_low = grad_from.astype(BF)
                grad_q = scale * (
                    nn(token_low, kv_all[m, window, k_cols]) + nn(from_low, state_kv[m, :, sk_cols])
                )
                r.dqkv[m, own_chunk(qi), :, head(h)] = grad_q.astype(BF)
                r.grad_kv[m, window, k_cols] += tn(token_low, q)
                r.grad_kv[m, window, v_cols] += tn(token.astype(BF), d)
                r.grad_state[m, :, sk_cols] += tn(from_low, q)
                r.grad_state[m, :, sv_cols] += tn(from_state.astype(BF), d)

        return step

    def pass_on(m):
        r.early[m, :, 0:256] = (scale * r.grad_kv[m, 0:512, 0:256]).astype(BF)
        r.early[m, :, 256:512] = r.grad_kv[m, 0:512, 256:512].astype(BF)
        for h in range(2):
            low = jnp.concatenate(
                [
                    (scale * r.grad_state[m, :, h * 256 : h * 256 + TILE]).astype(BF),
                    r.grad_state[m, :, h * 256 + TILE : (h + 1) * 256].astype(BF),
                ],
                1,
            )
            r.grad_prior[m, :, head(h)] = nt(low, r.state_proj.ref[h]).astype(BF)
            part = tn(r.prior.ref[m, :, head(h)], low)
            r.g_proj[h] = part if m == 0 else r.g_proj[h] + part
        there[m].start()
        shifts[m].start()

    def scan(m):
        def step(t, grad):
            b = count - 1 - t
            rows = tile_of(b, 16)
            r.held[m, rows] = grad.astype(BF)
            u = r.across.ref[m, rows].astype(F32)
            forget = jax.nn.sigmoid(r.bias[...] + r.slope[...] * u)
            moved = r.moved[m, rows].astype(F32)
            return r.keeps.ref[b, m : m + 1] * (moved + forget * grad)

        lax.fori_loop(0, count, step, jnp.zeros((16, 256), F32))

    def bucket_sums():
        row = lax.broadcasted_iota(jnp.int32, (TILE, TILE), 0)
        col = lax.broadcasted_iota(jnp.int32, (TILE, TILE), 1)
        distance = [row - col + TILE, row - col]

        def per_head(h):
            for t in range(BUCKETS):
                total = jnp.zeros((1, TILE), F32)
                for part in range(2):
                    d = distance[part]
                    inside = d >= STARTS[t]
                    if t + 1 < BUCKETS:
                        inside = inside & (d < STARTS[t + 1])
                    values = r.near[h, :, TILE * (part + 1) : TILE * (part + 2)]
                    total = total + jnp.sum(
                        jnp.where(inside, values, 0.0), axis=0, keepdims=True
                    )
                if t + 1 == BUCKETS:
                    total = total + jnp.sum(r.near[h, :, 0:TILE], axis=0, keepdims=True)
                r.sums[t : t + 1] = total
            r.g_rel[h] = lax.dot_general(
                jnp.ones((8, TILE), F32),
                r.sums[...],
                (((1,), (1,)), ((), ())),
                precision=lax.Precision.HIGHEST,
                preferred_element_type=F32,
            )

        loop(2, per_head)

    def update_tile(m):
        def step(t):
            rows = tile_of(t)
            for h in range(2):
                cols, k_cols, v_cols = head(h), head(h, base=256), head(h, base=512)
                grad = r.grad_after[m, rows, cols].astype(F32)
                u = r.update.ref[m, rows, cols]
                inverse = inverse_rms(u)
                unit = u * inverse
                forget = jax.nn.sigmoid(r.bias[:, cols] + r.slope[:, cols] * unit)
                gate = grad * (r.prior.ref[m, rows, cols].astype(F32) - unit)
                gate = gate * forget * (1.0 - forget)
                r.g_bias[:, cols] += jnp.sum(gate, axis=0, keepdims=True)
                r.g_scale[:, cols] += jnp.sum(gate * unit, axis=0, keepdims=True)
                grad_unit = grad * (1.0 - forget) + gate * r.slope[:, cols]
                inner = jnp.mean(grad_unit * unit, axis=-1, keepdims=True)
                low = (inverse * (grad_unit - unit * inner)).astype(BF)
                q = r.state_query.ref[rows, cols]
                probs = jnp.exp(nt(q, qkv[m, :, k_cols]) * scale - stats[m, rows, h : h + 1])
                grad_probs = nt(low, qkv[m, :, v_cols])
                delta = jnp.sum(probs * grad_probs, axis=-1, keepdims=True)
                grad_scores = (probs * (grad_probs - delta)).astype(BF)
                r.g_query[rows, cols] += scale * nn(grad_scores, qkv[m, :, k_cols])
                r.grad_kv[m, 512:1024, cols] += tn(grad_scores, q)
                r.grad_kv[m, 512:1024, head(h, base=256)] += tn(probs.astype(BF), low)

        return step

    def finish_rows(m):
        def step(t):
            rows = tile_of(t)
            full = r.grad_kv[m, pl.ds(pl.multiple_of(512 + t * TILE, TILE), TILE)]
            extra = r.later[m, rows].astype(F32)
            at = own_chunk(t)
            r.dqkv[m, at, :, 256:512] = (scale * full[:, 0:256] + extra[:, 0:256]).astype(BF)
            r.dqkv[m, at, :, 512:768] = (full[:, 256:512] + extra[:, 256:512]).astype(BF)

        return step

    ones = jnp.ones((8, 256), BF)

    def gain_row(part, p, rows):
        product = part * r.w.ref[p, rows].astype(F32)
        high = product.astype(BF)
        low = (product - high.astype(F32)).astype(BF)
        return (nt(ones, high) + nt(ones, low))[0:1]

    def weight_part(p, rows):
        whole, cols = r.whole.ref, slice(p * 256, (p + 1) * 256)
        part = tn(whole[0, :, :, rows].reshape(512, 256), r.dqkv[0, :, :, cols].reshape(512, 256))
        return part + tn(
            whole[1, :, :, rows].reshape(512, 256), r.dqkv[1, :, :, cols].reshape(512, 256)
        )

    def early_weights(n):
        rows = tile_of(n, 256)
        part = tn(r.att_rel.ref[0].reshape(512, 256), gm[0][:, :, rows].reshape(512, 256))
        part = part + tn(r.att_rel.ref[1].reshape(512, 256), gm[1][:, :, rows].reshape(512, 256))
        r.parts_a[rows, 256:512] = part.astype(BF)
        part = weight_part(0, rows)
        r.parts_a[rows, 0:256] = part.astype(BF)
        r.small[pl.ds(n, 1)] = gain_row(part, 0, rows)

    def end_terms(m):
        def columns(n):
            cols = tile_of(n, 256)
            part = nt(r.dqkv[m, :, :, 0:256].reshape(512, 256), r.w.ref[0, cols])
            for p in (1, 2):
                some = r.dqkv[m, :, :, p * 256 : (p + 1) * 256].reshape(512, 256)
                part = part + nt(some, r.w.ref[p, cols])
            part = part.astype(BF)
            split_rows(branch, m, cols, part)

        loop(4, columns)

    def late_weights(n):
        rows = tile_of(n, 256)
        total = r.small[pl.ds(n, 1)]
        for p in (1, 2):
            part = weight_part(p, rows)
            r.parts_b[rows, (p - 1) * 256 : p * 256] = part.astype(BF)
            total = total + gain_row(part, p, rows)
        r.small[pl.ds(n, 1)] = total / r.attn_gain[:, rows]

    def end_rows(m):
        grad_normed = ends[m].finish()
        rows = r.x.ref[m].astype(F32)
        inverse = inverse_rms(rows)
        unit = rows * inverse
        scaled = grad_normed * r.attn_gain[...]
        inner = jnp.mean(scaled * unit, axis=-1, keepdims=True)
        r.grad_x.ref[m] = r.grad_middle[m] + inverse * (scaled - unit * inner)

    def share(i):
        k, c = i // 2 + 1, i % 2
        slot = (3 - k) * 2 + core
        return remote(
            r.parts_b.at[768:784, 512:768],
            r.others.at[slot],
            r.s3.at[i],
            r.r3.at[slot],
            others[i],
        )

    def got(i):
        return remote(
            r.parts_b.at[768:784, 512:768], r.others.at[i], r.s3.at[i], r.r3.at[i], others[i]
        )

    def add_gains():
        for i in range(6):
            got(i).wait_recv()
        total = r.others[0].astype(F32)
        for i in range(1, 6):
            total = total + r.others[i].astype(F32)
        row = lax.broadcasted_iota(jnp.int32, (16, 256), 0)
        total = jnp.where(row < 8, total, 0.0) * core.astype(F32)
        at = slice(256, 272), slice(512, 768)
        r.half_b[at] = (r.half_b[at].astype(F32) + total).astype(BF)

    core_a = CoreSum(plane, r.parts_a, r.half_a)
    sum_a = PlaneReduce(plane, r.half_a, r.total_a, r.a_mid, r.a_into, r.a_quarter, r.a_small)
    all_a = PlaneGather(plane, r.total_a)
    core_b = CoreSum(plane, r.parts_b, r.half_b)
    sum_b = PlaneReduce(plane, r.half_b, r.total_b, r.b_mid, r.b_into, r.b_quarter, r.b_small)
    all_b = PlaneGather(plane, r.total_b)

    attention_rows(0)
    fourth.relay()
    for part in (r.half, r.qkv, r.kv_all, r.state_kv, r.stats, r.table):
        part.get()
    mlp_sum.advance()
    loop(4, attend(0))
    r.prior.get()
    r.state_proj.get()
    pass_on(0)
    mlp_sum.advance()
    fourth.finish()
    attention_rows(1)
    r.branch.get()
    outs[0].start()

    def between():
        mlp_sum.advance()
        outs[0].relay()
        outs[1].start()

    loop(4, attend(1), 1, between)
    pass_on(1)
    outs[1].relay()
    r.across.get()
    r.keeps.get()
    there[0].finish()
    scan(0)
    back[0].start()
    mlp_sum.advance()
    r.att_rel.get()
    r.w.get()
    r.whole.get()
    loop(4, early_weights)
    core_a.start()
    there[1].finish()
    scan(1)
    back[1].start()
    bucket_sums()
    core_a.finish()
    r.middle.get()
    for m in both:
        r.out.ref[m] = r.middle.ref[m] + outs[m].finish()
    r.out.put()
    r.update.get()
    r.state_query.get()
    for m in both:
        outs[m].close()
    back[0].finish()
    mlp_all.advance()
    loop(4, update_tile(0))
    shifts[0].wait_recv()
    loop(4, finish_rows(0))
    end_terms(0)
    ends[0].start()
    back[1].finish()
    mlp_all.advance()
    loop(4, update_tile(1))
    shifts[1].wait_recv()
    loop(4, finish_rows(1))
    ends[0].relay()
    mlp_all.advance()
    loop(4, late_weights)
    for n in range(4):
        r.small[4 + n : 5 + n] = r.g_mlp_gain[:, n * 256 : (n + 1) * 256]
    r.small[8:9] = r.g_bias[...]
    r.small[9:10] = r.g_scale[...]
    r.small[10:11] = r.g_rel[0, 0:1]
    r.small[11:12] = r.g_rel[1, 0:1]
    r.small[12:16] = jnp.zeros((4, 256), F32)
    r.parts_b[0:512, 512:768] = r.g_query[...].astype(BF)
    r.parts_b[512:768, 512:768] = r.g_proj[...].reshape(256, 256).astype(BF)
    r.parts_b[768:784, 512:768] = r.small[...].astype(BF)
    r.parts_b[784:1024, 512:768] = jnp.zeros((240, 256), BF)
    core_b.start()
    for i in range(6):
        share(i).start()
    sum_a.advance()
    mlp_all.advance()
    end_terms(1)
    ends[1].start()
    core_b.finish()
    add_gains()
    sum_b.advance()
    sum_a.advance()
    r.x.get()
    end_rows(0)
    sum_b.advance()
    ends[1].relay()
    mlp_all.advance()
    r.total_mlp.put()
    sum_a.advance()
    sum_b.advance()
    sum_a.advance()
    all_a.advance()
    sum_b.advance()
    all_b.advance()
    all_a.advance()
    all_b.advance()
    end_rows(1)
    r.grad_x.put()
    all_a.advance()
    all_b.advance()
    all_a.advance()
    all_b.advance()
    all_a.advance()
    all_b.advance()
    for step in (mlp_sum, mlp_all, core_a, sum_a, all_a, core_b, sum_b, all_b, fourth):
        step.close()
    for i in range(6):
        share(i).wait_send()
    for m in both:
        ends[m].close()
        shifts[m].wait_send()
        there[m].close()
        back[m].close()


class Late:
    def __init__(self, source, ref, sem):
        self.ref = ref
        self.copy = pltpu.make_async_copy(source, ref, sem)
        self.copy.start()
        self.open = True

    def get(self):
        if self.open:
            self.copy.wait()
            self.open = False


class Early:
    def __init__(self, target, ref, sem):
        self.ref = ref
        self.copy = pltpu.make_async_copy(ref, target, sem)
        self.sent = False

    def put(self):
        self.copy.start()
        self.sent = True


def call(kernel, name, number, now, late, small, outs, early, scratch, semaphores):
    anywhere = pl.BlockSpec(memory_space=pl.ANY)
    in_names = list(now) + list(small) + list(late)
    out_names = list(outs) + list(early)
    own = [a.shape for a in late.values()], [a.dtype for a in late.values()]
    buffers = list(zip(*own)) + list(early.values()) + list(scratch.values())

    def run(*refs):
        n, o = len(in_names), len(out_names)
        r = types.SimpleNamespace()
        held = refs[n + o : n + o + len(buffers)]
        rest = refs[n + o + len(buffers) :]
        fetch, store = rest[0], rest[1]
        for key, ref in zip(in_names[: len(now) + len(small)], refs):
            setattr(r, key, ref)
        for i, key in enumerate(late):
            setattr(r, key, Late(refs[len(now) + len(small) + i], held[i], fetch.at[i]))
        for key, ref in zip(outs, refs[n:]):
            setattr(r, key, ref)
        stores = []
        for i, key in enumerate(early):
            result = Early(refs[n + len(outs) + i], held[len(late) + i], store.at[i])
            setattr(r, key, result)
            stores.append(result)
        for key, ref in zip(scratch, held[len(late) + len(early) :]):
            setattr(r, key, ref)
        for key, ref in zip(semaphores, rest[2:]):
            setattr(r, key, ref)
        kernel(r)
        for result in stores:
            if not result.sent:
                result.put()
            result.copy.wait()

    shapes = list(outs.values()) + list(early.values())
    results = pl.pallas_call(
        run,
        out_shape=tuple(jax.ShapeDtypeStruct(shape, kind) for shape, kind in shapes),
        in_specs=[VMEM] * len(now) + [SMEM] * len(small) + [anywhere] * len(late),
        out_specs=tuple([VMEM] * len(outs) + [anywhere] * len(early)),
        scratch_shapes=[pltpu.VMEM(shape, kind) for shape, kind in buffers]
        + [sems(max(1, len(late))), sems(max(1, len(early)))]
        + list(semaphores.values()),
        compiler_params=pltpu.CompilerParams(
            collective_id=number, has_side_effects=True, vmem_limit_bytes=LIMIT
        ),
        name=name,
    )(*now.values(), *small.values(), *late.values())
    return dict(zip(out_names, results))


def finish_kernel(total_a, total_b, g_mlp, out, grad_x, state, *refs):
    results, (wide, low, some_a, some_b, rows_in, states_in, fetch, store) = refs[:14], refs[14:]
    places = [rows_in.at[0], rows_in.at[1], states_in]
    taken = [
        pltpu.make_async_copy(a, b, fetch.at[12 + i])
        for i, (a, b) in enumerate(zip((out, grad_x, state), places))
    ]
    passed = [
        pltpu.make_async_copy(a, b, store.at[i])
        for i, (a, b) in enumerate(zip(places, results[:3]))
    ]
    g_up, g_down, g_qkv, g_out, g_query, g_proj = results[3:9]
    attn_gain, mlp_gain, bias, slope, rel = results[9:]
    loads = []
    for n in range(4):
        rows = slice(n * 256, (n + 1) * 256)
        loads.append(
            [
                pltpu.make_async_copy(a.at[rows], b.at[rows], fetch.at[3 * n + i])
                for i, (a, b) in enumerate(((g_mlp, low), (total_a, some_a), (total_b, some_b)))
            ]
        )
    for copy in sum(loads, []) + taken:
        copy.start()
    stores = []

    def put(value, at, target):
        wide[at] = value.astype(F32)
        copy = pltpu.make_async_copy(wide.at[at], target, store.at[3 + len(stores)])
        copy.start()
        stores.append(copy)

    for n in range(4):
        rows = slice(n * 256, (n + 1) * 256)
        for copy in loads[n]:
            copy.wait()
        put(low[rows, 0:1024], (rows, slice(0, 1024)), g_up.at[rows])
        put(low[rows, 1024:2048], (rows, slice(1024, 2048)), g_down.at[rows])
        put(some_a[rows, 0:256], (rows, slice(2048, 2304)), g_qkv.at[0, rows])
        put(some_b[rows, 0:256], (rows, slice(2304, 2560)), g_qkv.at[1, rows])
        put(some_b[rows, 256:512], (rows, slice(2560, 2816)), g_qkv.at[2, rows])
        put(some_a[rows, 256:512], (rows, slice(2816, 3072)), g_out.at[:, rows])
    put(some_b[0:512, 512:768], (slice(0, 512), slice(3072, 3328)), g_query)
    put(some_b[512:768, 512:768], (slice(512, 768), slice(3072, 3328)), g_proj)
    for into, copy in zip(taken, passed):
        into.wait()
        copy.start()
    small = some_b[768:784, 512:768].astype(F32)
    attn_gain[...] = jnp.concatenate([small[n : n + 1] for n in range(4)], 1)
    mlp_gain[...] = jnp.concatenate([small[n : n + 1] for n in range(4, 8)], 1)
    bias[...] = small[8:9]
    slope[...] = small[9:10]
    rel[...] = small[10:12, 0:BUCKETS]
    for copy in stores + passed:
        copy.wait()


def sems(*shape):
    return pltpu.SemaphoreType.DMA(shape)


def body(
    tokens_in,
    grad_out,
    flags,
    attn_gain,
    mlp_gain,
    w_qkv,
    w_out,
    rel_bias,
    state_query,
    state_proj,
    forget_bias,
    forget_scale,
    w_up,
    w_down,
):
    micros, rows, width = tokens_in.shape
    block = rows * 4
    local = w_qkv.shape[2]
    heads = rel_bias.shape[1]
    states = state_query.shape[0]
    buckets = rel_bias.shape[0]
    count = lax.axis_size("blk")
    w = jnp.transpose(w_qkv, (1, 0, 2))
    small = dict(flags=jnp.transpose(flags))
    whole_shape = ((micros, 4, rows, width), BF)
    state_low = ((micros, states, local), BF)
    state_wide = ((micros, states, local), F32)
    rows_wide = ((micros, rows, width), F32)
    mlp_width = w_up.shape[1] + w_down.shape[1]
    exchange = dict(
        s0=sems(2),
        r0=sems(2),
        s1=sems(2),
        r1=sems(2),
        s2=sems(2),
        r2=sems(2),
        local=sems(4),
    )
    gates = dict(bias=forget_bias[None], slope=forget_scale[None])
    f = call(
        forward_kernel,
        "forward",
        1,
        dict(
            x=tokens_in,
            attn_gain=attn_gain[None],
            mlp_gain=mlp_gain[None],
            **gates,
        ),
        dict(
            w=w,
            state_query=state_query,
            g=grad_out,
            state_proj=state_proj,
            w_out=w_out,
            w_up=w_up,
            w_down=w_down,
        ),
        dict(rel=jnp.transpose(rel_bias), **small),
        dict(
            grad_middle=rows_wide,
            gm0=((4, rows, width), BF),
            g_gain=((1, width), F32),
        ),
        dict(
            whole=whole_shape,
            qkv=((micros, block, 3 * local), BF),
            kv_all=((micros, 2 * block, 2 * local), BF),
            state_kv=((micros, states, 2 * local), BF),
            prior=state_low,
            across=state_low,
            keeps=((count, 8, local), F32),
            update=state_wide,
            stats=((micros, block, TILE), F32),
            table=((heads, TILE, 5 * TILE), F32),
            state_after=state_wide,
            att_rel=((micros, 4, rows, local), BF),
            middle=rows_wide,
            branch=whole_shape,
            half=((512, mlp_width), BF),
        ),
        dict(
            whole_grad=whole_shape,
            own_keep=((count, 8, local), F32),
            unit_low=state_low,
            held=state_low,
            terms=whole_shape,
            whole_mlp=whole_shape,
            active=((micros, block, w_up.shape[1]), BF),
            grad_hidden=((micros, block, w_up.shape[1]), BF),
            mids=((4, 4, rows // 2, width), BF),
            intos=((4, 2, rows, width), BF),
            parts=((width, mlp_width), BF),
        ),
        dict(send=sems(80), recv=sems(80), s3=sems(1), r3=sems(1), **exchange),
    )
    b = call(
        backward_kernel,
        "backward",
        2,
        dict(
            gm0=f["gm0"],
            grad_middle=f["grad_middle"],
            w_out=w_out,
            attn_gain=attn_gain[None],
            g_mlp_gain=f["g_gain"],
            **gates,
        ),
        dict(
            half=f["half"],
            qkv=f["qkv"],
            kv_all=f["kv_all"],
            state_kv=f["state_kv"],
            stats=f["stats"],
            table=f["table"],
            branch=f["branch"],
            prior=f["prior"],
            state_proj=state_proj,
            across=f["across"],
            keeps=f["keeps"],
            att_rel=f["att_rel"],
            middle=f["middle"],
            update=f["update"],
            state_query=state_query,
            w=w,
            whole=f["whole"],
            x=tokens_in,
        ),
        small,
        dict(
            total_a=((width, 512), BF),
            total_b=((width, 768), BF),
        ),
        dict(out=rows_wide, grad_x=rows_wide, total_mlp=((width, mlp_width), BF)),
        dict(
            dqkv=((micros, 4, rows, 3 * local), BF),
            g_query=((states, local), F32),
            g_proj=(state_proj.shape, F32),
            g_rel=((heads, 8, local), F32),
            g_bias=((1, local), F32),
            g_scale=((1, local), F32),
            grad_att=((micros, block, local), BF),
            grad_kv=((micros, 2 * block, 2 * local), F32),
            grad_state=((micros, states, 2 * local), F32),
            early=((micros, block, 2 * local), BF),
            later=((micros, block, 2 * local), BF),
            grad_prior=state_low,
            moved=state_low,
            held=state_low,
            grad_after=state_low,
            near=((heads, TILE, 3 * TILE), F32),
            sums=((local, TILE), F32),
            mids=((4, 4, rows // 2, width), BF),
            intos=((4, 2, rows, width), BF),
            others=((6, 16, local), BF),
            small=((16, local), F32),
            gm1=((4, rows, width), BF),
            parts_a=((width, 512), BF),
            half_a=((512, 512), BF),
            parts_b=((width, 768), BF),
            half_b=((512, 768), BF),
            **reduce_scratch("mlp_", mlp_width),
            **reduce_scratch("a_", 512),
            **reduce_scratch("b_", 768),
        ),
        dict(send=sems(150), recv=sems(150), s3=sems(6), r3=sems(6), **exchange),
    )
    results = [
        rows_wide[0],
        rows_wide[0],
        state_wide[0],
        w_up.shape,
        w_down.shape,
        w.shape,
        w_out.shape,
        state_query.shape,
        (heads * state_proj.shape[1], local),
        (1, width),
        (1, width),
        (1, local),
        (1, local),
        (heads, buckets),
    ]
    anywhere = pl.BlockSpec(memory_space=pl.ANY)
    values = pl.pallas_call(
        finish_kernel,
        out_shape=tuple(jax.ShapeDtypeStruct(shape, F32) for shape in results),
        in_specs=[anywhere] * 6,
        out_specs=tuple([anywhere] * 9 + [VMEM] * 5),
        scratch_shapes=[
            pltpu.VMEM((width, 3328), F32),
            pltpu.VMEM((width, mlp_width), BF),
            pltpu.VMEM((width, 512), BF),
            pltpu.VMEM((width, 768), BF),
            pltpu.VMEM((2,) + rows_wide[0], F32),
            pltpu.VMEM(state_wide[0], F32),
            sems(15),
            sems(32),
        ],
        compiler_params=pltpu.CompilerParams(vmem_limit_bytes=LIMIT),
        name="finish",
    )(b["total_a"], b["total_b"], b["total_mlp"], b["out"], b["grad_x"], f["state_after"])
    out, grad_x, state_after, g_up, g_down, g_qkv, g_out, g_query, g_proj = values[:9]
    g_attn_gain, g_mlp_gain, g_bias, g_scale, g_rel = values[9:]
    return (
        out,
        grad_x,
        state_after[:, None],
        g_attn_gain[0],
        g_mlp_gain[0],
        jnp.transpose(g_qkv, (1, 0, 2)),
        g_out,
        jnp.transpose(g_rel),
        g_query,
        g_proj.reshape(state_proj.shape),
        g_bias[0],
        g_scale[0],
        g_up,
        g_down,
    )


def solution(mesh):
    return jax.shard_map(
        body,
        mesh=mesh,
        in_specs=(
            P(None, ("blk", "head"), None),
            P(None, ("blk", "head"), None),
            P(None, "blk"),
            P(),
            P(),
            P(None, None, "head"),
            P("head", None),
            P(None, "head"),
            P(None, "head"),
            P("head", None, None),
            P("head"),
            P("head"),
            P(None, "head"),
            P("head", None),
        ),
        out_specs=(
            P(None, ("blk", "head"), None),
            P(None, ("blk", "head"), None),
            P(None, "blk", None, "head"),
            P(),
            P(),
            P(None, None, "head"),
            P("head", None),
            P(None, "head"),
            P(None, "head"),
            P("head", None, None),
            P("head"),
            P("head"),
            P(None, "head"),
            P("head", None),
        ),
        check_vma=False,
    )
```

```python
import math
import types

import jax
import jax.numpy as jnp
from jax import lax
from jax.experimental import pallas as pl
from jax.experimental.pallas import tpu as pltpu
from jax.sharding import PartitionSpec as P

BUCKETS = 32
MAXDIST = 128
EPSILON = 1e-06
MASKED = -1e30
TILE = 128
MESH = pl.DeviceIdType.MESH
BF = jnp.bfloat16
F32 = jnp.float32
VMEM = pl.BlockSpec(memory_space=pltpu.VMEM)
SMEM = pl.BlockSpec(memory_space=pltpu.SMEM)
LIMIT = 60 * 2**20
ROOT = math.sqrt(2.0 / math.pi)
CUBIC = 0.044715


def bucket_starts():
    exact = BUCKETS // 2
    levels = [
        int(math.ceil(exact * (MAXDIST / exact) ** (t / (BUCKETS - exact))))
        for t in range(1, BUCKETS - exact)
    ]
    return list(range(exact + 1)) + levels


STARTS = bucket_starts()


def nn(a, b):
    return lax.dot_general(a, b, (((1,), (0,)), ((), ())), preferred_element_type=F32)


def nt(a, b):
    return lax.dot_general(a, b, (((1,), (1,)), ((), ())), preferred_element_type=F32)


def tn(a, b):
    return lax.dot_general(a, b, (((0,), (0,)), ((), ())), preferred_element_type=F32)


def inverse_rms(values):
    return lax.rsqrt(jnp.mean(values * values, axis=-1, keepdims=True) + EPSILON)


def tile_of(index, size=TILE):
    return pl.ds(pl.multiple_of(index * size, size), size)


def loop(count, step, after=None, action=None):
    def run(i, c):
        step(i)
        return c

    if after is not None:
        lax.fori_loop(0, after + 1, run, 0)
        action()
    lax.fori_loop(0 if after is None else after + 1, count, run, 0)


def remote(src, dst, send_sem, recv_sem, device):
    return pltpu.make_async_remote_copy(
        src_ref=src,
        dst_ref=dst,
        send_sem=send_sem,
        recv_sem=recv_sem,
        device_id=device,
        device_id_type=MESH,
    )


class Links:
    def __init__(self, send, recv):
        self.send, self.recv, self.used = send, recv, 0

    def go(self, src, dst, device):
        copy = remote(src, dst, self.send.at[self.used], self.recv.at[self.used], device)
        self.used += 1
        copy.start()
        return copy


class Ring:
    def __init__(self, links, me, device):
        self.links, self.me = links, me
        self.right = device(lax.rem(me + 1, 4))
        self.left = device(lax.rem(me + 3, 4))
        self.opposite = device(lax.rem(me + 2, 4))

    def go(self, src, dst, peer):
        return self.links.go(src, dst, peer)

    def greet(self):
        barrier = pltpu.get_barrier_semaphore()
        for peer in (self.right, self.left):
            pl.semaphore_signal(barrier, inc=1, device_id=peer, device_id_type=MESH)
        return 2

    def chunk(self, k):
        return lax.rem(self.me + k, 4)

    def row_chunk(self, k):
        return tile_of(self.chunk(k))


def head_ring(links):
    return Ring(links, lax.axis_index("head"), lambda i: {"head": i})


def by_rows(buf):
    half = buf.shape[1] // 2

    def piece(k, part=None, offset=0):
        return buf.at[k] if part is None else buf.at[k, part * half : (part + 1) * half]

    return piece


def by_columns(buf, base, rows, chunk):
    half = buf.shape[1] // 2
    starts = [pl.multiple_of(base + chunk(k) * rows, rows) for k in range(4)]

    def piece(k, part=None, offset=0):
        at = pl.ds(starts[(k + offset) % 4], rows)
        return buf.at[at] if part is None else buf.at[at, part * half : (part + 1) * half]

    return piece


class Gather:
    def __init__(self, ring, piece):
        self.ring, self.piece = ring, piece

    def start(self):
        r, p = self.ring, self.piece
        self.a0 = r.go(p(0, 0), p(3, 0, 1), r.right)
        self.b0 = r.go(p(0, 1), p(1, 1, 3), r.left)
        self.a1 = r.go(p(0, 1), p(3, 1, 1), r.right)
        self.b1 = r.go(p(0, 0), p(1, 0, 3), r.left)

    def relay(self):
        r, p = self.ring, self.piece
        self.a0.wait_recv()
        self.a2 = r.go(p(3, 0), p(2, 0, 1), r.right)
        self.b0.wait_recv()
        self.b2 = r.go(p(1, 1), p(2, 1, 3), r.left)

    def finish(self):
        for copy in (self.a1, self.b1, self.a2, self.b2):
            copy.wait_recv()

    def close(self):
        for copy in (self.a0, self.b0, self.a1, self.b1, self.a2, self.b2):
            copy.wait_send()


class Reduce:
    def __init__(self, ring, terms, mid, into):
        self.ring, self.terms, self.mid, self.into = ring, terms, mid, into
        if mid.shape[1] == into.shape[1]:
            half = into.shape[2] // 2
            self.place = lambda i, part: into.at[i, :, part * half : (part + 1) * half]
        else:
            half = into.shape[1] // 2
            self.place = lambda i, part: into.at[i, part * half : (part + 1) * half]

    def start(self):
        r, t = self.ring, self.terms
        self.a0 = r.go(t(2, 0), self.mid.at[0], r.right)
        self.b0 = r.go(t(2, 1), self.mid.at[1], r.left)
        self.a1 = r.go(t(1, 1), self.place(0, 1), r.right)
        self.b1 = r.go(t(3, 0), self.place(1, 0), r.left)

    def relay(self):
        r, t, mid = self.ring, self.terms, self.mid
        self.a0.wait_recv()
        mid[2] = (mid[0].astype(F32) + t(1, 0)[...].astype(F32)).astype(BF)
        self.a2 = r.go(mid.at[2], self.place(0, 0), r.right)
        self.b0.wait_recv()
        mid[3] = (mid[1].astype(F32) + t(3, 1)[...].astype(F32)).astype(BF)
        self.b2 = r.go(mid.at[3], self.place(1, 1), r.left)

    def finish(self):
        for copy in (self.a1, self.b1, self.a2, self.b2):
            copy.wait_recv()
        return (
            self.terms(0)[...].astype(F32)
            + self.into[0].astype(F32)
            + self.into[1].astype(F32)
        )

    def close(self):
        for copy in (self.a0, self.b0, self.a1, self.b1, self.a2, self.b2):
            copy.wait_send()


def block_device(x, z, c):
    return {"blk": (x * 4 + z) * 2 + c}


def block_place():
    place = lax.axis_index("blk")
    return place % 2, (place // 2) % 4, place // 8


class Plane:
    def __init__(self, links):
        c, z, x = block_place()
        self.links = links
        self.peer = block_device(x, z, 1 - c)
        rx = Ring(links, x, lambda i: block_device(i, z, c))
        rz = Ring(links, z, lambda i: block_device(x, i, c))
        self.rings = [rx, rz]
        self.first, self.second = (rx, rz), (rz, rx)
        self.base = c * 512
        self.own = pl.ds(pl.multiple_of(c * 512, 512), 512)
        self.away = pl.ds(pl.multiple_of((1 - c) * 512, 512), 512)
        self.top = [c * 512 + x * 64, c * 512 + 256 + z * 64]
        self.last = [
            pl.ds(pl.multiple_of(self.top[0] + z * 16, 16), 16),
            pl.ds(pl.multiple_of(self.top[1] + x * 16, 16), 16),
        ]

    def greet(self):
        barrier = pltpu.get_barrier_semaphore()
        pl.semaphore_signal(barrier, inc=1, device_id=self.peer, device_id_type=MESH)
        return 1 + sum(ring.greet() for ring in self.rings)


class Steps:
    def advance(self, steps=1):
        for _ in range(steps):
            if self.steps:
                self.steps.pop(0)()


class CoreSum:
    def __init__(self, plane, parts, half):
        self.plane, self.parts, self.half = plane, parts, half

    def start(self):
        plane = self.plane
        self.swap = plane.links.go(self.parts.at[plane.away], self.half, plane.peer)

    def finish(self):
        self.swap.wait_recv()

        def add(t):
            rows = tile_of(t, 64)
            own = pl.ds(pl.multiple_of(self.plane.base + t * 64, 64), 64)
            self.half[rows] = (
                self.parts[own].astype(F32) + self.half[rows].astype(F32)
            ).astype(BF)

        loop(8, add)

    def close(self):
        self.swap.wait_send()


class PlaneReduce(Steps):
    def __init__(self, plane, half, total, mid, into, quarter, small_into):
        self.plane, self.half, self.total, self.quarter = plane, half, total, quarter
        first, second = plane.first, plane.second
        self.reduce1 = [
            Reduce(first[i], by_columns(half, i * 256, 64, first[i].chunk), mid.at[i], into.at[i])
            for i in range(2)
        ]
        self.reduce2 = [
            ReduceDirect(
                second[i], by_columns(quarter.at[i], 0, 16, second[i].chunk), small_into.at[i]
            )
            for i in range(2)
        ]
        self.steps = [
            lambda: [r.start() for r in self.reduce1],
            lambda: [r.relay() for r in self.reduce1],
            self.start2,
            self.finish,
        ]

    def start2(self):
        for i, r in enumerate(self.reduce1):
            self.quarter[i] = r.finish().astype(BF)
            self.reduce2[i].start()

    def finish(self):
        for i, r in enumerate(self.reduce2):
            self.total[self.plane.last[i]] = r.finish().astype(BF)

    def close(self):
        for r in self.reduce1 + self.reduce2:
            r.close()


class PlaneGather(Steps):
    def __init__(self, plane, total):
        self.plane, self.total = plane, total
        first, second = plane.first, plane.second
        self.gather1 = [
            GatherDirect(second[i], by_columns(total, plane.top[i], 16, second[i].chunk))
            for i in range(2)
        ]
        self.gather2 = [
            Gather(first[i], by_columns(total, plane.base + i * 256, 64, first[i].chunk))
            for i in range(2)
        ]
        self.steps = [
            lambda: [g.start() for g in self.gather1],
            self.start2,
            lambda: [g.relay() for g in self.gather2],
            self.cores,
            lambda: self.swap.wait_recv(),
        ]

    def start2(self):
        for i, g in enumerate(self.gather1):
            g.finish()
            self.gather2[i].start()

    def cores(self):
        for g in self.gather2:
            g.finish()
        rows = self.total.at[self.plane.own]
        self.swap = self.plane.links.go(rows, rows, self.plane.peer)

    def close(self):
        self.swap.wait_send()
        for g in self.gather1 + self.gather2:
            g.close()


def reduce_scratch(name, width):
    return {
        name + "mid": ((2, 4, 64, width // 2), BF),
        name + "into": ((2, 2, 64, width), BF),
        name + "quarter": ((2, 64, width), BF),
        name + "small": ((2, 3, 16, width), BF),
    }


class GatherDirect:
    def __init__(self, ring, piece):
        self.ring, self.piece = ring, piece

    def start(self):
        r, p = self.ring, self.piece
        self.copies = [
            r.go(p(0), p(4 - k, None, k), peer)
            for k, peer in ((1, r.right), (3, r.left), (2, r.opposite))
        ]

    def finish(self):
        for copy in self.copies:
            copy.wait_recv()

    def close(self):
        for copy in self.copies:
            copy.wait_send()


class ReduceDirect:
    def __init__(self, ring, terms, into):
        self.ring, self.terms, self.into = ring, terms, into

    def start(self):
        r, t = self.ring, self.terms
        self.copies = [
            r.go(t(k), self.into.at[k - 1], peer)
            for k, peer in ((1, r.right), (3, r.left), (2, r.opposite))
        ]

    def finish(self):
        for copy in self.copies:
            copy.wait_recv()
        total = self.terms(0)[...].astype(F32)
        for k in range(3):
            total = total + self.into[k].astype(F32)
        return total

    def close(self):
        for copy in self.copies:
            copy.wait_send()


class Exchange:
    def __init__(self, source, target, send, recv, local):
        self.count = lax.axis_size("blk")
        self.place = lax.axis_index("blk")
        self.size = source.shape[0] // self.count
        self.source, self.target = source, target
        self.send, self.recv, self.local = send, recv, local

    def part(self, j):
        peer = lax.rem(self.place + j, self.count)
        return remote(
            self.source.at[tile_of(peer, self.size)],
            self.target.at[tile_of(self.place, self.size)],
            self.send,
            self.recv,
            {"blk": peer},
        )

    def all(self):
        rows = slice(0, (self.count - 1) * self.size)
        return remote(
            self.source.at[rows],
            self.target.at[rows],
            self.send,
            self.recv,
            {"blk": lax.rem(self.place + 1, self.count)},
        )

    def own(self):
        rows = tile_of(self.place, self.size)
        return pltpu.make_async_copy(self.source.at[rows], self.target.at[rows], self.local)

    def start(self):
        loop(self.count - 1, lambda j: self.part(j + 1).start())
        self.own().start()

    def finish(self):
        self.own().wait()
        self.all().wait_recv()

    def close(self):
        self.all().wait_send()


def greet_blocks():
    barrier = pltpu.get_barrier_semaphore()
    count, place = lax.axis_size("blk"), lax.axis_index("blk")

    def greet(j):
        pl.semaphore_signal(
            barrier, inc=1, device_id={"blk": lax.rem(place + j + 1, count)}, device_id_type=MESH
        )

    loop(count - 1, greet)
    return count - 1


def closed_row(flag, qi):
    column = lax.broadcasted_iota(jnp.int32, (1, 5 * TILE), 1) + qi * TILE
    return jnp.where(column < 512, MASKED * flag.astype(F32), 0.0)


def head(h, size=TILE, base=0):
    return slice(base + h * size, base + (h + 1) * size)


def window_of(qi):
    return pl.ds(pl.multiple_of(qi * TILE, TILE), 5 * TILE)


def split_rows(target, m, cols, part):
    for k in range(4):
        target[m, k, :, cols] = part[k * TILE : (k + 1) * TILE]


def write_table(table, rel):
    row = lax.broadcasted_iota(jnp.int32, (TILE, TILE), 0)
    col = lax.broadcasted_iota(jnp.int32, (TILE, TILE), 1)

    def per_head(h):
        far = jnp.full((TILE, TILE), rel[h, BUCKETS - 1], F32)
        table[h, :, 0:128] = jnp.where(row < col, far, MASKED)
        table[h, :, 128:256] = far
        table[h, :, 256:384] = far
        for shift, at in ((TILE, 384), (0, 512)):
            distance = row - col + shift
            total = jnp.full((TILE, TILE), rel[h, 0], F32)
            for t in range(1, BUCKETS):
                total = jnp.where(distance >= STARTS[t], rel[h, t], total)
            table[h, :, at : at + TILE] = jnp.where(distance >= 0, total, MASKED)

    loop(2, per_head)


def forward_kernel(r):
    scale = TILE**-0.5
    links = Links(r.send, r.recv)
    ring = head_ring(links)
    plane = Plane(links)
    place, count = lax.axis_index("blk"), lax.axis_size("blk")
    both = range(2)

    def norm_rows(m):
        rows = r.x[m].astype(F32)
        r.whole.ref[m, 0] = (rows * inverse_rms(rows) * r.attn_gain[...]).astype(BF)

    greeted = ring.greet() + greet_blocks()
    norm_rows(0)
    for m in both:
        keep = 1.0 - r.flags[0, m].astype(F32)
        r.own_keep[0, m : m + 1] = jnp.full((1, 256), keep, F32)
    r.own_keep[0, 2:8] = jnp.zeros((6, 256), F32)
    pl.semaphore_wait(pltpu.get_barrier_semaphore(), greeted)
    whole, qkv, kv_all = r.whole.ref, r.qkv.ref, r.kv_all.ref
    prior, across, keeps = r.prior.ref, r.across.ref, r.keeps.ref
    update, stats, state_kv = r.update.ref, r.stats.ref, r.state_kv.ref
    table, att_rel, middle, branch = r.table.ref, r.att_rel.ref, r.middle.ref, r.branch.ref
    gather_x = [Gather(ring, by_rows(whole.at[m])) for m in both]
    gather_g = [Gather(ring, by_rows(r.whole_grad.at[m])) for m in both]
    gather_x[0].start()
    norm_rows(1)

    def tell(j):
        peer = {"blk": lax.rem(place + j, count)}
        return remote(r.own_keep.at[0], keeps.at[place], r.s3.at[0], r.r3.at[0], peer)

    def tell_all():
        peer = {"blk": lax.rem(place + 1, count)}
        rows = slice(0, count - 1)
        return remote(r.own_keep.at[rows], keeps.at[rows], r.s3.at[0], r.r3.at[0], peer)

    loop(count - 1, lambda j: tell(j + 1).start())
    keeps[place] = r.own_keep[0]
    write_table(table, r.rel)
    r.table.put()
    after = {"blk": lax.rem(place + 1, count)}
    shifts = [
        remote(qkv.at[m, :, 256:768], kv_all.at[m, 0:512], r.s0.at[m], r.r0.at[m], after)
        for m in both
    ]
    there = [
        Exchange(r.unit_low.at[m], across.at[m], r.s1.at[m], r.r1.at[m], r.local.at[m])
        for m in both
    ]
    back = [
        Exchange(r.held.at[m], prior.at[m], r.s2.at[m], r.r2.at[m], r.local.at[2 + m])
        for m in both
    ]

    def project(m):
        def columns(n):
            cols = tile_of(n, 256)
            part = nn(whole[m].reshape(512, 1024), r.w.ref[n]).astype(BF)
            for k in range(4):
                qkv[m, ring.row_chunk(k), cols] = part[k * TILE : (k + 1) * TILE]

        loop(3, columns)
        shifts[m].start()
        kv_all[m, 512:1024] = qkv[m, :, 256:768]

    def update_tile(m):
        def step(t):
            rows = tile_of(t)
            for h in range(2):
                scores = nt(r.state_query.ref[rows, head(h)], qkv[m, :, head(h, base=256)]) * scale
                top = jnp.max(scores, axis=-1, keepdims=True)
                raised = jnp.exp(scores - top)
                total = jnp.sum(raised, axis=-1, keepdims=True)
                stats[m, rows, h : h + 1] = top + jnp.log(total)
                u = nn(raised.astype(BF), qkv[m, :, head(h, base=512)]) / total
                update[m, rows, head(h)] = u
                r.unit_low[m, rows, head(h)] = (u * inverse_rms(u)).astype(BF)

        return step

    def scan(m):
        def step(g, state):
            for k in range(4):
                b = g * 4 + k
                rows = tile_of(b, 16)
                u = across[m, rows].astype(F32)
                forget = jax.nn.sigmoid(r.bias[...] + r.slope[...] * u)
                before = keeps[b, m : m + 1] * state
                r.held[m, rows] = before.astype(BF)
                state = forget * before + (1.0 - forget) * u
            return state

        lax.fori_loop(0, count // 4, step, jnp.zeros((16, 256), F32))

    def state(m):
        def step(t):
            rows = tile_of(t)
            before = prior[m, rows]
            for h in range(2):
                state_kv[m, rows, head(h, 256)] = nn(before[:, head(h)], r.state_proj.ref[h]).astype(BF)
                u = update[m, rows, head(h)]
                u = u * inverse_rms(u)
                forget = jax.nn.sigmoid(r.bias[:, head(h)] + r.slope[:, head(h)] * u)
                r.state_after.ref[m, rows, head(h)] = (
                    forget * before[:, head(h)].astype(F32) + (1.0 - forget) * u
                )

        return step

    def attend(m):
        def step(qi):
            rows, window = tile_of(qi), window_of(qi)
            shut = closed_row(r.flags[0, m], qi)
            for h in range(2):
                q = qkv[m, rows, head(h)]
                token = nt(q, kv_all[m, window, head(h)]) * scale + (table[h] + shut)
                from_state = nt(q, state_kv[m, :, h * 256 : h * 256 + TILE]) * scale
                top = jnp.maximum(
                    jnp.max(token, axis=-1, keepdims=True),
                    jnp.max(from_state, axis=-1, keepdims=True),
                )
                token = jnp.exp(token - top)
                from_state = jnp.exp(from_state - top)
                total = jnp.sum(token, axis=-1, keepdims=True) + jnp.sum(
                    from_state, axis=-1, keepdims=True
                )
                stats[m, rows, 2 + h : 3 + h] = top + jnp.log(total)
                out = nn(token.astype(BF), kv_all[m, window, head(h, base=256)]) + nn(
                    from_state.astype(BF), state_kv[m, :, h * 256 + TILE : (h + 1) * 256]
                )
                att_rel[m, lax.rem(qi + 4 - ring.me, 4), :, head(h)] = (out / total).astype(BF)

        return step

    first = [
        Reduce(ring, by_rows(r.terms.at[m]), r.mids.at[m], r.intos.at[m]) for m in both
    ]
    second = [Gather(ring, by_rows(r.whole_mlp.at[m])) for m in both]
    third = [
        Reduce(ring, by_rows(r.terms.at[m]), r.mids.at[2 + m], r.intos.at[2 + m]) for m in both
    ]
    fourth = Gather(ring, by_rows(r.gm0))

    def out_terms(m):
        def columns(n):
            cols = tile_of(n, 256)
            part = nn(att_rel[m].reshape(512, 256), r.w_out.ref[:, cols]).astype(BF)
            split_rows(r.terms, m, cols, part)

        loop(4, columns)

    def normalise(m):
        rows = r.x[m].astype(F32) + first[m].finish()
        middle[m] = rows
        r.whole_mlp[m, 0] = (rows * inverse_rms(rows) * r.mlp_gain[...]).astype(BF)

    def hidden(m):
        def columns(n):
            cols = tile_of(n, 256)
            value = nn(r.whole_mlp[m].reshape(512, 1024), r.w_up.ref[:, cols])
            grad_active = nt(r.whole_grad[m].reshape(512, 1024), r.w_down.ref[cols])
            square = value * value
            bent = jnp.tanh(ROOT * value * (1.0 + CUBIC * square))
            r.active[m, :, cols] = (0.5 * value * (1.0 + bent)).astype(BF)
            rise = 0.5 * (1.0 + bent) + 0.5 * value * (1.0 - bent * bent) * ROOT * (
                1.0 + 3.0 * CUBIC * square
            )
            r.grad_hidden[m, :, cols] = (grad_active * rise).astype(BF)

        return columns

    def grad_terms(m):
        def columns(n):
            cols = tile_of(n, 256)
            part = nt(r.grad_hidden[m], r.w_up.ref[cols]).astype(BF)
            split_rows(r.terms, m, cols, part)

        loop(4, columns)

    def branch_terms(m):
        def columns(n):
            cols = tile_of(n, 256)
            part = nn(r.active[m], r.w_down.ref[:, cols]).astype(BF)
            split_rows(branch, m, cols, part)

        loop(4, columns)

    def grad_rows(m):
        grad_normed = third[m].finish()
        rows = middle[m]
        inverse = inverse_rms(rows)
        unit = rows * inverse
        part = jnp.sum(grad_normed * unit, axis=0, keepdims=True)
        r.g_gain[...] = part if m == 0 else r.g_gain[...] + part
        scaled = grad_normed * r.mlp_gain[...]
        inner = jnp.mean(scaled * unit, axis=-1, keepdims=True)
        total = r.g.ref[m].astype(F32) + inverse * (scaled - unit * inner)
        r.grad_middle[m] = total
        if m == 0:
            r.gm0[0] = total.astype(BF)

    def up_rows(n):
        rows = tile_of(n, 256)
        total = tn(r.whole_mlp[0, :, :, rows].reshape(512, 256), r.grad_hidden[0])
        total = total + tn(r.whole_mlp[1, :, :, rows].reshape(512, 256), r.grad_hidden[1])
        r.parts[rows, 0:1024] = total.astype(BF)

    def down_rows(n):
        rows = tile_of(n, 256)
        total = tn(r.active[0, :, rows], r.whole_grad[0].reshape(512, 1024))
        total = total + tn(r.active[1, :, rows], r.whole_grad[1].reshape(512, 1024))
        r.parts[rows, 1024:2048] = total.astype(BF)

    cores = CoreSum(plane, r.parts, r.half.ref)

    gather_x[0].relay()
    gather_x[1].start()
    r.w.get()
    gather_x[0].finish()
    project(0)
    gather_x[1].relay()
    r.state_query.get()
    loop(4, update_tile(0))
    there[0].start()
    gather_x[1].finish()
    r.g.get()
    for m in both:
        r.whole_grad[m, 0] = r.g.ref[m]
    gather_g[0].start()
    project(1)
    r.whole.put()
    r.qkv.put()
    loop(4, update_tile(1))
    there[1].start()
    r.update.put()
    gather_g[0].relay()
    gather_g[1].start()
    tell_all().wait_recv()
    there[0].finish()
    scan(0)
    back[0].start()
    there[1].finish()
    scan(1)
    back[1].start()
    gather_g[1].relay()
    r.across.put()
    r.keeps.put()
    shifts[0].wait_recv()
    shifts[1].wait_recv()
    r.kv_all.put()
    r.state_proj.get()
    back[0].finish()
    loop(4, state(0))
    loop(4, attend(0))
    r.w_out.get()
    out_terms(0)
    first[0].start()
    back[1].finish()
    r.prior.put()
    loop(4, state(1))
    r.state_kv.put()
    r.state_after.put()
    loop(4, attend(1), 0, first[0].relay)
    r.stats.put()
    out_terms(1)
    r.att_rel.put()
    first[1].start()
    normalise(0)
    second[0].start()
    first[1].relay()
    second[0].relay()
    r.w_up.get()
    r.w_down.get()
    gather_g[0].finish()
    gather_g[1].finish()
    normalise(1)
    second[1].start()
    r.middle.put()
    second[0].finish()
    loop(4, hidden(0), 1, second[1].relay)
    first[0].close()
    grad_terms(0)
    third[0].start()
    second[1].finish()
    loop(4, hidden(1), 1, third[0].relay)
    first[1].close()
    grad_terms(1)
    third[1].start()
    loop(4, up_rows)
    grad_rows(0)
    fourth.start()
    third[1].relay()
    loop(4, down_rows)
    cores.start()
    fourth.relay()
    branch_terms(0)
    branch_terms(1)
    r.branch.put()
    cores.finish()
    r.half.put()
    grad_rows(1)
    fourth.finish()
    cores.close()
    fourth.close()
    for m in both:
        for step in (gather_x, gather_g, second, third):
            step[m].close()
        shifts[m].wait_send()
        there[m].close()
        back[m].close()
    tell_all().wait_send()


def backward_kernel(r):
    scale = TILE**-0.5
    links = Links(r.send, r.recv)
    ring = head_ring(links)
    plane = Plane(links)
    place, count = lax.axis_index("blk"), lax.axis_size("blk")
    both = range(2)
    gm = [r.gm0, r.gm1]
    core = place % 2
    others = [
        {"head": ring.chunk(k), "blk": place - core + c} for k in range(1, 4) for c in range(2)
    ]
    barrier = pltpu.get_barrier_semaphore()
    for device in others:
        pl.semaphore_signal(barrier, inc=1, device_id=device, device_id_type=MESH)
    greeted = len(others) + greet_blocks()
    r.gm1[0] = r.grad_middle[1].astype(BF)
    for ref in (r.near, r.sums, r.g_query, r.g_bias, r.g_scale, r.grad_kv, r.grad_state):
        ref[...] = jnp.zeros(ref.shape, F32)
    pl.semaphore_wait(barrier, greeted)
    fourth = Gather(ring, by_rows(r.gm1))
    fourth.start()
    mlp_sum = PlaneReduce(
        plane, r.half.ref, r.total_mlp.ref, r.mlp_mid, r.mlp_into, r.mlp_quarter, r.mlp_small
    )
    mlp_all = PlaneGather(plane, r.total_mlp.ref)
    qkv, kv_all, state_kv, stats = r.qkv.ref, r.kv_all.ref, r.state_kv.ref, r.stats.ref
    r.branch.get()
    branch = r.branch.ref
    outs = [Reduce(ring, by_rows(branch.at[m]), r.mids.at[m], r.intos.at[m]) for m in both]
    ends = [
        Reduce(ring, by_rows(branch.at[m]), r.mids.at[2 + m], r.intos.at[2 + m]) for m in both
    ]
    before = {"blk": lax.rem(place + count - 1, count)}
    shifts = [
        remote(r.early.at[m], r.later.at[m], r.s0.at[m], r.r0.at[m], before) for m in both
    ]
    there = [
        Exchange(r.grad_prior.at[m], r.moved.at[m], r.s1.at[m], r.r1.at[m], r.local.at[m])
        for m in both
    ]
    back = [
        Exchange(r.held.at[m], r.grad_after.at[m], r.s2.at[m], r.r2.at[m], r.local.at[2 + m])
        for m in both
    ]

    def own_chunk(qi):
        return lax.rem(qi + 4 - ring.me, 4)

    def attention_rows(m):
        part = nt(gm[m][...].reshape(512, 1024), r.w_out[...]).astype(BF)
        for k in range(4):
            r.grad_att[m, ring.row_chunk(k)] = part[k * TILE : (k + 1) * TILE]

    def attend(m):
        def step(qi):
            rows, window = tile_of(qi), window_of(qi)
            shut = closed_row(r.flags[0, m], qi)
            for h in range(2):
                k_cols, v_cols = head(h), head(h, base=256)
                sk_cols = slice(h * 256, h * 256 + TILE)
                sv_cols = slice(h * 256 + TILE, (h + 1) * 256)
                q = qkv[m, rows, head(h)]
                d = r.grad_att[m, rows, head(h)]
                level = stats[m, rows, 2 + h : 3 + h]
                token = jnp.exp(
                    nt(q, kv_all[m, window, k_cols]) * scale + (r.table.ref[h] + shut) - level
                )
                from_state = jnp.exp(nt(q, state_kv[m, :, sk_cols]) * scale - level)
                grad_token = nt(d, kv_all[m, window, v_cols])
                grad_from = nt(d, state_kv[m, :, sv_cols])
                attended = r.att_rel.ref[m, own_chunk(qi), :, head(h)]
                delta = jnp.sum(
                    d.astype(F32) * attended.astype(F32), axis=-1, keepdims=True
                )
                grad_token = token * (grad_token - delta)
                grad_from = from_state * (grad_from - delta)
                r.near[h, :, 0:128] += (
                    grad_token[:, 0:128] + grad_token[:, 128:256] + grad_token[:, 256:384]
                )
                r.near[h, :, 128:384] += grad_token[:, 384:640]
                token_low = grad_token.astype(BF)
                from_low = grad_from.astype(BF)
                grad_q = scale * (
                    nn(token_low, kv_all[m, window, k_cols]) + nn(from_low, state_kv[m, :, sk_cols])
                )
                r.dqkv[m, own_chunk(qi), :, head(h)] = grad_q.astype(BF)
                r.grad_kv[m, window, k_cols] += tn(token_low, q)
                r.grad_kv[m, window, v_cols] += tn(token.astype(BF), d)
                r.grad_state[m, :, sk_cols] += tn(from_low, q)
                r.grad_state[m, :, sv_cols] += tn(from_state.astype(BF), d)

        return step

    def pass_on(m):
        r.early[m, :, 0:256] = (scale * r.grad_kv[m, 0:512, 0:256]).astype(BF)
        r.early[m, :, 256:512] = r.grad_kv[m, 0:512, 256:512].astype(BF)
        for h in range(2):
            low = jnp.concatenate(
                [
                    (scale * r.grad_state[m, :, h * 256 : h * 256 + TILE]).astype(BF),
                    r.grad_state[m, :, h * 256 + TILE : (h + 1) * 256].astype(BF),
                ],
                1,
            )
            r.grad_prior[m, :, head(h)] = nt(low, r.state_proj.ref[h]).astype(BF)
            part = tn(r.prior.ref[m, :, head(h)], low)
            r.g_proj[h] = part if m == 0 else r.g_proj[h] + part
        there[m].start()
        shifts[m].start()

    def scan(m):
        def step(g, grad):
            for k in range(4):
                b = count - 1 - (g * 4 + k)
                rows = tile_of(b, 16)
                r.held[m, rows] = grad.astype(BF)
                u = r.across.ref[m, rows].astype(F32)
                forget = jax.nn.sigmoid(r.bias[...] + r.slope[...] * u)
                moved = r.moved[m, rows].astype(F32)
                grad = r.keeps.ref[b, m : m + 1] * (moved + forget * grad)
            return grad

        lax.fori_loop(0, count // 4, step, jnp.zeros((16, 256), F32))

    def bucket_sums():
        row = lax.broadcasted_iota(jnp.int32, (TILE, TILE), 0)
        col = lax.broadcasted_iota(jnp.int32, (TILE, TILE), 1)
        distance = [row - col + TILE, row - col]

        def per_head(h):
            for t in range(BUCKETS):
                total = jnp.zeros((1, TILE), F32)
                for part in range(2):
                    d = distance[part]
                    inside = d >= STARTS[t]
                    if t + 1 < BUCKETS:
                        inside = inside & (d < STARTS[t + 1])
                    values = r.near[h, :, TILE * (part + 1) : TILE * (part + 2)]
                    total = total + jnp.sum(
                        jnp.where(inside, values, 0.0), axis=0, keepdims=True
                    )
                if t + 1 == BUCKETS:
                    total = total + jnp.sum(r.near[h, :, 0:TILE], axis=0, keepdims=True)
                r.sums[t : t + 1] = total
            r.g_rel[h] = lax.dot_general(
                jnp.ones((8, TILE), F32),
                r.sums[...],
                (((1,), (1,)), ((), ())),
                precision=lax.Precision.HIGHEST,
                preferred_element_type=F32,
            )

        loop(2, per_head)

    def update_tile(m):
        def step(t):
            rows = tile_of(t)
            for h in range(2):
                cols, k_cols, v_cols = head(h), head(h, base=256), head(h, base=512)
                grad = r.grad_after[m, rows, cols].astype(F32)
                u = r.update.ref[m, rows, cols]
                inverse = inverse_rms(u)
                unit = u * inverse
                forget = jax.nn.sigmoid(r.bias[:, cols] + r.slope[:, cols] * unit)
                gate = grad * (r.prior.ref[m, rows, cols].astype(F32) - unit)
                gate = gate * forget * (1.0 - forget)
                r.g_bias[:, cols] += jnp.sum(gate, axis=0, keepdims=True)
                r.g_scale[:, cols] += jnp.sum(gate * unit, axis=0, keepdims=True)
                grad_unit = grad * (1.0 - forget) + gate * r.slope[:, cols]
                inner = jnp.mean(grad_unit * unit, axis=-1, keepdims=True)
                low = (inverse * (grad_unit - unit * inner)).astype(BF)
                q = r.state_query.ref[rows, cols]
                probs = jnp.exp(nt(q, qkv[m, :, k_cols]) * scale - stats[m, rows, h : h + 1])
                grad_probs = nt(low, qkv[m, :, v_cols])
                delta = jnp.sum(probs * grad_probs, axis=-1, keepdims=True)
                grad_scores = (probs * (grad_probs - delta)).astype(BF)
                r.g_query[rows, cols] += scale * nn(grad_scores, qkv[m, :, k_cols])
                r.grad_kv[m, 512:1024, cols] += tn(grad_scores, q)
                r.grad_kv[m, 512:1024, head(h, base=256)] += tn(probs.astype(BF), low)

        return step

    def finish_rows(m):
        def step(t):
            rows = tile_of(t)
            full = r.grad_kv[m, pl.ds(pl.multiple_of(512 + t * TILE, TILE), TILE)]
            extra = r.later[m, rows].astype(F32)
            at = own_chunk(t)
            r.dqkv[m, at, :, 256:512] = (scale * full[:, 0:256] + extra[:, 0:256]).astype(BF)
            r.dqkv[m, at, :, 512:768] = (full[:, 256:512] + extra[:, 256:512]).astype(BF)

        return step

    ones = jnp.ones((8, 256), BF)

    def gain_row(part, p, rows):
        product = part * r.w.ref[p, rows].astype(F32)
        high = product.astype(BF)
        low = (product - high.astype(F32)).astype(BF)
        return (nt(ones, high) + nt(ones, low))[0:1]

    def weight_part(p, rows):
        whole, cols = r.whole.ref, slice(p * 256, (p + 1) * 256)
        part = tn(whole[0, :, :, rows].reshape(512, 256), r.dqkv[0, :, :, cols].reshape(512, 256))
        return part + tn(
            whole[1, :, :, rows].reshape(512, 256), r.dqkv[1, :, :, cols].reshape(512, 256)
        )

    def early_weights(n):
        rows = tile_of(n, 256)
        part = tn(r.att_rel.ref[0].reshape(512, 256), gm[0][:, :, rows].reshape(512, 256))
        part = part + tn(r.att_rel.ref[1].reshape(512, 256), gm[1][:, :, rows].reshape(512, 256))
        r.parts_a[rows, 256:512] = part.astype(BF)
        part = weight_part(0, rows)
        r.parts_a[rows, 0:256] = part.astype(BF)
        r.small[pl.ds(n, 1)] = gain_row(part, 0, rows)

    def end_terms(m):
        def columns(n):
            cols = tile_of(n, 256)
            part = nt(r.dqkv[m, :, :, 0:256].reshape(512, 256), r.w.ref[0, cols])
            for p in (1, 2):
                some = r.dqkv[m, :, :, p * 256 : (p + 1) * 256].reshape(512, 256)
                part = part + nt(some, r.w.ref[p, cols])
            part = part.astype(BF)
            split_rows(branch, m, cols, part)

        loop(4, columns)

    def late_weights(n):
        rows = tile_of(n, 256)
        total = r.small[pl.ds(n, 1)]
        for p in (1, 2):
            part = weight_part(p, rows)
            r.parts_b[rows, (p - 1) * 256 : p * 256] = part.astype(BF)
            total = total + gain_row(part, p, rows)
        r.small[pl.ds(n, 1)] = total / r.attn_gain[:, rows]

    def end_rows(m):
        grad_normed = ends[m].finish()
        rows = r.x.ref[m].astype(F32)
        inverse = inverse_rms(rows)
        unit = rows * inverse
        scaled = grad_normed * r.attn_gain[...]
        inner = jnp.mean(scaled * unit, axis=-1, keepdims=True)
        r.grad_x.ref[m] = r.grad_middle[m] + inverse * (scaled - unit * inner)

    def share(i):
        k, c = i // 2 + 1, i % 2
        slot = (3 - k) * 2 + core
        return remote(
            r.parts_b.at[768:784, 512:768],
            r.others.at[slot],
            r.s3.at[i],
            r.r3.at[slot],
            others[i],
        )

    def got(i):
        return remote(
            r.parts_b.at[768:784, 512:768], r.others.at[i], r.s3.at[i], r.r3.at[i], others[i]
        )

    def add_gains():
        for i in range(6):
            got(i).wait_recv()
        total = r.others[0].astype(F32)
        for i in range(1, 6):
            total = total + r.others[i].astype(F32)
        row = lax.broadcasted_iota(jnp.int32, (16, 256), 0)
        total = jnp.where(row < 8, total, 0.0) * core.astype(F32)
        at = slice(256, 272), slice(512, 768)
        r.half_b[at] = (r.half_b[at].astype(F32) + total).astype(BF)

    core_a = CoreSum(plane, r.parts_a, r.half_a)
    sum_a = PlaneReduce(plane, r.half_a, r.total_a, r.a_mid, r.a_into, r.a_quarter, r.a_small)
    all_a = PlaneGather(plane, r.total_a)
    core_b = CoreSum(plane, r.parts_b, r.half_b)
    sum_b = PlaneReduce(plane, r.half_b, r.total_b, r.b_mid, r.b_into, r.b_quarter, r.b_small)
    all_b = PlaneGather(plane, r.total_b)

    attention_rows(0)
    fourth.relay()
    for part in (r.half, r.qkv, r.kv_all, r.state_kv, r.stats, r.table, r.att_rel):
        part.get()
    mlp_sum.advance()
    loop(4, attend(0))
    r.prior.get()
    r.state_proj.get()
    pass_on(0)
    mlp_sum.advance()
    fourth.finish()
    attention_rows(1)
    r.branch.get()
    outs[0].start()

    def between():
        mlp_sum.advance()
        outs[0].relay()
        outs[1].start()

    loop(4, attend(1), 1, between)
    pass_on(1)
    outs[1].relay()
    r.across.get()
    r.keeps.get()
    there[0].finish()
    scan(0)
    back[0].start()
    mlp_sum.advance()
    r.att_rel.get()
    r.w.get()
    r.whole.get()
    loop(4, early_weights)
    core_a.start()
    there[1].finish()
    scan(1)
    back[1].start()
    bucket_sums()
    core_a.finish()
    r.middle.get()
    for m in both:
        r.out.ref[m] = r.middle.ref[m] + outs[m].finish()
    r.out.put()
    r.update.get()
    r.state_query.get()
    for m in both:
        outs[m].close()
    back[0].finish()
    mlp_all.advance()
    loop(4, update_tile(0))
    shifts[0].wait_recv()
    loop(4, finish_rows(0))
    end_terms(0)
    ends[0].start()
    back[1].finish()
    mlp_all.advance()
    loop(4, update_tile(1))
    shifts[1].wait_recv()
    loop(4, finish_rows(1))
    ends[0].relay()
    mlp_all.advance()
    loop(4, late_weights)
    for n in range(4):
        r.small[4 + n : 5 + n] = r.g_mlp_gain[:, n * 256 : (n + 1) * 256]
    r.small[8:9] = r.g_bias[...]
    r.small[9:10] = r.g_scale[...]
    r.small[10:11] = r.g_rel[0, 0:1]
    r.small[11:12] = r.g_rel[1, 0:1]
    r.small[12:16] = jnp.zeros((4, 256), F32)
    r.parts_b[0:512, 512:768] = r.g_query[...].astype(BF)
    r.parts_b[512:768, 512:768] = r.g_proj[...].reshape(256, 256).astype(BF)
    r.parts_b[768:784, 512:768] = r.small[...].astype(BF)
    r.parts_b[784:1024, 512:768] = jnp.zeros((240, 256), BF)
    core_b.start()
    for i in range(6):
        share(i).start()
    sum_a.advance()
    mlp_all.advance()
    end_terms(1)
    ends[1].start()
    core_b.finish()
    add_gains()
    sum_b.advance()
    sum_a.advance()
    r.x.get()
    end_rows(0)
    sum_b.advance()
    ends[1].relay()
    mlp_all.advance()
    r.total_mlp.put()
    sum_a.advance()
    sum_b.advance()
    sum_a.advance()
    all_a.advance()
    sum_b.advance()
    all_b.advance()
    all_a.advance()
    all_b.advance()
    end_rows(1)
    r.grad_x.put()
    all_a.advance()
    all_b.advance()
    all_a.advance()
    all_b.advance()
    all_a.advance()
    all_b.advance()
    for step in (mlp_sum, mlp_all, core_a, sum_a, all_a, core_b, sum_b, all_b, fourth):
        step.close()
    for i in range(6):
        share(i).wait_send()
    for m in both:
        ends[m].close()
        shifts[m].wait_send()
        there[m].close()
        back[m].close()


class Late:
    def __init__(self, source, ref, sem):
        self.ref = ref
        self.copy = pltpu.make_async_copy(source, ref, sem)
        self.copy.start()
        self.open = True

    def get(self):
        if self.open:
            self.copy.wait()
            self.open = False


class Early:
    def __init__(self, target, ref, sem):
        self.ref = ref
        self.copy = pltpu.make_async_copy(ref, target, sem)
        self.sent = False

    def put(self):
        self.copy.start()
        self.sent = True


def call(kernel, name, number, now, late, small, outs, early, scratch, semaphores):
    anywhere = pl.BlockSpec(memory_space=pl.ANY)
    in_names = list(now) + list(small) + list(late)
    out_names = list(outs) + list(early)
    own = [a.shape for a in late.values()], [a.dtype for a in late.values()]
    buffers = list(zip(*own)) + list(early.values()) + list(scratch.values())

    def run(*refs):
        n, o = len(in_names), len(out_names)
        r = types.SimpleNamespace()
        held = refs[n + o : n + o + len(buffers)]
        rest = refs[n + o + len(buffers) :]
        fetch, store = rest[0], rest[1]
        for key, ref in zip(in_names[: len(now) + len(small)], refs):
            setattr(r, key, ref)
        for i, key in enumerate(late):
            setattr(r, key, Late(refs[len(now) + len(small) + i], held[i], fetch.at[i]))
        for key, ref in zip(outs, refs[n:]):
            setattr(r, key, ref)
        stores = []
        for i, key in enumerate(early):
            result = Early(refs[n + len(outs) + i], held[len(late) + i], store.at[i])
            setattr(r, key, result)
            stores.append(result)
        for key, ref in zip(scratch, held[len(late) + len(early) :]):
            setattr(r, key, ref)
        for key, ref in zip(semaphores, rest[2:]):
            setattr(r, key, ref)
        kernel(r)
        for result in stores:
            if not result.sent:
                result.put()
            result.copy.wait()

    shapes = list(outs.values()) + list(early.values())
    results = pl.pallas_call(
        run,
        out_shape=tuple(jax.ShapeDtypeStruct(shape, kind) for shape, kind in shapes),
        in_specs=[VMEM] * len(now) + [SMEM] * len(small) + [anywhere] * len(late),
        out_specs=tuple([VMEM] * len(outs) + [anywhere] * len(early)),
        scratch_shapes=[pltpu.VMEM(shape, kind) for shape, kind in buffers]
        + [sems(max(1, len(late))), sems(max(1, len(early)))]
        + list(semaphores.values()),
        compiler_params=pltpu.CompilerParams(
            collective_id=number, has_side_effects=True, vmem_limit_bytes=LIMIT
        ),
        name=name,
    )(*now.values(), *small.values(), *late.values())
    return dict(zip(out_names, results))


def finish_kernel(total_a, total_b, g_mlp, out, grad_x, state, *refs):
    results, (wide, low, some_a, some_b, rows_in, states_in, fetch, store) = refs[:14], refs[14:]
    places = [rows_in.at[0], rows_in.at[1], states_in]
    taken = [
        pltpu.make_async_copy(a, b, fetch.at[12 + i])
        for i, (a, b) in enumerate(zip((out, grad_x, state), places))
    ]
    passed = [
        pltpu.make_async_copy(a, b, store.at[i])
        for i, (a, b) in enumerate(zip(places, results[:3]))
    ]
    g_up, g_down, g_qkv, g_out, g_query, g_proj = results[3:9]
    attn_gain, mlp_gain, bias, slope, rel = results[9:]
    loads = []
    for n in range(4):
        rows = slice(n * 256, (n + 1) * 256)
        loads.append(
            [
                pltpu.make_async_copy(a.at[rows], b.at[rows], fetch.at[3 * n + i])
                for i, (a, b) in enumerate(((g_mlp, low), (total_a, some_a), (total_b, some_b)))
            ]
        )
    for copy in sum(loads, []) + taken:
        copy.start()
    stores = []

    def put(value, at, target):
        wide[at] = value.astype(F32)
        copy = pltpu.make_async_copy(wide.at[at], target, store.at[3 + len(stores)])
        copy.start()
        stores.append(copy)

    for n in range(4):
        rows = slice(n * 256, (n + 1) * 256)
        for copy in loads[n]:
            copy.wait()
        put(low[rows, 0:1024], (rows, slice(0, 1024)), g_up.at[rows])
        put(low[rows, 1024:2048], (rows, slice(1024, 2048)), g_down.at[rows])
        put(some_a[rows, 0:256], (rows, slice(2048, 2304)), g_qkv.at[0, rows])
        put(some_b[rows, 0:256], (rows, slice(2304, 2560)), g_qkv.at[1, rows])
        put(some_b[rows, 256:512], (rows, slice(2560, 2816)), g_qkv.at[2, rows])
        put(some_a[rows, 256:512], (rows, slice(2816, 3072)), g_out.at[:, rows])
    put(some_b[0:512, 512:768], (slice(0, 512), slice(3072, 3328)), g_query)
    put(some_b[512:768, 512:768], (slice(512, 768), slice(3072, 3328)), g_proj)
    for into, copy in zip(taken, passed):
        into.wait()
        copy.start()
    small = some_b[768:784, 512:768].astype(F32)
    attn_gain[...] = jnp.concatenate([small[n : n + 1] for n in range(4)], 1)
    mlp_gain[...] = jnp.concatenate([small[n : n + 1] for n in range(4, 8)], 1)
    bias[...] = small[8:9]
    slope[...] = small[9:10]
    rel[...] = small[10:12, 0:BUCKETS]
    for copy in stores + passed:
        copy.wait()


def sems(*shape):
    return pltpu.SemaphoreType.DMA(shape)


def body(
    tokens_in,
    grad_out,
    flags,
    attn_gain,
    mlp_gain,
    w_qkv,
    w_out,
    rel_bias,
    state_query,
    state_proj,
    forget_bias,
    forget_scale,
    w_up,
    w_down,
):
    micros, rows, width = tokens_in.shape
    block = rows * 4
    local = w_qkv.shape[2]
    heads = rel_bias.shape[1]
    states = state_query.shape[0]
    buckets = rel_bias.shape[0]
    count = lax.axis_size("blk")
    w = jnp.transpose(w_qkv, (1, 0, 2))
    small = dict(flags=jnp.transpose(flags))
    whole_shape = ((micros, 4, rows, width), BF)
    state_low = ((micros, states, local), BF)
    state_wide = ((micros, states, local), F32)
    rows_wide = ((micros, rows, width), F32)
    mlp_width = w_up.shape[1] + w_down.shape[1]
    exchange = dict(
        s0=sems(2),
        r0=sems(2),
        s1=sems(2),
        r1=sems(2),
        s2=sems(2),
        r2=sems(2),
        local=sems(4),
    )
    gates = dict(bias=forget_bias[None], slope=forget_scale[None])
    f = call(
        forward_kernel,
        "forward",
        1,
        dict(
            x=tokens_in,
            attn_gain=attn_gain[None],
            mlp_gain=mlp_gain[None],
            **gates,
        ),
        dict(
            w=w,
            state_query=state_query,
            g=grad_out,
            state_proj=state_proj,
            w_out=w_out,
            w_up=w_up,
            w_down=w_down,
        ),
        dict(rel=jnp.transpose(rel_bias), **small),
        dict(
            grad_middle=rows_wide,
            gm0=((4, rows, width), BF),
            g_gain=((1, width), F32),
        ),
        dict(
            whole=whole_shape,
            qkv=((micros, block, 3 * local), BF),
            kv_all=((micros, 2 * block, 2 * local), BF),
            state_kv=((micros, states, 2 * local), BF),
            prior=state_low,
            across=state_low,
            keeps=((count, 8, local), F32),
            update=state_wide,
            stats=((micros, block, TILE), F32),
            table=((heads, TILE, 5 * TILE), F32),
            state_after=state_wide,
            att_rel=((micros, 4, rows, local), BF),
            middle=rows_wide,
            branch=whole_shape,
            half=((512, mlp_width), BF),
        ),
        dict(
            whole_grad=whole_shape,
            own_keep=((count, 8, local), F32),
            unit_low=state_low,
            held=state_low,
            terms=whole_shape,
            whole_mlp=whole_shape,
            active=((micros, block, w_up.shape[1]), BF),
            grad_hidden=((micros, block, w_up.shape[1]), BF),
            mids=((4, 4, rows // 2, width), BF),
            intos=((4, 2, rows, width), BF),
            parts=((width, mlp_width), BF),
        ),
        dict(send=sems(80), recv=sems(80), s3=sems(1), r3=sems(1), **exchange),
    )
    b = call(
        backward_kernel,
        "backward",
        2,
        dict(
            gm0=f["gm0"],
            grad_middle=f["grad_middle"],
            w_out=w_out,
            attn_gain=attn_gain[None],
            g_mlp_gain=f["g_gain"],
            **gates,
        ),
        dict(
            half=f["half"],
            att_rel=f["att_rel"],
            qkv=f["qkv"],
            kv_all=f["kv_all"],
            state_kv=f["state_kv"],
            stats=f["stats"],
            table=f["table"],
            branch=f["branch"],
            prior=f["prior"],
            state_proj=state_proj,
            across=f["across"],
            keeps=f["keeps"],
            middle=f["middle"],
            update=f["update"],
            state_query=state_query,
            w=w,
            whole=f["whole"],
            x=tokens_in,
        ),
        small,
        dict(
            total_a=((width, 512), BF),
            total_b=((width, 768), BF),
        ),
        dict(out=rows_wide, grad_x=rows_wide, total_mlp=((width, mlp_width), BF)),
        dict(
            dqkv=((micros, 4, rows, 3 * local), BF),
            g_query=((states, local), F32),
            g_proj=(state_proj.shape, F32),
            g_rel=((heads, 8, local), F32),
            g_bias=((1, local), F32),
            g_scale=((1, local), F32),
            grad_att=((micros, block, local), BF),
            grad_kv=((micros, 2 * block, 2 * local), F32),
            grad_state=((micros, states, 2 * local), F32),
            early=((micros, block, 2 * local), BF),
            later=((micros, block, 2 * local), BF),
            grad_prior=state_low,
            moved=state_low,
            held=state_low,
            grad_after=state_low,
            near=((heads, TILE, 3 * TILE), F32),
            sums=((local, TILE), F32),
            mids=((4, 4, rows // 2, width), BF),
            intos=((4, 2, rows, width), BF),
            others=((6, 16, local), BF),
            small=((16, local), F32),
            gm1=((4, rows, width), BF),
            parts_a=((width, 512), BF),
            half_a=((512, 512), BF),
            parts_b=((width, 768), BF),
            half_b=((512, 768), BF),
            **reduce_scratch("mlp_", mlp_width),
            **reduce_scratch("a_", 512),
            **reduce_scratch("b_", 768),
        ),
        dict(send=sems(150), recv=sems(150), s3=sems(6), r3=sems(6), **exchange),
    )
    results = [
        rows_wide[0],
        rows_wide[0],
        state_wide[0],
        w_up.shape,
        w_down.shape,
        w.shape,
        w_out.shape,
        state_query.shape,
        (heads * state_proj.shape[1], local),
        (1, width),
        (1, width),
        (1, local),
        (1, local),
        (heads, buckets),
    ]
    anywhere = pl.BlockSpec(memory_space=pl.ANY)
    values = pl.pallas_call(
        finish_kernel,
        out_shape=tuple(jax.ShapeDtypeStruct(shape, F32) for shape in results),
        in_specs=[anywhere] * 6,
        out_specs=tuple([anywhere] * 9 + [VMEM] * 5),
        scratch_shapes=[
            pltpu.VMEM((width, 3328), F32),
            pltpu.VMEM((width, mlp_width), BF),
            pltpu.VMEM((width, 512), BF),
            pltpu.VMEM((width, 768), BF),
            pltpu.VMEM((2,) + rows_wide[0], F32),
            pltpu.VMEM(state_wide[0], F32),
            sems(15),
            sems(32),
        ],
        compiler_params=pltpu.CompilerParams(vmem_limit_bytes=LIMIT),
        name="finish",
    )(b["total_a"], b["total_b"], b["total_mlp"], b["out"], b["grad_x"], f["state_after"])
    out, grad_x, state_after, g_up, g_down, g_qkv, g_out, g_query, g_proj = values[:9]
    g_attn_gain, g_mlp_gain, g_bias, g_scale, g_rel = values[9:]
    return (
        out,
        grad_x,
        state_after[:, None],
        g_attn_gain[0],
        g_mlp_gain[0],
        jnp.transpose(g_qkv, (1, 0, 2)),
        g_out,
        jnp.transpose(g_rel),
        g_query,
        g_proj.reshape(state_proj.shape),
        g_bias[0],
        g_scale[0],
        g_up,
        g_down,
    )


def solution(mesh):
    return jax.shard_map(
        body,
        mesh=mesh,
        in_specs=(
            P(None, ("blk", "head"), None),
            P(None, ("blk", "head"), None),
            P(None, "blk"),
            P(),
            P(),
            P(None, None, "head"),
            P("head", None),
            P(None, "head"),
            P(None, "head"),
            P("head", None, None),
            P("head"),
            P("head"),
            P(None, "head"),
            P("head", None),
        ),
        out_specs=(
            P(None, ("blk", "head"), None),
            P(None, ("blk", "head"), None),
            P(None, "blk", None, "head"),
            P(),
            P(),
            P(None, None, "head"),
            P("head", None),
            P(None, "head"),
            P(None, "head"),
            P("head", None, None),
            P("head"),
            P("head"),
            P(None, "head"),
            P("head", None),
        ),
        check_vma=False,
    )
```
